32 devices in a mesh: pipe: 4 (over x, core), dp: 8 (over z, y).
Axes of the slice: x: 2, y: 2, z: 4, core: 2. Of those that a mesh axis runs over, the one named last changes fastest.
Arguments:
- text_embed: bfloat16 [256, 64, 768], P(('pipe', 'dp')), may hold values from -9 to 9
- image_feats: bfloat16 [256, 145, 1024], P(('pipe', 'dp')), may hold values from -6 to 6
- caption_len: int32 [256], P(('pipe', 'dp')), may hold values from 8 to 31
- phrase_len: int32 [256, 6], P(('pipe', 'dp')), may hold values from 1 to 8
- box_count: int32 [256], P(('pipe', 'dp')), may hold values from 0 to 6
- patch_mask: int32 [256, 145], P(('pipe', 'dp')), may hold values 0 or 1
- attn_qkv: bfloat16 [1536, 2304], P('pipe', 'dp'), may hold values from -0.21875 to 0.21875
- attn_out: bfloat16 [1536, 768], P('pipe', 'dp'), may hold values from -1.25 to 1.25
- ffn_up: bfloat16 [1536, 3072], P('pipe', 'dp'), may hold values from -0.21875 to 0.21875
- ffn_down: bfloat16 [6144, 768], P('pipe', 'dp'), may hold values from -0.109375 to 0.109375
- layer_vectors: bfloat16 [24, 768], P('pipe', 'dp'), may hold values from -1.203125 to 1.3984375, as said below
- cross_query: bfloat16 [768, 768], P(('pipe', 'dp')), may hold values from -0.21875 to 0.21875
- cross_kv: bfloat16 [1024, 1536], P(('pipe', 'dp')), may hold values from -0.1875 to 0.1875
- cross_out: bfloat16 [768, 768], P(('pipe', 'dp')), may hold values from -2 to 2
- cross_vectors: bfloat16 [768, 5], P(('pipe', 'dp')), may hold values from -1.203125 to 1.3984375, as said below
- cotangent: bfloat16 [256, 64, 768], P(('pipe', 'dp')), may hold values from -6 to 6
Outputs:
- joined: float32 [256, 64, 768], P(('pipe', 'dp'))
- embed_grad: float32 [256, 64, 768], P(('pipe', 'dp'))
- grad_attn_qkv: float32 [1536, 2304], P('pipe', 'dp')
- grad_attn_out: float32 [1536, 768], P('pipe', 'dp')
- grad_ffn_up: float32 [1536, 3072], P('pipe', 'dp')
- grad_ffn_down: float32 [6144, 768], P('pipe', 'dp')
- grad_layer_vectors: float32 [24, 768], P('pipe', 'dp')
- grad_cross_query: float32 [768, 768], P(('pipe', 'dp'))
- grad_cross_kv: float32 [1024, 1536], P(('pipe', 'dp'))
- grad_cross_out: float32 [768, 768], P(('pipe', 'dp'))
- grad_cross_vectors: float32 [768, 5], P(('pipe', 'dp'))
The draws below stay inside these ranges and needn't reach their ends.
Inputs may be any that keep to these rules, and one draw needn't show every extreme that they name: `layer_vectors`: norm gains near one and biases of the two layers. `cross_vectors`: biases and a norm gain of the cross-attention.
All inputs are finite; a program needn't handle non-finite values. No bound on the sum of `patch_mask` on one device may be relied on, other than what follows from the above.
Results may differ from the reference program's by a relative error of at most 0.035.
Values may be sent and summed in bfloat16 or wider, within the bound.
No kernel may reach another device: no remote copies, remote signals or barrier semaphores. Data moves between devices by JAX's collectives and lax.ppermute only.
A program may use at most 448 MiB of HBM per device.

```python
import math
import jax
import jax.numpy as jnp
import numpy as np
from jax import lax

D = 768
HEADS = 12
FF = 3072
DI = 1024
PATCHES = 145
L = 64
MAXBOX = 6
SAMPLES = 256


def draw_layer_vectors(key, part):
    key = jax.random.fold_in(key, 17)
    noise_key, place_key = jax.random.split(key)
    noise = jnp.clip(jax.random.normal(noise_key, (24, D), jnp.float32), -4.0, 4.0)
    columns = jax.random.randint(place_key, (2,), 0, D)
    row_index = lax.broadcasted_iota(jnp.int32, (24, D), 0)
    column_index = lax.broadcasted_iota(jnp.int32, (24, D), 1)
    noise = jnp.where((row_index == 3) & (column_index == columns[0]), 4.0, noise)
    noise = jnp.where((row_index == 0) & (column_index == columns[1]), -4.0, noise)
    row_kind = row_index % 12
    gain_rows = (row_kind == 3) | (row_kind == 6)
    values = jnp.where(gain_rows, 1.0 + 0.1 * noise, 0.3 * noise)
    return values.astype(jnp.bfloat16)


def draw_cross_vectors(key, part):
    key = jax.random.fold_in(key, 29)
    noise = jnp.clip(jax.random.normal(key, (D, 5), jnp.float32), -4.0, 4.0)
    column_kind = lax.broadcasted_iota(jnp.int32, (D, 5), 1)
    values = jnp.where(column_kind == 3, 1.0 + 0.1 * noise, 0.3 * noise)
    return values.astype(jnp.bfloat16)


def place_ends(result, stream_key, smallest, top_value):
    longest = result.shape.index(max(result.shape))
    spots = []
    for shift in (0, 1):
        where = [jax.random.randint(jax.random.fold_in(stream_key, axis), (), 0, length) for axis, length in enumerate(result.shape)]
        where[longest] = (where[longest] + shift) % result.shape[longest]
        spots.append(tuple(where))
    return result.at[spots[0]].set(smallest).at[spots[1]].set(top_value)


def level_of(key, shape, pieces, low, top_value):
    def one(position, shards_of):
        steps = jax.random.uniform(jax.random.fold_in(jax.random.fold_in(key, 6), position), (shards_of,), jnp.float32, low / len(pieces), top_value / len(pieces))
        return jnp.repeat(jnp.exp(steps), shape[position] // shards_of).reshape((-1,) + (1,) * (len(shape) - position - 1))

    level = one(*pieces[0])
    for cut in pieces[1:]:
        level = level * one(*cut)
    return level


def rank_bounds(amount, slope):
    weights = [(1 << 20) // math.isqrt(grade ** slope) + 1 for grade in range(1, amount + 1)]
    deviation = 1 + sum(weights) // (1 << 30)
    return np.cumsum(np.array([max(1, weight // deviation) for weight in weights]))


def ranked_ids(own_key, shape, count, skew):
    listing = rank_bounds(count, skew)
    ticket = jax.random.randint(jax.random.fold_in(own_key, 1), shape, 0, int(listing[count - 1]))
    rank = jnp.searchsorted(jnp.asarray(listing, jnp.int32), ticket, side="right")
    return jax.random.permutation(jax.random.fold_in(own_key, 2), count)[rank].astype(jnp.int32)


def gaussian(key, dims, deviation, limit, shards=(), kind=jnp.bfloat16):
    loudness = level_of(key, dims, shards, -0.22, 0.18) if shards else 1.0
    drawn = jax.random.normal(key, dims, jnp.float32) * deviation * loudness
    return jnp.minimum(jnp.maximum(drawn, -limit), limit).astype(kind)


def setup_inputs(seed: int = 0) -> dict:
    key_of = jax.random.split(jax.random.key(seed), 17)
    text_embed = gaussian(key_of[0], (SAMPLES, L, D), 1.5, 9.0, ((0, 32),))
    image_feats = gaussian(key_of[1], (SAMPLES, PATCHES, DI), 1.0, 6.0, ((0, 32),))
    caption_len = place_ends(jax.random.randint(key_of[2], (SAMPLES,), L // 8, L // 2), jax.random.fold_in(key_of[2], 1), L // 8, (L // 2) - 1).astype(jnp.int32)
    phrase_len = place_ends(jax.random.randint(key_of[3], (SAMPLES, MAXBOX), 1, L // 8 + 1), jax.random.fold_in(key_of[3], 1), 1, (L // 8 + 1) - 1).astype(jnp.int32)
    box_count = place_ends(ranked_ids(key_of[4], (SAMPLES,), MAXBOX + 1, 2), jax.random.fold_in(key_of[4], 3), 0, MAXBOX).astype(jnp.int32)
    patch_mask = place_ends((jax.random.randint(key_of[5], (SAMPLES, PATCHES), 0, 4) < 3).astype(jnp.int32), jax.random.fold_in(key_of[5], 1), 0, 1)
    attn_qkv = gaussian(key_of[6], (2 * D, 3 * D), D ** -0.5, 0.21875, ((0, 4), (1, 8)))
    attn_out = gaussian(key_of[7], (2 * D, D), (D * 2 // L) ** -0.5, 1.25, ((0, 4), (1, 8)))
    ffn_up = gaussian(key_of[8], (2 * D, FF), D ** -0.5, 0.21875, ((0, 4), (1, 8)))
    ffn_down = gaussian(key_of[9], (2 * FF, D), FF ** -0.5, 0.109375, ((0, 4), (1, 8)))
    layer_vectors = draw_layer_vectors(jax.random.fold_in(key_of[16], 71), 0)
    cross_query = gaussian(key_of[11], (D, D), D ** -0.5, 0.21875, ((0, 32),))
    cross_kv = gaussian(key_of[12], (DI, 2 * D), DI ** -0.5, 0.1875, ((0, 32),))
    cross_out = gaussian(key_of[13], (D, D), (D * 4 // (3 * PATCHES)) ** -0.5, 2.0, ((0, 32),))
    cross_vectors = draw_cross_vectors(jax.random.fold_in(key_of[16], 71), 0)
    cotangent = gaussian(key_of[15], (SAMPLES, L, D), 1.0, 6.0, ((0, 32),))
    return dict(text_embed=text_embed, image_feats=image_feats, caption_len=caption_len, phrase_len=phrase_len, box_count=box_count, patch_mask=patch_mask, attn_qkv=attn_qkv, attn_out=attn_out, ffn_up=ffn_up, ffn_down=ffn_down, layer_vectors=layer_vectors, cross_query=cross_query, cross_kv=cross_kv, cross_out=cross_out, cross_vectors=cross_vectors, cotangent=cotangent)


@jax.custom_vjp
def low(v):
    return lax.optimization_barrier(v.astype(jnp.bfloat16)).astype(jnp.float32)

@jax.custom_vjp
def low_back(v):
    return v

def low_keep(v):
    return (low(v), None)

def low_pass(kept, grad):
    return (grad,)

def back_keep(v):
    return (v, None)

def back_low(kept, grad):
    return (low(grad),)
low.defvjp(low_keep, low_pass)
low_back.defvjp(back_keep, back_low)
NORM_EPS = 1e-12
MASK_FILL = -1000000000.0

def project(inputs, weight):
    return jnp.einsum('...k,kn->...n', inputs, weight, precision=lax.Precision.HIGHEST)

def layer_norm(summed, gain, offset):
    center = summed - lax.optimization_barrier(jnp.mean(summed, axis=-1, keepdims=True))
    spread = lax.optimization_barrier(jnp.mean(center * center, axis=-1, keepdims=True))
    return center * lax.rsqrt(spread + NORM_EPS) * gain + offset

def attend(queries, keys, values, key_keep):
    samples, query_rows, model_width = queries.shape
    head_size = model_width // HEADS
    query_heads = queries.reshape(samples, query_rows, HEADS, head_size)
    key_heads = keys.reshape(samples, keys.shape[1], HEADS, head_size)
    value_heads = values.reshape(samples, values.shape[1], HEADS, head_size)
    scores = jnp.einsum('sqhd,skhd->shqk', query_heads, key_heads, precision=lax.Precision.HIGHEST) * head_size ** (-0.5)
    scores = low_back(scores)
    scores = jnp.where(key_keep[:, None, None, :] > 0, scores, MASK_FILL)
    row_top = lax.optimization_barrier(jnp.max(scores, axis=-1, keepdims=True))
    exponent = jnp.exp(scores - row_top)
    attention = exponent / lax.optimization_barrier(jnp.sum(exponent, axis=-1, keepdims=True))
    mixed = jnp.einsum('shqk,skhd->sqhd', low(attention), value_heads, precision=lax.Precision.HIGHEST)
    return mixed.reshape(samples, query_rows, model_width)

def self_block(state, key_keep, vectors, qkv_weight, out_weight):
    model_width = state.shape[-1]
    zero_bias = jnp.zeros((model_width,), state.dtype)
    projected = project(low(state), qkv_weight) + jnp.concatenate([vectors[0], zero_bias, vectors[1]])
    projected = low(low_back(projected))
    mixed = attend(projected[..., :model_width], projected[..., model_width:2 * model_width], projected[..., 2 * model_width:], key_keep)
    mixed = low(low_back(mixed))
    branch = low_back(project(mixed, out_weight) + vectors[2])
    return layer_norm(state + branch, vectors[3], vectors[4])

def cross_block(state, image, patch_keep, cross_vec, query_weight, kv_weight, out_weight):
    model_width = state.shape[-1]
    zero_bias = jnp.zeros((model_width,), state.dtype)
    queries = low(low_back(project(low(state), query_weight) + cross_vec[:, 0]))
    kv_pairs = low(low_back(project(image, kv_weight) + jnp.concatenate([zero_bias, cross_vec[:, 1]])))
    mixed = low(low_back(attend(queries, kv_pairs[..., :model_width], kv_pairs[..., model_width:], patch_keep)))
    branch = low_back(project(mixed, out_weight) + cross_vec[:, 2])
    return layer_norm(state + branch, cross_vec[:, 3], cross_vec[:, 4])

def feed_block(state, vectors, up_weight, down_weight):
    hidden = low_back(project(low(state), up_weight) + vectors[8:12].reshape(-1))
    activated = low(jax.nn.gelu(hidden, approximate=False))
    branch = low_back(project(activated, down_weight) + vectors[5])
    return layer_norm(state + branch, vectors[6], vectors[7])

def two_layers(params, embed, image, text_keep, patch_keep):
    qkv_all, out_all, up_all, down_all, vector_all, cross_q, cross_pairs, cross_o, cross_vec = params
    text_vectors = vector_all[:12]
    joining_vectors = vector_all[12:]
    text_state = self_block(embed, text_keep, text_vectors, qkv_all[:D], out_all[:D])
    text_state = feed_block(text_state, text_vectors, up_all[:D], down_all[:FF])
    passed = low(low_back(text_state))
    joining_state = self_block(passed, text_keep, joining_vectors, qkv_all[D:], out_all[D:])
    joining_state = cross_block(joining_state, image, patch_keep, cross_vec, cross_q, cross_pairs, cross_o)
    return feed_block(joining_state, joining_vectors, up_all[D:], down_all[FF:])

def reference(text_embed, image_feats, caption_len, phrase_len, box_count, patch_mask, attn_qkv, attn_out, ffn_up, ffn_down, layer_vectors, cross_query, cross_kv, cross_out, cross_vectors, cotangent):
    slots = jnp.arange(MAXBOX, dtype=jnp.int32)
    phrase_total = lax.optimization_barrier(jnp.sum(jnp.where(slots[None, :] < box_count[:, None], phrase_len, 0), axis=1)).astype(jnp.int32)
    lengths = jnp.minimum(caption_len + phrase_total, L).astype(jnp.int32)
    positions = jnp.arange(L, dtype=jnp.int32)
    text_keep = (positions[None, :] < lengths[:, None]).astype(jnp.float32)
    first_patch = (jnp.arange(PATCHES, dtype=jnp.int32) == 0).astype(jnp.int32)
    patch_keep = jnp.maximum(patch_mask, first_patch[None, :]).astype(jnp.float32)
    params = tuple((weight.astype(jnp.float32) for weight in (attn_qkv, attn_out, ffn_up, ffn_down, layer_vectors, cross_query, cross_kv, cross_out, cross_vectors)))
    group_size = math.gcd(SAMPLES, max(1, 4096 // L))
    group_count = SAMPLES // group_size

    def grouped(array):
        return array.reshape((group_count, group_size) + array.shape[1:])
    image_groups = grouped(image_feats.astype(jnp.float32))
    keep_groups = grouped(text_keep)
    patch_groups = grouped(patch_keep)

    def whole(weights, embed_groups):

        def group_step(group_items):
            return two_layers(weights, group_items[0], group_items[1], group_items[2], group_items[3])
        return lax.map(jax.checkpoint(group_step), (embed_groups, image_groups, keep_groups, patch_groups))
    joined, pull = jax.vjp(whole, params, grouped(text_embed.astype(jnp.float32)))
    grad_params, grad_embed = pull(grouped(cotangent.astype(jnp.float32)))
    return (joined.reshape(SAMPLES, L, D), grad_embed.reshape(SAMPLES, L, D), grad_params[0], grad_params[1], grad_params[2], grad_params[3], grad_params[4], grad_params[5], grad_params[6], grad_params[7], grad_params[8])
```

```python
from functools import partial

import jax
import jax.numpy as jnp
import numpy as np
from jax import lax
from jax.sharding import PartitionSpec as P

HEADS = 12


NORM_EPS = 1e-12
MASK_FILL = -1000000000.0


def rows_product(inputs, weight):
    flat = inputs.reshape(-1, inputs.shape[-1])
    result = jnp.dot(flat, weight, preferred_element_type=jnp.float32)
    return result.reshape(inputs.shape[:-1] + (weight.shape[1],))


def input_grad(grads, weight):
    flat = grads.reshape(-1, grads.shape[-1])
    result = lax.dot_general(
        flat, weight, (((1,), (1,)), ((), ())), preferred_element_type=jnp.float32
    )
    return result.reshape(grads.shape[:-1] + (weight.shape[0],))


def row_total(grads):
    return jnp.sum(grads.reshape(-1, grads.shape[-1]).astype(jnp.float32), axis=0)


def norm_forward(summed, gain, offset):
    center = summed - jnp.mean(summed, axis=-1, keepdims=True)
    scale_row = lax.rsqrt(jnp.mean(center * center, axis=-1, keepdims=True) + NORM_EPS)
    normed = center * scale_row
    return (normed * gain + offset, (normed, scale_row))


def norm_backward(grad_output, norm_saved, gain):
    normed, scale_row = norm_saved
    flat_grad = grad_output.reshape(-1, grad_output.shape[-1])
    grad_gain = jnp.sum(flat_grad * normed.reshape(flat_grad.shape), axis=0)
    grad_offset = jnp.sum(flat_grad, axis=0)
    scaled = grad_output * gain
    grad_input = scale_row * (
        scaled
        - jnp.mean(scaled, axis=-1, keepdims=True)
        - normed * jnp.mean(scaled * normed, axis=-1, keepdims=True)
    )
    return (grad_input, grad_gain, grad_offset)


def attention_forward(queries, keys, values, key_keep, head_count):
    samples, query_rows, model_width = queries.shape
    head_size = model_width // head_count
    query_heads = queries.reshape(samples, query_rows, head_count, head_size)
    key_heads = keys.reshape(samples, keys.shape[1], head_count, head_size)
    value_heads = values.reshape(samples, values.shape[1], head_count, head_size)
    scores = jnp.einsum(
        "sqhd,skhd->shqk", query_heads, key_heads, preferred_element_type=jnp.float32
    ) * head_size ** (-0.5)
    scores = jnp.where(key_keep[:, None, None, :] > 0, scores, MASK_FILL)
    row_top = jnp.max(scores, axis=-1, keepdims=True)
    exponent = jnp.exp(scores - row_top)
    attention = exponent / jnp.sum(exponent, axis=-1, keepdims=True)
    mixed = jnp.einsum(
        "shqk,skhd->sqhd",
        attention.astype(jnp.bfloat16),
        value_heads,
        preferred_element_type=jnp.float32,
    )
    return (mixed.reshape(samples, query_rows, model_width), attention)


def attention_backward(grad_mixed, attention, queries, keys, values, head_count):
    samples, query_rows, model_width = queries.shape
    key_rows = keys.shape[1]
    head_size = model_width // head_count
    query_heads = queries.reshape(samples, query_rows, head_count, head_size)
    key_heads = keys.reshape(samples, key_rows, head_count, head_size)
    value_heads = values.reshape(samples, key_rows, head_count, head_size)
    grad_heads = grad_mixed.reshape(samples, query_rows, head_count, head_size)
    grad_values = jnp.einsum(
        "shqk,sqhd->skhd",
        attention.astype(jnp.bfloat16),
        grad_heads,
        preferred_element_type=jnp.float32,
    )
    grad_attention = jnp.einsum(
        "sqhd,skhd->shqk", grad_heads, value_heads, preferred_element_type=jnp.float32
    )
    grad_scores = attention * (
        grad_attention - jnp.sum(grad_attention * attention, axis=-1, keepdims=True)
    )
    grad_scores = grad_scores.astype(jnp.bfloat16)
    grad_queries = jnp.einsum(
        "shqk,skhd->sqhd", grad_scores, key_heads, preferred_element_type=jnp.float32
    ) * head_size ** (-0.5)
    grad_keys = jnp.einsum(
        "shqk,sqhd->skhd", grad_scores, query_heads, preferred_element_type=jnp.float32
    ) * head_size ** (-0.5)
    return (
        grad_queries.reshape(samples, query_rows, model_width),
        grad_keys.reshape(samples, key_rows, model_width),
        grad_values.reshape(samples, key_rows, model_width),
    )


def mm(x, wt):
    flat = x.reshape(-1, x.shape[-1])
    y = lax.dot_general(flat, wt, (((1,), (1,)), ((), ())), preferred_element_type=jnp.float32)
    return y.reshape(x.shape[:-1] + (wt.shape[0],))


def mm_back(dy, wt):
    flat = dy.reshape(-1, dy.shape[-1])
    dx = jnp.dot(flat, wt, preferred_element_type=jnp.float32)
    return dx.reshape(dy.shape[:-1] + (wt.shape[1],))


def wgrad(dy, x):
    return lax.dot_general(
        dy.reshape(-1, dy.shape[-1]),
        x.reshape(-1, x.shape[-1]),
        (((0,), (0,)), ((), ())),
        preferred_element_type=jnp.float32,
    ).astype(jnp.bfloat16)


def self_forward(state, key_keep, vec, qkv, out):
    width = state.shape[-1]
    low = state.astype(jnp.bfloat16)
    bias = jnp.concatenate([vec[0], jnp.zeros((width,), jnp.float32), vec[1]])
    proj = (mm(low, qkv) + bias).astype(jnp.bfloat16)
    mixed, attention = attention_forward(
        proj[..., :width], proj[..., width : 2 * width], proj[..., 2 * width :], key_keep, HEADS
    )
    mixed = mixed.astype(jnp.bfloat16)
    y, saved = norm_forward(state + (mm(mixed, out) + vec[2]), vec[3], vec[4])
    return y, (low, proj, attention, mixed, saved)


def self_backward(dy, saved, vec, qkv, out):
    low, proj, attention, mixed, norm_saved = saved
    width = low.shape[-1]
    du, d_gain, d_offset = norm_backward(dy, norm_saved, vec[3])
    db = du.astype(jnp.bfloat16)
    g_out = wgrad(db, mixed)
    dmixed = mm_back(db, out).astype(jnp.bfloat16)
    dq, dk, dv = attention_backward(
        dmixed, attention, proj[..., :width], proj[..., width : 2 * width], proj[..., 2 * width :], HEADS
    )
    dproj = jnp.concatenate([dq, dk, dv], axis=-1).astype(jnp.bfloat16)
    g_qkv = wgrad(dproj, low)
    totals = row_total(dproj)
    dx = du + mm_back(dproj, qkv)
    g_vec = [totals[:width], totals[2 * width :], row_total(db), d_gain, d_offset]
    return dx, g_qkv, g_out, g_vec


def cross_forward(state, image, patch_keep, vec, wq, wkv, wo):
    width = state.shape[-1]
    low = state.astype(jnp.bfloat16)
    q = (rows_product(low, wq) + vec[0]).astype(jnp.bfloat16)
    kv_bias = jnp.concatenate([jnp.zeros((width,), jnp.float32), vec[1]])
    kv = (rows_product(image, wkv) + kv_bias).astype(jnp.bfloat16)
    mixed, attention = attention_forward(q, kv[..., :width], kv[..., width:], patch_keep, HEADS)
    mixed = mixed.astype(jnp.bfloat16)
    y, saved = norm_forward(state + (rows_product(mixed, wo) + vec[2]), vec[3], vec[4])
    return y, (low, q, kv, attention, mixed, saved)


def cross_backward(dy, saved, image, vec, wq, wo):
    low, q, kv, attention, mixed, norm_saved = saved
    width = low.shape[-1]
    du, d_gain, d_offset = norm_backward(dy, norm_saved, vec[3])
    db = du.astype(jnp.bfloat16)
    g_out = wgrad(mixed, db)
    dmixed = input_grad(db, wo).astype(jnp.bfloat16)
    dq, dk, dv = attention_backward(dmixed, attention, q, kv[..., :width], kv[..., width:], HEADS)
    dq = dq.astype(jnp.bfloat16)
    dkv = jnp.concatenate([dk, dv], axis=-1).astype(jnp.bfloat16)
    g_q = wgrad(low, dq)
    g_kv = wgrad(image, dkv)
    g_vec = [row_total(dq), row_total(dkv)[width:], row_total(db), d_gain, d_offset]
    return du + input_grad(dq, wq), g_q, g_kv, g_out, g_vec


def gelu_pair(h):
    value, pull = jax.vjp(partial(jax.nn.gelu, approximate=False), h)
    return value.astype(jnp.bfloat16), pull(jnp.ones_like(h))[0].astype(jnp.bfloat16)


def feed_forward(state, vec, up, down):
    low = state.astype(jnp.bfloat16)
    act, slope = gelu_pair(mm(low, up) + vec[8:12].reshape(-1))
    y, saved = norm_forward(state + (mm(act, down) + vec[5]), vec[6], vec[7])
    return y, (low, act, slope, saved)


def feed_backward(dy, saved, vec, up, down):
    low, act, slope, norm_saved = saved
    du, d_gain, d_offset = norm_backward(dy, norm_saved, vec[6])
    db = du.astype(jnp.bfloat16)
    g_down = wgrad(db, act)
    dh = (mm_back(db, down) * slope).astype(jnp.bfloat16)
    g_up = wgrad(dh, low)
    dx = du + mm_back(dh, up)
    g_vec = [row_total(db), d_gain, d_offset, row_total(dh)]
    return dx, g_up, g_down, g_vec


def lane_slices(a, lanes):
    return jnp.concatenate([a[:, i : i + lanes] for i in range(0, a.shape[1], lanes)], axis=0)


def lane_join(a, count):
    rows = a.shape[-2] // count
    return jnp.concatenate([a[..., i * rows : (i + 1) * rows, :] for i in range(count)], axis=-1)


def pad_lanes(a, lanes):
    return jnp.pad(a, ((0, 0), (0, lanes - a.shape[1])))


def on_device(
    text_embed,
    image_feats,
    caption_len,
    phrase_len,
    box_count,
    patch_mask,
    attn_qkv,
    attn_out,
    ffn_up,
    ffn_down,
    layer_vectors,
    cross_query,
    cross_kv,
    cross_out,
    cross_vectors,
    cotangent,
):
    n_pipe, n_dp = lax.axis_size("pipe"), lax.axis_size("dp")
    half = n_pipe // 2
    width = text_embed.shape[-1]
    text_rows = text_embed.shape[1]
    lanes = attn_qkv.shape[0]
    everyone = ("pipe", "dp")
    slots = jnp.arange(phrase_len.shape[1], dtype=jnp.int32)
    phrase_total = jnp.sum(jnp.where(slots[None, :] < box_count[:, None], phrase_len, 0), axis=1)
    lengths = jnp.minimum(caption_len + phrase_total, text_rows)
    text_keep = (jnp.arange(text_rows, dtype=jnp.int32)[None, :] < lengths[:, None]).astype(jnp.float32)
    first_patch = (jnp.arange(patch_mask.shape[1], dtype=jnp.int32) == 0).astype(jnp.int32)
    patch_keep = jnp.maximum(patch_mask, first_patch[None, :]).astype(jnp.float32)

    k_down = ffn_down.shape[0] // lanes
    k_q = width // lanes
    k_kv = cross_kv.shape[1] // lanes
    parts = [
        attn_qkv.T,
        attn_out.T,
        ffn_up.T,
        lane_slices(ffn_down.T, lanes),
        lane_slices(cross_query, lanes),
        lane_slices(cross_kv, lanes),
        lane_slices(cross_out, lanes),
        pad_lanes(layer_vectors, lanes),
        pad_lanes(cross_vectors.T, lanes),
    ]
    counts = [p.shape[0] for p in parts]
    ends = np.cumsum(counts)
    pack = jnp.concatenate(parts, axis=0)
    whole = lax.all_gather(pack, everyone, axis=0, tiled=False)
    whole = whole.reshape(n_pipe, n_dp, pack.shape[0], lanes)

    def part(i):
        return whole[:, :, ends[i] - counts[i] : ends[i]]

    def section(piece, layer):
        piece = piece[layer * half : (layer + 1) * half]
        piece = jnp.moveaxis(piece, 0, 2)
        return piece.reshape(n_dp * piece.shape[1], half * piece.shape[-1])

    def section_vectors(layer):
        v = part(7)[layer * half : (layer + 1) * half, :, :, : layer_vectors.shape[1]]
        return jnp.moveaxis(v, 1, 2).reshape(12, width).astype(jnp.float32)

    layers = []
    for layer in range(2):
        layers.append(
            (
                section(part(0), layer),
                section(part(1), layer),
                section(part(2), layer),
                section(lane_join(part(3), k_down), layer),
                section_vectors(layer),
            )
        )
    wq = lane_join(part(4), k_q).reshape(width, width)
    wkv = lane_join(part(5), k_kv).reshape(-1, 2 * width)
    wo = lane_join(part(6), k_q).reshape(width, width)
    cvec = part(8)[..., : cross_vectors.shape[0]].reshape(n_pipe * n_dp, 5, -1)
    cvec = jnp.moveaxis(cvec, 1, 0).reshape(5, width).astype(jnp.float32)

    qkv, out, up, down, vec = layers[0]
    state, s_self = self_forward(text_embed.astype(jnp.float32), text_keep, vec, qkv, out)
    state, s_feed = feed_forward(state, vec, up, down)
    passed = state.astype(jnp.bfloat16).astype(jnp.float32)
    qkv2, out2, up2, down2, vec2 = layers[1]
    state, s_self2 = self_forward(passed, text_keep, vec2, qkv2, out2)
    state, s_cross = cross_forward(state, image_feats, patch_keep, cvec, wq, wkv, wo)
    joined, s_feed2 = feed_forward(state, vec2, up2, down2)

    grad = cotangent.astype(jnp.float32)
    grad, g_up2, g_down2, v_feed2 = feed_backward(grad, s_feed2, vec2, up2, down2)
    grad, g_cq, g_ckv, g_co, g_cvec = cross_backward(grad, s_cross, image_feats, cvec, wq, wo)
    grad, g_qkv2, g_out2, v_self2 = self_backward(grad, s_self2, vec2, qkv2, out2)
    grad = grad.astype(jnp.bfloat16).astype(jnp.float32)
    grad, g_up1, g_down1, v_feed1 = feed_backward(grad, s_feed, vec, up, down)
    embed_grad, g_qkv1, g_out1, v_self1 = self_backward(grad, s_self, vec, qkv, out)

    def split(first, second):
        both = jnp.stack([first, second])
        rows = both.shape[1] // n_dp
        k = both.shape[2] // (half * lanes)
        both = both.reshape(2, n_dp, rows, half, k, lanes)
        return both.transpose(0, 3, 1, 4, 2, 5).reshape(n_pipe, n_dp, k * rows, lanes)

    def split_cross(g):
        rows = g.shape[0] // (n_pipe * n_dp)
        k = g.shape[1] // lanes
        g = g.reshape(n_pipe, n_dp, rows, k, lanes)
        return jnp.moveaxis(g, 3, 2).reshape(n_pipe, n_dp, k * rows, lanes)

    def split_vectors(v_self, v_feed):
        v = jnp.concatenate([jnp.stack(v_self + v_feed[:3]), v_feed[3].reshape(4, width)], axis=0)
        v = v.reshape(half, 12 // half, n_dp, width // n_dp)
        v = jnp.moveaxis(v, 2, 1)
        return jnp.pad(v, ((0, 0), (0, 0), (0, 0), (0, lanes - v.shape[-1])))

    cv = jnp.stack(g_cvec).reshape(5, n_pipe, n_dp, width // (n_pipe * n_dp))
    cv = jnp.moveaxis(cv, 0, 2)
    cv = jnp.pad(cv, ((0, 0), (0, 0), (0, 0), (0, lanes - cv.shape[-1])))
    vs = jnp.concatenate([split_vectors(v_self1, v_feed1), split_vectors(v_self2, v_feed2)], axis=0)
    packed = jnp.concatenate(
        [
            split(g_qkv1, g_qkv2),
            split(g_out1, g_out2),
            split(g_up1, g_up2),
            split(g_down1, g_down2),
            split_cross(g_cq),
            split_cross(g_ckv),
            split_cross(g_co),
            vs.astype(jnp.bfloat16),
            cv.astype(jnp.bfloat16),
        ],
        axis=2,
    )
    mine = lax.psum_scatter(packed.reshape(-1, lanes), everyone, scatter_dimension=0, tiled=True)
    mine = mine.astype(jnp.float32)
    got = [mine[ends[i] - counts[i] : ends[i]] for i in range(len(counts))]
    return (
        joined,
        embed_grad,
        got[0].T,
        got[1].T,
        got[2].T,
        lane_join(got[3], k_down).T,
        got[7][:, : layer_vectors.shape[1]],
        lane_join(got[4], k_q),
        lane_join(got[5], k_kv),
        lane_join(got[6], k_q),
        got[8][:, : cross_vectors.shape[0]].T,
    )


def solution(mesh):
    in_specs = (
        P(("pipe", "dp"), None, None),
        P(("pipe", "dp"), None, None),
        P(("pipe", "dp")),
        P(("pipe", "dp"), None),
        P(("pipe", "dp")),
        P(("pipe", "dp"), None),
        P("pipe", "dp"),
        P("pipe", "dp"),
        P("pipe", "dp"),
        P("pipe", "dp"),
        P("pipe", "dp"),
        P(("pipe", "dp"), None),
        P(("pipe", "dp"), None),
        P(("pipe", "dp"), None),
        P(("pipe", "dp"), None),
        P(("pipe", "dp"), None, None),
    )
    out_specs = (
        P(("pipe", "dp"), None, None),
        P(("pipe", "dp"), None, None),
        P("pipe", "dp"),
        P("pipe", "dp"),
        P("pipe", "dp"),
        P("pipe", "dp"),
        P("pipe", "dp"),
        P(("pipe", "dp"), None),
        P(("pipe", "dp"), None),
        P(("pipe", "dp"), None),
        P(("pipe", "dp"), None),
    )
    return jax.shard_map(
        on_device, mesh=mesh, in_specs=in_specs, out_specs=out_specs, check_vma=False
    )
```

```python
from functools import partial

import jax
import jax.numpy as jnp
import numpy as np
from jax import lax
from jax.experimental import pallas as pl
from jax.experimental.pallas import tpu as pltpu
from jax.sharding import PartitionSpec as P

HEADS = 12
NORM_EPS = 1e-12
MASKED = -1e30
BF = jnp.bfloat16
F32 = jnp.float32
NT = (((1,), (1,)), ((), ()))
NN = (((1,), (0,)), ((), ()))
TN = (((0,), (0,)), ((), ()))
VMEM_BYTES = 58 * 2**20
TILE = 256


def dot(a, b, dims=NN):
    return lax.dot_general(a, b, dims, preferred_element_type=F32)


def span(start, size, unit=128):
    return pl.ds(pl.multiple_of(start, unit), size)


def tiles(count, body):
    def step(i, carry):
        body(i)
        return carry

    lax.fori_loop(0, count, step, 0)


def fetch(copies, sems):
    started = [pltpu.make_async_copy(s, t, sems.at[i]) for i, (s, t) in enumerate(copies)]
    for copy in started:
        copy.start()
    return started


def settle(started):
    for copy in started:
        copy.wait()


def placed(refs, where_ref, layout, target, lanes):
    if len(refs) == 1:
        return [(refs[0], target)]
    core, z, y = where_ref[0], where_ref[1], where_ref[2]
    copies = []
    for i, ref in enumerate(refs):
        c_rel, y_rel, z_rel = i // 8, (i // 4) % 2, i % 4
        block = lax.rem(z - z_rel + 4, 4) * 2 + lax.rem(y + y_rel, 2)
        side = lax.rem(core + c_rel, 2)
        for first, rows, shift in layout:
            place = target.at[
                span(block * rows, rows, 16),
                span(side * lanes + shift * ref.shape[1], ref.shape[1]),
            ]
            copies.append((ref.at[pl.ds(first, rows)], place))
    return copies


def norm_rows(u_ref, gain, offset, y_ref, low_ref, n_ref, r_ref):
    for i in range(0, u_ref.shape[0], 128):
        rows = pl.ds(i, 128)
        u = u_ref[rows, :]
        center = u - jnp.mean(u, axis=-1, keepdims=True)
        scale = lax.rsqrt(jnp.mean(center * center, axis=-1, keepdims=True) + NORM_EPS)
        normed = center * scale
        y = normed * gain + offset
        y_ref[rows, :] = y
        low_ref[rows, :] = y.astype(BF)
        n_ref[rows, :] = normed
        r_ref[rows, :] = scale


def norm_rows_back(dy_ref, n_ref, r_ref, gain, du_ref, db_ref):
    sums = [jnp.zeros((1, dy_ref.shape[1]), F32)] * 3
    for i in range(0, dy_ref.shape[0], 128):
        rows = pl.ds(i, 128)
        dy = dy_ref[rows, :].astype(F32)
        n = n_ref[rows, :]
        s = dy * gain
        du = r_ref[rows, :] * (
            s - jnp.mean(s, axis=-1, keepdims=True) - n * jnp.mean(s * n, axis=-1, keepdims=True)
        )
        db = du.astype(BF)
        du_ref[rows, :] = du
        db_ref[rows, :] = db
        sums = [
            sums[0] + jnp.sum(dy * n, axis=0, keepdims=True),
            sums[1] + jnp.sum(dy, axis=0, keepdims=True),
            sums[2] + jnp.sum(db.astype(F32), axis=0, keepdims=True),
        ]
    return sums


def split_heads(a):
    first = lax.broadcasted_iota(jnp.int32, a.shape, 1) < a.shape[1] // 2
    zero = jnp.zeros_like(a)
    return jnp.concatenate([jnp.where(first, a, zero), jnp.where(first, zero, a)], axis=0)


def join_heads(a):
    rows = a.shape[0] // 2
    first = lax.broadcasted_iota(jnp.int32, (rows, a.shape[1]), 1) < a.shape[1] // 2
    return jnp.where(first, a[:rows], a[rows:])


def softmax(scores, valid):
    scores = jnp.where(valid, scores * 0.125, MASKED)
    e = jnp.exp(scores - jnp.max(scores, axis=-1, keepdims=True))
    return (e / jnp.sum(e, axis=-1, keepdims=True)).astype(BF)


def score_back(weights, d_weights):
    a = weights.astype(F32)
    t = a * d_weights
    return (t - a * jnp.sum(t, axis=-1, keepdims=True)).astype(BF)


def project_and_norm(x_ref, o_ref, w_ref, dims, bias, gain, offset, outs):
    y_ref, low_ref, n_ref, r_ref = outs
    width = y_ref.shape[1]

    def tile(j):
        cols = span(j * TILE, TILE)
        w = w_ref[cols, :] if dims is NT else w_ref[:, cols]
        y_ref[:, cols] = dot(o_ref[...], w, dims)

    tiles(width // TILE, tile)
    for i in range(0, y_ref.shape[0], 128):
        rows = pl.ds(i, 128)
        y_ref[rows, :] = x_ref[rows, :].astype(F32) + (y_ref[rows, :] + bias)
    norm_rows(y_ref, gain, offset, y_ref, low_ref, n_ref, r_ref)


def self_forward_kernel(count, lengths, where_ref, x_ref, vec_ref, *rest):
    refs, rest = rest[:count], rest[count:]
    p_ref, a_ref, o_ref, y_ref, low_ref, n_ref, r_ref, qkv, out, bias_ref, sems, sems2 = rest
    width = x_ref.shape[1]
    n, m = qkv.shape[0] // 8, out.shape[0] // 8
    whole = count == 2
    first = fetch(placed(refs[:1] if whole else refs, where_ref, [(0, n, 0)], qkv, width // 2), sems)
    second = fetch(placed(refs[1:] if whole else refs, where_ref, [(n, m, 0)], out, width // 2), sems2)
    bias_ref[:, :width] = vec_ref[0:1, :]
    bias_ref[:, width : 2 * width] = jnp.zeros((1, width), F32)
    bias_ref[:, 2 * width :] = vec_ref[1:2, :]
    settle(first)

    def tile(j):
        cols = span(j * TILE, TILE)
        p_ref[:, cols] = (dot(x_ref[...], qkv[cols, :], NT) + bias_ref[:, cols]).astype(BF)

    tiles(3 * width // TILE, tile)
    pairs = width // 128
    row = lax.broadcasted_iota(jnp.int32, (256, 128), 0)
    lane = lax.broadcasted_iota(jnp.int32, (256, 128), 1)
    same = ((row // 64) % 2) == (lane // 64)
    key_lane = lax.broadcasted_iota(jnp.int32, (1, 128), 1)

    def attend(i):
        s, h = i // pairs, lax.rem(i, pairs)
        rows = span(s * 128, 128)
        q = p_ref[rows, span(h * 128, 128)]
        k = p_ref[rows, span(width + h * 128, 128)]
        v = p_ref[rows, span(2 * width + h * 128, 128)]
        length = jnp.where(key_lane < 64, lengths[2 * s], lengths[2 * s + 1])
        valid = same & (lax.rem(key_lane, 64) < length)
        a = softmax(dot(split_heads(q), k, NT), valid)
        a_ref[i] = a
        o_ref[rows, span(h * 128, 128)] = join_heads(dot(a, v)).astype(BF)

    tiles(x_ref.shape[0] // 128 * pairs, attend)
    settle(second)
    project_and_norm(
        x_ref, o_ref, out, NT, vec_ref[2:3, :], vec_ref[3:4, :], vec_ref[4:5, :], (y_ref, low_ref, n_ref, r_ref)
    )


def self_backward_kernel(count, where_ref, dy_ref, x_ref, vec_ref, p_ref, a_ref, o_ref, n_ref, r_ref, *rest):
    refs, rest = rest[:count], rest[count:]
    dx_ref, gq_own, gq_other, go_own, go_other, gv_ref = rest[:6]
    qkv, out, db_ref, dmix_ref, dp_ref, rel_ref, sems, sems2 = rest[6:]
    width = x_ref.shape[1]
    half = width // 2
    n, m = qkv.shape[0] // 8, out.shape[0] // 8
    whole = count == 2
    second = fetch(placed(refs[1:] if whole else refs, where_ref, [(n, m, 0)], out, half), sems2)
    first = fetch(placed(refs[:1] if whole else refs, where_ref, [(0, n, 0)], qkv, half), sems)
    core = where_ref[0]
    g_gain, g_offset, g_bias = norm_rows_back(dy_ref, n_ref, r_ref, vec_ref[3:4, :], dx_ref, db_ref)
    settle(second)

    def mix(j):
        cols = span(j * TILE, TILE)
        dmix_ref[:, cols] = dot(db_ref[...], out[:, cols]).astype(BF)

    tiles(width // TILE, mix)
    rel_ref[:, :half] = o_ref[:, span(core * half, half)]
    rel_ref[:, half:] = o_ref[:, span((1 - core) * half, half)]

    def out_grad(j):
        rows = span(j * TILE, TILE)
        g = dot(db_ref[:, rows], rel_ref[...], TN).astype(BF)
        go_own[rows, :] = g[:, :half]
        go_other[rows, :] = g[:, half:]

    tiles(width // TILE, out_grad)
    pairs = width // 128

    def attend(i):
        s, h = i // pairs, lax.rem(i, pairs)
        rows = span(s * 128, 128)
        q2 = split_heads(p_ref[rows, span(h * 128, 128)])
        k = p_ref[rows, span(width + h * 128, 128)]
        v = p_ref[rows, span(2 * width + h * 128, 128)]
        do2 = split_heads(dmix_ref[rows, span(h * 128, 128)])
        a = a_ref[i]
        ds = score_back(a, dot(do2, v, NT))
        dp_ref[rows, span(h * 128, 128)] = (join_heads(dot(ds, k)) * 0.125).astype(BF)
        dp_ref[rows, span(width + h * 128, 128)] = (dot(ds, q2, TN) * 0.125).astype(BF)
        dp_ref[rows, span(2 * width + h * 128, 128)] = dot(a, do2, TN).astype(BF)

    tiles(x_ref.shape[0] // 128 * pairs, attend)
    settle(first)

    def back(j):
        cols = span(j * TILE, TILE)
        dx_ref[:, cols] += dot(dp_ref[...], qkv[:, cols])

    tiles(width // TILE, back)
    rel_ref[:, :half] = x_ref[:, span(core * half, half)]
    rel_ref[:, half:] = x_ref[:, span((1 - core) * half, half)]

    def qkv_grad(j):
        rows = span(j * TILE, TILE)
        g = dot(dp_ref[:, rows], rel_ref[...], TN).astype(BF)
        gq_own[rows, :] = g[:, :half]
        gq_other[rows, :] = g[:, half:]

    tiles(3 * width // TILE, qkv_grad)
    gv_ref[0:1, :] = jnp.sum(dp_ref[:, :width].astype(F32), axis=0, keepdims=True)
    gv_ref[1:2, :] = jnp.sum(dp_ref[:, 2 * width :].astype(F32), axis=0, keepdims=True)
    gv_ref[2:3, :] = g_bias
    gv_ref[3:4, :] = g_gain
    gv_ref[4:5, :] = g_offset


def cross_forward_kernel(x_ref, low_x_ref, keep_ref, kv_ref, vec_ref, wq_ref, wo_ref, *rest):
    q_ref, a_ref, o_ref, y_ref, low_ref, n_ref, r_ref = rest
    width = x_ref.shape[1]
    patches = kv_ref.shape[0] // keep_ref.shape[0]

    def tile(j):
        cols = span(j * TILE, TILE)
        q_ref[:, cols] = (dot(low_x_ref[...], wq_ref[:, cols]) + vec_ref[0:1, cols]).astype(BF)

    tiles(width // TILE, tile)
    pairs = width // 128

    def attend(i):
        s, h = i // pairs, lax.rem(i, pairs)
        rows, keys = span(s * 64, 64, 64), span(s * patches, patches, 16)
        q = q_ref[rows, span(h * 128, 128)]
        k = kv_ref[keys, span(h * 128, 128)]
        v = kv_ref[keys, span(width + h * 128, 128)]
        a = softmax(dot(split_heads(q), k, NT), keep_ref[pl.ds(s, 1), :] > 0)
        a_ref[i] = a
        o_ref[rows, span(h * 128, 128)] = join_heads(dot(a, v)).astype(BF)

    tiles(keep_ref.shape[0] * pairs, attend)
    project_and_norm(
        x_ref, o_ref, wo_ref, NN, vec_ref[2:3, :], vec_ref[3:4, :], vec_ref[4:5, :], (y_ref, low_ref, n_ref, r_ref)
    )


def cross_backward_kernel(dy_ref, low_x_ref, kv_ref, vec_ref, wq_ref, wo_ref, q_ref, a_ref, o_ref, n_ref, r_ref, *rest):
    dx_ref, dkv_ref, gq_ref, go_ref, gv_ref, db_ref, dmix_ref, dq_ref = rest
    width = low_x_ref.shape[1]
    patches = a_ref.shape[2]
    g_gain, g_offset, g_bias = norm_rows_back(dy_ref, n_ref, r_ref, vec_ref[3:4, :], dx_ref, db_ref)

    def mix(j):
        cols = span(j * TILE, TILE)
        dmix_ref[:, cols] = dot(db_ref[...], wo_ref[cols, :], NT).astype(BF)
        go_ref[cols, :] = dot(o_ref[:, cols], db_ref[...], TN).astype(BF)

    tiles(width // TILE, mix)
    pairs = width // 128

    def attend(i):
        s, h = i // pairs, lax.rem(i, pairs)
        rows, keys = span(s * 64, 64, 64), span(s * patches, patches, 16)
        q2 = split_heads(q_ref[rows, span(h * 128, 128)])
        k = kv_ref[keys, span(h * 128, 128)]
        v = kv_ref[keys, span(width + h * 128, 128)]
        do2 = split_heads(dmix_ref[rows, span(h * 128, 128)])
        a = a_ref[i]
        ds = score_back(a, dot(do2, v, NT))
        dq_ref[rows, span(h * 128, 128)] = (join_heads(dot(ds, k)) * 0.125).astype(BF)
        dkv_ref[keys, span(h * 128, 128)] = (dot(ds, q2, TN) * 0.125).astype(BF)
        dkv_ref[keys, span(width + h * 128, 128)] = dot(a, do2, TN).astype(BF)

    tiles(a_ref.shape[0], attend)

    def back(j):
        cols = span(j * TILE, TILE)
        dx_ref[:, cols] += dot(dq_ref[...], wq_ref[cols, :], NT)
        gq_ref[cols, :] = dot(low_x_ref[:, cols], dq_ref[...], TN).astype(BF)

    tiles(width // TILE, back)
    gv_ref[0:1, :] = jnp.sum(dq_ref[...].astype(F32), axis=0, keepdims=True)
    gv_ref[1:2, :] = jnp.sum(dkv_ref[:, width:].astype(F32), axis=0, keepdims=True)
    gv_ref[2:3, :] = g_bias
    gv_ref[3:4, :] = g_gain
    gv_ref[4:5, :] = g_offset


def gelu_parts(h):
    size = jnp.abs(h) * 0.7071067811865476
    t = 1.0 / (1.0 + 0.3275911 * size)
    e = jnp.exp(-size * size)
    poly = t * (0.254829592 + t * (-0.284496736 + t * (1.421413741 + t * (-1.453152027 + t * 1.061405429))))
    tail = 0.5 * poly * e
    cdf = jnp.where(h < 0, tail, 1.0 - tail)
    return h * cdf, cdf + h * (e * 0.3989422804014327)


def feed_forward_kernel(count, where_ref, x_ref, low_x_ref, vec_ref, bias_ref, *rest):
    refs, rest = rest[: 2 * count], rest[2 * count :]
    act_ref, slope_ref, y_ref, low_ref, n_ref, r_ref, up, down, sems, sems2 = rest
    width, hidden = x_ref.shape[1], up.shape[0]
    n, m = hidden // 8, width // 8
    quarter = [(m * i, m, i) for i in range(hidden // width)]
    first = fetch(placed(refs[:count], where_ref, [(0, n, 0)], up, width // 2), sems)
    second = fetch(placed(refs[count:], where_ref, quarter, down, hidden // 2), sems2)
    settle(first)

    def tile(j):
        cols = span(j * TILE, TILE)
        h = dot(low_x_ref[...], up[cols, :], NT) + bias_ref[:, cols]
        act, slope = gelu_parts(h)
        act_ref[:, cols] = act.astype(BF)
        slope_ref[:, cols] = slope.astype(BF)

    tiles(hidden // TILE, tile)
    settle(second)
    project_and_norm(
        x_ref, act_ref, down, NT, vec_ref[5:6, :], vec_ref[6:7, :], vec_ref[7:8, :], (y_ref, low_ref, n_ref, r_ref)
    )


def feed_backward_kernel(count, where_ref, dy_ref, low_x_ref, vec_ref, act_ref, slope_ref, n_ref, r_ref, *rest):
    refs, rest = rest[: 2 * count], rest[2 * count :]
    dx_ref, gu_own, gu_other, gd_own, gd_other, gv_ref, gb_ref = rest[:7]
    up, down, db_ref, dh_ref, rel_ref, sems, sems2 = rest[7:]
    width, hidden = low_x_ref.shape[1], up.shape[0]
    n, m, half = hidden // 8, width // 8, width // 2
    quarter = [(m * i, m, i) for i in range(hidden // width)]
    second = fetch(placed(refs[count:], where_ref, quarter, down, hidden // 2), sems2)
    first = fetch(placed(refs[:count], where_ref, [(0, n, 0)], up, half), sems)
    core = where_ref[0]
    g_gain, g_offset, g_bias = norm_rows_back(dy_ref, n_ref, r_ref, vec_ref[6:7, :], dx_ref, db_ref)
    settle(second)
    per_side = hidden // 2 // TILE

    def down_tile(j):
        cols = span(j * TILE, TILE)
        dh = (dot(db_ref[...], down[:, cols]) * slope_ref[:, cols].astype(F32)).astype(BF)
        dh_ref[:, cols] = dh
        gb_ref[:, cols] = jnp.sum(dh.astype(F32), axis=0, keepdims=True)

    tiles(hidden // TILE, down_tile)

    def down_grad(j):
        cols = span(j * TILE, TILE)
        own = span(core * (hidden // 2) + j * TILE, TILE)
        other = span((1 - core) * (hidden // 2) + j * TILE, TILE)
        gd_own[:, cols] = dot(db_ref[...], act_ref[:, own], TN).astype(BF)
        gd_other[:, cols] = dot(db_ref[...], act_ref[:, other], TN).astype(BF)

    tiles(per_side, down_grad)
    rel_ref[:, :half] = low_x_ref[:, span(core * half, half)]
    rel_ref[:, half:] = low_x_ref[:, span((1 - core) * half, half)]

    def up_grad(j):
        rows = span(j * TILE, TILE)
        g = dot(dh_ref[:, rows], rel_ref[...], TN).astype(BF)
        gu_own[rows, :] = g[:, :half]
        gu_other[rows, :] = g[:, half:]

    tiles(hidden // TILE, up_grad)
    settle(first)

    def back(j):
        cols = span(j * TILE, TILE)
        dx_ref[:, cols] += dot(dh_ref[...], up[:, cols])

    tiles(width // TILE, back)
    gv_ref[0:1, :] = g_bias
    gv_ref[1:2, :] = g_gain
    gv_ref[2:3, :] = g_offset


def struct(*shape, dtype=F32):
    return jax.ShapeDtypeStruct(shape, dtype)


VMEM = pl.BlockSpec(memory_space=pltpu.VMEM)
SMEM = pl.BlockSpec(memory_space=pltpu.SMEM)
ANYWHERE = pl.BlockSpec(memory_space=pl.ANY)


def call(kernel, outs, specs, scratch, flops, args):
    return pl.pallas_call(
        kernel,
        out_shape=outs,
        in_specs=specs,
        out_specs=[VMEM] * len(outs),
        scratch_shapes=scratch,
        cost_estimate=pl.CostEstimate(flops=flops, bytes_accessed=20 * 2**20, transcendentals=0),
        compiler_params=pltpu.CompilerParams(vmem_limit_bytes=VMEM_BYTES),
    )(*args)


def copy_sems(count, parts=1):
    return pltpu.SemaphoreType.DMA((max(1, (count if count > 2 else 1) * parts),))


def self_forward(x, lengths, where, vec, weights):
    rows, width = x.shape
    blocks = rows // 128 * (width // 128)
    count = len(weights)
    outs = [
        struct(rows, 3 * width, dtype=BF),
        struct(blocks, 256, 128, dtype=BF),
        struct(rows, width, dtype=BF),
        struct(rows, width),
        struct(rows, width, dtype=BF),
        struct(rows, width),
        struct(rows, 1),
    ]
    scratch = [
        pltpu.VMEM((3 * width, width), BF),
        pltpu.VMEM((width, width), BF),
        pltpu.VMEM((1, 3 * width), F32),
        copy_sems(count),
        copy_sems(count),
    ]
    p, a, o, y, low, n, r = call(
        partial(self_forward_kernel, count),
        outs,
        [SMEM, SMEM, VMEM, VMEM] + [ANYWHERE] * count,
        scratch,
        10 * rows * width * width,
        (lengths, where, x, vec, *weights),
    )
    return y, low, (x, p, a, o, n, r)


def self_backward(dy, saved, where, vec, weights):
    x, p, a, o, n, r = saved
    rows, width = x.shape
    half = width // 2
    count = len(weights)
    outs = [
        struct(rows, width),
        struct(3 * width, half, dtype=BF),
        struct(3 * width, half, dtype=BF),
        struct(width, half, dtype=BF),
        struct(width, half, dtype=BF),
        struct(8, width),
    ]
    scratch = [
        pltpu.VMEM((3 * width, width), BF),
        pltpu.VMEM((width, width), BF),
        pltpu.VMEM((rows, width), BF),
        pltpu.VMEM((rows, width), BF),
        pltpu.VMEM((rows, 3 * width), BF),
        pltpu.VMEM((rows, width), BF),
        copy_sems(count),
        copy_sems(count),
    ]
    return call(
        partial(self_backward_kernel, count),
        outs,
        [SMEM] + [VMEM] * 8 + [ANYWHERE] * count,
        scratch,
        20 * rows * width * width,
        (where, dy, x, vec, p, a, o, n, r, *weights),
    )


def cross_forward(x, low_x, keep, kv, vec, wq, wo):
    rows, width = x.shape
    samples, patches = keep.shape
    outs = [
        struct(rows, width, dtype=BF),
        struct(samples * (width // 128), 128, patches, dtype=BF),
        struct(rows, width, dtype=BF),
        struct(rows, width),
        struct(rows, width, dtype=BF),
        struct(rows, width),
        struct(rows, 1),
    ]
    q, a, o, y, low, n, r = call(
        cross_forward_kernel, outs, [VMEM] * 7, [], 8 * rows * width * width, (x, low_x, keep, kv, vec, wq, wo)
    )
    return y, low, (low_x, kv, q, a, o, n, r)


def cross_backward(dy, saved, vec, wq, wo):
    low_x, kv, q, a, o, n, r = saved
    rows, width = low_x.shape
    outs = [
        struct(rows, width),
        struct(*kv.shape, dtype=BF),
        struct(width, width, dtype=BF),
        struct(width, width, dtype=BF),
        struct(8, width),
    ]
    scratch = [pltpu.VMEM((rows, width), BF)] * 3
    return call(
        cross_backward_kernel,
        outs,
        [VMEM] * 11,
        scratch,
        16 * rows * width * width,
        (dy, low_x, kv, vec, wq, wo, q, a, o, n, r),
    )


def feed_forward(x, low_x, where, vec, bias, up, down):
    rows, width = x.shape
    hidden = bias.shape[1]
    count = len(up)
    outs = [
        struct(rows, hidden, dtype=BF),
        struct(rows, hidden, dtype=BF),
        struct(rows, width),
        struct(rows, width, dtype=BF),
        struct(rows, width),
        struct(rows, 1),
    ]
    scratch = [
        pltpu.VMEM((hidden, width), BF),
        pltpu.VMEM((width, hidden), BF),
        copy_sems(count),
        copy_sems(count, hidden // width),
    ]
    act, slope, y, low, n, r = call(
        partial(feed_forward_kernel, count),
        outs,
        [SMEM] + [VMEM] * 4 + [ANYWHERE] * (2 * count),
        scratch,
        4 * rows * width * hidden,
        (where, x, low_x, vec, bias, *up, *down),
    )
    return y, low, (low_x, act, slope, n, r)


def feed_backward(dy, saved, where, vec, up, down):
    low_x, act, slope, n, r = saved
    rows, width = low_x.shape
    hidden = act.shape[1]
    count = len(up)
    outs = [
        struct(rows, width),
        struct(hidden, width // 2, dtype=BF),
        struct(hidden, width // 2, dtype=BF),
        struct(width, hidden // 2, dtype=BF),
        struct(width, hidden // 2, dtype=BF),
        struct(8, width),
        struct(1, hidden),
    ]
    scratch = [
        pltpu.VMEM((hidden, width), BF),
        pltpu.VMEM((width, hidden), BF),
        pltpu.VMEM((rows, width), BF),
        pltpu.VMEM((rows, hidden), BF),
        pltpu.VMEM((rows, width), BF),
        copy_sems(count),
        copy_sems(count, hidden // width),
    ]
    return call(
        partial(feed_backward_kernel, count),
        outs,
        [SMEM] + [VMEM] * 7 + [ANYWHERE] * (2 * count),
        scratch,
        8 * rows * width * hidden,
        (where, dy, low_x, vec, act, slope, n, r, *up, *down),
    )


def lane_slices(a, lanes):
    return jnp.concatenate([a[:, i : i + lanes] for i in range(0, a.shape[1], lanes)], axis=0)


def lane_join(a, count):
    rows = a.shape[-2] // count
    return jnp.concatenate([a[..., i * rows : (i + 1) * rows, :] for i in range(count)], axis=-1)


def pad_to(a, rows, lanes):
    return jnp.pad(a, ((0, rows - a.shape[0]), (0, lanes - a.shape[1])))


def dynamic(a, index, axis):
    return lax.dynamic_index_in_dim(a, index, axis, keepdims=False)


class Grid:
    def __init__(self):
        pipe, dp = lax.axis_index("pipe"), lax.axis_index("dp")
        self.x, self.core = pipe // 2, pipe % 2
        self.z, self.y = dp // 2, dp % 2

    def swap_x(self, a):
        return lax.ppermute(a, "pipe", [(i, i ^ 2) for i in range(4)])

    def over_x(self, a, to):
        return lax.ppermute(a, "pipe", [(i ^ 2, i) for i in (2 * to, 2 * to + 1)])

    def swap_core(self, a):
        return lax.ppermute(a, "pipe", [(i, i ^ 1) for i in range(4)])

    def swap_y(self, a):
        return lax.ppermute(a, "dp", [(i, i ^ 1) for i in range(8)])

    def ring_z(self, a):
        return lax.ppermute(a, "dp", [(i, (i + 2) % 8) for i in range(8)])

    def gather(self, piece):
        along_z = [piece]
        for _ in range(3):
            along_z.append(self.ring_z(along_z[-1]))
        across = along_z + [self.swap_y(p) for p in along_z]
        return across + [self.swap_core(p) for p in across]

    def gather_small(self, block):
        a = block[None]
        for swap, place in ((self.swap_y, self.y), (self.swap_x, self.x), (self.swap_core, self.core)):
            other = swap(a)
            low = place == 0
            a = jnp.stack([jnp.where(low, a, other), jnp.where(low, other, a)])
        ring = [a]
        for _ in range(3):
            ring.append(self.ring_z(ring[-1]))
        order = jnp.stack([ring[0], ring[3], ring[2], ring[1]] * 2)
        a = lax.dynamic_slice_in_dim(order, (4 - self.z) % 4, 4, 0)[:, :, :, :, 0]
        return a.transpose(2, 1, 0, 3, 4, 5)

    def reduce(self, own, other):
        came = self.swap_core(other)
        rows = own.shape[0] // 8
        own = own.reshape(4, 2, rows, own.shape[1])
        came = came.reshape(own.shape)

        def both(index):
            return dynamic(own, index, 1).astype(F32) + dynamic(came, index, 1).astype(F32)

        across = self.swap_y(both(1 - self.y).astype(own.dtype))
        keep = both(self.y)

        def block(step):
            at = (self.z + 3 - step) % 4
            return dynamic(keep, at, 0) + dynamic(across, at, 0).astype(F32)

        total = block(0)
        for step in range(3):
            total = self.ring_z(total.astype(own.dtype)).astype(F32) + block(step + 1)
        return total

    def reduce_small(self, a):
        for swap, place, axis in ((self.swap_core, self.core, 1), (self.swap_x, self.x, 0), (self.swap_y, self.y, -3)):
            a = dynamic(a, place, axis) + swap(dynamic(a, 1 - place, axis))
        total = dynamic(a, (self.z + 3) % 4, 0)
        for step in range(3):
            total = self.ring_z(total) + dynamic(a, (self.z + 2 - step) % 4, 0)
        return total


def masks(caption_len, phrase_len, box_count, patch_mask, text_rows, patches):
    slots = jnp.arange(phrase_len.shape[1], dtype=jnp.int32)
    phrase_total = jnp.sum(jnp.where(slots[None, :] < box_count[:, None], phrase_len, 0), axis=1)
    lengths = jnp.minimum(caption_len + phrase_total, text_rows)
    first_patch = (jnp.arange(patch_mask.shape[1], dtype=jnp.int32) == 0).astype(jnp.int32)
    keep = jnp.maximum(patch_mask, first_patch[None, :]).astype(F32)
    return lengths, jnp.pad(keep, ((0, 0), (0, patches - keep.shape[1])))


def on_device(
    text_embed,
    image_feats,
    caption_len,
    phrase_len,
    box_count,
    patch_mask,
    attn_qkv,
    attn_out,
    ffn_up,
    ffn_down,
    layer_vectors,
    cross_query,
    cross_kv,
    cross_out,
    cross_vectors,
    cotangent,
):
    n_pipe, n_dp = lax.axis_size("pipe"), lax.axis_size("dp")
    everyone = ("pipe", "dp")
    shards, half = n_pipe * n_dp, n_pipe // 2
    samples, text_rows, width = text_embed.shape
    hidden = ffn_up.shape[1] * n_dp
    lanes = attn_qkv.shape[0]
    patches = -(-image_feats.shape[1] // 32) * 32
    direct = (n_pipe, n_dp) == (4, 8) and lanes % 128 == 0
    lengths, patch_keep = masks(caption_len, phrase_len, box_count, patch_mask, text_rows, patches)
    x = text_embed.reshape(-1, width)
    image = jnp.pad(image_feats, ((0, 0), (0, patches - image_feats.shape[1]), (0, 0)))
    image = image.reshape(samples * patches, -1)

    c_rows = cross_query.shape[0]
    kv_slices = cross_kv.shape[1] // width
    cross_pack = jnp.concatenate([cross_query, cross_out, lane_slices(cross_kv, width)], axis=0)
    cross_whole = lax.all_gather(cross_pack, everyone, axis=0, tiled=True).reshape(shards, -1, width)
    wq = cross_whole[:, :c_rows].reshape(-1, width)
    wo = cross_whole[:, c_rows : 2 * c_rows].reshape(-1, width)
    wkv = lane_join(cross_whole[:, 2 * c_rows :], kv_slices).reshape(-1, kv_slices * width)

    v_rows, v_lanes = layer_vectors.shape
    x_rows = cross_vectors.shape[1]
    small = jnp.concatenate([pad_to(layer_vectors, v_rows, 128), pad_to(cross_vectors.T, x_rows, 128)], axis=0)
    small = pad_to(small, 16, 128).astype(F32)
    packs = [
        jnp.concatenate([attn_qkv.T, attn_out.T], axis=0),
        ffn_up.T,
        lane_slices(ffn_down.T, lanes),
    ]
    if direct:
        grid = Grid()
        where = jnp.stack([grid.core, grid.z, grid.y]).astype(jnp.int32)
        vectors = grid.gather_small(small)
        vectors = vectors.reshape(n_pipe, n_dp, 16, 128)
        weights = [[], []]
        swapped = [grid.swap_x(p) for p in packs]
        for layer in range(2):
            for pack, other in zip(packs, swapped):
                weights[layer].append(grid.gather(jnp.where(grid.x == layer, pack, other)))
    else:
        where = jnp.zeros((3,), jnp.int32)
        vectors = lax.all_gather(small, everyone, axis=0, tiled=False).reshape(n_pipe, n_dp, 16, 128)
        whole = lax.all_gather(jnp.concatenate(packs, axis=0), everyone, axis=0, tiled=False)
        whole = whole.reshape(n_pipe, n_dp, -1, lanes)

        def section(piece, layer):
            piece = jnp.moveaxis(piece[layer * half : (layer + 1) * half], 0, 2)
            return piece.reshape(n_dp * piece.shape[1], half * piece.shape[-1])

        ends = np.cumsum([0, attn_qkv.shape[1], attn_out.shape[1], ffn_up.shape[1], packs[2].shape[0]])
        cut = [whole[:, :, a:b] for a, b in zip(ends[:-1], ends[1:])]
        cut[3] = lane_join(cut[3], hidden // width)
        weights = []
        for layer in range(2):
            qkv, out, up, down = (section(c, layer) for c in cut)
            weights.append([[qkv, out], [up], [down]])

    def layer_vec(layer):
        v = vectors[layer * half : (layer + 1) * half, :, :v_rows, :v_lanes]
        return jnp.moveaxis(v, 1, 2).reshape(12, width)

    vecs = [layer_vec(0), layer_vec(1)]
    biases = [v[8:12].reshape(1, hidden) for v in vecs]
    cvec = vectors.reshape(shards, 16, 128)[:, v_rows : v_rows + x_rows, :c_rows]
    cvec = jnp.moveaxis(cvec, 1, 0).reshape(x_rows, width)

    state, low, s_self = self_forward(x, lengths, where, vecs[0], weights[0][0])
    state, passed, s_feed = feed_forward(state, low, where, vecs[0], biases[0], *weights[0][1:])
    kv_bias = jnp.concatenate([jnp.zeros((width,), F32), cvec[1]])
    kv = (jnp.dot(image, wkv, preferred_element_type=F32) + kv_bias).astype(BF)
    state, low, s_self2 = self_forward(passed, lengths, where, vecs[1], weights[1][0])
    state, low, s_cross = cross_forward(state, low, patch_keep, kv, cvec, wq, wo)
    joined, _, s_feed2 = feed_forward(state, low, where, vecs[1], biases[1], *weights[1][1:])

    grad = cotangent.reshape(-1, width)
    grad, gu_own, gu_other, gd_own, gd_other, v_feed2, v_up2 = feed_backward(
        grad, s_feed2, where, vecs[1], *weights[1][1:]
    )
    halves2 = [None, None, (gu_own, gu_other), (gd_own, gd_other)]
    grad, dkv, g_cq, g_co, v_cross = cross_backward(grad, s_cross, cvec, wq, wo)
    g_ckv = dot(image, dkv, TN).astype(BF)
    grad, gq_own, gq_other, go_own, go_other, v_self2 = self_backward(
        grad, s_self2, where, vecs[1], weights[1][0]
    )
    halves2[:2] = [(gq_own, gq_other), (go_own, go_other)]
    grad, gu_own, gu_other, gd_own, gd_other, v_feed, v_up = feed_backward(
        grad.astype(BF), s_feed, where, vecs[0], *weights[0][1:]
    )
    halves = [None, None, (gu_own, gu_other), (gd_own, gd_other)]
    embed_grad, gq_own, gq_other, go_own, go_other, v_self = self_backward(
        grad, s_self, where, vecs[0], weights[0][0]
    )
    halves[:2] = [(gq_own, gq_other), (go_own, go_other)]

    def cross_rows(g):
        g = g.reshape(shards, c_rows, width)
        return g

    g_kv = g_ckv.reshape(shards, -1, kv_slices, width)
    g_kv = jnp.moveaxis(g_kv, 2, 1).reshape(shards, -1, width)
    cross_grads = jnp.concatenate([cross_rows(g_cq), cross_rows(g_co), g_kv], axis=1)
    cross_grads = lax.psum_scatter(cross_grads.reshape(-1, width), everyone, scatter_dimension=0, tiled=True)
    cross_grads = cross_grads.astype(F32)

    def vector_block(v_self, v_feed, v_up):
        v = jnp.concatenate([v_self[:5], v_feed[:3], v_up.reshape(4, width)], axis=0)
        return jnp.moveaxis(v.reshape(half, v_rows, n_dp, v_lanes), 2, 1)

    section_vec = jnp.concatenate([vector_block(v_self, v_feed, v_up), vector_block(v_self2, v_feed2, v_up2)], axis=0)
    cross_vec = jnp.moveaxis(v_cross[:x_rows].reshape(x_rows, n_pipe, n_dp, c_rows), 0, 2)

    def padded(v):
        return jnp.pad(v, ((0, 0), (0, 0), (0, 0), (0, 128 - v.shape[3])))

    small = jnp.concatenate([padded(section_vec), padded(cross_vec)], axis=2)
    small = jnp.pad(small, ((0, 0), (0, 0), (0, 16 - small.shape[2]), (0, 0)))
    if direct:
        mine = []
        for pair, pair2 in zip(halves, halves2):
            first, second = grid.reduce(*pair), grid.reduce(*pair2)
            came2 = grid.over_x(second.astype(BF), 1).astype(F32)
            came = grid.over_x(first.astype(BF), 0).astype(F32)
            mine.append(jnp.where(grid.x == 0, first + came, second + came2))
        small = grid.reduce_small(small.reshape(2, 2, 4, 2, 16, 128))
    else:

        def split(pair, pair2):
            both = jnp.stack([jnp.concatenate(pair, axis=1), jnp.concatenate(pair2, axis=1)])
            rows, k = both.shape[1] // n_dp, both.shape[2] // (half * lanes)
            both = both.reshape(2, n_dp, rows, half, k, lanes)
            return both.transpose(0, 3, 1, 4, 2, 5).reshape(n_pipe, n_dp, k * rows, lanes)

        parts = [split(pair, pair2) for pair, pair2 in zip(halves, halves2)]
        ends = np.cumsum([0] + [p.shape[2] for p in parts])
        packed = jnp.concatenate(parts, axis=2).reshape(-1, lanes)
        packed = lax.psum_scatter(packed, everyone, scatter_dimension=0, tiled=True).astype(F32)
        mine = [packed[a:b] for a, b in zip(ends[:-1], ends[1:])]
        mine[3] = lane_join(mine[3], hidden // width)
        small = lax.psum_scatter(small.reshape(-1, 128), everyone, scatter_dimension=0, tiled=True)
    return (
        joined.reshape(text_embed.shape),
        embed_grad.reshape(text_embed.shape),
        mine[0].T,
        mine[1].T,
        mine[2].T,
        mine[3].T,
        small[:v_rows, :v_lanes],
        cross_grads[:c_rows],
        lane_join(cross_grads[2 * c_rows :], kv_slices),
        cross_grads[c_rows : 2 * c_rows],
        small[v_rows : v_rows + x_rows, :c_rows].T,
    )


def solution(mesh):
    in_specs = (
        P(("pipe", "dp"), None, None),
        P(("pipe", "dp"), None, None),
        P(("pipe", "dp")),
        P(("pipe", "dp"), None),
        P(("pipe", "dp")),
        P(("pipe", "dp"), None),
        P("pipe", "dp"),
        P("pipe", "dp"),
        P("pipe", "dp"),
        P("pipe", "dp"),
        P("pipe", "dp"),
        P(("pipe", "dp"), None),
        P(("pipe", "dp"), None),
        P(("pipe", "dp"), None),
        P(("pipe", "dp"), None),
        P(("pipe", "dp"), None, None),
    )
    out_specs = (
        P(("pipe", "dp"), None, None),
        P(("pipe", "dp"), None, None),
        P("pipe", "dp"),
        P("pipe", "dp"),
        P("pipe", "dp"),
        P("pipe", "dp"),
        P("pipe", "dp"),
        P(("pipe", "dp"), None),
        P(("pipe", "dp"), None),
        P(("pipe", "dp"), None),
        P(("pipe", "dp"), None),
    )
    return jax.shard_map(
        on_device, mesh=mesh, in_specs=in_specs, out_specs=out_specs, check_vma=False
    )
```

```python
from functools import partial

import jax
import jax.numpy as jnp
import numpy as np
from jax import lax
from jax.experimental import pallas as pl
from jax.experimental.pallas import tpu as pltpu
from jax.sharding import PartitionSpec as P

HEADS = 12
NORM_EPS = 1e-12
MASKED = -1e30
BF = jnp.bfloat16
F32 = jnp.float32
NT = (((1,), (1,)), ((), ()))
NN = (((1,), (0,)), ((), ()))
TN = (((0,), (0,)), ((), ()))
VMEM_BYTES = 58 * 2**20
TILE = 768
SLACK = 1


def dot(a, b, dims=NN):
    return lax.dot_general(a, b, dims, preferred_element_type=F32)


def span(start, size, unit=128):
    return pl.ds(pl.multiple_of(start, unit), size)


def tiles(count, body):
    def step(i, carry):
        body(i)
        return carry

    lax.fori_loop(0, count, step, 0)


def fetch(copies, sems):
    started = [pltpu.make_async_copy(s, t, sems.at[i]) for i, (s, t) in enumerate(copies)]
    for copy in started:
        copy.start()
    return started


def settle(started):
    for copy in started:
        copy.wait()


def placed(refs, where_ref, layout, target, lanes):
    if len(refs) == 1:
        return [(refs[0], target)]
    core, z, y = where_ref[0], where_ref[1], where_ref[2]
    copies = []
    for i, ref in enumerate(refs):
        c_rel, y_rel, z_rel = i // 8, (i // 4) % 2, i % 4
        block = lax.rem(z - z_rel + 4, 4) * 2 + lax.rem(y + y_rel, 2)
        side = lax.rem(core + c_rel, 2)
        for first, rows, shift in layout:
            place = target.at[
                span(block * rows, rows, 16),
                span(side * lanes + shift * ref.shape[1], ref.shape[1]),
            ]
            copies.append((ref.at[pl.ds(first, rows)], place))
    return copies


def relative(where_ref, block):
    z = lax.rem(block // 2 - where_ref[1] + 4, 4)
    return z * 2 + lax.rem(block % 2 + where_ref[2], 2)


def norm_rows(u_ref, gain, offset, y_ref, low_ref, n_ref, r_ref):
    for i in range(0, u_ref.shape[0], 128):
        rows = pl.ds(i, 128)
        u = u_ref[rows, :]
        center = u - jnp.mean(u, axis=-1, keepdims=True)
        scale = lax.rsqrt(jnp.mean(center * center, axis=-1, keepdims=True) + NORM_EPS)
        normed = center * scale
        y = normed * gain + offset
        y_ref[rows, :] = y
        low_ref[rows, :] = y.astype(BF)
        n_ref[rows, :] = normed
        r_ref[rows, :] = scale


def norm_rows_back(dy_ref, n_ref, r_ref, gain, du_ref, db_ref):
    sums = [jnp.zeros((1, dy_ref.shape[1]), F32)] * 3
    for i in range(0, dy_ref.shape[0], 128):
        rows = pl.ds(i, 128)
        dy = dy_ref[rows, :].astype(F32)
        n = n_ref[rows, :]
        s = dy * gain
        du = r_ref[rows, :] * (
            s - jnp.mean(s, axis=-1, keepdims=True) - n * jnp.mean(s * n, axis=-1, keepdims=True)
        )
        db = du.astype(BF)
        du_ref[rows, :] = du
        db_ref[rows, :] = db
        sums = [
            sums[0] + jnp.sum(dy * n, axis=0, keepdims=True),
            sums[1] + jnp.sum(dy, axis=0, keepdims=True),
            sums[2] + jnp.sum(db.astype(F32), axis=0, keepdims=True),
        ]
    return sums


def split_heads(a):
    first = lax.broadcasted_iota(jnp.int32, a.shape, 1) < a.shape[1] // 2
    zero = jnp.zeros_like(a)
    return jnp.concatenate([jnp.where(first, a, zero), jnp.where(first, zero, a)], axis=0)


def join_heads(a):
    rows = a.shape[0] // 2
    first = lax.broadcasted_iota(jnp.int32, (rows, a.shape[1]), 1) < a.shape[1] // 2
    return jnp.where(first, a[:rows], a[rows:])


def softmax(scores, valid):
    scores = jnp.where(valid, scores * 0.125, MASKED)
    e = jnp.exp(scores - jnp.max(scores, axis=-1, keepdims=True))
    return (e / jnp.sum(e, axis=-1, keepdims=True)).astype(BF)


def score_back(weights, d_weights):
    a = weights.astype(F32)
    t = a * d_weights
    return (t - a * jnp.sum(t, axis=-1, keepdims=True)).astype(BF)


def project_and_norm(x_ref, o_ref, w_ref, dims, bias, gain, offset, outs):
    y_ref, low_ref, n_ref, r_ref = outs
    width = y_ref.shape[1]

    def tile(j):
        cols = span(j * TILE, TILE)
        w = w_ref[cols, :] if dims is NT else w_ref[:, cols]
        y_ref[:, cols] = dot(o_ref[...], w, dims)

    tiles(width // TILE, tile)
    for i in range(0, y_ref.shape[0], 128):
        rows = pl.ds(i, 128)
        y_ref[rows, :] = x_ref[rows, :].astype(F32) + (y_ref[rows, :] + bias)
    norm_rows(y_ref, gain, offset, y_ref, low_ref, n_ref, r_ref)


def self_forward_kernel(count, lengths, where_ref, x_ref, vec_ref, *rest):
    refs, rest = rest[:count], rest[count:]
    p_ref, a_ref, o_ref, y_ref, low_ref, n_ref, r_ref, qkv, out, bias_ref, sems, sems2 = rest
    width = x_ref.shape[1]
    n, m = qkv.shape[0] // 8, out.shape[0] // 8
    whole = count == 2
    first = fetch(placed(refs[:1] if whole else refs, where_ref, [(0, n, 0)], qkv, width // 2), sems)
    second = fetch(placed(refs[1:] if whole else refs, where_ref, [(n, m, 0)], out, width // 2), sems2)
    bias_ref[:, :width] = vec_ref[0:1, :]
    bias_ref[:, width : 2 * width] = jnp.zeros((1, width), F32)
    bias_ref[:, 2 * width :] = vec_ref[1:2, :]
    settle(first)

    def tile(j):
        cols = span(j * TILE, TILE)
        p_ref[:, cols] = (dot(x_ref[...], qkv[cols, :], NT) + bias_ref[:, cols]).astype(BF)

    tiles(3 * width // TILE, tile)
    pairs = width // 128
    row = lax.broadcasted_iota(jnp.int32, (256, 128), 0)
    lane = lax.broadcasted_iota(jnp.int32, (256, 128), 1)
    same = ((row // 64) % 2) == (lane // 64)
    key_lane = lax.broadcasted_iota(jnp.int32, (1, 128), 1)

    def attend(s):
        rows = span(s * 128, 128)
        length = jnp.where(key_lane < 64, lengths[2 * s], lengths[2 * s + 1])
        valid = same & (lax.rem(key_lane, 64) < length)
        for h in range(pairs):
            q = p_ref[rows, pl.ds(h * 128, 128)]
            k = p_ref[rows, pl.ds(width + h * 128, 128)]
            v = p_ref[rows, pl.ds(2 * width + h * 128, 128)]
            a = softmax(dot(split_heads(q), k, NT), valid)
            a_ref[s * pairs + h] = a
            o_ref[rows, pl.ds(h * 128, 128)] = join_heads(dot(a, v)).astype(BF)

    tiles(x_ref.shape[0] // 128, attend)
    settle(second)
    project_and_norm(
        x_ref, o_ref, out, NT, vec_ref[2:3, :], vec_ref[3:4, :], vec_ref[4:5, :], (y_ref, low_ref, n_ref, r_ref)
    )


def self_backward_kernel(count, where_ref, dy_ref, x_ref, vec_ref, p_ref, a_ref, o_ref, n_ref, r_ref, *rest):
    refs, rest = rest[:count], rest[count:]
    dx_ref, own_ref, other_ref, gv_ref = rest[:4]
    qkv, out, db_ref, dmix_ref, dp_ref, rel_ref, g_ref, sems, sems2 = rest[4:]
    width = x_ref.shape[1]
    half = width // 2
    n, m = qkv.shape[0] // 8, out.shape[0] // 8
    whole = count == 2
    second = fetch(placed(refs[1:] if whole else refs, where_ref, [(n, m, 0)], out, half), sems2)
    first = fetch(placed(refs[:1] if whole else refs, where_ref, [(0, n, 0)], qkv, half), sems)
    core = where_ref[0]
    g_gain, g_offset, g_bias = norm_rows_back(dy_ref, n_ref, r_ref, vec_ref[3:4, :], dx_ref, db_ref)
    settle(second)

    def mix(j):
        cols = span(j * TILE, TILE)
        dmix_ref[:, cols] = dot(db_ref[...], out[:, cols]).astype(BF)

    tiles(width // TILE, mix)
    rel_ref[:, :half] = o_ref[:, span(core * half, half)]
    rel_ref[:, half:] = o_ref[:, span((1 - core) * half, half)]

    g_ref[:width, :] = dot(db_ref[...], rel_ref[...], TN).astype(BF)
    for b in range(8):
        to, at = span(relative(where_ref, b) * (n + m) + n, m, 16), pl.ds(b * m, m)
        own_ref[to, :] = g_ref[at, :half]
        other_ref[to, :] = g_ref[at, half:]
    pairs = width // 128

    def attend(s):
        rows = span(s * 128, 128)
        for h in range(pairs):
            q2 = split_heads(p_ref[rows, pl.ds(h * 128, 128)])
            k = p_ref[rows, pl.ds(width + h * 128, 128)]
            v = p_ref[rows, pl.ds(2 * width + h * 128, 128)]
            do2 = split_heads(dmix_ref[rows, pl.ds(h * 128, 128)])
            a = a_ref[s * pairs + h]
            ds = score_back(a, dot(do2, v, NT))
            dp_ref[rows, pl.ds(h * 128, 128)] = (join_heads(dot(ds, k)) * 0.125).astype(BF)
            dp_ref[rows, pl.ds(width + h * 128, 128)] = (dot(ds, q2, TN) * 0.125).astype(BF)
            dp_ref[rows, pl.ds(2 * width + h * 128, 128)] = dot(a, do2, TN).astype(BF)

    tiles(x_ref.shape[0] // 128, attend)
    settle(first)

    def back(j):
        cols = span(j * TILE, TILE)
        dx_ref[:, cols] += dot(dp_ref[...], qkv[:, cols])

    tiles(width // TILE, back)
    rel_ref[:, :half] = x_ref[:, span(core * half, half)]
    rel_ref[:, half:] = x_ref[:, span((1 - core) * half, half)]

    def qkv_grad(j):
        rows = span(j * TILE, TILE)
        g_ref[rows, :] = dot(dp_ref[:, rows], rel_ref[...], TN).astype(BF)

    tiles(3 * width // TILE, qkv_grad)
    for b in range(8):
        to, at = span(relative(where_ref, b) * (n + m), n, 16), pl.ds(b * n, n)
        own_ref[to, :] = g_ref[at, :half]
        other_ref[to, :] = g_ref[at, half:]
    gv_ref[0:1, :] = jnp.sum(dp_ref[:, :width].astype(F32), axis=0, keepdims=True)
    gv_ref[1:2, :] = jnp.sum(dp_ref[:, 2 * width :].astype(F32), axis=0, keepdims=True)
    gv_ref[2:3, :] = g_bias
    gv_ref[3:4, :] = g_gain
    gv_ref[4:5, :] = g_offset


def cross_forward_kernel(x_ref, low_x_ref, keep_ref, k_ref, v_ref, vec_ref, wq_ref, wo_ref, *rest):
    q_ref, a_ref, o_ref, y_ref, low_ref, n_ref, r_ref = rest
    width = x_ref.shape[1]
    patches = k_ref.shape[0] // keep_ref.shape[0]

    def tile(j):
        cols = span(j * TILE, TILE)
        q_ref[:, cols] = (dot(low_x_ref[...], wq_ref[:, cols]) + vec_ref[0:1, cols]).astype(BF)

    tiles(width // TILE, tile)
    pairs = width // 128

    def attend(s):
        rows, keys = span(s * 64, 64, 64), span(s * patches, patches, 16)
        valid = keep_ref[pl.ds(s, 1), :] > 0
        for h in range(pairs):
            q = q_ref[rows, pl.ds(h * 128, 128)]
            k = k_ref[keys, pl.ds(h * 128, 128)]
            v = v_ref[keys, pl.ds(h * 128, 128)]
            a = softmax(dot(split_heads(q), k, NT), valid)
            a_ref[s * pairs + h] = a
            o_ref[rows, pl.ds(h * 128, 128)] = join_heads(dot(a, v)).astype(BF)

    tiles(keep_ref.shape[0], attend)
    project_and_norm(
        x_ref, o_ref, wo_ref, NN, vec_ref[2:3, :], vec_ref[3:4, :], vec_ref[4:5, :], (y_ref, low_ref, n_ref, r_ref)
    )


def cross_backward_kernel(dy_ref, low_x_ref, k_ref, v_ref, vec_ref, wq_ref, wo_ref, q_ref, a_ref, o_ref, n_ref, r_ref, *rest):
    dx_ref, dk_ref, dv_ref, gq_ref, go_ref, gv_ref, db_ref, dmix_ref, dq_ref = rest
    width = low_x_ref.shape[1]
    patches = a_ref.shape[2]
    g_gain, g_offset, g_bias = norm_rows_back(dy_ref, n_ref, r_ref, vec_ref[3:4, :], dx_ref, db_ref)

    def mix(j):
        cols = span(j * TILE, TILE)
        dmix_ref[:, cols] = dot(db_ref[...], wo_ref[cols, :], NT).astype(BF)
        go_ref[cols, :] = dot(o_ref[:, cols], db_ref[...], TN).astype(BF)

    tiles(width // TILE, mix)
    pairs = width // 128

    def attend(s):
        rows, keys = span(s * 64, 64, 64), span(s * patches, patches, 16)
        for h in range(pairs):
            q2 = split_heads(q_ref[rows, pl.ds(h * 128, 128)])
            k = k_ref[keys, pl.ds(h * 128, 128)]
            v = v_ref[keys, pl.ds(h * 128, 128)]
            do2 = split_heads(dmix_ref[rows, pl.ds(h * 128, 128)])
            a = a_ref[s * pairs + h]
            ds = score_back(a, dot(do2, v, NT))
            dq_ref[rows, pl.ds(h * 128, 128)] = (join_heads(dot(ds, k)) * 0.125).astype(BF)
            dk_ref[keys, pl.ds(h * 128, 128)] = (dot(ds, q2, TN) * 0.125).astype(BF)
            dv_ref[keys, pl.ds(h * 128, 128)] = dot(a, do2, TN).astype(BF)

    tiles(a_ref.shape[0] // pairs, attend)

    def back(j):
        cols = span(j * TILE, TILE)
        dx_ref[:, cols] += dot(dq_ref[...], wq_ref[cols, :], NT)
        gq_ref[cols, :] = dot(low_x_ref[:, cols], dq_ref[...], TN).astype(BF)

    tiles(width // TILE, back)
    gv_ref[0:1, :] = jnp.sum(dq_ref[...].astype(F32), axis=0, keepdims=True)
    gv_ref[1:2, :] = jnp.sum(dv_ref[...].astype(F32), axis=0, keepdims=True)
    gv_ref[2:3, :] = g_bias
    gv_ref[3:4, :] = g_gain
    gv_ref[4:5, :] = g_offset


def gelu_parts(h):
    size = jnp.abs(h) * 0.7071067811865476
    t = 1.0 / (1.0 + 0.3275911 * size)
    e = jnp.exp(-size * size)
    poly = t * (0.254829592 + t * (-0.284496736 + t * (1.421413741 + t * (-1.453152027 + t * 1.061405429))))
    tail = 0.5 * poly * e
    cdf = jnp.where(h < 0, tail, 1.0 - tail)
    return h * cdf, cdf + h * (e * 0.3989422804014327)


def feed_forward_kernel(count, base, where_ref, x_ref, low_x_ref, vec_ref, bias_ref, *rest):
    refs, rest = rest[:count], rest[count:]
    whole = count == 2
    act_ref, slope_ref, y_ref, low_ref, n_ref, r_ref, up, down, sems, sems2 = rest
    width, hidden = x_ref.shape[1], up.shape[0]
    n, m = hidden // 8, width // 8
    quarter = [(base + n + m * i, m, i) for i in range(hidden // width)]
    first = fetch(placed(refs[:1] if whole else refs, where_ref, [(base, n, 0)], up, width // 2), sems)
    second = fetch(placed(refs[1:] if whole else refs, where_ref, quarter, down, hidden // 2), sems2)
    settle(first)

    def tile(j):
        cols = span(j * TILE, TILE)
        h = dot(low_x_ref[...], up[cols, :], NT) + bias_ref[:, cols]
        act, slope = gelu_parts(h)
        act_ref[:, cols] = act.astype(BF)
        slope_ref[:, cols] = slope.astype(BF)

    tiles(hidden // TILE, tile)
    settle(second)
    project_and_norm(
        x_ref, act_ref, down, NT, vec_ref[5:6, :], vec_ref[6:7, :], vec_ref[7:8, :], (y_ref, low_ref, n_ref, r_ref)
    )


def feed_backward_kernel(count, base, where_ref, dy_ref, low_x_ref, vec_ref, act_ref, slope_ref, n_ref, r_ref, *rest):
    refs, rest = rest[:count], rest[count:]
    whole = count == 2
    dx_ref, own_ref, other_ref, gv_ref, gb_ref = rest[:5]
    up, down, db_ref, dbt_ref, dh_ref, rel_ref, sems, sems2 = rest[5:]
    width, hidden = low_x_ref.shape[1], up.shape[0]
    n, m, half = hidden // 8, width // 8, width // 2
    quarter = [(base + n + m * i, m, i) for i in range(hidden // width)]
    second = fetch(placed(refs[1:] if whole else refs, where_ref, quarter, down, hidden // 2), sems2)
    first = fetch(placed(refs[:1] if whole else refs, where_ref, [(base, n, 0)], up, half), sems)
    core = where_ref[0]
    g_gain, g_offset, g_bias = norm_rows_back(dy_ref, n_ref, r_ref, vec_ref[6:7, :], dx_ref, db_ref)
    settle(second)
    def down_tile(j):
        cols = span(j * TILE, TILE)
        dh = (dot(db_ref[...], down[:, cols]) * slope_ref[:, cols].astype(F32)).astype(BF)
        dh_ref[:, cols] = dh
        gb_ref[:, cols] = jnp.sum(dh.astype(F32), axis=0, keepdims=True)

    tiles(hidden // TILE, down_tile)
    dbt_ref[...] = db_ref[...].T

    def down_grad(j):
        for ref, side in ((own_ref, core), (other_ref, 1 - core)):
            g = dot(dbt_ref[...], act_ref[:, span(side * (hidden // 2) + j * width, width)]).astype(BF)
            for b in range(8):
                for k in range(2):
                    to = span(relative(where_ref, b) * (n + 4 * m) + n + (2 * j + k) * m, m, 16)
                    ref[to, :] = g[b * m : (b + 1) * m, k * half : (k + 1) * half]

    tiles(hidden // 2 // width, down_grad)
    rel_ref[:, :half] = low_x_ref[:, span(core * half, half)]
    rel_ref[:, half:] = low_x_ref[:, span((1 - core) * half, half)]

    def up_grad(j):
        g = dot(dh_ref[:, span(j * 2 * n, 2 * n)], rel_ref[...], TN).astype(BF)
        for k in range(2):
            to = span(relative(where_ref, 2 * j + k) * (n + 4 * m), n, 16)
            own_ref[to, :] = g[k * n : (k + 1) * n, :half]
            other_ref[to, :] = g[k * n : (k + 1) * n, half:]

    tiles(4, up_grad)
    settle(first)

    def back(j):
        cols = span(j * TILE, TILE)
        dx_ref[:, cols] += dot(dh_ref[...], up[:, cols])

    tiles(width // TILE, back)
    gv_ref[0:1, :] = g_bias
    gv_ref[1:2, :] = g_gain
    gv_ref[2:3, :] = g_offset


def struct(*shape, dtype=F32):
    return jax.ShapeDtypeStruct(shape, dtype)


VMEM = pl.BlockSpec(memory_space=pltpu.VMEM)
SMEM = pl.BlockSpec(memory_space=pltpu.SMEM)
ANYWHERE = pl.BlockSpec(memory_space=pl.ANY)


def call(kernel, outs, specs, scratch, us, args):
    return pl.pallas_call(
        kernel,
        out_shape=outs,
        in_specs=specs,
        out_specs=[VMEM] * len(outs),
        scratch_shapes=scratch,
        cost_estimate=pl.CostEstimate(flops=int(us * 1.1e9), bytes_accessed=int(us * 3.5e6), transcendentals=0),
        compiler_params=pltpu.CompilerParams(vmem_limit_bytes=VMEM_BYTES),
    )(*args)


def copy_sems(count, parts=1):
    return pltpu.SemaphoreType.DMA((max(1, (count if count > 2 else 1) * parts),))


def self_forward(x, lengths, where, vec, weights):
    rows, width = x.shape
    blocks = rows // 128 * (width // 128)
    count = len(weights)
    outs = [
        struct(rows, 3 * width, dtype=BF),
        struct(blocks, 256, 128, dtype=BF),
        struct(rows, width, dtype=BF),
        struct(rows, width),
        struct(rows, width, dtype=BF),
        struct(rows, width),
        struct(rows, 1),
    ]
    scratch = [
        pltpu.VMEM((3 * width, width), BF),
        pltpu.VMEM((width, width), BF),
        pltpu.VMEM((1, 3 * width), F32),
        copy_sems(count),
        copy_sems(count),
    ]
    p, a, o, y, low, n, r = call(
        partial(self_forward_kernel, count),
        outs,
        [SMEM, SMEM, VMEM, VMEM] + [ANYWHERE] * count,
        scratch,
        14,
        (lengths, where, x, vec, *weights),
    )
    return y, low, (x, p, a, o, n, r)


def self_backward(dy, saved, where, vec, weights):
    x, p, a, o, n, r = saved
    rows, width = x.shape
    half = width // 2
    count = len(weights)
    outs = [
        struct(rows, width),
        struct(4 * width, half, dtype=BF),
        struct(4 * width, half, dtype=BF),
        struct(8, width),
    ]
    scratch = [
        pltpu.VMEM((3 * width, width), BF),
        pltpu.VMEM((width, width), BF),
        pltpu.VMEM((rows, width), BF),
        pltpu.VMEM((rows, width), BF),
        pltpu.VMEM((rows, 3 * width), BF),
        pltpu.VMEM((rows, width), BF),
        pltpu.VMEM((3 * width, width), BF),
        copy_sems(count),
        copy_sems(count),
    ]
    return call(
        partial(self_backward_kernel, count),
        outs,
        [SMEM] + [VMEM] * 8 + [ANYWHERE] * count,
        scratch,
        22,
        (where, dy, x, vec, p, a, o, n, r, *weights),
    )


def cross_forward(x, low_x, keep, k, v, vec, wq, wo):
    rows, width = x.shape
    samples, patches = keep.shape
    outs = [
        struct(rows, width, dtype=BF),
        struct(samples * (width // 128), 128, patches, dtype=BF),
        struct(rows, width, dtype=BF),
        struct(rows, width),
        struct(rows, width, dtype=BF),
        struct(rows, width),
        struct(rows, 1),
    ]
    q, a, o, y, low, n, r = call(
        cross_forward_kernel, outs, [VMEM] * 8, [], 21, (x, low_x, keep, k, v, vec, wq, wo)
    )
    return y, low, (low_x, k, v, q, a, o, n, r)


def cross_backward(dy, saved, vec, wq, wo):
    low_x, k, v, q, a, o, n, r = saved
    rows, width = low_x.shape
    outs = [
        struct(rows, width),
        struct(*k.shape, dtype=BF),
        struct(*k.shape, dtype=BF),
        struct(width, width, dtype=BF),
        struct(width, width, dtype=BF),
        struct(8, width),
    ]
    scratch = [pltpu.VMEM((rows, width), BF)] * 3
    return call(
        cross_backward_kernel,
        outs,
        [VMEM] * 12,
        scratch,
        26,
        (dy, low_x, k, v, vec, wq, wo, q, a, o, n, r),
    )


def feed_forward(x, low_x, where, vec, bias, weights, base=0):
    rows, width = x.shape
    hidden = bias.shape[1]
    count = len(weights)
    outs = [
        struct(rows, hidden, dtype=BF),
        struct(rows, hidden, dtype=BF),
        struct(rows, width),
        struct(rows, width, dtype=BF),
        struct(rows, width),
        struct(rows, 1),
    ]
    scratch = [
        pltpu.VMEM((hidden, width), BF),
        pltpu.VMEM((width, hidden), BF),
        copy_sems(count),
        copy_sems(count, hidden // width),
    ]
    act, slope, y, low, n, r = call(
        partial(feed_forward_kernel, count, base),
        outs,
        [SMEM] + [VMEM] * 4 + [ANYWHERE] * count,
        scratch,
        20,
        (where, x, low_x, vec, bias, *weights),
    )
    return y, low, (low_x, act, slope, n, r)


def feed_backward(dy, saved, where, vec, weights, base=0):
    low_x, act, slope, n, r = saved
    rows, width = low_x.shape
    hidden = act.shape[1]
    count = len(weights)
    outs = [
        struct(rows, width),
        struct(2 * hidden, width // 2, dtype=BF),
        struct(2 * hidden, width // 2, dtype=BF),
        struct(8, width),
        struct(1, hidden),
    ]
    scratch = [
        pltpu.VMEM((hidden, width), BF),
        pltpu.VMEM((width, hidden), BF),
        pltpu.VMEM((rows, width), BF),
        pltpu.VMEM((width, rows), BF),
        pltpu.VMEM((rows, hidden), BF),
        pltpu.VMEM((rows, width), BF),
        copy_sems(count),
        copy_sems(count, hidden // width),
    ]
    return call(
        partial(feed_backward_kernel, count, base),
        outs,
        [SMEM] + [VMEM] * 7 + [ANYWHERE] * count,
        scratch,
        22,
        (where, dy, low_x, vec, act, slope, n, r, *weights),
    )


def lane_slices(a, lanes):
    return jnp.concatenate([a[:, i : i + lanes] for i in range(0, a.shape[1], lanes)], axis=0)


def lane_join(a, count):
    rows = a.shape[-2] // count
    return jnp.concatenate([a[..., i * rows : (i + 1) * rows, :] for i in range(count)], axis=-1)


def pad_to(a, rows, lanes):
    return jnp.pad(a, ((0, rows - a.shape[0]), (0, lanes - a.shape[1])))


def dynamic(a, index, axis):
    return lax.dynamic_index_in_dim(a, index, axis, keepdims=False)


def after(value, tokens):
    return lax.optimization_barrier((value, tokens))[0] if tokens else value


class Grid:
    def __init__(self):
        pipe, dp = lax.axis_index("pipe"), lax.axis_index("dp")
        self.x, self.core = pipe // 2, pipe % 2
        self.z, self.y = dp // 2, dp % 2
        self.arrived, self.computed = [()] * 2, ()

    def swap_x(self, a):
        return lax.ppermute(a, "pipe", [(i, i ^ 2) for i in range(4)])

    def to_text(self, a):
        return lax.ppermute(a, "pipe", [(2, 0), (3, 1)])

    def to_joining(self, a):
        return lax.ppermute(a, "pipe", [(0, 2), (1, 3)])

    def swap_core(self, a):
        return lax.ppermute(a, "pipe", [(i, i ^ 1) for i in range(4)])

    def swap_y(self, a):
        return lax.ppermute(a, "dp", [(i, i ^ 1) for i in range(8)])

    def ring_z(self, a, step=1):
        return lax.ppermute(a, "dp", [(i, (i + 2 * step) % 8) for i in range(8)])

    def in_order(self, place, own, other):
        return jnp.where(place == 0, jnp.stack([own, other]), jnp.stack([other, own]))

    def z_order(self, ring):
        order = jnp.stack([ring[0], ring[3], ring[2], ring[1]] * 2)
        return lax.dynamic_slice_in_dim(order, (4 - self.z) % 4, 4, 0)

    def turn(self, *moves, pre=(), compute=None, args=()):
        tokens = (*self.arrived[-SLACK], *self.computed)
        arrived = []

        def begin(asked):
            asked = [ask for group in asked for ask in group()]
            values = after([value for _, value, _ in asked], tokens)
            for (move, _, keep), value in zip(asked, values):
                result = move(value)
                arrived.append(result)
                keep(result)
            return tuple(values)

        begin(pre)
        values = begin(moves)
        self.arrived.append(tuple(arrived))
        self.computed = ()
        if compute is None:
            return None
        result = compute(*after(tuple(args), tokens + values))
        self.computed = tuple(jax.tree.leaves(result))
        return result


class Gather:
    def __init__(self, grid, piece, y_first=False):
        self.grid, self.y_first = grid, y_first
        self.ring, self.across, self.swapped = [piece], [], {}

    def z(self):
        rings = [self.ring, self.across] if self.y_first else [self.ring]
        return [(self.grid.ring_z, ring[-1], ring.append) for ring in rings]

    def y(self, count=1):
        at = len(self.across)
        return [(self.grid.swap_y, p, self.across.append) for p in self.ring[at : at + count]]

    def y2(self):
        return self.y(2)

    def c(self):
        here = dict([((0, k), p) for k, p in enumerate(self.ring)] + [((1, k), p) for k, p in enumerate(self.across)])
        return [
            (self.grid.swap_core, p, partial(self.swapped.__setitem__, key))
            for key, p in here.items()
            if key not in self.swapped
        ]

    def pieces(self):
        other = [self.swapped[side, k] for side in range(2) for k in range(4)]
        return [*self.ring, *self.across, *other]


class BlockGather:
    def __init__(self, grid, block):
        self.grid, self.ring, self.sets = grid, [block], {}

    def keep(self, *key):
        return partial(self.sets.__setitem__, key)

    def z(self):
        return [(self.grid.ring_z, self.ring[-1], self.ring.append)]

    def z_all(self):
        return [(partial(self.grid.ring_z, step=k), self.ring[0], self.ring.append) for k in (1, 2, 3)]

    def start(self):
        if (0, 0, 0) not in self.sets:
            self.sets[0, 0, 0] = self.grid.z_order(self.ring)

    def y(self):
        self.start()
        return [(self.grid.swap_y, self.sets[0, 0, 0], self.keep(0, 0, 1))]

    def x0(self):
        self.start()
        return [(self.grid.swap_x, self.sets[0, 0, 0], self.keep(0, 1, 0))]

    def x1(self):
        return [(self.grid.swap_x, self.sets[0, 0, 1], self.keep(0, 1, 1))]

    def c(self):
        return [
            (self.grid.swap_core, self.sets[0, x, y], self.keep(1, x, y)) for x in range(2) for y in range(2)
        ]

    def whole(self):
        g = self.grid
        rel = jnp.stack([self.sets[c, x, y] for c in range(2) for x in range(2) for y in range(2)])
        rows = []
        for x in range(2):
            for c in range(2):
                sides = [dynamic(rel, (g.core ^ c) * 4 + (g.x ^ x) * 2 + (g.y ^ y), 0) for y in range(2)]
                rows.append(jnp.stack(sides, axis=1))
        return jnp.stack(rows).reshape((2, 2) + rows[0].shape)


class Sum:
    def __init__(self, grid, own, other, z_first=False):
        self.grid, self.z_first = grid, z_first
        rows = own.shape[0] // 8
        self.own = own.reshape(4, 2, rows, own.shape[1])
        self.other = other
        self.across, self.ring = {}, [[], []]
        self.came = self.far = None

    def c(self):
        def keep(a):
            self.came = a.reshape(self.own.shape)

        return [(self.grid.swap_core, self.other, keep)]

    def both(self, step, side):
        return self.own[step, side].astype(F32) + self.came[step, side].astype(F32)

    def y(self, *steps):
        if self.z_first:
            value = self.both(0, 1) + self.ring[1][-1].astype(F32)
            return [(self.grid.swap_y, value.astype(BF), partial(self.across.__setitem__, 0))]
        return [
            (self.grid.swap_y, self.both(step, 1).astype(BF), partial(self.across.__setitem__, step)) for step in steps
        ]

    def y32(self):
        return self.y(3, 2)

    def y10(self):
        return self.y(1, 0)

    def y3210(self):
        return self.y(3, 2, 1, 0)

    def block(self, step, side):
        total = self.both(step, side)
        if not self.z_first:
            total = total + self.across[step].astype(F32)
        if self.ring[side]:
            total = total + self.ring[side][-1].astype(F32)
        return total

    def z(self):
        sides = (0, 1) if self.z_first else (0,)
        return [
            (self.grid.ring_z, self.block(3 - len(self.ring[side]), side).astype(BF), self.ring[side].append)
            for side in sides
        ]

    def near(self):
        total = self.block(0, 0)
        return total + self.across[0].astype(F32) if self.z_first else total

    def x(self, to):
        move = self.grid.to_joining if to else self.grid.to_text
        return [(move, self.near().astype(BF), partial(setattr, self, "far"))]

    def x_text(self):
        return self.x(0)

    def x_joining(self):
        return self.x(1)

    def total(self):
        return self.near() + self.far.astype(F32)


class BlockSum:
    def __init__(self, grid, a, dtype):
        self.grid, self.a, self.dtype = grid, a, dtype
        self.ring = None

    def step(self, swap, place, axis):
        own = dynamic(self.a, place, axis)

        def keep(came):
            self.a = own.astype(F32) + came.astype(F32)

        return [(swap, dynamic(self.a, 1 - place, axis).astype(self.dtype), keep)]

    def c(self):
        return self.step(self.grid.swap_core, self.grid.core, 1)

    def x(self):
        return self.step(self.grid.swap_x, self.grid.x, 0)

    def y(self):
        return self.step(self.grid.swap_y, self.grid.y, 1)

    def z(self):
        if self.ring is None:
            self.ring = []
        value = self.block(3 - len(self.ring))
        return [(self.grid.ring_z, value.astype(self.dtype), self.ring.append)]

    def block(self, step):
        value = dynamic(self.a, (self.grid.z + step) % 4, 0).astype(F32)
        return value + self.ring[-1].astype(F32) if self.ring else value

    def total(self):
        return self.block(0)


def masks(caption_len, phrase_len, box_count, patch_mask, text_rows, patches):
    slots = jnp.arange(phrase_len.shape[1], dtype=jnp.int32)
    phrase_total = jnp.sum(jnp.where(slots[None, :] < box_count[:, None], phrase_len, 0), axis=1)
    lengths = jnp.minimum(caption_len + phrase_total, text_rows)
    first_patch = (jnp.arange(patch_mask.shape[1], dtype=jnp.int32) == 0).astype(jnp.int32)
    keep = jnp.maximum(patch_mask, first_patch[None, :]).astype(F32)
    return lengths, jnp.pad(keep, ((0, 0), (0, patches - keep.shape[1])))


def on_device(
    text_embed,
    image_feats,
    caption_len,
    phrase_len,
    box_count,
    patch_mask,
    attn_qkv,
    attn_out,
    ffn_up,
    ffn_down,
    layer_vectors,
    cross_query,
    cross_kv,
    cross_out,
    cross_vectors,
    cotangent,
):
    n_pipe, n_dp = lax.axis_size("pipe"), lax.axis_size("dp")
    everyone = ("pipe", "dp")
    shards, half = n_pipe * n_dp, n_pipe // 2
    samples, text_rows, width = text_embed.shape
    hidden = ffn_up.shape[1] * n_dp
    lanes = attn_qkv.shape[0]
    patches = -(-image_feats.shape[1] // 32) * 32
    direct = (n_pipe, n_dp) == (4, 8) and lanes % 128 == 0
    lengths, patch_keep = masks(caption_len, phrase_len, box_count, patch_mask, text_rows, patches)
    x = text_embed.reshape(-1, width)
    image = jnp.pad(image_feats, ((0, 0), (0, patches - image_feats.shape[1]), (0, 0)))
    image = image.reshape(samples * patches, -1)

    c_rows = cross_query.shape[0]
    kv_slices = cross_kv.shape[1] // width
    cross_pack = jnp.concatenate([cross_query, cross_out, lane_slices(cross_kv, width)], axis=0)
    v_rows, v_lanes = layer_vectors.shape
    x_rows = cross_vectors.shape[1]
    small = jnp.concatenate([pad_to(layer_vectors, v_rows, 128), pad_to(cross_vectors.T, x_rows, 128)], axis=0)
    small = pad_to(small, 16, 128).astype(F32)
    pack_attn = jnp.concatenate([attn_qkv.T, attn_out.T], axis=0)
    pack_feed = jnp.concatenate([ffn_up.T, lane_slices(ffn_down.T, lanes)], axis=0)

    def cross_weights(blocks):
        blocks = blocks.reshape(shards, -1, width)
        i_rows = cross_kv.shape[0]
        ends = np.cumsum([0, c_rows, c_rows, i_rows, i_rows])
        return [blocks[:, a:b].reshape(-1, width) for a, b in zip(ends[:-1], ends[1:])]

    def vectors_of(blocks):
        blocks = blocks.reshape(n_pipe, n_dp, 16, 128)
        vecs = []
        for layer in range(2):
            v = blocks[layer * half : (layer + 1) * half, :, :v_rows, :v_lanes]
            vecs.append(jnp.moveaxis(v, 1, 2).reshape(12, width))
        cvec = blocks.reshape(shards, 16, 128)[:, v_rows : v_rows + x_rows, :c_rows]
        return vecs, [v[8:12].reshape(1, hidden) for v in vecs], jnp.moveaxis(cvec, 1, 0).reshape(x_rows, width)

    def keys_values(wk, wv, cvec):
        keys = jnp.dot(image, wk, preferred_element_type=F32).astype(BF)
        return keys, (jnp.dot(image, wv, preferred_element_type=F32) + cvec[1]).astype(BF)

    def pack_cross(dk, dv, g_cq, g_co):
        grads = [g_cq, g_co, dot(image, dk, TN).astype(BF), dot(image, dv, TN).astype(BF)]
        return jnp.concatenate([g.reshape(shards, -1, width) for g in grads], axis=1)

    def vector_block(v_self, v_feed, v_up):
        v = jnp.concatenate([v_self[:5], v_feed[:3], v_up.reshape(4, width)], axis=0)
        return jnp.moveaxis(v.reshape(half, v_rows, n_dp, v_lanes), 2, 1)

    def pack_vectors(text, joining, v_cross):
        section = jnp.concatenate([vector_block(*text), vector_block(*joining)], axis=0)
        cross = jnp.moveaxis(v_cross[:x_rows].reshape(x_rows, n_pipe, n_dp, c_rows), 0, 2)
        wide = [jnp.pad(v, ((0, 0), (0, 0), (0, 0), (0, 128 - v.shape[3]))) for v in (section, cross)]
        wide = jnp.concatenate(wide, axis=2)
        return jnp.pad(wide, ((0, 0), (0, 0), (0, 16 - wide.shape[2]), (0, 0)))

    seed = cotangent.reshape(-1, width)
    if direct:
        grid = Grid()
        turn = grid.turn
        n_attn = pack_attn.shape[0]
        where = jnp.stack([grid.core, grid.z, grid.y]).astype(jnp.int32)
        vec_gather = BlockGather(grid, small)
        cross_whole = lax.all_gather(cross_pack, everyone, axis=0, tiled=True)
        met = {}

        def meet(name, pack):
            return [(grid.swap_x, pack, partial(met.__setitem__, name))]

        def of_layer(layer, pack, other, **how):
            return Gather(grid, jnp.where(grid.x == layer, pack, other), **how)

        turn(partial(meet, "attn", pack_attn), partial(meet, "feed", pack_feed), vec_gather.z_all)
        both = [jnp.concatenate([pack_attn, pack_feed]), jnp.concatenate([met["attn"], met["feed"]])]
        text = of_layer(0, *both)
        attn2 = of_layer(1, pack_attn, met["attn"])
        feed2 = of_layer(1, pack_feed, met["feed"])
        turn(text.z, text.y, vec_gather.y)
        turn(text.z, text.y, vec_gather.x0, vec_gather.x1)
        turn(text.z, text.y, text.c, vec_gather.c)
        turn(text.y, text.c, attn2.z, attn2.y)
        vecs, biases, cvec = vectors_of(vec_gather.whole())
        state, low, s_self = turn(
            attn2.y, attn2.z, feed2.y, feed2.z, pre=(text.c,),
            compute=lambda x: self_forward(x, lengths, where, vecs[0], text.pieces()), args=(x,),
        )
        state, passed, s_feed = turn(
            attn2.y, attn2.z, feed2.y, feed2.z,
            compute=lambda state, low: feed_forward(state, low, where, vecs[0], biases[0], text.pieces(), n_attn),
            args=(state, low),
        )

        def third(cross_whole):
            wq, wo, wk, wv = cross_weights(cross_whole)
            return *keys_values(wk, wv, cvec), wq, wo

        keys, values, wq, wo = turn(
            attn2.y, feed2.y, feed2.z, attn2.c, compute=third, args=(cross_whole,)
        )
        state, low, s_self2 = turn(
            feed2.y, feed2.c, pre=(attn2.c,),
            compute=lambda passed: self_forward(passed, lengths, where, vecs[1], attn2.pieces()), args=(passed,),
        )
        state, low, s_cross = turn(
            feed2.c, compute=lambda *a: cross_forward(*a, patch_keep, keys, values, cvec, wq, wo), args=(state, low)
        )

        def last(state, low):
            joined, _, s_feed2 = feed_forward(state, low, where, vecs[1], biases[1], feed2.pieces())
            return joined, feed_backward(seed, s_feed2, where, vecs[1], feed2.pieces())

        joined, (grad, *g_feed2, v_feed2, v_up2) = turn(compute=last, args=(state, low))

        sum3 = Sum(grid, *g_feed2)
        grad, dk, dv, g_cq, g_co, v_cross = turn(
            sum3.y32, pre=(sum3.c,), compute=lambda grad: cross_backward(grad, s_cross, cvec, wq, wo), args=(grad,)
        )
        grad, *g_self2, v_self2 = turn(
            sum3.y10, sum3.z,
            compute=lambda grad: self_backward(grad, s_self2, where, vecs[1], attn2.pieces()), args=(grad,),
        )
        sum2 = Sum(grid, *g_self2)
        cross_grads, grad = turn(
            sum2.c, sum3.z, compute=lambda *a: (pack_cross(*a[:4]), a[4].astype(BF)), args=(dk, dv, g_cq, g_co, grad)
        )
        sum_cross = BlockSum(grid, cross_grads.reshape(2, 2, 4, 2, -1, width), BF)
        grad, *g_feed1, v_feed, v_up = turn(
            sum2.y3210, sum3.z, sum_cross.c,
            compute=lambda grad: feed_backward(grad, s_feed, where, vecs[0], text.pieces(), n_attn), args=(grad,),
        )
        sum1 = Sum(grid, *g_feed1)
        embed_grad, *g_self1, v_self = turn(
            sum1.y32, sum2.z, sum_cross.x, pre=(sum1.c,),
            compute=lambda grad: self_backward(grad, s_self, where, vecs[0], text.pieces()), args=(grad,),
        )
        sum0 = Sum(grid, *g_self1)
        sum_vec = BlockSum(
            grid,
            pack_vectors((v_self, v_feed, v_up), (v_self2, v_feed2, v_up2), v_cross).reshape(2, 2, 4, 2, 16, 128),
            F32,
        )
        turn(sum1.y10, sum1.z, sum2.z, sum3.x_joining, sum_vec.c, pre=(sum0.c,))
        turn(sum0.y3210, sum1.z, sum2.z, sum_vec.x)
        turn(sum0.z, sum1.z, sum2.x_joining, sum_cross.y, sum_vec.y)
        turn(sum0.z, sum1.x_text, sum_cross.z, sum_vec.z)
        turn(sum0.z, sum_cross.z, sum_vec.z)
        turn(sum0.x_text, sum_cross.z, sum_vec.z)
        text = grid.x == 0
        attn_grads = jnp.where(text, sum0.total(), sum2.total())
        feed_grads = jnp.where(text, sum1.total(), sum3.total())
        n_qkv, n_up = attn_qkv.shape[1], ffn_up.shape[1]
        mine = [attn_grads[:n_qkv], attn_grads[n_qkv:], feed_grads[:n_up], feed_grads[n_up:]]
        cross_grads, small = sum_cross.total(), sum_vec.total()
    else:
        where = jnp.zeros((3,), jnp.int32)
        vectors = lax.all_gather(small, everyone, axis=0, tiled=False)
        whole = lax.all_gather(jnp.concatenate([pack_attn, pack_feed], axis=0), everyone, axis=0, tiled=False)
        whole = whole.reshape(n_pipe, n_dp, -1, lanes)

        def section(piece, layer):
            piece = jnp.moveaxis(piece[layer * half : (layer + 1) * half], 0, 2)
            return piece.reshape(n_dp * piece.shape[1], half * piece.shape[-1])

        counts = [attn_qkv.shape[1], attn_out.shape[1], ffn_up.shape[1], attn_out.shape[1] * (hidden // width)]
        ends = np.cumsum([0] + counts)
        cut = [whole[:, :, a:b] for a, b in zip(ends[:-1], ends[1:])]
        cut[3] = lane_join(cut[3], hidden // width)
        (qkv1, out1, up1, down1), (qkv2, out2, up2, down2) = ([section(c, k) for c in cut] for k in range(2))
        vecs, biases, cvec = vectors_of(vectors)
        wq, wo, wk, wv = cross_weights(lax.all_gather(cross_pack, everyone, axis=0, tiled=False))
        state, low, s_self = self_forward(x, lengths, where, vecs[0], [qkv1, out1])
        state, passed, s_feed = feed_forward(state, low, where, vecs[0], biases[0], [up1, down1])
        state, low, s_self2 = self_forward(passed, lengths, where, vecs[1], [qkv2, out2])
        keys, values = keys_values(wk, wv, cvec)
        state, low, s_cross = cross_forward(state, low, patch_keep, keys, values, cvec, wq, wo)
        joined, _, s_feed2 = feed_forward(state, low, where, vecs[1], biases[1], [up2, down2])
        grad, *g_feed2, v_feed2, v_up2 = feed_backward(seed, s_feed2, where, vecs[1], [up2, down2])
        grad, dk, dv, g_cq, g_co, v_cross = cross_backward(grad, s_cross, cvec, wq, wo)
        grad, *g_self2, v_self2 = self_backward(grad, s_self2, where, vecs[1], [qkv2, out2])
        grad, *g_feed1, v_feed, v_up = feed_backward(grad.astype(BF), s_feed, where, vecs[0], [up1, down1])
        embed_grad, *g_self1, v_self = self_backward(grad, s_self, where, vecs[0], [qkv1, out1])

        def unpack(pair, rows, slices):
            parts = []
            at = 0
            for r, k in zip(rows, slices):
                sides = [p.reshape(8, -1, p.shape[1])[:, at : at + r * k] for p in pair]
                sides = [lane_join(p, k).reshape(8 * r, -1) for p in sides]
                parts.append(jnp.concatenate(sides, axis=1))
                at += r * k
            return parts

        def split(first, second):
            both = jnp.stack([first, second])
            rows, k = both.shape[1] // n_dp, both.shape[2] // (half * lanes)
            both = both.reshape(2, n_dp, rows, half, k, lanes)
            return both.transpose(0, 3, 1, 4, 2, 5).reshape(n_pipe, n_dp, k * rows, lanes)

        attn = ((3 * width // 8, width // 8), (1, 1))
        feed = ((hidden // 8, width // 8), (1, hidden // width))
        parts = []
        for first, second, shape in ((g_self1, g_self2, attn), (g_feed1, g_feed2, feed)):
            parts += [split(a, b) for a, b in zip(unpack(first, *shape), unpack(second, *shape))]
        packed = jnp.concatenate(parts, axis=2).reshape(-1, lanes)
        packed = lax.psum_scatter(packed, everyone, scatter_dimension=0, tiled=True).astype(F32)
        mine = [packed[a:b] for a, b in zip(ends[:-1], ends[1:])]
        cross_grads = pack_cross(dk, dv, g_cq, g_co).reshape(-1, width)
        cross_grads = lax.psum_scatter(cross_grads, everyone, scatter_dimension=0, tiled=True).astype(F32)
        small = pack_vectors((v_self, v_feed, v_up), (v_self2, v_feed2, v_up2), v_cross)
        small = lax.psum_scatter(small.reshape(-1, 128), everyone, scatter_dimension=0, tiled=True)
    mine[3] = lane_join(mine[3], hidden // width)
    return (
        joined.reshape(text_embed.shape),
        embed_grad.reshape(text_embed.shape),
        mine[0].T,
        mine[1].T,
        mine[2].T,
        mine[3].T,
        small[:v_rows, :v_lanes],
        cross_grads[:c_rows],
        lane_join(cross_grads[2 * c_rows :], kv_slices),
        cross_grads[c_rows : 2 * c_rows],
        small[v_rows : v_rows + x_rows, :c_rows].T,
    )


def solution(mesh):
    in_specs = (
        P(("pipe", "dp"), None, None),
        P(("pipe", "dp"), None, None),
        P(("pipe", "dp")),
        P(("pipe", "dp"), None),
        P(("pipe", "dp")),
        P(("pipe", "dp"), None),
        P("pipe", "dp"),
        P("pipe", "dp"),
        P("pipe", "dp"),
        P("pipe", "dp"),
        P("pipe", "dp"),
        P(("pipe", "dp"), None),
        P(("pipe", "dp"), None),
        P(("pipe", "dp"), None),
        P(("pipe", "dp"), None),
        P(("pipe", "dp"), None, None),
    )
    out_specs = (
        P(("pipe", "dp"), None, None),
        P(("pipe", "dp"), None, None),
        P("pipe", "dp"),
        P("pipe", "dp"),
        P("pipe", "dp"),
        P("pipe", "dp"),
        P("pipe", "dp"),
        P(("pipe", "dp"), None),
        P(("pipe", "dp"), None),
        P(("pipe", "dp"), None),
        P(("pipe", "dp"), None),
    )
    return jax.shard_map(
        on_device, mesh=mesh, in_specs=in_specs, out_specs=out_specs, check_vma=False
    )
```

```python
from functools import partial

import jax
import jax.numpy as jnp
import numpy as np
from jax import lax
from jax.experimental import pallas as pl
from jax.experimental.pallas import tpu as pltpu
from jax.sharding import PartitionSpec as P

HEADS = 12
NORM_EPS = 1e-12
MASKED = -1e30
BF = jnp.bfloat16
F32 = jnp.float32
NT = (((1,), (1,)), ((), ()))
NN = (((1,), (0,)), ((), ()))
TN = (((0,), (0,)), ((), ()))
VMEM_BYTES = 58 * 2**20
TILE = 768
CHUNK = 128


def dot(a, b, dims=NN):
    return lax.dot_general(a, b, dims, preferred_element_type=F32)


def span(start, size, unit=128):
    return pl.ds(pl.multiple_of(start, unit), size)


def tiles(count, body):
    def step(i, carry):
        body(i)
        return carry

    lax.fori_loop(0, count, step, 0)


class Copies:
    def __init__(self, sems):
        self.sems, self.used = sems, 0
        self.coming, self.going, self.sent = [], [], []

    def copy(self, source, target):
        self.used += 1
        copy = pltpu.make_async_copy(source, target, self.sems.at[self.used - 1])
        copy.start()
        return copy

    def begin(self, *refs):
        for k, (held, source, _) in enumerate(self.coming):
            if any(held is ref for ref in refs):
                self.coming[k] = (held, source, self.copy(source, held))

    def need(self, *refs):
        for k, (held, source, copy) in enumerate(self.coming):
            if any(held is ref for ref in refs):
                copy.wait()
                self.coming[k] = (None, source, None)

    def send(self, *refs, part=()):
        for held, target in self.going:
            if any(held is ref for ref in refs):
                self.sent.append(self.copy(held.at[part], target.at[part]) if part else self.copy(held, target))

    def finish(self):
        settle(self.sent)


def fetch(copies, sems, here=None):
    started = []
    for k in range(len(copies[0][0])):
        started.append([pltpu.make_async_copy(s[k], t, sems.at[i]) for i, (s, t) in enumerate(copies)])

    def start(group):
        for copy in group:
            copy.start()

    if len(started) == 1:
        start(started[0])
    else:
        pl.when(here)(lambda: start(started[0]))
        pl.when(jnp.logical_not(here))(lambda: start(started[1]))
    return started[0]


def settle(started):
    for copy in started:
        copy.wait()


def placed(refs, where_ref, layout, target, lanes):
    if len(refs) == 1:
        return [(refs, target)]
    core, z, y = where_ref[0], where_ref[1], where_ref[2]
    copies = []
    for i, pair in enumerate(zip(refs[:16], refs[16:])):
        c_rel, y_rel, z_rel = i // 8, (i // 4) % 2, i % 4
        block = lax.rem(z - z_rel + 4, 4) * 2 + lax.rem(y + y_rel, 2)
        side = lax.rem(core + c_rel, 2)
        for first, rows, shift in layout:
            place = target.at[
                span(block * rows, rows, 16),
                span(side * lanes + shift * pair[0].shape[1], pair[0].shape[1]),
            ]
            copies.append(([ref.at[pl.ds(first, rows)] for ref in pair], place))
    return copies


def relative(where_ref, block):
    z = lax.rem(block // 2 - where_ref[1] + 4, 4)
    return z * 2 + lax.rem(block % 2 + where_ref[2], 2)


def norm_rows(x_ref, bias, gain, offset, y_ref, low_ref, n_ref, r_ref):
    for i in range(0, y_ref.shape[0], CHUNK):
        rows = pl.ds(i, CHUNK)
        u = x_ref[rows, :].astype(F32) + (y_ref[rows, :] + bias)
        center = u - jnp.mean(u, axis=-1, keepdims=True)
        scale = lax.rsqrt(jnp.mean(center * center, axis=-1, keepdims=True) + NORM_EPS)
        normed = center * scale
        y = normed * gain + offset
        y_ref[rows, :] = y
        low_ref[rows, :] = y.astype(BF)
        n_ref[rows, :] = normed.astype(BF)
        r_ref[rows, :] = scale


def norm_rows_back(dy_ref, n_ref, r_ref, gain, du_ref, db_ref):
    def chunk(i, sums):
        rows = span(i * CHUNK, CHUNK, CHUNK)
        dy = dy_ref[rows, :].astype(F32)
        n = n_ref[rows, :].astype(F32)
        s = dy * gain
        du = r_ref[rows, :] * (
            s - jnp.mean(s, axis=-1, keepdims=True) - n * jnp.mean(s * n, axis=-1, keepdims=True)
        )
        db = du.astype(BF)
        du_ref[rows, :] = du
        db_ref[rows, :] = db
        terms = (dy * n, dy, db.astype(F32))
        return tuple(a + jnp.sum(t, axis=0, keepdims=True) for a, t in zip(sums, terms))

    zero = jnp.zeros((1, dy_ref.shape[1]), F32)
    return lax.fori_loop(0, dy_ref.shape[0] // CHUNK, chunk, (zero, zero, zero))


def split_heads(a):
    first = lax.broadcasted_iota(jnp.int32, a.shape, 1) < a.shape[1] // 2
    zero = jnp.zeros_like(a)
    return jnp.concatenate([jnp.where(first, a, zero), jnp.where(first, zero, a)], axis=0)


def join_heads(a):
    rows = a.shape[0] // 2
    first = lax.broadcasted_iota(jnp.int32, (rows, a.shape[1]), 1) < a.shape[1] // 2
    return jnp.where(first, a[:rows], a[rows:])


def softmax(scores, mask):
    scores = scores + mask
    e = jnp.exp(scores - jnp.max(scores, axis=-1, keepdims=True))
    return (e * (1.0 / jnp.sum(e, axis=-1, keepdims=True))).astype(BF)


def score_back(weights, d_weights):
    a = weights.astype(F32)
    t = a * d_weights
    return (t - a * jnp.sum(t, axis=-1, keepdims=True)).astype(BF)


def project_and_norm(x_ref, o_ref, w_ref, dims, bias, gain, offset, outs):
    y_ref, low_ref, n_ref, r_ref = outs
    width = y_ref.shape[1]

    def tile(j):
        cols = span(j * TILE, TILE)
        w = w_ref[cols, :] if dims is NT else w_ref[:, cols]
        y_ref[:, cols] = dot(o_ref[...], w, dims)

    tiles(width // TILE, tile)
    norm_rows(x_ref, bias, gain, offset, y_ref, low_ref, n_ref, r_ref)


def self_forward_kernel(count, layer, io, ins, outs, scratch):
    lengths, where_ref, x_ref, vec_ref, *refs = ins
    p_ref, a_ref, o_ref, y_ref, low_ref, n_ref, r_ref = outs
    qkv, out, bias_ref, sems, sems2 = scratch
    width = x_ref.shape[1]
    n, m = qkv.shape[0] // 8, out.shape[0] // 8
    whole = count == 2
    here = where_ref[3] == layer
    first = fetch(placed(refs[:1] if whole else refs, where_ref, [(0, n, 0)], qkv, width // 2), sems, here)
    bias_ref[:, :width] = vec_ref[0:1, :]
    bias_ref[:, width : 2 * width] = jnp.zeros((1, width), F32)
    bias_ref[:, 2 * width :] = vec_ref[1:2, :]
    settle(first)
    second = fetch(placed(refs[1:] if whole else refs, where_ref, [(n, m, 0)], out, width // 2), sems2, here)

    def tile(j):
        cols = span(j * TILE, TILE)
        p_ref[:, cols] = (dot(x_ref[...], qkv[cols, :], NT) + bias_ref[:, cols]).astype(BF)

    tiles(3 * width // TILE, tile)
    io.send(p_ref)
    pairs = width // 128
    row = lax.broadcasted_iota(jnp.int32, (256, 128), 0)
    lane = lax.broadcasted_iota(jnp.int32, (256, 128), 1)
    same = ((row // 64) % 2) == (lane // 64)
    key_lane = lax.broadcasted_iota(jnp.int32, (1, 128), 1)

    def attend(s):
        rows = span(s * 128, 128)
        length = jnp.where(key_lane < 64, lengths[2 * s], lengths[2 * s + 1])
        mask = jnp.where(same & (lax.rem(key_lane, 64) < length), 0.0, MASKED)
        for h in range(pairs):
            q = p_ref[rows, pl.ds(h * 128, 128)]
            k = p_ref[rows, pl.ds(width + h * 128, 128)]
            v = p_ref[rows, pl.ds(2 * width + h * 128, 128)]
            a = softmax(dot(split_heads(q * 0.125), k, NT), mask)
            a_ref[s * pairs + h] = a
            o_ref[rows, pl.ds(h * 128, 128)] = join_heads(dot(a, v)).astype(BF)

    tiles(x_ref.shape[0] // 128, attend)
    io.send(a_ref, o_ref)
    settle(second)
    project_and_norm(
        x_ref, o_ref, out, NT, vec_ref[2:3, :], vec_ref[3:4, :], vec_ref[4:5, :], (y_ref, low_ref, n_ref, r_ref)
    )


def self_backward_kernel(count, layer, io, ins, outs, scratch):
    where_ref, dy_ref, x_ref, vec_ref, p_ref, a_ref, o_ref, n_ref, r_ref, *refs = ins
    dx_ref, own_ref, other_ref, gv_ref = outs
    qkv, out, db_ref, dmix_ref, dp_ref, rel_ref, g_ref, sems, sems2 = scratch
    width = x_ref.shape[1]
    half = width // 2
    n, m = qkv.shape[0] // 8, out.shape[0] // 8
    whole = count == 2
    here = where_ref[3] == layer
    second = fetch(placed(refs[1:] if whole else refs, where_ref, [(n, m, 0)], out, half), sems2, here)
    io.begin(o_ref, p_ref, a_ref)
    core = where_ref[0]
    g_gain, g_offset, g_bias = norm_rows_back(dy_ref, n_ref, r_ref, vec_ref[3:4, :], dx_ref, db_ref)
    settle(second)

    def mix(j):
        cols = span(j * TILE, TILE)
        dmix_ref[:, cols] = dot(db_ref[...], out[:, cols]).astype(BF)

    tiles(width // TILE, mix)
    io.need(o_ref, p_ref, a_ref)
    rel_ref[:, :half] = o_ref[:, span(core * half, half)]
    rel_ref[:, half:] = o_ref[:, span((1 - core) * half, half)]

    g_ref[:width, :] = dot(db_ref[...], rel_ref[...], TN).astype(BF)
    for b in range(8):
        to, at = relative(where_ref, b), pl.ds(b * m, m)
        own_ref[to, n:, :] = g_ref[at, :half]
        other_ref[to, n:, :] = g_ref[at, half:]
    io.begin(x_ref)
    first = fetch(placed(refs[:1] if whole else refs, where_ref, [(0, n, 0)], qkv, half), sems, here)
    pairs = width // 128

    def attend(s):
        rows = span(s * 128, 128)
        for h in range(pairs):
            q2 = split_heads(p_ref[rows, pl.ds(h * 128, 128)])
            k = p_ref[rows, pl.ds(width + h * 128, 128)]
            v = p_ref[rows, pl.ds(2 * width + h * 128, 128)]
            do2 = split_heads(dmix_ref[rows, pl.ds(h * 128, 128)])
            a = a_ref[s * pairs + h]
            ds = score_back(a, dot(do2, v, NT))
            dp_ref[rows, pl.ds(h * 128, 128)] = (join_heads(dot(ds, k)) * 0.125).astype(BF)
            dp_ref[rows, pl.ds(width + h * 128, 128)] = (dot(ds, q2, TN) * 0.125).astype(BF)
            dp_ref[rows, pl.ds(2 * width + h * 128, 128)] = dot(a, do2, TN).astype(BF)

    tiles(x_ref.shape[0] // 128, attend)
    io.need(x_ref)
    rel_ref[:, :half] = x_ref[:, span(core * half, half)]
    rel_ref[:, half:] = x_ref[:, span((1 - core) * half, half)]

    def qkv_grad(j):
        rows = span(j * TILE, TILE)
        g_ref[rows, :] = dot(dp_ref[:, rows], rel_ref[...], TN).astype(BF)

    tiles(3 * width // TILE, qkv_grad)
    for b in range(8):
        to, at = relative(where_ref, b), pl.ds(b * n, n)
        own_ref[to, :n, :] = g_ref[at, :half]
        other_ref[to, :n, :] = g_ref[at, half:]
    io.send(other_ref, own_ref)
    settle(first)

    def back(j):
        cols = span(j * TILE, TILE)
        dx_ref[:, cols] += dot(dp_ref[...], qkv[:, cols])

    tiles(width // TILE, back)
    gv_ref[0:1, :] = jnp.sum(dp_ref[:, :width].astype(F32), axis=0, keepdims=True)
    gv_ref[1:2, :] = jnp.sum(dp_ref[:, 2 * width :].astype(F32), axis=0, keepdims=True)
    gv_ref[2:3, :] = g_bias
    gv_ref[3:4, :] = g_gain
    gv_ref[4:5, :] = g_offset


def cross_forward_kernel(io, ins, outs, scratch):
    x_ref, low_x_ref, keep_ref, k_ref, v_ref, vec_ref, wq_ref, wo_ref = ins
    q_ref, a_ref, o_ref, y_ref, low_ref, n_ref, r_ref = outs
    io.begin(k_ref, v_ref)
    width = x_ref.shape[1]
    patches = k_ref.shape[0] // keep_ref.shape[0]

    def tile(j):
        cols = span(j * TILE, TILE)
        q_ref[:, cols] = (dot(low_x_ref[...], wq_ref[:, cols]) + vec_ref[0:1, cols]).astype(BF)

    tiles(width // TILE, tile)
    io.send(q_ref)
    io.need(k_ref, v_ref)
    io.begin(x_ref, wo_ref)
    pairs = width // 128

    def attend(s):
        rows, keys = span(s * 64, 64, 64), span(s * patches, patches, 16)
        mask = jnp.where(keep_ref[pl.ds(s, 1), :] > 0, 0.0, MASKED)
        for h in range(pairs):
            q = q_ref[rows, pl.ds(h * 128, 128)]
            k = k_ref[keys, pl.ds(h * 128, 128)]
            v = v_ref[keys, pl.ds(h * 128, 128)]
            a = softmax(dot(split_heads(q * 0.125), k, NT), mask)
            a_ref[s * pairs + h] = a
            o_ref[rows, pl.ds(h * 128, 128)] = join_heads(dot(a, v)).astype(BF)

    tiles(keep_ref.shape[0], attend)
    io.send(a_ref, o_ref)
    io.need(x_ref, wo_ref)
    project_and_norm(
        x_ref, o_ref, wo_ref, NN, vec_ref[2:3, :], vec_ref[3:4, :], vec_ref[4:5, :], (y_ref, low_ref, n_ref, r_ref)
    )


def cross_backward_kernel(io, ins, outs, scratch):
    dy_ref, low_x_ref, k_ref, v_ref, vec_ref, wq_ref, wo_ref, q_ref, a_ref, o_ref, n_ref, r_ref = ins
    dx_ref, dk_ref, dv_ref, gq_ref, go_ref, gv_ref = outs
    db_ref, dmix_ref, dq_ref = scratch
    width = low_x_ref.shape[1]
    patches = a_ref.shape[2]
    io.begin(wo_ref, o_ref)
    g_gain, g_offset, g_bias = norm_rows_back(dy_ref, n_ref, r_ref, vec_ref[3:4, :], dx_ref, db_ref)

    io.begin(q_ref, k_ref, v_ref, a_ref)
    io.need(wo_ref, o_ref)

    def mix(j):
        cols = span(j * TILE, TILE)
        dmix_ref[:, cols] = dot(db_ref[...], wo_ref[cols, :], NT).astype(BF)
        go_ref[cols, :] = dot(o_ref[:, cols], db_ref[...], TN).astype(BF)

    tiles(width // TILE, mix)
    io.send(go_ref)
    io.need(q_ref, k_ref, v_ref, a_ref)
    io.begin(wq_ref, low_x_ref)
    pairs = width // 128

    def attend(s):
        rows, keys = span(s * 64, 64, 64), span(s * patches, patches, 16)
        for h in range(pairs):
            q2 = split_heads(q_ref[rows, pl.ds(h * 128, 128)])
            k = k_ref[keys, pl.ds(h * 128, 128)]
            v = v_ref[keys, pl.ds(h * 128, 128)]
            do2 = split_heads(dmix_ref[rows, pl.ds(h * 128, 128)])
            a = a_ref[s * pairs + h]
            ds = score_back(a, dot(do2, v, NT))
            dq_ref[rows, pl.ds(h * 128, 128)] = (join_heads(dot(ds, k)) * 0.125).astype(BF)
            dk_ref[keys, pl.ds(h * 128, 128)] = (dot(ds, q2, TN) * 0.125).astype(BF)
            dv_ref[keys, pl.ds(h * 128, 128)] = dot(a, do2, TN).astype(BF)

    tiles(a_ref.shape[0] // pairs, attend)
    io.send(dk_ref, dv_ref)
    io.need(wq_ref, low_x_ref)

    def back(j):
        cols = span(j * TILE, TILE)
        dx_ref[:, cols] += dot(dq_ref[...], wq_ref[cols, :], NT)
        gq_ref[cols, :] = dot(low_x_ref[:, cols], dq_ref[...], TN).astype(BF)

    tiles(width // TILE, back)
    gv_ref[0:1, :] = jnp.sum(dq_ref[...].astype(F32), axis=0, keepdims=True)
    gv_ref[1:2, :] = jnp.sum(dv_ref[...].astype(F32), axis=0, keepdims=True)
    gv_ref[2:3, :] = g_bias
    gv_ref[3:4, :] = g_gain
    gv_ref[4:5, :] = g_offset


def gelu_parts(h):
    size = jnp.abs(h) * 0.7071067811865476
    t = 1.0 / (1.0 + 0.3275911 * size)
    e = jnp.exp(-size * size)
    poly = t * (0.254829592 + t * (-0.284496736 + t * (1.421413741 + t * (-1.453152027 + t * 1.061405429))))
    tail = 0.5 * poly * e
    cdf = jnp.where(h < 0, tail, 1.0 - tail)
    return h * cdf, cdf + h * (e * 0.3989422804014327)


def feed_weights(count, layer, where_ref, refs, up, down, sems, sems2):
    width, hidden = up.shape[1], up.shape[0]
    n, m, whole = hidden // 8, width // 8, count == 2
    base = 4 * m
    slices = [(base + n + m * i, m, i) for i in range(hidden // width)]
    here = where_ref[3] == layer
    return (
        lambda: fetch(placed(refs[:1] if whole else refs, where_ref, [(base, n, 0)], up, width // 2), sems, here),
        lambda: fetch(placed(refs[1:] if whole else refs, where_ref, slices, down, hidden // 2), sems2, here),
    )


def feed_forward_body(io, x_ref, low_x_ref, vec_ref, bias_ref, act_ref, slope_ref, norm_outs, up, down, get_up, get_down):
    settle(get_up())
    second = get_down()
    io.begin(x_ref)

    def tile(j):
        cols = span(j * TILE, TILE)
        h = dot(low_x_ref[...], up[cols, :], NT) + bias_ref[:, cols]
        act, slope = gelu_parts(h)
        act_ref[:, cols] = act.astype(BF)
        slope_ref[:, cols] = slope.astype(BF)

    tiles(up.shape[0] // TILE, tile)
    io.send(act_ref, slope_ref)
    settle(second)
    io.need(x_ref)
    project_and_norm(x_ref, act_ref, down, NT, vec_ref[5:6, :], vec_ref[6:7, :], vec_ref[7:8, :], norm_outs)


def feed_backward_body(
    io, where_ref, dy_ref, low_x_ref, vec_ref, act_ref, slope_ref, n_ref, r_ref, outs, work, up, down, get_up, get_down
):
    dx_ref, own_ref, other_ref, gv_ref, gb_ref = outs
    db_ref, dbt_ref, dh_ref, rel_ref = work
    width, hidden = up.shape[1], up.shape[0]
    n, m, half = hidden // 8, width // 8, width // 2
    core = where_ref[0]
    second = get_down()
    io.begin(slope_ref)
    g_gain, g_offset, g_bias = norm_rows_back(dy_ref, n_ref, r_ref, vec_ref[6:7, :], dx_ref, db_ref)
    dbt_ref[...] = db_ref[...].T
    settle(second)
    io.need(slope_ref)
    io.begin(act_ref, low_x_ref)

    def down_tile(j):
        cols = span(j * TILE, TILE)
        dh = (dot(db_ref[...], down[:, cols]) * slope_ref[:, cols].astype(F32)).astype(BF)
        dh_ref[:, cols] = dh
        gb_ref[:, cols] = jnp.sum(dh.astype(F32), axis=0, keepdims=True)

    tiles(hidden // TILE, down_tile)
    io.need(act_ref)

    def down_grad(j):
        for ref, side in ((own_ref, core), (other_ref, 1 - core)):
            g = dot(dbt_ref[...], act_ref[:, span(side * (hidden // 2) + j * width, width)]).astype(BF)
            for b in range(8):
                to = relative(where_ref, b)
                for k in range(2):
                    ref[to, span(n + (2 * j + k) * m, m, 16), :] = g[b * m : (b + 1) * m, k * half : (k + 1) * half]

    tiles(hidden // 2 // width, down_grad)
    io.send(other_ref, own_ref, part=(slice(None), pl.ds(n, n)))
    first = get_up()
    io.need(low_x_ref)
    rel_ref[:, :half] = low_x_ref[:, span(core * half, half)]
    rel_ref[:, half:] = low_x_ref[:, span((1 - core) * half, half)]

    def up_grad(j):
        g = dot(dh_ref[:, span(j * 2 * n, 2 * n)], rel_ref[...], TN).astype(BF)
        for k in range(2):
            to = relative(where_ref, 2 * j + k)
            own_ref[to, :n, :] = g[k * n : (k + 1) * n, :half]
            other_ref[to, :n, :] = g[k * n : (k + 1) * n, half:]

    tiles(4, up_grad)
    io.send(other_ref, own_ref, part=(slice(None), pl.ds(0, n)))
    settle(first)

    def back(j):
        cols = span(j * TILE, TILE)
        dx_ref[:, cols] += dot(dh_ref[...], up[:, cols])

    tiles(width // TILE, back)
    gv_ref[0:1, :] = g_bias
    gv_ref[1:2, :] = g_gain
    gv_ref[2:3, :] = g_offset


def feed_forward_kernel(count, layer, io, ins, outs, scratch):
    where_ref, x_ref, low_x_ref, vec_ref, bias_ref, *refs = ins
    act_ref, slope_ref, *norm_outs = outs
    up, down, sems, sems2 = scratch
    get = feed_weights(count, layer, where_ref, refs, up, down, sems, sems2)
    feed_forward_body(io, x_ref, low_x_ref, vec_ref, bias_ref, act_ref, slope_ref, norm_outs, up, down, *get)


def feed_backward_kernel(count, layer, io, ins, outs, scratch):
    where_ref, dy_ref, low_x_ref, vec_ref, act_ref, slope_ref, n_ref, r_ref, *refs = ins
    up, down, *work, sems, sems2 = scratch
    get = feed_weights(count, layer, where_ref, refs, up, down, sems, sems2)
    feed_backward_body(
        io, where_ref, dy_ref, low_x_ref, vec_ref, act_ref, slope_ref, n_ref, r_ref, outs, work, up, down, *get
    )


def feed_both_kernel(count, layer, io, ins, outs, scratch):
    where_ref, x_ref, low_x_ref, vec_ref, bias_ref, dy_ref, *refs = ins
    y_ref, *grads = outs
    up, down, *work, act_ref, slope_ref, low_ref, n_ref, r_ref, sems, sems2 = scratch
    get = feed_weights(count, layer, where_ref, refs, up, down, sems, sems2)
    norm_outs = (y_ref, low_ref, n_ref, r_ref)
    feed_forward_body(io, x_ref, low_x_ref, vec_ref, bias_ref, act_ref, slope_ref, norm_outs, up, down, *get)
    io.send(y_ref)
    feed_backward_body(
        io, where_ref, dy_ref, low_x_ref, vec_ref, act_ref, slope_ref, n_ref, r_ref, grads, work, up, down, list, list
    )


def vector_kernel(first, v_rows, v_lanes, x_rows, c_rows, *refs):
    where_ref, *pieces = refs[:33]
    vec_refs, bias_refs, cross_ref = refs[33:35], refs[35:37], refs[37]
    held, sems = refs[38:]
    core, z, y, x = where_ref[0], where_ref[1], where_ref[2], where_ref[3]
    copies = []
    for i, ref in enumerate(pieces):
        x_rel, c_rel, y_rel, z_rel = i // 16, (i // 8) % 2, (i // 4) % 2, i % 4
        pipe = lax.rem(x + x_rel, 2) * 2 + lax.rem(core + c_rel, 2)
        device = pipe * 8 + lax.rem(z - z_rel + 4, 4) * 2 + lax.rem(y + y_rel, 2)
        copies.append(([ref.at[pl.ds(first, 16), pl.ds(0, 128)]], held.at[device]))
    settle(fetch(copies, sems))
    for device in range(32):
        block = held[device].astype(F32)
        pipe, dp = device // 8, device % 8
        rows = pl.ds(pipe % 2 * v_rows, v_rows)
        vec_refs[pipe // 2][rows, pl.ds(dp * v_lanes, v_lanes)] = block[:v_rows, :v_lanes]
        cross_ref[0:x_rows, pl.ds(device * c_rows, c_rows)] = block[v_rows : v_rows + x_rows, :c_rows]
    width = cross_ref.shape[1]
    for vec_ref, bias_ref in zip(vec_refs, bias_refs):
        for j in range(4):
            bias_ref[:, j * width : (j + 1) * width] = vec_ref[8 + j : 9 + j, :]


def struct(*shape, dtype=F32):
    return jax.ShapeDtypeStruct(shape, dtype)


VMEM = pl.BlockSpec(memory_space=pltpu.VMEM)
SMEM = pl.BlockSpec(memory_space=pltpu.SMEM)
ANYWHERE = pl.BlockSpec(memory_space=pl.ANY)


def call(kernel, outs, specs, scratch, us, args, late=(), early=()):
    n_in, n_out, n_scratch = len(args), len(outs), len(scratch)
    held = [pltpu.VMEM(args[i].shape, args[i].dtype) for i in late]
    held += [pltpu.VMEM(outs[i].shape, outs[i].dtype) for i in early]

    def body(*refs):
        ins, out, rest = list(refs[:n_in]), list(refs[n_in : n_in + n_out]), refs[n_in + n_out :]
        buffers = rest[n_scratch:-1]
        io = Copies(rest[-1])
        for k, i in enumerate(late):
            io.coming.append((buffers[k], ins[i], None))
            ins[i] = buffers[k]
        for k, i in enumerate(early, len(late)):
            io.going.append((buffers[k], out[i]))
            out[i] = buffers[k]
        kernel(io, ins, out, rest[:n_scratch])
        io.finish()

    specs = [ANYWHERE if i in late else spec for i, spec in enumerate(specs)]
    return pl.pallas_call(
        body,
        out_shape=outs,
        in_specs=specs,
        out_specs=[ANYWHERE if i in early else VMEM for i in range(n_out)],
        scratch_shapes=[*scratch, *held, pltpu.SemaphoreType.DMA((24,))],
        cost_estimate=pl.CostEstimate(flops=int(us * 1.1e9), bytes_accessed=int(us * 3.5e6), transcendentals=0),
        compiler_params=pltpu.CompilerParams(vmem_limit_bytes=VMEM_BYTES),
    )(*args)


def gathered_vectors(pieces, where, first, v_rows, v_lanes, x_rows, c_rows):
    width = 8 * v_lanes
    return pl.pallas_call(
        partial(vector_kernel, first, v_rows, v_lanes, x_rows, c_rows),
        out_shape=[struct(12, width)] * 2 + [struct(1, 4 * width)] * 2 + [struct(8, width)],
        in_specs=[SMEM] + [ANYWHERE] * len(pieces),
        out_specs=[VMEM] * 5,
        scratch_shapes=[pltpu.VMEM((32, 16, 128), BF), pltpu.SemaphoreType.DMA((32,))],
        cost_estimate=pl.CostEstimate(flops=0, bytes_accessed=10**7, transcendentals=0),
    )(where, *pieces)


def copy_sems(count, parts=1):
    return pltpu.SemaphoreType.DMA((16 * parts if count > 2 else 1,))


def self_forward(x, lengths, where, vec, weights, layer):
    rows, width = x.shape
    blocks = rows // 128 * (width // 128)
    count = len(weights)
    outs = [
        struct(rows, 3 * width, dtype=BF),
        struct(blocks, 256, 128, dtype=BF),
        struct(rows, width, dtype=BF),
        struct(rows, width),
        struct(rows, width, dtype=BF),
        struct(rows, width, dtype=BF),
        struct(rows, 1),
    ]
    scratch = [
        pltpu.VMEM((3 * width, width), BF),
        pltpu.VMEM((width, width), BF),
        pltpu.VMEM((1, 3 * width), F32),
        copy_sems(count),
        copy_sems(count),
    ]
    p, a, o, y, low, n, r = call(
        partial(self_forward_kernel, count, layer),
        outs,
        [SMEM, SMEM, VMEM, VMEM] + [ANYWHERE] * count,
        scratch,
        14,
        (lengths, where, x, vec, *weights),
        early=(0, 1, 2),
    )
    return y, low, (x, p, a, o, n, r)


def self_backward(dy, saved, where, vec, weights, layer):
    x, p, a, o, n, r = saved
    rows, width = x.shape
    half = width // 2
    count = len(weights)
    outs = [
        struct(rows, width),
        struct(8, width // 2, half, dtype=BF),
        struct(8, width // 2, half, dtype=BF),
        struct(8, width),
    ]
    scratch = [
        pltpu.VMEM((3 * width, width), BF),
        pltpu.VMEM((width, width), BF),
        pltpu.VMEM((rows, width), BF),
        pltpu.VMEM((rows, width), BF),
        pltpu.VMEM((rows, 3 * width), BF),
        pltpu.VMEM((rows, width), BF),
        pltpu.VMEM((3 * width, width), BF),
        copy_sems(count),
        copy_sems(count),
    ]
    return call(
        partial(self_backward_kernel, count, layer),
        outs,
        [SMEM] + [VMEM] * 8 + [ANYWHERE] * count,
        scratch,
        22,
        (where, dy, x, vec, p, a, o, n, r, *weights),
        late=(6, 4, 5, 2),
        early=(1, 2),
    )


def cross_forward(x, low_x, keep, k, v, vec, wq, wo):
    rows, width = x.shape
    samples, patches = keep.shape
    outs = [
        struct(rows, width, dtype=BF),
        struct(samples * (width // 128), 128, patches, dtype=BF),
        struct(rows, width, dtype=BF),
        struct(rows, width),
        struct(rows, width, dtype=BF),
        struct(rows, width, dtype=BF),
        struct(rows, 1),
    ]
    q, a, o, y, low, n, r = call(
        cross_forward_kernel,
        outs,
        [VMEM] * 8,
        [],
        21,
        (x, low_x, keep, k, v, vec, wq, wo),
        late=(3, 4, 7, 0),
        early=(0, 1, 2),
    )
    return y, low, (low_x, k, v, q, a, o, n, r)


def cross_backward(dy, saved, vec, wq, wo):
    low_x, k, v, q, a, o, n, r = saved
    rows, width = low_x.shape
    outs = [
        struct(rows, width),
        struct(*k.shape, dtype=BF),
        struct(*k.shape, dtype=BF),
        struct(width, width, dtype=BF),
        struct(width, width, dtype=BF),
        struct(8, width),
    ]
    scratch = [pltpu.VMEM((rows, width), BF)] * 3
    return call(
        cross_backward_kernel,
        outs,
        [VMEM] * 12,
        scratch,
        26,
        (dy, low_x, k, v, vec, wq, wo, q, a, o, n, r),
        late=(6, 9, 7, 2, 3, 8, 5, 1),
        early=(1, 2, 4),
    )


def feed_forward(x, low_x, where, vec, bias, weights, layer):
    rows, width = x.shape
    hidden = bias.shape[1]
    count = len(weights)
    outs = [
        struct(rows, hidden, dtype=BF),
        struct(rows, hidden, dtype=BF),
        struct(rows, width),
        struct(rows, width, dtype=BF),
        struct(rows, width, dtype=BF),
        struct(rows, 1),
    ]
    scratch = [
        pltpu.VMEM((hidden, width), BF),
        pltpu.VMEM((width, hidden), BF),
        copy_sems(count),
        copy_sems(count, hidden // width),
    ]
    act, slope, y, low, n, r = call(
        partial(feed_forward_kernel, count, layer),
        outs,
        [SMEM] + [VMEM] * 4 + [ANYWHERE] * count,
        scratch,
        20,
        (where, x, low_x, vec, bias, *weights),
        late=(1,),
        early=(0, 1),
    )
    return y, low, (low_x, act, slope, n, r)


def feed_backward(dy, saved, where, vec, weights, layer):
    low_x, act, slope, n, r = saved
    rows, width = low_x.shape
    hidden = act.shape[1]
    count = len(weights)
    outs = [
        struct(rows, width),
        struct(8, 2 * hidden // 8, width // 2, dtype=BF),
        struct(8, 2 * hidden // 8, width // 2, dtype=BF),
        struct(8, width),
        struct(1, hidden),
    ]
    scratch = [
        pltpu.VMEM((hidden, width), BF),
        pltpu.VMEM((width, hidden), BF),
        pltpu.VMEM((rows, width), BF),
        pltpu.VMEM((width, rows), BF),
        pltpu.VMEM((rows, hidden), BF),
        pltpu.VMEM((rows, width), BF),
        copy_sems(count),
        copy_sems(count, hidden // width),
    ]
    return call(
        partial(feed_backward_kernel, count, layer),
        outs,
        [SMEM] + [VMEM] * 7 + [ANYWHERE] * count,
        scratch,
        22,
        (where, dy, low_x, vec, act, slope, n, r, *weights),
        late=(5, 4, 2),
        early=(1, 2),
    )


def feed_both(x, low_x, where, vec, bias, dy, weights, layer):
    rows, width = x.shape
    hidden = bias.shape[1]
    count = len(weights)
    outs = [
        struct(rows, width),
        struct(rows, width),
        struct(8, 2 * hidden // 8, width // 2, dtype=BF),
        struct(8, 2 * hidden // 8, width // 2, dtype=BF),
        struct(8, width),
        struct(1, hidden),
    ]
    scratch = [
        pltpu.VMEM((hidden, width), BF),
        pltpu.VMEM((width, hidden), BF),
        pltpu.VMEM((rows, width), BF),
        pltpu.VMEM((width, rows), BF),
        pltpu.VMEM((rows, hidden), BF),
        pltpu.VMEM((rows, width), BF),
        pltpu.VMEM((rows, hidden), BF),
        pltpu.VMEM((rows, hidden), BF),
        pltpu.VMEM((rows, width), BF),
        pltpu.VMEM((rows, width), BF),
        pltpu.VMEM((rows, 1), F32),
        copy_sems(count),
        copy_sems(count, hidden // width),
    ]
    return call(
        partial(feed_both_kernel, count, layer),
        outs,
        [SMEM] + [VMEM] * 5 + [ANYWHERE] * count,
        scratch,
        28,
        (where, x, low_x, vec, bias, dy, *weights),
        late=(1,),
        early=(0, 2, 3),
    )


def lane_slices(a, lanes):
    return jnp.concatenate([a[:, i : i + lanes] for i in range(0, a.shape[1], lanes)], axis=0)


def lane_join(a, count):
    rows = a.shape[-2] // count
    return jnp.concatenate([a[..., i * rows : (i + 1) * rows, :] for i in range(count)], axis=-1)


def pad_to(a, rows, lanes):
    return jnp.pad(a, ((0, rows - a.shape[0]), (0, lanes - a.shape[1])))


def dynamic(a, index, axis):
    return lax.dynamic_index_in_dim(a, index, axis, keepdims=False)


def after(value, tokens):
    return lax.optimization_barrier((value, tokens))[0] if tokens else value


class Grid:
    def __init__(self):
        pipe, dp = lax.axis_index("pipe"), lax.axis_index("dp")
        self.x, self.core = pipe // 2, pipe % 2
        self.z, self.y = dp // 2, dp % 2
        self.arrived, self.computed, self.slack = [()] * 2, (), 1

    def swap_x(self, a):
        return lax.ppermute(a, "pipe", [(i, i ^ 2) for i in range(4)])

    def swap_core(self, a):
        return lax.ppermute(a, "pipe", [(i, i ^ 1) for i in range(4)])

    def swap_y(self, a):
        return lax.ppermute(a, "dp", [(i, i ^ 1) for i in range(8)])

    def ring_z(self, a, step=1):
        return lax.ppermute(a, "dp", [(i, (i + 2 * step) % 8) for i in range(8)])

    def turn(self, *moves, pre=(), compute=None, args=()):
        tokens = (*self.arrived[-self.slack], *self.computed)
        arrived = []

        def begin(asked):
            asked = [ask for group in asked for ask in group()]
            values = after([value for _, value, _ in asked], tokens)
            for (move, _, keep), value in zip(asked, values):
                result = move(value)
                arrived.append(result)
                keep(result)
            return tuple(values)

        begin(pre)
        values = begin(moves)
        self.arrived.append(tuple(arrived))
        self.computed = ()
        if compute is None:
            return None
        result = compute(*after(tuple(args), tokens + values))
        self.computed = tuple(jax.tree.leaves(result))
        return result


class Gather:
    def __init__(self, grid, piece):
        self.grid, self.here, self.swapped = grid, {(0, 0, 0): piece}, {}

    def get(self, layer, y, z, over):
        sources = {"z": (layer, y, z - 1), "y": (layer, 1 - y, z), "x": (1 - layer, y, z)}
        move = {"z": self.grid.ring_z, "y": self.grid.swap_y, "x": self.grid.swap_x}[over]
        return lambda: [(move, self.here[sources[over]], partial(self.here.__setitem__, (layer, y, z)))]

    def c(self, count=16):
        ready = [key for key in self.here if key not in self.swapped][:count]
        return [(self.grid.swap_core, self.here[key], partial(self.swapped.__setitem__, key)) for key in ready]

    def c2(self):
        return self.c(2)

    def pieces(self):
        keys = [[(layer, y, z) for y in range(2) for z in range(4)] for layer in range(2)]
        return [held[key] for half in keys for held in (self.here, self.swapped) for key in half]


class PairSum:
    def __init__(self, grid, joining):
        self.grid, self.packs = grid, [None, self.pack(joining)]
        self.came, self.got = [None, None], {}

    def pack(self, pair):
        return [a.reshape((4, 2) + a.shape[1:]) for a in pair]

    def add_text(self, text):
        self.packs[0] = self.pack(text)

    def c(self, layer):
        return lambda: [(self.grid.swap_core, self.packs[layer][1], partial(self.came.__setitem__, layer))]

    def block(self, own, y, z):
        sums = [p[0][z, y].astype(F32) + c[z, y].astype(F32) for p, c in zip(self.packs, self.came)]
        total = jnp.where((self.grid.x == 0) == own, *sums)
        for part in self.got.get((own, y, z), []):
            total = total + part.astype(F32)
        return total

    def move(self, over, own, y, z):
        to = {"z": (own, y, z - 1), "y": (own, 1 - y, z), "x": (True, y, z)}[over]
        move = {"z": self.grid.ring_z, "y": self.grid.swap_y, "x": self.grid.swap_x}[over]

        def ask():
            return [(move, self.block(own, y, z).astype(BF), self.got.setdefault(to, []).append)]

        return ask

    def steps(self):
        own, other = partial(self.move, own=True), partial(self.move, own=False)
        return [
            (other("z", y=0, z=2), other("y", y=1, z=3), other("x", y=1, z=2)),
            (other("z", y=1, z=1), own("y", y=1, z=3), other("x", y=0, z=3)),
            (own("z", y=0, z=3), own("y", y=1, z=2), other("x", y=1, z=0)),
            (own("z", y=0, z=2), own("y", y=1, z=1), other("x", y=0, z=1)),
            (own("z", y=0, z=1), own("y", y=1, z=0), other("x", y=0, z=0)),
        ]

    def total(self):
        return self.block(True, 0, 0)


class BlockSum:
    def __init__(self, grid, a, dtype):
        self.grid, self.a, self.dtype = grid, a, dtype
        self.ring = []

    def step(self, swap, place, axis):
        own = dynamic(self.a, place, axis)

        def keep(came):
            self.a = own.astype(F32) + came.astype(F32)

        return [(swap, dynamic(self.a, 1 - place, axis).astype(self.dtype), keep)]

    def c(self):
        return self.step(self.grid.swap_core, self.grid.core, 1)

    def x(self):
        return self.step(self.grid.swap_x, self.grid.x, 0)

    def x0(self):
        self.halves = [dynamic(self.a, place, 0) for place in (self.grid.x, 1 - self.grid.x)]
        return self.x_half(0)

    def x1(self):
        return self.x_half(1)

    def x_half(self, k):
        own, other = (h[2 * k : 2 * k + 2] for h in self.halves)

        def keep(came):
            total = own.astype(F32) + came.astype(F32)
            self.a = total if k == 0 else jnp.concatenate([self.a, total])

        return [(self.grid.swap_x, other.astype(self.dtype), keep)]

    def y(self):
        return self.step(self.grid.swap_y, self.grid.y, 1)

    def round(self):
        value = self.block(3 - len(self.ring))
        return [(self.grid.ring_z, value.astype(self.dtype), self.ring.append)]

    def block(self, step):
        value = dynamic(self.a, (self.grid.z + step) % 4, 0).astype(F32)
        return value + self.ring[-1].astype(F32) if self.ring else value

    def z(self):
        steps = [dynamic(self.a, (self.grid.z + k) % 4, 0) for k in range(4)]
        self.ring = [steps[0]]
        return [(partial(self.grid.ring_z, step=k), steps[k].astype(self.dtype), self.ring.append) for k in (1, 2, 3)]

    def total(self):
        return self.block(0) if len(self.ring) == 3 else sum(a.astype(F32) for a in self.ring)


def masks(caption_len, phrase_len, box_count, patch_mask, text_rows, patches):
    slots = jnp.arange(phrase_len.shape[1], dtype=jnp.int32)
    phrase_total = jnp.sum(jnp.where(slots[None, :] < box_count[:, None], phrase_len, 0), axis=1)
    lengths = jnp.minimum(caption_len + phrase_total, text_rows)
    first_patch = (jnp.arange(patch_mask.shape[1], dtype=jnp.int32) == 0).astype(jnp.int32)
    keep = jnp.maximum(patch_mask, first_patch[None, :]).astype(F32)
    return lengths, jnp.pad(keep, ((0, 0), (0, patches - keep.shape[1])))


def on_device(
    text_embed,
    image_feats,
    caption_len,
    phrase_len,
    box_count,
    patch_mask,
    attn_qkv,
    attn_out,
    ffn_up,
    ffn_down,
    layer_vectors,
    cross_query,
    cross_kv,
    cross_out,
    cross_vectors,
    cotangent,
):
    n_pipe, n_dp = lax.axis_size("pipe"), lax.axis_size("dp")
    everyone = ("pipe", "dp")
    shards, half = n_pipe * n_dp, n_pipe // 2
    samples, text_rows, width = text_embed.shape
    hidden = ffn_up.shape[1] * n_dp
    lanes = attn_qkv.shape[0]
    patches = -(-image_feats.shape[1] // 32) * 32
    direct = (n_pipe, n_dp) == (4, 8) and lanes % 128 == 0
    lengths, patch_keep = masks(caption_len, phrase_len, box_count, patch_mask, text_rows, patches)
    x = text_embed.reshape(-1, width)
    image = jnp.pad(image_feats, ((0, 0), (0, patches - image_feats.shape[1]), (0, 0)))
    image = image.reshape(samples * patches, -1)

    c_rows = cross_query.shape[0]
    kv_slices = cross_kv.shape[1] // width
    cross_pack = jnp.concatenate([cross_query, cross_out, lane_slices(cross_kv, width)], axis=0)
    v_rows, v_lanes = layer_vectors.shape
    x_rows = cross_vectors.shape[1]
    small = jnp.concatenate([pad_to(layer_vectors, v_rows, 128), pad_to(cross_vectors.T, x_rows, 128)], axis=0)
    small = pad_to(small, 16, 128)
    pack_attn = jnp.concatenate([attn_qkv.T, attn_out.T], axis=0)
    pack_feed = jnp.concatenate([ffn_up.T, lane_slices(ffn_down.T, lanes)], axis=0)
    n_pack = pack_attn.shape[0] + pack_feed.shape[0]

    def cross_weights(blocks):
        blocks = blocks.reshape(shards, -1, width)
        i_rows = cross_kv.shape[0]
        ends = np.cumsum([0, c_rows, c_rows, i_rows, i_rows])
        return [blocks[:, a:b].reshape(-1, width) for a, b in zip(ends[:-1], ends[1:])]

    def vectors_of(blocks):
        blocks = blocks.reshape(n_pipe, n_dp, 16, 128).astype(F32)
        vecs = []
        for layer in range(2):
            v = blocks[layer * half : (layer + 1) * half, :, :v_rows, :v_lanes]
            vecs.append(jnp.moveaxis(v, 1, 2).reshape(12, width))
        cvec = blocks.reshape(shards, 16, 128)[:, v_rows : v_rows + x_rows, :c_rows]
        return vecs, [v[8:12].reshape(1, hidden) for v in vecs], jnp.moveaxis(cvec, 1, 0).reshape(x_rows, width)

    def keys_values(wk, wv, cvec):
        keys = jnp.dot(image, wk, preferred_element_type=F32).astype(BF)
        return keys, (jnp.dot(image, wv, preferred_element_type=F32) + cvec[1]).astype(BF)

    def pack_cross(dk, dv, g_cq, g_co):
        grads = [g_cq, g_co, dot(image, dk, TN).astype(BF), dot(image, dv, TN).astype(BF)]
        return jnp.concatenate([g.reshape(shards, -1, width) for g in grads], axis=1)

    def vector_block(v_self, v_feed, v_up):
        v = jnp.concatenate([v_self[:5], v_feed[:3], v_up.reshape(4, width)], axis=0)
        return jnp.moveaxis(v.reshape(half, v_rows, n_dp, v_lanes), 2, 1)

    def pack_vectors(text, joining, v_cross):
        section = jnp.concatenate([vector_block(*text), vector_block(*joining)], axis=0)
        cross = jnp.moveaxis(v_cross[:x_rows].reshape(x_rows, n_pipe, n_dp, c_rows), 0, 2)
        wide = [jnp.pad(v, ((0, 0), (0, 0), (0, 0), (0, 128 - v.shape[3]))) for v in (section, cross)]
        wide = jnp.concatenate(wide, axis=2)
        return jnp.pad(wide, ((0, 0), (0, 0), (0, 16 - wide.shape[2]), (0, 0)))

    seed = cotangent.reshape(-1, width)
    if direct:
        grid = Grid()
        turn = grid.turn
        where = jnp.stack([grid.core, grid.z, grid.y, grid.x]).astype(jnp.int32)
        gather = Gather(grid, jnp.concatenate([pack_attn, pack_feed, pad_to(small, 16, lanes)]))
        get = gather.get
        turn(get(0, 0, 1, "z"), get(0, 1, 0, "y"), get(1, 0, 0, "x"), gather.c2)
        turn(get(0, 0, 2, "z"), get(0, 1, 1, "y"), get(1, 0, 1, "x"), gather.c2)
        turn(get(0, 0, 3, "z"), get(0, 1, 2, "y"), get(1, 1, 0, "x"), gather.c2)
        turn(get(1, 1, 1, "z"), get(0, 1, 3, "y"), get(1, 0, 3, "x"), gather.c2)
        turn(get(1, 0, 2, "z"), get(1, 1, 3, "y"), get(1, 1, 2, "x"), gather.c2)
        turn(gather.c)
        weights = gather.pieces()
        cross_whole = lax.all_gather(after(cross_pack, grid.arrived[-2]), everyone, axis=0, tiled=True)
        *vectors, cvec = gathered_vectors(weights, where, n_pack, v_rows, v_lanes, x_rows, c_rows)
        vecs, biases = vectors[:2], vectors[2:]
        state, low, s_self = self_forward(x, lengths, where, vecs[0], weights, 0)
        state, passed, s_feed = feed_forward(state, low, where, vecs[0], biases[0], weights, 0)
        state, low, s_self2 = self_forward(passed, lengths, where, vecs[1], weights, 1)
        wq, wo, wk, wv = cross_weights(cross_whole)
        keys, values = keys_values(wk, wv, cvec)
        state, low, s_cross = cross_forward(state, low, patch_keep, keys, values, cvec, wq, wo)
        joined, grad, *g_feed2, v_feed2, v_up2 = feed_both(state, low, where, vecs[1], biases[1], seed, weights, 1)
        grid.computed = (grad,)

        feed = PairSum(grid, g_feed2)

        def fourth(grad):
            grad, dk, dv, g_cq, g_co, v_cross = cross_backward(grad, s_cross, cvec, wq, wo)
            return grad, v_cross, pack_cross(dk, dv, g_cq, g_co)

        grad, v_cross, cross_grads = turn(feed.c(1), compute=fourth, args=(grad,))
        sum_cross = BlockSum(grid, cross_grads.reshape(2, 2, 4, 2, -1, width), BF)
        turn(sum_cross.c)
        grad, *g_self2, v_self2 = turn(
            sum_cross.x0, compute=lambda grad: self_backward(grad, s_self2, where, vecs[1], weights, 1), args=(grad,)
        )
        attn = PairSum(grid, g_self2)
        grad, *g_feed1, v_feed, v_up = turn(
            attn.c(1), sum_cross.x1,
            compute=lambda grad: feed_backward(grad, s_feed, where, vecs[0], weights, 0), args=(grad.astype(BF),),
        )
        feed.add_text(g_feed1)
        f0, f1, f2, f3, f4 = feed.steps()
        a0, a1, a2, a3, a4 = attn.steps()
        embed_grad, *g_self1, v_self = turn(
            *f0, sum_cross.y, pre=(feed.c(0),),
            compute=lambda grad: self_backward(grad, s_self, where, vecs[0], weights, 0), args=(grad,),
        )
        attn.add_text(g_self1)
        sum_vec = BlockSum(
            grid,
            pack_vectors((v_self, v_feed, v_up), (v_self2, v_feed2, v_up2), v_cross).reshape(2, 2, 4, 2, 16, 128),
            F32,
        )
        turn(*f1, attn.c(0), sum_cross.round)
        turn(*f2, *a0, sum_vec.c)
        turn(*f3, *a1, sum_vec.x)
        turn(*f4, *a2, sum_vec.y)
        turn(*a3, sum_cross.round, sum_vec.z)
        turn(*a4, sum_cross.round)
        attn_grads, feed_grads = attn.total(), feed.total()
        n_qkv, n_up = attn_qkv.shape[1], ffn_up.shape[1]
        mine = [attn_grads[:n_qkv], attn_grads[n_qkv:], feed_grads[:n_up], feed_grads[n_up:]]
        cross_grads, small = sum_cross.total(), sum_vec.total()
    else:
        where = jnp.zeros((4,), jnp.int32)
        vectors = lax.all_gather(small, everyone, axis=0, tiled=False)
        whole = lax.all_gather(jnp.concatenate([pack_attn, pack_feed], axis=0), everyone, axis=0, tiled=False)
        whole = whole.reshape(n_pipe, n_dp, -1, lanes)

        def section(piece, layer):
            piece = jnp.moveaxis(piece[layer * half : (layer + 1) * half], 0, 2)
            return piece.reshape(n_dp * piece.shape[1], half * piece.shape[-1])

        counts = [attn_qkv.shape[1], attn_out.shape[1], ffn_up.shape[1], attn_out.shape[1] * (hidden // width)]
        ends = np.cumsum([0] + counts)
        cut = [whole[:, :, a:b] for a, b in zip(ends[:-1], ends[1:])]
        cut[3] = lane_join(cut[3], hidden // width)
        (qkv1, out1, up1, down1), (qkv2, out2, up2, down2) = ([section(c, k) for c in cut] for k in range(2))
        vecs, biases, cvec = vectors_of(vectors)
        wq, wo, wk, wv = cross_weights(lax.all_gather(cross_pack, everyone, axis=0, tiled=False))
        state, low, s_self = self_forward(x, lengths, where, vecs[0], [qkv1, out1], 0)
        state, passed, s_feed = feed_forward(state, low, where, vecs[0], biases[0], [up1, down1], 0)
        state, low, s_self2 = self_forward(passed, lengths, where, vecs[1], [qkv2, out2], 1)
        keys, values = keys_values(wk, wv, cvec)
        state, low, s_cross = cross_forward(state, low, patch_keep, keys, values, cvec, wq, wo)
        joined, grad, *g_feed2, v_feed2, v_up2 = feed_both(state, low, where, vecs[1], biases[1], seed, [up2, down2], 1)
        grad, dk, dv, g_cq, g_co, v_cross = cross_backward(grad, s_cross, cvec, wq, wo)
        grad, *g_self2, v_self2 = self_backward(grad, s_self2, where, vecs[1], [qkv2, out2], 1)
        grad, *g_feed1, v_feed, v_up = feed_backward(grad.astype(BF), s_feed, where, vecs[0], [up1, down1], 0)
        embed_grad, *g_self1, v_self = self_backward(grad, s_self, where, vecs[0], [qkv1, out1], 0)

        def unpack(pair, rows, slices):
            parts = []
            at = 0
            for r, k in zip(rows, slices):
                sides = [p[:, at : at + r * k] for p in pair]
                sides = [lane_join(p, k).reshape(8 * r, -1) for p in sides]
                parts.append(jnp.concatenate(sides, axis=1))
                at += r * k
            return parts

        def split(first, second):
            both = jnp.stack([first, second])
            rows, k = both.shape[1] // n_dp, both.shape[2] // (half * lanes)
            both = both.reshape(2, n_dp, rows, half, k, lanes)
            return both.transpose(0, 3, 1, 4, 2, 5).reshape(n_pipe, n_dp, k * rows, lanes)

        attn = ((3 * width // 8, width // 8), (1, 1))
        feed = ((hidden // 8, width // 8), (1, hidden // width))
        parts = []
        for first, second, shape in ((g_self1, g_self2, attn), (g_feed1, g_feed2, feed)):
            parts += [split(a, b) for a, b in zip(unpack(first, *shape), unpack(second, *shape))]
        packed = jnp.concatenate(parts, axis=2).reshape(-1, lanes)
        packed = lax.psum_scatter(packed, everyone, scatter_dimension=0, tiled=True).astype(F32)
        mine = [packed[a:b] for a, b in zip(ends[:-1], ends[1:])]
        cross_grads = pack_cross(dk, dv, g_cq, g_co).reshape(-1, width)
        cross_grads = lax.psum_scatter(cross_grads, everyone, scatter_dimension=0, tiled=True).astype(F32)
        small = pack_vectors((v_self, v_feed, v_up), (v_self2, v_feed2, v_up2), v_cross)
        small = lax.psum_scatter(small.reshape(-1, 128), everyone, scatter_dimension=0, tiled=True)
    mine[3] = lane_join(mine[3], hidden // width)
    return (
        joined.reshape(text_embed.shape),
        embed_grad.reshape(text_embed.shape),
        mine[0].T,
        mine[1].T,
        mine[2].T,
        mine[3].T,
        small[:v_rows, :v_lanes],
        cross_grads[:c_rows],
        lane_join(cross_grads[2 * c_rows :], kv_slices),
        cross_grads[c_rows : 2 * c_rows],
        small[v_rows : v_rows + x_rows, :c_rows].T,
    )


def solution(mesh):
    in_specs = (
        P(("pipe", "dp"), None, None),
        P(("pipe", "dp"), None, None),
        P(("pipe", "dp")),
        P(("pipe", "dp"), None),
        P(("pipe", "dp")),
        P(("pipe", "dp"), None),
        P("pipe", "dp"),
        P("pipe", "dp"),
        P("pipe", "dp"),
        P("pipe", "dp"),
        P("pipe", "dp"),
        P(("pipe", "dp"), None),
        P(("pipe", "dp"), None),
        P(("pipe", "dp"), None),
        P(("pipe", "dp"), None),
        P(("pipe", "dp"), None, None),
    )
    out_specs = (
        P(("pipe", "dp"), None, None),
        P(("pipe", "dp"), None, None),
        P("pipe", "dp"),
        P("pipe", "dp"),
        P("pipe", "dp"),
        P("pipe", "dp"),
        P("pipe", "dp"),
        P(("pipe", "dp"), None),
        P(("pipe", "dp"), None),
        P(("pipe", "dp"), None),
        P(("pipe", "dp"), None),
    )
    return jax.shard_map(
        on_device, mesh=mesh, in_specs=in_specs, out_specs=out_specs, check_vma=False
    )
```

```python
from functools import partial

import jax
import jax.numpy as jnp
import numpy as np
from jax import lax
from jax.experimental import pallas as pl
from jax.experimental.pallas import tpu as pltpu
from jax.sharding import PartitionSpec as P

HEADS = 12
NORM_EPS = 1e-12
MASKED = -1e30
BF = jnp.bfloat16
F32 = jnp.float32
NT = (((1,), (1,)), ((), ()))
NN = (((1,), (0,)), ((), ()))
TN = (((0,), (0,)), ((), ()))
VMEM_BYTES = 58 * 2**20
TILE = 768
CHUNK = 128


def dot(a, b, dims=NN):
    return lax.dot_general(a, b, dims, preferred_element_type=F32)


def span(start, size, unit=128):
    return pl.ds(pl.multiple_of(start, unit), size)


def tiles(count, body):
    def step(i, carry):
        body(i)
        return carry

    lax.fori_loop(0, count, step, 0)


class Copies:
    def __init__(self, sems):
        self.sems, self.used = sems, 0
        self.coming, self.going, self.sent = [], [], []

    def copy(self, source, target):
        self.used += 1
        copy = pltpu.make_async_copy(source, target, self.sems.at[self.used - 1])
        copy.start()
        return copy

    def begin(self, *refs):
        for k, (held, source, _) in enumerate(self.coming):
            if any(held is ref for ref in refs):
                self.coming[k] = (held, source, self.copy(source, held))

    def need(self, *refs):
        for k, (held, source, copy) in enumerate(self.coming):
            if any(held is ref for ref in refs):
                copy.wait()
                self.coming[k] = (None, source, None)

    def send(self, *refs, part=()):
        for held, target in self.going:
            if any(held is ref for ref in refs):
                self.sent.append(self.copy(held.at[part], target.at[part]) if part else self.copy(held, target))

    def finish(self):
        settle(self.sent)


def fetch(copies, sems, here=None):
    started = []
    for k in range(len(copies[0][0])):
        started.append([pltpu.make_async_copy(s[k], t, sems.at[i]) for i, (s, t) in enumerate(copies)])

    def start(group):
        for copy in group:
            copy.start()

    if len(started) == 1:
        start(started[0])
    else:
        pl.when(here)(lambda: start(started[0]))
        pl.when(jnp.logical_not(here))(lambda: start(started[1]))
    return started[0]


def settle(started):
    for copy in started:
        copy.wait()


def placed(refs, where_ref, layout, target, lanes):
    if len(refs) == 1:
        return [(refs, target)]
    core, z, y = where_ref[0], where_ref[1], where_ref[2]
    copies = []
    for i, pair in enumerate(zip(refs[:16], refs[16:])):
        c_rel, y_rel, z_rel = i // 8, (i // 4) % 2, i % 4
        block = lax.rem(z - z_rel + 4, 4) * 2 + lax.rem(y + y_rel, 2)
        side = lax.rem(core + c_rel, 2)
        for first, rows, shift in layout:
            place = target.at[
                span(block * rows, rows, 16),
                span(side * lanes + shift * pair[0].shape[1], pair[0].shape[1]),
            ]
            copies.append(([ref.at[pl.ds(first, rows)] for ref in pair], place))
    return copies


def relative(where_ref, block):
    z = lax.rem(block // 2 - where_ref[1] + 4, 4)
    return z * 2 + lax.rem(block % 2 + where_ref[2], 2)


def norm_rows(x_ref, bias, gain, offset, y_ref, low_ref, n_ref, r_ref):
    for i in range(0, y_ref.shape[0], CHUNK):
        rows = pl.ds(i, CHUNK)
        u = x_ref[rows, :].astype(F32) + (y_ref[rows, :] + bias)
        center = u - jnp.mean(u, axis=-1, keepdims=True)
        scale = lax.rsqrt(jnp.mean(center * center, axis=-1, keepdims=True) + NORM_EPS)
        normed = center * scale
        y = normed * gain + offset
        y_ref[rows, :] = y
        low_ref[rows, :] = y.astype(BF)
        n_ref[rows, :] = normed.astype(BF)
        r_ref[rows, :] = scale


def norm_rows_back(dy_ref, n_ref, r_ref, gain, du_ref, db_ref):
    def chunk(i, sums):
        rows = span(i * CHUNK, CHUNK, CHUNK)
        dy = dy_ref[rows, :].astype(F32)
        n = n_ref[rows, :].astype(F32)
        s = dy * gain
        du = r_ref[rows, :] * (
            s - jnp.mean(s, axis=-1, keepdims=True) - n * jnp.mean(s * n, axis=-1, keepdims=True)
        )
        db = du.astype(BF)
        du_ref[rows, :] = du
        db_ref[rows, :] = db
        terms = (dy * n, dy, db.astype(F32))
        return tuple(a + jnp.sum(t, axis=0, keepdims=True) for a, t in zip(sums, terms))

    zero = jnp.zeros((1, dy_ref.shape[1]), F32)
    return lax.fori_loop(0, dy_ref.shape[0] // CHUNK, chunk, (zero, zero, zero))


def split_heads(a):
    first = lax.broadcasted_iota(jnp.int32, a.shape, 1) < a.shape[1] // 2
    zero = jnp.zeros_like(a)
    return jnp.concatenate([jnp.where(first, a, zero), jnp.where(first, zero, a)], axis=0)


def join_heads(a):
    rows = a.shape[0] // 2
    first = lax.broadcasted_iota(jnp.int32, (rows, a.shape[1]), 1) < a.shape[1] // 2
    return jnp.where(first, a[:rows], a[rows:])


def softmax(scores, mask, axis):
    scores = scores + mask
    e = jnp.exp(scores - jnp.max(scores, axis=axis, keepdims=True))
    return (e * (1.0 / jnp.sum(e, axis=axis, keepdims=True))).astype(BF)


def score_back(weights, d_weights):
    a = weights.astype(F32)
    t = a * d_weights
    return (t - a * jnp.sum(t, axis=0, keepdims=True)).astype(BF)


def project_and_norm(x_ref, o_ref, w_ref, dims, bias, gain, offset, outs):
    y_ref, low_ref, n_ref, r_ref = outs
    width = y_ref.shape[1]

    def tile(j):
        cols = span(j * TILE, TILE)
        w = w_ref[cols, :] if dims is NT else w_ref[:, cols]
        y_ref[:, cols] = dot(o_ref[...], w, dims)

    tiles(width // TILE, tile)
    norm_rows(x_ref, bias, gain, offset, y_ref, low_ref, n_ref, r_ref)


def self_forward_kernel(count, layer, io, ins, outs, scratch):
    lengths, where_ref, x_ref, vec_ref, *refs = ins
    p_ref, a_ref, o_ref, y_ref, low_ref, n_ref, r_ref = outs
    qkv, out, bias_ref, sems, sems2 = scratch
    width = x_ref.shape[1]
    n, m = qkv.shape[0] // 8, out.shape[0] // 8
    whole = count == 2
    here = where_ref[3] == layer
    first = fetch(placed(refs[:1] if whole else refs, where_ref, [(0, n, 0)], qkv, width // 2), sems, here)
    bias_ref[:, :width] = vec_ref[0:1, :]
    bias_ref[:, width : 2 * width] = jnp.zeros((1, width), F32)
    bias_ref[:, 2 * width :] = vec_ref[1:2, :]
    settle(first)
    second = fetch(placed(refs[1:] if whole else refs, where_ref, [(n, m, 0)], out, width // 2), sems2, here)

    def tile(j):
        cols = span(j * TILE, TILE)
        p_ref[:, cols] = (dot(x_ref[...], qkv[cols, :], NT) + bias_ref[:, cols]).astype(BF)

    tiles(3 * width // TILE, tile)
    io.send(p_ref)
    pairs = width // 128
    key = lax.broadcasted_iota(jnp.int32, (128, 256), 0)
    query = lax.broadcasted_iota(jnp.int32, (128, 256), 1)
    same = ((query // 64) % 2) == (key // 64)

    def attend(s):
        rows = span(s * 128, 128)
        length = jnp.where(key < 64, lengths[2 * s], lengths[2 * s + 1])
        mask = jnp.where(same & (lax.rem(key, 64) < length), 0.0, MASKED)
        for h in range(pairs):
            q = p_ref[rows, pl.ds(h * 128, 128)]
            k = p_ref[rows, pl.ds(width + h * 128, 128)]
            v = p_ref[rows, pl.ds(2 * width + h * 128, 128)]
            a = softmax(dot(k, split_heads(q * 0.125), NT), mask, 0)
            a_ref[s * pairs + h] = a
            o_ref[rows, pl.ds(h * 128, 128)] = join_heads(dot(a, v, TN)).astype(BF)

    tiles(x_ref.shape[0] // 128, attend)
    io.send(a_ref, o_ref)
    settle(second)
    project_and_norm(
        x_ref, o_ref, out, NT, vec_ref[2:3, :], vec_ref[3:4, :], vec_ref[4:5, :], (y_ref, low_ref, n_ref, r_ref)
    )


def self_backward_kernel(count, layer, io, ins, outs, scratch):
    where_ref, dy_ref, x_ref, vec_ref, p_ref, a_ref, o_ref, n_ref, r_ref, *refs = ins
    dx_ref, own_ref, other_ref, gv_ref = outs
    qkv, out, du_ref, db_ref, dmix_ref, dp_ref, rel_ref, g_ref, sems, sems2 = scratch
    width = x_ref.shape[1]
    half = width // 2
    n, m = qkv.shape[0] // 8, out.shape[0] // 8
    whole = count == 2
    here = where_ref[3] == layer
    second = fetch(placed(refs[1:] if whole else refs, where_ref, [(n, m, 0)], out, half), sems2, here)
    io.begin(o_ref, p_ref, a_ref)
    core = where_ref[0]
    g_gain, g_offset, g_bias = norm_rows_back(dy_ref, n_ref, r_ref, vec_ref[3:4, :], du_ref, db_ref)
    settle(second)

    def mix(j):
        cols = span(j * TILE, TILE)
        dmix_ref[:, cols] = dot(db_ref[...], out[:, cols]).astype(BF)

    tiles(width // TILE, mix)
    io.need(o_ref, p_ref, a_ref)
    rel_ref[:, :half] = o_ref[:, span(core * half, half)]
    rel_ref[:, half:] = o_ref[:, span((1 - core) * half, half)]

    g_ref[:width, :] = dot(db_ref[...], rel_ref[...], TN).astype(BF)
    for b in range(8):
        to, at = relative(where_ref, b), pl.ds(b * m, m)
        own_ref[to, n:, :] = g_ref[at, :half]
        other_ref[to, n:, :] = g_ref[at, half:]
    io.begin(x_ref)
    first = fetch(placed(refs[:1] if whole else refs, where_ref, [(0, n, 0)], qkv, half), sems, here)
    pairs = width // 128

    def attend(s):
        rows = span(s * 128, 128)
        for h in range(pairs):
            q2 = split_heads(p_ref[rows, pl.ds(h * 128, 128)])
            k = p_ref[rows, pl.ds(width + h * 128, 128)]
            v = p_ref[rows, pl.ds(2 * width + h * 128, 128)]
            do2 = split_heads(dmix_ref[rows, pl.ds(h * 128, 128)])
            a = a_ref[s * pairs + h]
            ds = score_back(a, dot(v, do2, NT))
            dp_ref[rows, pl.ds(h * 128, 128)] = (join_heads(dot(ds, k, TN)) * 0.125).astype(BF)
            dp_ref[rows, pl.ds(width + h * 128, 128)] = (dot(ds, q2) * 0.125).astype(BF)
            dp_ref[rows, pl.ds(2 * width + h * 128, 128)] = dot(a, do2).astype(BF)

    tiles(x_ref.shape[0] // 128, attend)
    io.need(x_ref)
    rel_ref[:, :half] = x_ref[:, span(core * half, half)]
    rel_ref[:, half:] = x_ref[:, span((1 - core) * half, half)]

    def qkv_grad(j):
        rows = span(j * TILE, TILE)
        g_ref[rows, :] = dot(dp_ref[:, rows], rel_ref[...], TN).astype(BF)

    tiles(3 * width // TILE, qkv_grad)
    for b in range(8):
        to, at = relative(where_ref, b), pl.ds(b * n, n)
        own_ref[to, :n, :] = g_ref[at, :half]
        other_ref[to, :n, :] = g_ref[at, half:]
    io.send(other_ref, own_ref)
    settle(first)

    def back(j):
        cols = span(j * TILE, TILE)
        dx_ref[:, cols] = (du_ref[:, cols] + dot(dp_ref[...], qkv[:, cols])).astype(dx_ref.dtype)

    tiles(width // TILE, back)
    gv_ref[0:1, :] = jnp.sum(dp_ref[:, :width].astype(F32), axis=0, keepdims=True)
    gv_ref[1:2, :] = jnp.sum(dp_ref[:, 2 * width :].astype(F32), axis=0, keepdims=True)
    gv_ref[2:3, :] = g_bias
    gv_ref[3:4, :] = g_gain
    gv_ref[4:5, :] = g_offset


def cross_forward_kernel(io, ins, outs, scratch):
    x_ref, low_x_ref, keep_ref, k_ref, v_ref, vec_ref, wq_ref, wo_ref = ins
    q_ref, a_ref, o_ref, y_ref, low_ref, n_ref, r_ref = outs
    io.begin(k_ref, v_ref)
    width = x_ref.shape[1]
    patches = k_ref.shape[0] // keep_ref.shape[0]

    def tile(j):
        cols = span(j * TILE, TILE)
        q_ref[:, cols] = (dot(low_x_ref[...], wq_ref[:, cols]) + vec_ref[0:1, cols]).astype(BF)

    tiles(width // TILE, tile)
    io.send(q_ref)
    io.need(k_ref, v_ref)
    io.begin(x_ref, wo_ref)
    pairs = width // 128

    def attend(s):
        rows, keys = span(s * 64, 64, 64), span(s * patches, patches, 16)
        mask = jnp.where(keep_ref[pl.ds(s, 1), :] > 0, 0.0, MASKED)
        for h in range(pairs):
            q = q_ref[rows, pl.ds(h * 128, 128)]
            k = k_ref[keys, pl.ds(h * 128, 128)]
            v = v_ref[keys, pl.ds(h * 128, 128)]
            a = softmax(dot(split_heads(q * 0.125), k, NT), mask, 1)
            a_ref[s * pairs + h] = a.T
            o_ref[rows, pl.ds(h * 128, 128)] = join_heads(dot(a, v)).astype(BF)

    tiles(keep_ref.shape[0], attend)
    io.send(a_ref, o_ref)
    io.need(x_ref, wo_ref)
    project_and_norm(
        x_ref, o_ref, wo_ref, NN, vec_ref[2:3, :], vec_ref[3:4, :], vec_ref[4:5, :], (y_ref, low_ref, n_ref, r_ref)
    )


def cross_backward_kernel(io, ins, outs, scratch):
    dy_ref, low_x_ref, k_ref, v_ref, vec_ref, wq_ref, wo_ref, q_ref, a_ref, o_ref, n_ref, r_ref = ins
    dx_ref, dk_ref, dv_ref, gq_ref, go_ref, gv_ref = outs
    db_ref, dmix_ref, dq_ref = scratch
    width = low_x_ref.shape[1]
    patches = a_ref.shape[1]
    io.begin(wo_ref, o_ref)
    g_gain, g_offset, g_bias = norm_rows_back(dy_ref, n_ref, r_ref, vec_ref[3:4, :], dx_ref, db_ref)

    io.begin(q_ref, k_ref, v_ref, a_ref)
    io.need(wo_ref, o_ref)

    def mix(j):
        cols = span(j * TILE, TILE)
        dmix_ref[:, cols] = dot(db_ref[...], wo_ref[cols, :], NT).astype(BF)
        go_ref[cols, :] = dot(o_ref[:, cols], db_ref[...], TN).astype(BF)

    tiles(width // TILE, mix)
    io.send(go_ref)
    io.need(q_ref, k_ref, v_ref, a_ref)
    io.begin(wq_ref, low_x_ref)
    pairs = width // 128

    def attend(s):
        rows, keys = span(s * 64, 64, 64), span(s * patches, patches, 16)
        for h in range(pairs):
            q2 = split_heads(q_ref[rows, pl.ds(h * 128, 128)])
            k = k_ref[keys, pl.ds(h * 128, 128)]
            v = v_ref[keys, pl.ds(h * 128, 128)]
            do2 = split_heads(dmix_ref[rows, pl.ds(h * 128, 128)])
            a = a_ref[s * pairs + h]
            ds = score_back(a, dot(v, do2, NT))
            dq_ref[rows, pl.ds(h * 128, 128)] = (join_heads(dot(ds, k, TN)) * 0.125).astype(BF)
            dk_ref[keys, pl.ds(h * 128, 128)] = (dot(ds, q2) * 0.125).astype(BF)
            dv_ref[keys, pl.ds(h * 128, 128)] = dot(a, do2).astype(BF)

    tiles(a_ref.shape[0] // pairs, attend)
    io.send(dk_ref, dv_ref)
    io.need(wq_ref, low_x_ref)

    def back(j):
        cols = span(j * TILE, TILE)
        dx_ref[:, cols] += dot(dq_ref[...], wq_ref[cols, :], NT)
        gq_ref[cols, :] = dot(low_x_ref[:, cols], dq_ref[...], TN).astype(BF)

    tiles(width // TILE, back)
    gv_ref[0:1, :] = jnp.sum(dq_ref[...].astype(F32), axis=0, keepdims=True)
    gv_ref[1:2, :] = jnp.sum(dv_ref[...].astype(F32), axis=0, keepdims=True)
    gv_ref[2:3, :] = g_bias
    gv_ref[3:4, :] = g_gain
    gv_ref[4:5, :] = g_offset


def gelu_parts(h):
    size = jnp.abs(h) * 0.7071067811865476
    t = 1.0 / (1.0 + 0.3275911 * size)
    e = jnp.exp(-size * size)
    poly = t * (0.254829592 + t * (-0.284496736 + t * (1.421413741 + t * (-1.453152027 + t * 1.061405429))))
    tail = 0.5 * poly * e
    cdf = jnp.where(h < 0, tail, 1.0 - tail)
    return h * cdf, cdf + h * (e * 0.3989422804014327)


def feed_weights(count, layer, where_ref, refs, up, down, sems, sems2):
    width, hidden = up.shape[1], up.shape[0]
    n, m, whole = hidden // 8, width // 8, count == 2
    base = 4 * m
    slices = [(base + n + m * i, m, i) for i in range(hidden // width)]
    here = where_ref[3] == layer
    return (
        lambda: fetch(placed(refs[:1] if whole else refs, where_ref, [(base, n, 0)], up, width // 2), sems, here),
        lambda: fetch(placed(refs[1:] if whole else refs, where_ref, slices, down, hidden // 2), sems2, here),
    )


def feed_forward_body(io, x_ref, low_x_ref, vec_ref, bias_ref, act_ref, slope_ref, norm_outs, up, down, get_up, get_down):
    settle(get_up())
    second = get_down()
    io.begin(x_ref)

    def tile(j):
        cols = span(j * TILE, TILE)
        h = dot(low_x_ref[...], up[cols, :], NT) + bias_ref[:, cols]
        act, slope = gelu_parts(h)
        act_ref[:, cols] = act.astype(BF)
        slope_ref[:, cols] = slope.astype(BF)

    tiles(up.shape[0] // TILE, tile)
    io.send(act_ref, slope_ref)
    settle(second)
    io.need(x_ref)
    project_and_norm(x_ref, act_ref, down, NT, vec_ref[5:6, :], vec_ref[6:7, :], vec_ref[7:8, :], norm_outs)


def feed_backward_body(
    io, where_ref, dy_ref, low_x_ref, vec_ref, act_ref, slope_ref, n_ref, r_ref, outs, work, up, down, get_up, get_down
):
    dx_ref, own_ref, other_ref, gv_ref, gb_ref = outs
    db_ref, dbt_ref, dh_ref, rel_ref = work
    width, hidden = up.shape[1], up.shape[0]
    n, m, half = hidden // 8, width // 8, width // 2
    core = where_ref[0]
    second = get_down()
    io.begin(slope_ref)
    g_gain, g_offset, g_bias = norm_rows_back(dy_ref, n_ref, r_ref, vec_ref[6:7, :], dx_ref, db_ref)
    dbt_ref[...] = db_ref[...].T
    settle(second)
    io.need(slope_ref)
    io.begin(act_ref, low_x_ref)

    def down_tile(j):
        cols = span(j * TILE, TILE)
        dh = (dot(db_ref[...], down[:, cols]) * slope_ref[:, cols].astype(F32)).astype(BF)
        dh_ref[:, cols] = dh
        gb_ref[:, cols] = jnp.sum(dh.astype(F32), axis=0, keepdims=True)

    tiles(hidden // TILE, down_tile)
    io.need(act_ref)

    def down_grad(j):
        for ref, side in ((own_ref, core), (other_ref, 1 - core)):
            g = dot(dbt_ref[...], act_ref[:, span(side * (hidden // 2) + j * width, width)]).astype(BF)
            for b in range(8):
                to = relative(where_ref, b)
                for k in range(2):
                    ref[to, span(n + (2 * j + k) * m, m, 16), :] = g[b * m : (b + 1) * m, k * half : (k + 1) * half]

    tiles(hidden // 2 // width, down_grad)
    io.send(other_ref, own_ref, part=(slice(None), pl.ds(n, n)))
    first = get_up()
    io.need(low_x_ref)
    rel_ref[:, :half] = low_x_ref[:, span(core * half, half)]
    rel_ref[:, half:] = low_x_ref[:, span((1 - core) * half, half)]

    def up_grad(j):
        g = dot(dh_ref[:, span(j * 2 * n, 2 * n)], rel_ref[...], TN).astype(BF)
        for k in range(2):
            to = relative(where_ref, 2 * j + k)
            own_ref[to, :n, :] = g[k * n : (k + 1) * n, :half]
            other_ref[to, :n, :] = g[k * n : (k + 1) * n, half:]

    tiles(4, up_grad)
    io.send(other_ref, own_ref, part=(slice(None), pl.ds(0, n)))
    settle(first)

    def back(j):
        cols = span(j * TILE, TILE)
        dx_ref[:, cols] += dot(dh_ref[...], up[:, cols])

    tiles(width // TILE, back)
    gv_ref[0:1, :] = g_bias
    gv_ref[1:2, :] = g_gain
    gv_ref[2:3, :] = g_offset


def feed_forward_kernel(count, layer, io, ins, outs, scratch):
    where_ref, x_ref, low_x_ref, vec_ref, bias_ref, *refs = ins
    act_ref, slope_ref, *norm_outs = outs
    up, down, sems, sems2 = scratch
    get = feed_weights(count, layer, where_ref, refs, up, down, sems, sems2)
    feed_forward_body(io, x_ref, low_x_ref, vec_ref, bias_ref, act_ref, slope_ref, norm_outs, up, down, *get)


def feed_backward_kernel(count, layer, io, ins, outs, scratch):
    where_ref, dy_ref, low_x_ref, vec_ref, act_ref, slope_ref, n_ref, r_ref, *refs = ins
    up, down, *work, sems, sems2 = scratch
    get = feed_weights(count, layer, where_ref, refs, up, down, sems, sems2)
    feed_backward_body(
        io, where_ref, dy_ref, low_x_ref, vec_ref, act_ref, slope_ref, n_ref, r_ref, outs, work, up, down, *get
    )


def feed_both_kernel(count, layer, io, ins, outs, scratch):
    where_ref, x_ref, low_x_ref, vec_ref, bias_ref, dy_ref, *refs = ins
    y_ref, *grads = outs
    up, down, *work, act_ref, slope_ref, low_ref, n_ref, r_ref, sems, sems2 = scratch
    get = feed_weights(count, layer, where_ref, refs, up, down, sems, sems2)
    norm_outs = (y_ref, low_ref, n_ref, r_ref)
    feed_forward_body(io, x_ref, low_x_ref, vec_ref, bias_ref, act_ref, slope_ref, norm_outs, up, down, *get)
    io.send(y_ref)
    feed_backward_body(
        io, where_ref, dy_ref, low_x_ref, vec_ref, act_ref, slope_ref, n_ref, r_ref, grads, work, up, down, list, list
    )


def vector_kernel(first, v_rows, v_lanes, x_rows, c_rows, *refs):
    where_ref, *pieces = refs[:33]
    vec_refs, bias_refs, cross_ref = refs[33:35], refs[35:37], refs[37]
    held, sems = refs[38:]
    core, z, y, x = where_ref[0], where_ref[1], where_ref[2], where_ref[3]
    copies = []
    for i, ref in enumerate(pieces):
        x_rel, c_rel, y_rel, z_rel = i // 16, (i // 8) % 2, (i // 4) % 2, i % 4
        pipe = lax.rem(x + x_rel, 2) * 2 + lax.rem(core + c_rel, 2)
        device = pipe * 8 + lax.rem(z - z_rel + 4, 4) * 2 + lax.rem(y + y_rel, 2)
        copies.append(([ref.at[pl.ds(first, 16), pl.ds(0, 128)]], held.at[device]))
    settle(fetch(copies, sems))
    for device in range(32):
        block = held[device].astype(F32)
        pipe, dp = device // 8, device % 8
        rows = pl.ds(pipe % 2 * v_rows, v_rows)
        vec_refs[pipe // 2][rows, pl.ds(dp * v_lanes, v_lanes)] = block[:v_rows, :v_lanes]
        cross_ref[0:x_rows, pl.ds(device * c_rows, c_rows)] = block[v_rows : v_rows + x_rows, :c_rows]
    width = cross_ref.shape[1]
    for vec_ref, bias_ref in zip(vec_refs, bias_refs):
        for j in range(4):
            bias_ref[:, j * width : (j + 1) * width] = vec_ref[8 + j : 9 + j, :]


def struct(*shape, dtype=F32):
    return jax.ShapeDtypeStruct(shape, dtype)


VMEM = pl.BlockSpec(memory_space=pltpu.VMEM)
SMEM = pl.BlockSpec(memory_space=pltpu.SMEM)
ANYWHERE = pl.BlockSpec(memory_space=pl.ANY)


def call(kernel, outs, specs, scratch, us, args, late=(), early=(), packs=(), layer=0, onto=None):
    n_in, n_out, n_scratch = len(args), len(outs), len(scratch)
    early = (*early, *packs)
    held = [pltpu.VMEM(args[i].shape, args[i].dtype) for i in late]
    held += [pltpu.VMEM(outs[i].shape, outs[i].dtype) for i in early]
    outs = [struct(2, *o.shape, dtype=o.dtype) if i in packs else o for i, o in enumerate(outs)]
    taken = tuple(onto) if onto else ()
    n_all = n_in + len(taken)

    def body(*refs):
        ins, out, rest = list(refs[:n_in]), list(refs[n_all : n_all + n_out]), refs[n_all + n_out :]
        buffers = rest[n_scratch:-1]
        io = Copies(rest[-1])
        for k, i in enumerate(late):
            io.coming.append((buffers[k], ins[i], None))
            ins[i] = buffers[k]
        for k, i in enumerate(early, len(late)):
            target = out[i].at[lax.rem(ins[0][3] + layer, 2)] if i in packs else out[i]
            io.going.append((buffers[k], target))
            out[i] = buffers[k]
        kernel(io, ins, out, rest[:n_scratch])
        io.finish()

    specs = [ANYWHERE if i in late else spec for i, spec in enumerate(specs)] + [ANYWHERE] * len(taken)
    return pl.pallas_call(
        body,
        out_shape=outs,
        in_specs=specs,
        out_specs=[ANYWHERE if i in early else VMEM for i in range(n_out)],
        scratch_shapes=[*scratch, *held, pltpu.SemaphoreType.DMA((24,))],
        input_output_aliases={n_in + k: i for k, i in enumerate(packs)} if taken else {},
        cost_estimate=pl.CostEstimate(flops=int(us * 1.1e9), bytes_accessed=int(us * 3.5e6), transcendentals=0),
        compiler_params=pltpu.CompilerParams(vmem_limit_bytes=VMEM_BYTES),
    )(*args, *taken)


def gathered_vectors(pieces, where, first, v_rows, v_lanes, x_rows, c_rows):
    width = 8 * v_lanes
    return pl.pallas_call(
        partial(vector_kernel, first, v_rows, v_lanes, x_rows, c_rows),
        out_shape=[struct(12, width)] * 2 + [struct(1, 4 * width)] * 2 + [struct(8, width)],
        in_specs=[SMEM] + [ANYWHERE] * len(pieces),
        out_specs=[VMEM] * 5,
        scratch_shapes=[pltpu.VMEM((32, 16, 128), BF), pltpu.SemaphoreType.DMA((32,))],
        cost_estimate=pl.CostEstimate(flops=0, bytes_accessed=10**7, transcendentals=0),
    )(where, *pieces)


def copy_sems(count, parts=1):
    return pltpu.SemaphoreType.DMA((16 * parts if count > 2 else 1,))


def self_forward(x, lengths, where, vec, weights, layer):
    rows, width = x.shape
    blocks = rows // 128 * (width // 128)
    count = len(weights)
    outs = [
        struct(rows, 3 * width, dtype=BF),
        struct(blocks, 128, 256, dtype=BF),
        struct(rows, width, dtype=BF),
        struct(rows, width),
        struct(rows, width, dtype=BF),
        struct(rows, width, dtype=BF),
        struct(rows, 1),
    ]
    scratch = [
        pltpu.VMEM((3 * width, width), BF),
        pltpu.VMEM((width, width), BF),
        pltpu.VMEM((1, 3 * width), F32),
        copy_sems(count),
        copy_sems(count),
    ]
    p, a, o, y, low, n, r = call(
        partial(self_forward_kernel, count, layer),
        outs,
        [SMEM, SMEM, VMEM, VMEM] + [ANYWHERE] * count,
        scratch,
        14,
        (lengths, where, x, vec, *weights),
        early=(0, 1, 2),
    )
    return y, low, (x, p, a, o, n, r)


def self_backward(dy, saved, where, vec, weights, layer, dtype=F32, onto=None):
    x, p, a, o, n, r = saved
    rows, width = x.shape
    half = width // 2
    count = len(weights)
    outs = [
        struct(rows, width, dtype=dtype),
        struct(8, width // 2, half, dtype=BF),
        struct(8, width // 2, half, dtype=BF),
        struct(8, width),
    ]
    scratch = [
        pltpu.VMEM((3 * width, width), BF),
        pltpu.VMEM((width, width), BF),
        pltpu.VMEM((rows, width), F32),
        pltpu.VMEM((rows, width), BF),
        pltpu.VMEM((rows, width), BF),
        pltpu.VMEM((rows, 3 * width), BF),
        pltpu.VMEM((rows, width), BF),
        pltpu.VMEM((3 * width, width), BF),
        copy_sems(count),
        copy_sems(count),
    ]
    return call(
        partial(self_backward_kernel, count, layer),
        outs,
        [SMEM] + [VMEM] * 8 + [ANYWHERE] * count,
        scratch,
        22,
        (where, dy, x, vec, p, a, o, n, r, *weights),
        late=(6, 4, 5, 2),
        packs=(1, 2),
        layer=layer,
        onto=onto,
    )


def cross_forward(x, low_x, keep, k, v, vec, wq, wo):
    rows, width = x.shape
    samples, patches = keep.shape
    outs = [
        struct(rows, width, dtype=BF),
        struct(samples * (width // 128), patches, 128, dtype=BF),
        struct(rows, width, dtype=BF),
        struct(rows, width),
        struct(rows, width, dtype=BF),
        struct(rows, width, dtype=BF),
        struct(rows, 1),
    ]
    q, a, o, y, low, n, r = call(
        cross_forward_kernel,
        outs,
        [VMEM] * 8,
        [],
        21,
        (x, low_x, keep, k, v, vec, wq, wo),
        late=(3, 4, 7, 0),
        early=(0, 1, 2),
    )
    return y, low, (low_x, k, v, q, a, o, n, r)


def cross_backward(dy, saved, vec, wq, wo):
    low_x, k, v, q, a, o, n, r = saved
    rows, width = low_x.shape
    outs = [
        struct(rows, width),
        struct(*k.shape, dtype=BF),
        struct(*k.shape, dtype=BF),
        struct(width, width, dtype=BF),
        struct(width, width, dtype=BF),
        struct(8, width),
    ]
    scratch = [pltpu.VMEM((rows, width), BF)] * 3
    return call(
        cross_backward_kernel,
        outs,
        [VMEM] * 12,
        scratch,
        26,
        (dy, low_x, k, v, vec, wq, wo, q, a, o, n, r),
        late=(6, 9, 7, 2, 3, 8, 5, 1),
        early=(1, 2, 4),
    )


def feed_forward(x, low_x, where, vec, bias, weights, layer):
    rows, width = x.shape
    hidden = bias.shape[1]
    count = len(weights)
    outs = [
        struct(rows, hidden, dtype=BF),
        struct(rows, hidden, dtype=BF),
        struct(rows, width),
        struct(rows, width, dtype=BF),
        struct(rows, width, dtype=BF),
        struct(rows, 1),
    ]
    scratch = [
        pltpu.VMEM((hidden, width), BF),
        pltpu.VMEM((width, hidden), BF),
        copy_sems(count),
        copy_sems(count, hidden // width),
    ]
    act, slope, y, low, n, r = call(
        partial(feed_forward_kernel, count, layer),
        outs,
        [SMEM] + [VMEM] * 4 + [ANYWHERE] * count,
        scratch,
        20,
        (where, x, low_x, vec, bias, *weights),
        late=(1,),
        early=(0, 1),
    )
    return y, low, (low_x, act, slope, n, r)


def feed_backward(dy, saved, where, vec, weights, layer, onto=None):
    low_x, act, slope, n, r = saved
    rows, width = low_x.shape
    hidden = act.shape[1]
    count = len(weights)
    outs = [
        struct(rows, width),
        struct(8, 2 * hidden // 8, width // 2, dtype=BF),
        struct(8, 2 * hidden // 8, width // 2, dtype=BF),
        struct(8, width),
        struct(1, hidden),
    ]
    scratch = [
        pltpu.VMEM((hidden, width), BF),
        pltpu.VMEM((width, hidden), BF),
        pltpu.VMEM((rows, width), BF),
        pltpu.VMEM((width, rows), BF),
        pltpu.VMEM((rows, hidden), BF),
        pltpu.VMEM((rows, width), BF),
        copy_sems(count),
        copy_sems(count, hidden // width),
    ]
    return call(
        partial(feed_backward_kernel, count, layer),
        outs,
        [SMEM] + [VMEM] * 7 + [ANYWHERE] * count,
        scratch,
        22,
        (where, dy, low_x, vec, act, slope, n, r, *weights),
        late=(5, 4, 2),
        packs=(1, 2),
        layer=layer,
        onto=onto,
    )


def feed_both(x, low_x, where, vec, bias, dy, weights, layer):
    rows, width = x.shape
    hidden = bias.shape[1]
    count = len(weights)
    outs = [
        struct(rows, width),
        struct(rows, width),
        struct(8, 2 * hidden // 8, width // 2, dtype=BF),
        struct(8, 2 * hidden // 8, width // 2, dtype=BF),
        struct(8, width),
        struct(1, hidden),
    ]
    scratch = [
        pltpu.VMEM((hidden, width), BF),
        pltpu.VMEM((width, hidden), BF),
        pltpu.VMEM((rows, width), BF),
        pltpu.VMEM((width, rows), BF),
        pltpu.VMEM((rows, hidden), BF),
        pltpu.VMEM((rows, width), BF),
        pltpu.VMEM((rows, hidden), BF),
        pltpu.VMEM((rows, hidden), BF),
        pltpu.VMEM((rows, width), BF),
        pltpu.VMEM((rows, width), BF),
        pltpu.VMEM((rows, 1), F32),
        copy_sems(count),
        copy_sems(count, hidden // width),
    ]
    return call(
        partial(feed_both_kernel, count, layer),
        outs,
        [SMEM] + [VMEM] * 5 + [ANYWHERE] * count,
        scratch,
        28,
        (where, x, low_x, vec, bias, dy, *weights),
        late=(1,),
        early=(0,),
        packs=(2, 3),
        layer=layer,
    )


def lane_slices(a, lanes):
    return jnp.concatenate([a[:, i : i + lanes] for i in range(0, a.shape[1], lanes)], axis=0)


def lane_join(a, count):
    rows = a.shape[-2] // count
    return jnp.concatenate([a[..., i * rows : (i + 1) * rows, :] for i in range(count)], axis=-1)


def pad_to(a, rows, lanes):
    return jnp.pad(a, ((0, rows - a.shape[0]), (0, lanes - a.shape[1])))


def dynamic(a, index, axis):
    return lax.dynamic_index_in_dim(a, index, axis, keepdims=False)


def after(value, tokens):
    return lax.optimization_barrier((value, tokens))[0] if tokens else value


class Grid:
    def __init__(self):
        pipe, dp = lax.axis_index("pipe"), lax.axis_index("dp")
        self.x, self.core = pipe // 2, pipe % 2
        self.z, self.y = dp // 2, dp % 2
        self.arrived, self.computed, self.slack = [()] * 2, (), 1

    def swap_x(self, a):
        return lax.ppermute(a, "pipe", [(i, i ^ 2) for i in range(4)])

    def swap_core(self, a):
        return lax.ppermute(a, "pipe", [(i, i ^ 1) for i in range(4)])

    def swap_y(self, a):
        return lax.ppermute(a, "dp", [(i, i ^ 1) for i in range(8)])

    def ring_z(self, a, step=1):
        return lax.ppermute(a, "dp", [(i, (i + 2 * step) % 8) for i in range(8)])

    def turn(self, *moves, pre=(), compute=None, args=()):
        tokens = (*self.arrived[-self.slack], *self.computed)
        arrived = []

        def begin(asked):
            asked = [ask for group in asked for ask in group()]
            values = after([value for _, value, _ in asked], tokens)
            for (move, _, keep), value in zip(asked, values):
                result = move(value)
                arrived.append(result)
                keep(result)
            return tuple(values)

        begin(pre)
        values = begin(moves)
        self.arrived.append(tuple(arrived))
        self.computed = ()
        if compute is None:
            return None
        result = compute(*after(tuple(args), tokens + values))
        self.computed = tuple(jax.tree.leaves(result))
        return result


class Gather:
    def __init__(self, grid, piece):
        self.grid, self.here, self.swapped = grid, {(0, 0, 0): piece}, {}

    def get(self, layer, y, z, over):
        sources = {"z": (layer, y, z - 1), "y": (layer, 1 - y, z), "x": (1 - layer, y, z)}
        move = {"z": self.grid.ring_z, "y": self.grid.swap_y, "x": self.grid.swap_x}[over]
        return lambda: [(move, self.here[sources[over]], partial(self.here.__setitem__, (layer, y, z)))]

    def c(self, count=16):
        ready = [key for key in self.here if key not in self.swapped][:count]
        return [(self.grid.swap_core, self.here[key], partial(self.swapped.__setitem__, key)) for key in ready]

    def c2(self):
        return self.c(2)

    def pieces(self):
        keys = [[(layer, y, z) for y in range(2) for z in range(4)] for layer in range(2)]
        return [held[key] for half in keys for held in (self.here, self.swapped) for key in half]


class PairSum:
    def __init__(self, grid, own, other):
        self.grid, self.other = grid, other
        self.own = own.reshape((2, 4, 2) + own.shape[2:])
        self.came, self.got = None, {}

    def c(self):
        def keep(a):
            self.came = a.reshape(self.own.shape)

        return [(self.grid.swap_core, self.other, keep)]

    def block(self, own, y, z):
        layer = 0 if own else 1
        parts = [self.own[layer, z, y], self.came[layer, z, y], *self.got.get((own, y, z), [])]
        return sum(part.astype(F32) for part in parts)

    def move(self, over, own, y, z):
        to = {"z": (own, y, z - 1), "y": (own, 1 - y, z), "x": (True, y, z)}[over]
        move = {"z": self.grid.ring_z, "y": self.grid.swap_y, "x": self.grid.swap_x}[over]

        def ask():
            return [(move, self.block(own, y, z).astype(BF), self.got.setdefault(to, []).append)]

        return ask

    def steps(self):
        own, other = partial(self.move, own=True), partial(self.move, own=False)
        return [
            (other("z", y=0, z=2), other("y", y=1, z=3), other("x", y=1, z=2)),
            (other("z", y=1, z=1), own("y", y=1, z=3), other("x", y=0, z=3)),
            (own("z", y=0, z=3), own("y", y=1, z=2), other("x", y=1, z=0)),
            (own("z", y=0, z=2), own("y", y=1, z=1), other("x", y=0, z=1)),
            (own("z", y=0, z=1), own("y", y=1, z=0), other("x", y=0, z=0)),
        ]

    def total(self):
        return self.block(True, 0, 0)


class BlockSum:
    def __init__(self, grid, a, dtype):
        self.grid, self.a, self.dtype = grid, a, dtype
        self.ring = []

    def step(self, swap, place, axis):
        own = dynamic(self.a, place, axis)

        def keep(came):
            self.a = own.astype(F32) + came.astype(F32)

        return [(swap, dynamic(self.a, 1 - place, axis).astype(self.dtype), keep)]

    def c(self):
        return self.step(self.grid.swap_core, self.grid.core, 1)

    def x(self):
        return self.step(self.grid.swap_x, self.grid.x, 0)

    def x0(self):
        self.halves = [dynamic(self.a, place, 0) for place in (self.grid.x, 1 - self.grid.x)]
        return self.x_half(0)

    def x1(self):
        return self.x_half(1)

    def x_half(self, k):
        own, other = (h[2 * k : 2 * k + 2] for h in self.halves)

        def keep(came):
            total = own.astype(F32) + came.astype(F32)
            self.a = total if k == 0 else jnp.concatenate([self.a, total])

        return [(self.grid.swap_x, other.astype(self.dtype), keep)]

    def y(self):
        return self.step(self.grid.swap_y, self.grid.y, 1)

    def round(self):
        value = self.block(3 - len(self.ring))
        return [(self.grid.ring_z, value.astype(self.dtype), self.ring.append)]

    def block(self, step):
        value = dynamic(self.a, (self.grid.z + step) % 4, 0).astype(F32)
        return value + self.ring[-1].astype(F32) if self.ring else value

    def z(self):
        steps = [dynamic(self.a, (self.grid.z + k) % 4, 0) for k in range(4)]
        self.ring = [steps[0]]
        return [(partial(self.grid.ring_z, step=k), steps[k].astype(self.dtype), self.ring.append) for k in (1, 2, 3)]

    def total(self):
        return self.block(0) if len(self.ring) == 3 else sum(a.astype(F32) for a in self.ring)


def masks(caption_len, phrase_len, box_count, patch_mask, text_rows, patches):
    slots = jnp.arange(phrase_len.shape[1], dtype=jnp.int32)
    phrase_total = jnp.sum(jnp.where(slots[None, :] < box_count[:, None], phrase_len, 0), axis=1)
    lengths = jnp.minimum(caption_len + phrase_total, text_rows)
    first_patch = (jnp.arange(patch_mask.shape[1], dtype=jnp.int32) == 0).astype(jnp.int32)
    keep = jnp.maximum(patch_mask, first_patch[None, :]).astype(F32)
    return lengths, jnp.pad(keep, ((0, 0), (0, patches - keep.shape[1])))


def on_device(
    text_embed,
    image_feats,
    caption_len,
    phrase_len,
    box_count,
    patch_mask,
    attn_qkv,
    attn_out,
    ffn_up,
    ffn_down,
    layer_vectors,
    cross_query,
    cross_kv,
    cross_out,
    cross_vectors,
    cotangent,
):
    n_pipe, n_dp = lax.axis_size("pipe"), lax.axis_size("dp")
    everyone = ("pipe", "dp")
    shards, half = n_pipe * n_dp, n_pipe // 2
    samples, text_rows, width = text_embed.shape
    hidden = ffn_up.shape[1] * n_dp
    lanes = attn_qkv.shape[0]
    patches = -(-image_feats.shape[1] // 32) * 32
    direct = (n_pipe, n_dp) == (4, 8) and lanes % 128 == 0
    lengths, patch_keep = masks(caption_len, phrase_len, box_count, patch_mask, text_rows, patches)
    x = text_embed.reshape(-1, width)

    def padded(image_feats):
        wide = jnp.pad(image_feats, ((0, 0), (0, patches - image_feats.shape[1]), (0, 0)))
        return wide.reshape(samples * patches, -1)


    c_rows = cross_query.shape[0]
    kv_slices = cross_kv.shape[1] // width
    cross_pack = jnp.concatenate([cross_query, cross_out, lane_slices(cross_kv, width)], axis=0)
    v_rows, v_lanes = layer_vectors.shape
    x_rows = cross_vectors.shape[1]
    small = jnp.concatenate([pad_to(layer_vectors, v_rows, 128), pad_to(cross_vectors.T, x_rows, 128)], axis=0)
    small = pad_to(small, 16, 128)
    pack_attn = jnp.concatenate([attn_qkv.T, attn_out.T], axis=0)
    pack_feed = jnp.concatenate([ffn_up.T, lane_slices(ffn_down.T, lanes)], axis=0)
    n_pack = pack_attn.shape[0] + pack_feed.shape[0]

    def cross_weights(blocks):
        blocks = blocks.reshape(shards, -1, width)
        i_rows = cross_kv.shape[0]
        ends = np.cumsum([0, c_rows, c_rows, i_rows, i_rows])
        return [blocks[:, a:b].reshape(-1, width) for a, b in zip(ends[:-1], ends[1:])]

    def vectors_of(blocks):
        blocks = blocks.reshape(n_pipe, n_dp, 16, 128).astype(F32)
        vecs = []
        for layer in range(2):
            v = blocks[layer * half : (layer + 1) * half, :, :v_rows, :v_lanes]
            vecs.append(jnp.moveaxis(v, 1, 2).reshape(12, width))
        cvec = blocks.reshape(shards, 16, 128)[:, v_rows : v_rows + x_rows, :c_rows]
        return vecs, [v[8:12].reshape(1, hidden) for v in vecs], jnp.moveaxis(cvec, 1, 0).reshape(x_rows, width)

    def keys_values(image, wk, wv, cvec):
        keys = jnp.dot(image, wk, preferred_element_type=F32).astype(BF)
        return keys, (jnp.dot(image, wv, preferred_element_type=F32) + cvec[1]).astype(BF)

    def pack_cross(image, dk, dv, g_cq, g_co):
        grads = [g_cq, g_co, dot(image, dk, TN).astype(BF), dot(image, dv, TN).astype(BF)]
        return jnp.concatenate([g.reshape(shards, -1, width) for g in grads], axis=1)

    def vector_block(v_self, v_feed, v_up):
        v = jnp.concatenate([v_self[:5], v_feed[:3], v_up.reshape(4, width)], axis=0)
        return jnp.moveaxis(v.reshape(half, v_rows, n_dp, v_lanes), 2, 1)

    def pack_vectors(text, joining, v_cross):
        section = jnp.concatenate([vector_block(*text), vector_block(*joining)], axis=0)
        cross = jnp.moveaxis(v_cross[:x_rows].reshape(x_rows, n_pipe, n_dp, c_rows), 0, 2)
        wide = [jnp.pad(v, ((0, 0), (0, 0), (0, 0), (0, 128 - v.shape[3]))) for v in (section, cross)]
        wide = jnp.concatenate(wide, axis=2)
        return jnp.pad(wide, ((0, 0), (0, 0), (0, 16 - wide.shape[2]), (0, 0)))

    seed = cotangent.reshape(-1, width)
    if direct:
        grid = Grid()
        turn = grid.turn
        where = jnp.stack([grid.core, grid.z, grid.y, grid.x]).astype(jnp.int32)
        gather = Gather(grid, jnp.concatenate([pack_attn, pack_feed, pad_to(small, 16, lanes)]))
        get = gather.get
        turn(get(0, 0, 1, "z"), get(0, 1, 0, "y"), get(1, 0, 0, "x"), gather.c2)
        image = turn(
            get(0, 0, 2, "z"), get(0, 1, 1, "y"), get(1, 0, 1, "x"), gather.c2, compute=padded, args=(image_feats,)
        )
        turn(get(0, 0, 3, "z"), get(0, 1, 2, "y"), get(1, 1, 0, "x"), gather.c2)
        turn(get(1, 1, 1, "z"), get(0, 1, 3, "y"), get(1, 0, 3, "x"), gather.c2)
        turn(get(1, 0, 2, "z"), get(1, 1, 3, "y"), get(1, 1, 2, "x"), gather.c2)
        turn(gather.c)
        weights = gather.pieces()
        cross_whole = lax.all_gather(after(cross_pack, grid.arrived[-3]), everyone, axis=0, tiled=True)
        *vectors, cvec = gathered_vectors(weights, where, n_pack, v_rows, v_lanes, x_rows, c_rows)
        vecs, biases = vectors[:2], vectors[2:]
        state, low, s_self = self_forward(x, lengths, where, vecs[0], weights, 0)
        state, passed, s_feed = feed_forward(state, low, where, vecs[0], biases[0], weights, 0)
        state, low, s_self2 = self_forward(passed, lengths, where, vecs[1], weights, 1)
        wq, wo, wk, wv = cross_weights(cross_whole)
        keys, values = keys_values(image, wk, wv, cvec)
        state, low, s_cross = cross_forward(state, low, patch_keep, keys, values, cvec, wq, wo)
        joined, grad, *g_feed2, v_feed2, v_up2 = feed_both(state, low, where, vecs[1], biases[1], seed, weights, 1)
        grid.computed = (grad,)

        def fourth(grad):
            grad, dk, dv, g_cq, g_co, v_cross = cross_backward(grad, s_cross, cvec, wq, wo)
            return grad, v_cross, pack_cross(image, dk, dv, g_cq, g_co)

        grad, v_cross, cross_grads = fourth(grad)
        sum_cross = BlockSum(grid, cross_grads.reshape(2, 2, 4, 2, -1, width), BF)
        turn(sum_cross.c)
        grad, *g_self, v_self2 = turn(
            sum_cross.x0,
            compute=lambda grad: self_backward(grad, s_self2, where, vecs[1], weights, 1, BF), args=(grad,),
        )
        grad, *g_feed, v_feed, v_up = turn(
            sum_cross.x1,
            compute=lambda grad: feed_backward(grad, s_feed, where, vecs[0], weights, 0, g_feed2), args=(grad,),
        )
        feed = PairSum(grid, *g_feed)
        embed_grad, *g_self, v_self = turn(
            feed.c, sum_cross.y,
            compute=lambda grad: self_backward(grad, s_self, where, vecs[0], weights, 0, F32, g_self), args=(grad,),
        )
        attn = PairSum(grid, *g_self)
        sum_vec = BlockSum(
            grid,
            pack_vectors((v_self, v_feed, v_up), (v_self2, v_feed2, v_up2), v_cross).reshape(2, 2, 4, 2, 16, 128),
            F32,
        )
        f0, f1, f2, f3, f4 = feed.steps()
        a0, a1, a2, a3, a4 = attn.steps()
        turn(*f0, attn.c, sum_cross.round)
        turn(*f1, *a0, sum_vec.c, sum_cross.round)
        turn(*f2, *a1, sum_vec.x, sum_cross.round)
        turn(*f3, *a2, sum_vec.y)
        turn(*f4, *a3)
        turn(*a4, sum_vec.z)
        attn_grads, feed_grads = attn.total(), feed.total()
        n_qkv, n_up = attn_qkv.shape[1], ffn_up.shape[1]
        mine = [attn_grads[:n_qkv], attn_grads[n_qkv:], feed_grads[:n_up], feed_grads[n_up:]]
        cross_grads, small = sum_cross.total(), sum_vec.total()
    else:
        where = jnp.zeros((4,), jnp.int32)
        image = padded(image_feats)
        vectors = lax.all_gather(small, everyone, axis=0, tiled=False)
        whole = lax.all_gather(jnp.concatenate([pack_attn, pack_feed], axis=0), everyone, axis=0, tiled=False)
        whole = whole.reshape(n_pipe, n_dp, -1, lanes)

        def section(piece, layer):
            piece = jnp.moveaxis(piece[layer * half : (layer + 1) * half], 0, 2)
            return piece.reshape(n_dp * piece.shape[1], half * piece.shape[-1])

        counts = [attn_qkv.shape[1], attn_out.shape[1], ffn_up.shape[1], attn_out.shape[1] * (hidden // width)]
        ends = np.cumsum([0] + counts)
        cut = [whole[:, :, a:b] for a, b in zip(ends[:-1], ends[1:])]
        cut[3] = lane_join(cut[3], hidden // width)
        (qkv1, out1, up1, down1), (qkv2, out2, up2, down2) = ([section(c, k) for c in cut] for k in range(2))
        vecs, biases, cvec = vectors_of(vectors)
        wq, wo, wk, wv = cross_weights(lax.all_gather(cross_pack, everyone, axis=0, tiled=False))
        state, low, s_self = self_forward(x, lengths, where, vecs[0], [qkv1, out1], 0)
        state, passed, s_feed = feed_forward(state, low, where, vecs[0], biases[0], [up1, down1], 0)
        state, low, s_self2 = self_forward(passed, lengths, where, vecs[1], [qkv2, out2], 1)
        keys, values = keys_values(image, wk, wv, cvec)
        state, low, s_cross = cross_forward(state, low, patch_keep, keys, values, cvec, wq, wo)
        joined, grad, *g_feed2, v_feed2, v_up2 = feed_both(state, low, where, vecs[1], biases[1], seed, [up2, down2], 1)
        grad, dk, dv, g_cq, g_co, v_cross = cross_backward(grad, s_cross, cvec, wq, wo)
        grad, *g_self, v_self2 = self_backward(grad, s_self2, where, vecs[1], [qkv2, out2], 1, BF)
        grad, *g_feed, v_feed, v_up = feed_backward(grad, s_feed, where, vecs[0], [up1, down1], 0, g_feed2)
        embed_grad, *g_self, v_self = self_backward(grad, s_self, where, vecs[0], [qkv1, out1], 0, F32, g_self)
        g_self1, g_self2 = ([g[k] for g in g_self] for k in range(2))
        g_feed1, g_feed2 = ([g[k] for g in g_feed] for k in range(2))

        def unpack(pair, rows, slices):
            parts = []
            at = 0
            for r, k in zip(rows, slices):
                sides = [p[:, at : at + r * k] for p in pair]
                sides = [lane_join(p, k).reshape(8 * r, -1) for p in sides]
                parts.append(jnp.concatenate(sides, axis=1))
                at += r * k
            return parts

        def split(first, second):
            both = jnp.stack([first, second])
            rows, k = both.shape[1] // n_dp, both.shape[2] // (half * lanes)
            both = both.reshape(2, n_dp, rows, half, k, lanes)
            return both.transpose(0, 3, 1, 4, 2, 5).reshape(n_pipe, n_dp, k * rows, lanes)

        attn = ((3 * width // 8, width // 8), (1, 1))
        feed = ((hidden // 8, width // 8), (1, hidden // width))
        parts = []
        for first, second, shape in ((g_self1, g_self2, attn), (g_feed1, g_feed2, feed)):
            parts += [split(a, b) for a, b in zip(unpack(first, *shape), unpack(second, *shape))]
        packed = jnp.concatenate(parts, axis=2).reshape(-1, lanes)
        packed = lax.psum_scatter(packed, everyone, scatter_dimension=0, tiled=True).astype(F32)
        mine = [packed[a:b] for a, b in zip(ends[:-1], ends[1:])]
        cross_grads = pack_cross(image, dk, dv, g_cq, g_co).reshape(-1, width)
        cross_grads = lax.psum_scatter(cross_grads, everyone, scatter_dimension=0, tiled=True).astype(F32)
        small = pack_vectors((v_self, v_feed, v_up), (v_self2, v_feed2, v_up2), v_cross)
        small = lax.psum_scatter(small.reshape(-1, 128), everyone, scatter_dimension=0, tiled=True)
    mine[3] = lane_join(mine[3], hidden // width)
    return (
        joined.reshape(text_embed.shape),
        embed_grad.reshape(text_embed.shape),
        mine[0].T,
        mine[1].T,
        mine[2].T,
        mine[3].T,
        small[:v_rows, :v_lanes],
        cross_grads[:c_rows],
        lane_join(cross_grads[2 * c_rows :], kv_slices),
        cross_grads[c_rows : 2 * c_rows],
        small[v_rows : v_rows + x_rows, :c_rows].T,
    )


def solution(mesh):
    in_specs = (
        P(("pipe", "dp"), None, None),
        P(("pipe", "dp"), None, None),
        P(("pipe", "dp")),
        P(("pipe", "dp"), None),
        P(("pipe", "dp")),
        P(("pipe", "dp"), None),
        P("pipe", "dp"),
        P("pipe", "dp"),
        P("pipe", "dp"),
        P("pipe", "dp"),
        P("pipe", "dp"),
        P(("pipe", "dp"), None),
        P(("pipe", "dp"), None),
        P(("pipe", "dp"), None),
        P(("pipe", "dp"), None),
        P(("pipe", "dp"), None, None),
    )
    out_specs = (
        P(("pipe", "dp"), None, None),
        P(("pipe", "dp"), None, None),
        P("pipe", "dp"),
        P("pipe", "dp"),
        P("pipe", "dp"),
        P("pipe", "dp"),
        P("pipe", "dp"),
        P(("pipe", "dp"), None),
        P(("pipe", "dp"), None),
        P(("pipe", "dp"), None),
        P(("pipe", "dp"), None),
    )
    return jax.shard_map(
        on_device, mesh=mesh, in_specs=in_specs, out_specs=out_specs, check_vma=False
    )
```

```python
from functools import partial

import jax
import jax.numpy as jnp
import numpy as np
from jax import lax
from jax.experimental import pallas as pl
from jax.experimental.pallas import tpu as pltpu
from jax.sharding import PartitionSpec as P

HEADS = 12
NORM_EPS = 1e-12
MASKED = -1e30
BF = jnp.bfloat16
F32 = jnp.float32
NT = (((1,), (1,)), ((), ()))
NN = (((1,), (0,)), ((), ()))
TN = (((0,), (0,)), ((), ()))
VMEM_BYTES = 58 * 2**20
TILE = 768
CHUNK = 128


def dot(a, b, dims=NN):
    return lax.dot_general(a, b, dims, preferred_element_type=F32)


def span(start, size, unit=128):
    return pl.ds(pl.multiple_of(start, unit), size)


def tiles(count, body):
    def step(i, carry):
        body(i)
        return carry

    lax.fori_loop(0, count, step, 0)


class Copies:
    def __init__(self, sems):
        self.sems, self.used = sems, 0
        self.coming, self.going, self.sent = [], [], []

    def copy(self, source, target):
        self.used += 1
        copy = pltpu.make_async_copy(source, target, self.sems.at[self.used - 1])
        copy.start()
        return copy

    def begin(self, *refs):
        for k, (held, source, _) in enumerate(self.coming):
            if any(held is ref for ref in refs):
                self.coming[k] = (held, source, self.copy(source, held))

    def need(self, *refs):
        for k, (held, source, copy) in enumerate(self.coming):
            if any(held is ref for ref in refs):
                copy.wait()
                self.coming[k] = (None, source, None)

    def send(self, *refs, part=()):
        for held, target in self.going:
            if any(held is ref for ref in refs):
                self.sent.append(self.copy(held.at[part], target.at[part]) if part else self.copy(held, target))

    def finish(self):
        settle(self.sent)


def fetch(copies, sems, here=None):
    started = []
    for k in range(len(copies[0][0])):
        started.append([pltpu.make_async_copy(s[k], t, sems.at[i]) for i, (s, t) in enumerate(copies)])

    def start(group):
        for copy in group:
            copy.start()

    if len(started) == 1:
        start(started[0])
    else:
        pl.when(here)(lambda: start(started[0]))
        pl.when(jnp.logical_not(here))(lambda: start(started[1]))
    return started[0]


def settle(started):
    for copy in started:
        copy.wait()


def placed(refs, where_ref, layout, target, lanes):
    if len(refs) == 1:
        return [(refs, target)]
    core, z, y = where_ref[0], where_ref[1], where_ref[2]
    copies = []
    for i, pair in enumerate(zip(refs[:16], refs[16:])):
        c_rel, y_rel, z_rel = i // 8, (i // 4) % 2, i % 4
        block = lax.rem(z - z_rel + 4, 4) * 2 + lax.rem(y + y_rel, 2)
        side = lax.rem(core + c_rel, 2)
        for first, rows, shift in layout:
            place = target.at[
                span(block * rows, rows, 16),
                span(side * lanes + shift * pair[0].shape[1], pair[0].shape[1]),
            ]
            copies.append(([ref.at[pl.ds(first, rows)] for ref in pair], place))
    return copies


def relative(where_ref, block):
    z = lax.rem(block // 2 - where_ref[1] + 4, 4)
    return z * 2 + lax.rem(block % 2 + where_ref[2], 2)


def norm_rows(x_ref, bias, gain, offset, y_ref, low_ref, n_ref, r_ref):
    for i in range(0, y_ref.shape[0], CHUNK):
        rows = pl.ds(i, CHUNK)
        u = x_ref[rows, :].astype(F32) + (y_ref[rows, :] + bias)
        center = u - jnp.mean(u, axis=-1, keepdims=True)
        scale = lax.rsqrt(jnp.mean(center * center, axis=-1, keepdims=True) + NORM_EPS)
        normed = center * scale
        y = normed * gain + offset
        y_ref[rows, :] = y
        low_ref[rows, :] = y.astype(BF)
        n_ref[rows, :] = normed.astype(BF)
        r_ref[rows, :] = scale


def norm_rows_back(dy_ref, n_ref, r_ref, gain, du_ref, db_ref):
    def chunk(i, sums):
        rows = span(i * CHUNK, CHUNK, CHUNK)
        dy = dy_ref[rows, :].astype(F32)
        n = n_ref[rows, :].astype(F32)
        s = dy * gain
        du = r_ref[rows, :] * (
            s - jnp.mean(s, axis=-1, keepdims=True) - n * jnp.mean(s * n, axis=-1, keepdims=True)
        )
        db = du.astype(BF)
        du_ref[rows, :] = du
        db_ref[rows, :] = db
        terms = (dy * n, dy, db.astype(F32))
        return tuple(a + jnp.sum(t, axis=0, keepdims=True) for a, t in zip(sums, terms))

    zero = jnp.zeros((1, dy_ref.shape[1]), F32)
    return lax.fori_loop(0, dy_ref.shape[0] // CHUNK, chunk, (zero, zero, zero))


def split_heads(a):
    first = lax.broadcasted_iota(jnp.int32, a.shape, 1) < a.shape[1] // 2
    zero = jnp.zeros_like(a)
    return jnp.concatenate([jnp.where(first, a, zero), jnp.where(first, zero, a)], axis=0)


def join_heads(a):
    rows = a.shape[0] // 2
    first = lax.broadcasted_iota(jnp.int32, (rows, a.shape[1]), 1) < a.shape[1] // 2
    return jnp.where(first, a[:rows], a[rows:])


def softmax(scores, mask, axis):
    scores = scores + mask
    e = jnp.exp(scores - jnp.max(scores, axis=axis, keepdims=True))
    return (e * (1.0 / jnp.sum(e, axis=axis, keepdims=True))).astype(BF)


def score_back(weights, d_weights):
    a = weights.astype(F32)
    t = a * d_weights
    return (t - a * jnp.sum(t, axis=0, keepdims=True)).astype(BF)


def project_and_norm(x_ref, o_ref, w_ref, dims, bias, gain, offset, outs):
    y_ref, low_ref, n_ref, r_ref = outs
    width = y_ref.shape[1]

    def tile(j):
        cols = span(j * TILE, TILE)
        w = w_ref[cols, :] if dims is NT else w_ref[:, cols]
        y_ref[:, cols] = dot(o_ref[...], w, dims)

    tiles(width // TILE, tile)
    norm_rows(x_ref, bias, gain, offset, y_ref, low_ref, n_ref, r_ref)


def self_weights(count, layer, where_ref, refs, qkv, out, sems, sems2):
    width, whole = out.shape[1], count == 2
    n, m = qkv.shape[0] // 8, out.shape[0] // 8
    here = where_ref[3] == layer
    return (
        lambda: fetch(placed(refs[:1] if whole else refs, where_ref, [(0, n, 0)], qkv, width // 2), sems, here),
        lambda: fetch(placed(refs[1:] if whole else refs, where_ref, [(n, m, 0)], out, width // 2), sems2, here),
    )


def self_project(x_ref, vec_ref, p_ref, qkv, bias_ref):
    width = x_ref.shape[1]
    bias_ref[:, :width] = vec_ref[0:1, :]
    bias_ref[:, width : 2 * width] = jnp.zeros((1, width), F32)
    bias_ref[:, 2 * width :] = vec_ref[1:2, :]

    def tile(j):
        cols = span(j * TILE, TILE)
        p_ref[:, cols] = (dot(x_ref[...], qkv[cols, :], NT) + bias_ref[:, cols]).astype(BF)

    tiles(3 * width // TILE, tile)


def self_attend(lengths, p_ref, a_ref, o_ref):
    width = o_ref.shape[1]
    pairs = width // 128
    key = lax.broadcasted_iota(jnp.int32, (128, 256), 0)
    query = lax.broadcasted_iota(jnp.int32, (128, 256), 1)
    same = ((query // 64) % 2) == (key // 64)

    def attend(s):
        rows = span(s * 128, 128)
        length = jnp.where(key < 64, lengths[2 * s], lengths[2 * s + 1])
        mask = jnp.where(same & (lax.rem(key, 64) < length), 0.0, MASKED)
        for h in range(pairs):
            q = p_ref[rows, pl.ds(h * 128, 128)]
            k = p_ref[rows, pl.ds(width + h * 128, 128)]
            v = p_ref[rows, pl.ds(2 * width + h * 128, 128)]
            a = softmax(dot(k, split_heads(q * 0.125), NT), mask, 0)
            a_ref[s * pairs + h] = a
            o_ref[rows, pl.ds(h * 128, 128)] = join_heads(dot(a, v, TN)).astype(BF)

    tiles(o_ref.shape[0] // 128, attend)


def self_backward_kernel(count, layer, io, ins, outs, scratch):
    where_ref, dy_ref, x_ref, vec_ref, p_ref, a_ref, o_ref, n_ref, r_ref, *refs = ins
    dx_ref, own_ref, other_ref, gv_ref = outs
    qkv, out, du_ref, db_ref, dmix_ref, dp_ref, rel_ref, g_ref, sems, sems2 = scratch
    width = x_ref.shape[1]
    half = width // 2
    n, m = qkv.shape[0] // 8, out.shape[0] // 8
    whole = count == 2
    here = where_ref[3] == layer
    second = fetch(placed(refs[1:] if whole else refs, where_ref, [(n, m, 0)], out, half), sems2, here)
    io.begin(o_ref, p_ref, a_ref)
    core = where_ref[0]
    g_gain, g_offset, g_bias = norm_rows_back(dy_ref, n_ref, r_ref, vec_ref[3:4, :], du_ref, db_ref)
    settle(second)

    def mix(j):
        cols = span(j * TILE, TILE)
        dmix_ref[:, cols] = dot(db_ref[...], out[:, cols]).astype(BF)

    tiles(width // TILE, mix)
    io.need(o_ref, p_ref, a_ref)
    rel_ref[:, :half] = o_ref[:, span(core * half, half)]
    rel_ref[:, half:] = o_ref[:, span((1 - core) * half, half)]

    g_ref[:width, :] = dot(db_ref[...], rel_ref[...], TN).astype(BF)
    for b in range(8):
        to, at = relative(where_ref, b), pl.ds(b * m, m)
        own_ref[to, n:, :] = g_ref[at, :half]
        other_ref[to, n:, :] = g_ref[at, half:]
    io.begin(x_ref)
    first = fetch(placed(refs[:1] if whole else refs, where_ref, [(0, n, 0)], qkv, half), sems, here)
    pairs = width // 128

    def attend(s):
        rows = span(s * 128, 128)
        for h in range(pairs):
            q2 = split_heads(p_ref[rows, pl.ds(h * 128, 128)])
            k = p_ref[rows, pl.ds(width + h * 128, 128)]
            v = p_ref[rows, pl.ds(2 * width + h * 128, 128)]
            do2 = split_heads(dmix_ref[rows, pl.ds(h * 128, 128)])
            a = a_ref[s * pairs + h]
            ds = score_back(a, dot(v, do2, NT))
            dp_ref[rows, pl.ds(h * 128, 128)] = (join_heads(dot(ds, k, TN)) * 0.125).astype(BF)
            dp_ref[rows, pl.ds(width + h * 128, 128)] = (dot(ds, q2) * 0.125).astype(BF)
            dp_ref[rows, pl.ds(2 * width + h * 128, 128)] = dot(a, do2).astype(BF)

    tiles(x_ref.shape[0] // 128, attend)
    io.need(x_ref)
    rel_ref[:, :half] = x_ref[:, span(core * half, half)]
    rel_ref[:, half:] = x_ref[:, span((1 - core) * half, half)]

    def qkv_grad(j):
        rows = span(j * TILE, TILE)
        g_ref[rows, :] = dot(dp_ref[:, rows], rel_ref[...], TN).astype(BF)

    tiles(3 * width // TILE, qkv_grad)
    for b in range(8):
        to, at = relative(where_ref, b), pl.ds(b * n, n)
        own_ref[to, :n, :] = g_ref[at, :half]
        other_ref[to, :n, :] = g_ref[at, half:]
    io.send(other_ref, own_ref)
    settle(first)

    def back(j):
        cols = span(j * TILE, TILE)
        dx_ref[:, cols] = (du_ref[:, cols] + dot(dp_ref[...], qkv[:, cols])).astype(dx_ref.dtype)

    tiles(width // TILE, back)
    gv_ref[0:1, :] = jnp.sum(dp_ref[:, :width].astype(F32), axis=0, keepdims=True)
    gv_ref[1:2, :] = jnp.sum(dp_ref[:, 2 * width :].astype(F32), axis=0, keepdims=True)
    gv_ref[2:3, :] = g_bias
    gv_ref[3:4, :] = g_gain
    gv_ref[4:5, :] = g_offset


def cross_forward_kernel(io, ins, outs, scratch):
    x_ref, low_x_ref, keep_ref, k_ref, v_ref, vec_ref, wq_ref, wo_ref = ins
    q_ref, a_ref, o_ref, y_ref, low_ref, n_ref, r_ref = outs
    io.begin(k_ref, v_ref)
    width = x_ref.shape[1]
    patches = k_ref.shape[0] // keep_ref.shape[0]

    def tile(j):
        cols = span(j * TILE, TILE)
        q_ref[:, cols] = (dot(low_x_ref[...], wq_ref[:, cols]) + vec_ref[0:1, cols]).astype(BF)

    tiles(width // TILE, tile)
    io.send(q_ref)
    io.need(k_ref, v_ref)
    io.begin(x_ref, wo_ref)
    pairs = width // 128

    def attend(s):
        rows, keys = span(s * 64, 64, 64), span(s * patches, patches, 16)
        mask = jnp.where(keep_ref[pl.ds(s, 1), :] > 0, 0.0, MASKED)
        for h in range(pairs):
            q = q_ref[rows, pl.ds(h * 128, 128)]
            k = k_ref[keys, pl.ds(h * 128, 128)]
            v = v_ref[keys, pl.ds(h * 128, 128)]
            a = softmax(dot(split_heads(q * 0.125), k, NT), mask, 1)
            a_ref[s * pairs + h] = a.T
            o_ref[rows, pl.ds(h * 128, 128)] = join_heads(dot(a, v)).astype(BF)

    tiles(keep_ref.shape[0], attend)
    io.send(a_ref, o_ref)
    io.need(x_ref, wo_ref)
    project_and_norm(
        x_ref, o_ref, wo_ref, NN, vec_ref[2:3, :], vec_ref[3:4, :], vec_ref[4:5, :], (y_ref, low_ref, n_ref, r_ref)
    )


def cross_backward_kernel(io, ins, outs, scratch):
    dy_ref, low_x_ref, k_ref, v_ref, vec_ref, wq_ref, wo_ref, q_ref, a_ref, o_ref, n_ref, r_ref = ins
    dx_ref, dk_ref, dv_ref, gq_ref, go_ref, gv_ref = outs
    db_ref, dmix_ref, dq_ref = scratch
    width = low_x_ref.shape[1]
    patches = a_ref.shape[1]
    io.begin(wo_ref, o_ref)
    g_gain, g_offset, g_bias = norm_rows_back(dy_ref, n_ref, r_ref, vec_ref[3:4, :], dx_ref, db_ref)

    io.begin(q_ref, k_ref, v_ref, a_ref)
    io.need(wo_ref, o_ref)

    def mix(j):
        cols = span(j * TILE, TILE)
        dmix_ref[:, cols] = dot(db_ref[...], wo_ref[cols, :], NT).astype(BF)
        go_ref[cols, :] = dot(o_ref[:, cols], db_ref[...], TN).astype(BF)

    tiles(width // TILE, mix)
    io.send(go_ref)
    io.need(q_ref, k_ref, v_ref, a_ref)
    io.begin(wq_ref, low_x_ref)
    pairs = width // 128

    def attend(s):
        rows, keys = span(s * 64, 64, 64), span(s * patches, patches, 16)
        for h in range(pairs):
            q2 = split_heads(q_ref[rows, pl.ds(h * 128, 128)])
            k = k_ref[keys, pl.ds(h * 128, 128)]
            v = v_ref[keys, pl.ds(h * 128, 128)]
            do2 = split_heads(dmix_ref[rows, pl.ds(h * 128, 128)])
            a = a_ref[s * pairs + h]
            ds = score_back(a, dot(v, do2, NT))
            dq_ref[rows, pl.ds(h * 128, 128)] = (join_heads(dot(ds, k, TN)) * 0.125).astype(BF)
            dk_ref[keys, pl.ds(h * 128, 128)] = (dot(ds, q2) * 0.125).astype(BF)
            dv_ref[keys, pl.ds(h * 128, 128)] = dot(a, do2).astype(BF)

    tiles(a_ref.shape[0] // pairs, attend)
    io.send(dk_ref, dv_ref)
    io.need(wq_ref, low_x_ref)

    def back(j):
        cols = span(j * TILE, TILE)
        dx_ref[:, cols] += dot(dq_ref[...], wq_ref[cols, :], NT)
        gq_ref[cols, :] = dot(low_x_ref[:, cols], dq_ref[...], TN).astype(BF)

    tiles(width // TILE, back)
    gv_ref[0:1, :] = jnp.sum(dq_ref[...].astype(F32), axis=0, keepdims=True)
    gv_ref[1:2, :] = jnp.sum(dv_ref[...].astype(F32), axis=0, keepdims=True)
    gv_ref[2:3, :] = g_bias
    gv_ref[3:4, :] = g_gain
    gv_ref[4:5, :] = g_offset


def gelu_parts(h):
    size = jnp.abs(h) * 0.7071067811865476
    t = 1.0 / (1.0 + 0.3275911 * size)
    e = jnp.exp(-size * size)
    poly = t * (0.254829592 + t * (-0.284496736 + t * (1.421413741 + t * (-1.453152027 + t * 1.061405429))))
    tail = 0.5 * poly * e
    cdf = jnp.where(h < 0, tail, 1.0 - tail)
    return h * cdf, cdf + h * (e * 0.3989422804014327)


def feed_weights(count, layer, where_ref, refs, up, down, sems, sems2):
    width, hidden = up.shape[1], up.shape[0]
    n, m, whole = hidden // 8, width // 8, count == 2
    base = 4 * m
    slices = [(base + n + m * i, m, i) for i in range(hidden // width)]
    here = where_ref[3] == layer
    return (
        lambda: fetch(placed(refs[:1] if whole else refs, where_ref, [(base, n, 0)], up, width // 2), sems, here),
        lambda: fetch(placed(refs[1:] if whole else refs, where_ref, slices, down, hidden // 2), sems2, here),
    )


def feed_activate(low_x_ref, up, bias_ref, act_ref, slope_ref):
    def tile(j):
        cols = span(j * TILE, TILE)
        h = dot(low_x_ref[...], up[cols, :], NT) + bias_ref[:, cols]
        act, slope = gelu_parts(h)
        act_ref[:, cols] = act.astype(BF)
        slope_ref[:, cols] = slope.astype(BF)

    tiles(up.shape[0] // TILE, tile)


def text_forward_kernel(count, io, ins, outs, scratch):
    lengths, where_ref, x_ref, vec_ref, vec2_ref, up_bias_ref, *refs = ins
    p1, a1, o1, low1, n1, act, slope, low2, n2, p2, a2, o2, r1, r2, y3, low3, n3, r3 = outs
    qkv, out, up, down, y1, y2, bias_ref, *sems = scratch
    whole = count == 6
    count = 2 if whole else count
    get_qkv, get_out = self_weights(count, 0, where_ref, refs[:2] if whole else refs, qkv, out, *sems[:2])
    get_up, get_down = feed_weights(count, 0, where_ref, refs[2:4] if whole else refs, up, down, *sems[2:])
    get_qkv2, get_out2 = self_weights(count, 1, where_ref, refs[4:] if whole else refs, qkv, out, *sems[:2])
    settle(get_qkv())
    coming = get_out()
    self_project(x_ref, vec_ref, p1, qkv, bias_ref)
    io.send(p1)
    coming_up = get_up()
    self_attend(lengths, p1, a1, o1)
    io.send(a1, o1)
    settle(coming)
    norm = vec_ref[2:3, :], vec_ref[3:4, :], vec_ref[4:5, :]
    project_and_norm(x_ref, o1, out, NT, *norm, (y1, low1, n1, r1))
    io.send(low1, n1)
    coming_down = get_down()
    settle(coming_up)
    coming = get_qkv2()
    feed_activate(low1, up, up_bias_ref, act, slope)
    io.send(act, slope)
    settle(coming_down)
    coming_out = get_out2()
    norm = vec_ref[5:6, :], vec_ref[6:7, :], vec_ref[7:8, :]
    project_and_norm(y1, act, down, NT, *norm, (y2, low2, n2, r2))
    io.send(low2, n2)
    settle(coming)
    self_project(low2, vec2_ref, p2, qkv, bias_ref)
    io.send(p2)
    self_attend(lengths, p2, a2, o2)
    io.send(a2, o2)
    settle(coming_out)
    norm = vec2_ref[2:3, :], vec2_ref[3:4, :], vec2_ref[4:5, :]
    project_and_norm(low2, o2, out, NT, *norm, (y3, low3, n3, r3))


def feed_backward_body(
    io, where_ref, dy_ref, low_x_ref, vec_ref, act_ref, slope_ref, n_ref, r_ref, outs, work, up, down, get_up, get_down
):
    dx_ref, own_ref, other_ref, gv_ref, gb_ref = outs
    db_ref, dbt_ref, dh_ref, rel_ref = work
    width, hidden = up.shape[1], up.shape[0]
    n, m, half = hidden // 8, width // 8, width // 2
    core = where_ref[0]
    second = get_down()
    io.begin(slope_ref)
    g_gain, g_offset, g_bias = norm_rows_back(dy_ref, n_ref, r_ref, vec_ref[6:7, :], dx_ref, db_ref)
    dbt_ref[...] = db_ref[...].T
    settle(second)
    io.need(slope_ref)
    io.begin(act_ref, low_x_ref)

    def down_tile(j):
        cols = span(j * TILE, TILE)
        dh = (dot(db_ref[...], down[:, cols]) * slope_ref[:, cols].astype(F32)).astype(BF)
        dh_ref[:, cols] = dh
        gb_ref[:, cols] = jnp.sum(dh.astype(F32), axis=0, keepdims=True)

    tiles(hidden // TILE, down_tile)
    io.need(act_ref)

    def down_grad(j):
        for ref, side in ((own_ref, core), (other_ref, 1 - core)):
            g = dot(dbt_ref[...], act_ref[:, span(side * (hidden // 2) + j * width, width)]).astype(BF)
            for b in range(8):
                to = relative(where_ref, b)
                for k in range(2):
                    ref[to, span(n + (2 * j + k) * m, m, 16), :] = g[b * m : (b + 1) * m, k * half : (k + 1) * half]

    tiles(hidden // 2 // width, down_grad)
    io.send(other_ref, own_ref, part=(slice(None), pl.ds(n, n)))
    first = get_up()
    io.need(low_x_ref)
    rel_ref[:, :half] = low_x_ref[:, span(core * half, half)]
    rel_ref[:, half:] = low_x_ref[:, span((1 - core) * half, half)]

    def up_grad(j):
        g = dot(dh_ref[:, span(j * 2 * n, 2 * n)], rel_ref[...], TN).astype(BF)
        for k in range(2):
            to = relative(where_ref, 2 * j + k)
            own_ref[to, :n, :] = g[k * n : (k + 1) * n, :half]
            other_ref[to, :n, :] = g[k * n : (k + 1) * n, half:]

    tiles(4, up_grad)
    io.send(other_ref, own_ref, part=(slice(None), pl.ds(0, n)))
    settle(first)

    def back(j):
        cols = span(j * TILE, TILE)
        dx_ref[:, cols] += dot(dh_ref[...], up[:, cols])

    tiles(width // TILE, back)
    gv_ref[0:1, :] = g_bias
    gv_ref[1:2, :] = g_gain
    gv_ref[2:3, :] = g_offset


def feed_backward_kernel(count, layer, io, ins, outs, scratch):
    where_ref, dy_ref, low_x_ref, vec_ref, act_ref, slope_ref, n_ref, r_ref, *refs = ins
    up, down, *work, sems, sems2 = scratch
    get = feed_weights(count, layer, where_ref, refs, up, down, sems, sems2)
    feed_backward_body(
        io, where_ref, dy_ref, low_x_ref, vec_ref, act_ref, slope_ref, n_ref, r_ref, outs, work, up, down, *get
    )


def feed_both_kernel(count, layer, io, ins, outs, scratch):
    where_ref, x_ref, low_x_ref, vec_ref, bias_ref, dy_ref, *refs = ins
    y_ref, *grads = outs
    up, down, *work, act_ref, slope_ref, low_ref, n_ref, r_ref, sems, sems2 = scratch
    get = feed_weights(count, layer, where_ref, refs, up, down, sems, sems2)
    settle(get[0]())
    second = get[1]()
    io.begin(x_ref)
    feed_activate(low_x_ref, up, bias_ref, act_ref, slope_ref)
    settle(second)
    io.need(x_ref)
    norm = vec_ref[5:6, :], vec_ref[6:7, :], vec_ref[7:8, :]
    project_and_norm(x_ref, act_ref, down, NT, *norm, (y_ref, low_ref, n_ref, r_ref))
    io.send(y_ref)
    feed_backward_body(
        io, where_ref, dy_ref, low_x_ref, vec_ref, act_ref, slope_ref, n_ref, r_ref, grads, work, up, down, list, list
    )


def vector_kernel(first, v_rows, v_lanes, x_rows, c_rows, *refs):
    where_ref, *pieces = refs[:33]
    vec_refs, bias_refs, cross_ref = refs[33:35], refs[35:37], refs[37]
    held, sems = refs[38:]
    core, z, y, x = where_ref[0], where_ref[1], where_ref[2], where_ref[3]
    copies = []
    for i, ref in enumerate(pieces):
        x_rel, c_rel, y_rel, z_rel = i // 16, (i // 8) % 2, (i // 4) % 2, i % 4
        pipe = lax.rem(x + x_rel, 2) * 2 + lax.rem(core + c_rel, 2)
        device = pipe * 8 + lax.rem(z - z_rel + 4, 4) * 2 + lax.rem(y + y_rel, 2)
        copies.append(([ref.at[pl.ds(first, 16), pl.ds(0, 128)]], held.at[device]))
    settle(fetch(copies, sems))
    for device in range(32):
        block = held[device].astype(F32)
        pipe, dp = device // 8, device % 8
        rows = pl.ds(pipe % 2 * v_rows, v_rows)
        vec_refs[pipe // 2][rows, pl.ds(dp * v_lanes, v_lanes)] = block[:v_rows, :v_lanes]
        cross_ref[0:x_rows, pl.ds(device * c_rows, c_rows)] = block[v_rows : v_rows + x_rows, :c_rows]
    width = cross_ref.shape[1]
    for vec_ref, bias_ref in zip(vec_refs, bias_refs):
        for j in range(4):
            bias_ref[:, j * width : (j + 1) * width] = vec_ref[8 + j : 9 + j, :]


def struct(*shape, dtype=F32):
    return jax.ShapeDtypeStruct(shape, dtype)


VMEM = pl.BlockSpec(memory_space=pltpu.VMEM)
SMEM = pl.BlockSpec(memory_space=pltpu.SMEM)
ANYWHERE = pl.BlockSpec(memory_space=pl.ANY)


def call(kernel, outs, specs, scratch, us, args, late=(), early=(), packs=(), layer=0, onto=None):
    n_in, n_out, n_scratch = len(args), len(outs), len(scratch)
    early = (*early, *packs)
    held = [pltpu.VMEM(args[i].shape, args[i].dtype) for i in late]
    held += [pltpu.VMEM(outs[i].shape, outs[i].dtype) for i in early]
    outs = [struct(2, *o.shape, dtype=o.dtype) if i in packs else o for i, o in enumerate(outs)]
    taken = tuple(onto) if onto else ()
    n_all = n_in + len(taken)

    def body(*refs):
        ins, out, rest = list(refs[:n_in]), list(refs[n_all : n_all + n_out]), refs[n_all + n_out :]
        buffers = rest[n_scratch:-1]
        io = Copies(rest[-1])
        for k, i in enumerate(late):
            io.coming.append((buffers[k], ins[i], None))
            ins[i] = buffers[k]
        for k, i in enumerate(early, len(late)):
            target = out[i].at[lax.rem(ins[0][3] + layer, 2)] if i in packs else out[i]
            io.going.append((buffers[k], target))
            out[i] = buffers[k]
        kernel(io, ins, out, rest[:n_scratch])
        io.finish()

    specs = [ANYWHERE if i in late else spec for i, spec in enumerate(specs)] + [ANYWHERE] * len(taken)
    return pl.pallas_call(
        body,
        out_shape=outs,
        in_specs=specs,
        out_specs=[ANYWHERE if i in early else VMEM for i in range(n_out)],
        scratch_shapes=[*scratch, *held, pltpu.SemaphoreType.DMA((24,))],
        input_output_aliases={n_in + k: i for k, i in enumerate(packs)} if taken else {},
        cost_estimate=pl.CostEstimate(flops=int(us * 1.1e9), bytes_accessed=int(us * 3.5e6), transcendentals=0),
        compiler_params=pltpu.CompilerParams(vmem_limit_bytes=VMEM_BYTES),
    )(*args, *taken)


def gathered_vectors(pieces, where, first, v_rows, v_lanes, x_rows, c_rows):
    width = 8 * v_lanes
    return pl.pallas_call(
        partial(vector_kernel, first, v_rows, v_lanes, x_rows, c_rows),
        out_shape=[struct(12, width)] * 2 + [struct(1, 4 * width)] * 2 + [struct(8, width)],
        in_specs=[SMEM] + [ANYWHERE] * len(pieces),
        out_specs=[VMEM] * 5,
        scratch_shapes=[pltpu.VMEM((32, 16, 128), BF), pltpu.SemaphoreType.DMA((32,))],
        cost_estimate=pl.CostEstimate(flops=0, bytes_accessed=10**7, transcendentals=0),
    )(where, *pieces)


def copy_sems(count, parts=1):
    return pltpu.SemaphoreType.DMA((16 * parts if count > 2 else 1,))


def text_forward(x, lengths, where, vecs, bias, weights):
    rows, width = x.shape
    hidden = bias.shape[1]
    blocks = rows // 128 * (width // 128)
    count = len(weights)
    low = struct(rows, width, dtype=BF)
    attention = [struct(rows, 3 * width, dtype=BF), struct(blocks, 128, 256, dtype=BF), low]
    outs = [
        *attention,
        low,
        low,
        struct(rows, hidden, dtype=BF),
        struct(rows, hidden, dtype=BF),
        low,
        low,
        *attention,
        struct(rows, 1),
        struct(rows, 1),
        struct(rows, width),
        low,
        low,
        struct(rows, 1),
    ]
    scratch = [
        pltpu.VMEM((3 * width, width), BF),
        pltpu.VMEM((width, width), BF),
        pltpu.VMEM((hidden, width), BF),
        pltpu.VMEM((width, hidden), BF),
        pltpu.VMEM((rows, width), F32),
        pltpu.VMEM((rows, width), F32),
        pltpu.VMEM((1, 3 * width), F32),
        copy_sems(count),
        copy_sems(count),
        copy_sems(count),
        copy_sems(count, hidden // width),
    ]
    p1, a1, o1, low1, n1, act, slope, low2, n2, p2, a2, o2, r1, r2, y3, low3, n3, r3 = call(
        partial(text_forward_kernel, count),
        outs,
        [SMEM, SMEM] + [VMEM] * 4 + [ANYWHERE] * count,
        scratch,
        38,
        (lengths, where, x, *vecs, bias, *weights),
        early=tuple(range(12)),
    )
    return y3, low3, (x, p1, a1, o1, n1, r1), (low1, act, slope, n2, r2), (low2, p2, a2, o2, n3, r3)


def self_backward(dy, saved, where, vec, weights, layer, dtype=F32, onto=None):
    x, p, a, o, n, r = saved
    rows, width = x.shape
    half = width // 2
    count = len(weights)
    outs = [
        struct(rows, width, dtype=dtype),
        struct(8, width // 2, half, dtype=BF),
        struct(8, width // 2, half, dtype=BF),
        struct(8, width),
    ]
    scratch = [
        pltpu.VMEM((3 * width, width), BF),
        pltpu.VMEM((width, width), BF),
        pltpu.VMEM((rows, width), F32),
        pltpu.VMEM((rows, width), BF),
        pltpu.VMEM((rows, width), BF),
        pltpu.VMEM((rows, 3 * width), BF),
        pltpu.VMEM((rows, width), BF),
        pltpu.VMEM((3 * width, width), BF),
        copy_sems(count),
        copy_sems(count),
    ]
    return call(
        partial(self_backward_kernel, count, layer),
        outs,
        [SMEM] + [VMEM] * 8 + [ANYWHERE] * count,
        scratch,
        22,
        (where, dy, x, vec, p, a, o, n, r, *weights),
        late=(6, 4, 5, 2),
        packs=(1, 2),
        layer=layer,
        onto=onto,
    )


def cross_forward(x, low_x, keep, k, v, vec, wq, wo):
    rows, width = x.shape
    samples, patches = keep.shape
    outs = [
        struct(rows, width, dtype=BF),
        struct(samples * (width // 128), patches, 128, dtype=BF),
        struct(rows, width, dtype=BF),
        struct(rows, width),
        struct(rows, width, dtype=BF),
        struct(rows, width, dtype=BF),
        struct(rows, 1),
    ]
    q, a, o, y, low, n, r = call(
        cross_forward_kernel,
        outs,
        [VMEM] * 8,
        [],
        21,
        (x, low_x, keep, k, v, vec, wq, wo),
        late=(3, 4, 7, 0),
        early=(0, 1, 2),
    )
    return y, low, (low_x, k, v, q, a, o, n, r)


def cross_backward(dy, saved, vec, wq, wo):
    low_x, k, v, q, a, o, n, r = saved
    rows, width = low_x.shape
    outs = [
        struct(rows, width),
        struct(*k.shape, dtype=BF),
        struct(*k.shape, dtype=BF),
        struct(width, width, dtype=BF),
        struct(width, width, dtype=BF),
        struct(8, width),
    ]
    scratch = [pltpu.VMEM((rows, width), BF)] * 3
    return call(
        cross_backward_kernel,
        outs,
        [VMEM] * 12,
        scratch,
        26,
        (dy, low_x, k, v, vec, wq, wo, q, a, o, n, r),
        late=(6, 9, 7, 2, 3, 8, 5, 1),
        early=(1, 2, 4),
    )


def feed_backward(dy, saved, where, vec, weights, layer, onto=None):
    low_x, act, slope, n, r = saved
    rows, width = low_x.shape
    hidden = act.shape[1]
    count = len(weights)
    outs = [
        struct(rows, width),
        struct(8, 2 * hidden // 8, width // 2, dtype=BF),
        struct(8, 2 * hidden // 8, width // 2, dtype=BF),
        struct(8, width),
        struct(1, hidden),
    ]
    scratch = [
        pltpu.VMEM((hidden, width), BF),
        pltpu.VMEM((width, hidden), BF),
        pltpu.VMEM((rows, width), BF),
        pltpu.VMEM((width, rows), BF),
        pltpu.VMEM((rows, hidden), BF),
        pltpu.VMEM((rows, width), BF),
        copy_sems(count),
        copy_sems(count, hidden // width),
    ]
    return call(
        partial(feed_backward_kernel, count, layer),
        outs,
        [SMEM] + [VMEM] * 7 + [ANYWHERE] * count,
        scratch,
        22,
        (where, dy, low_x, vec, act, slope, n, r, *weights),
        late=(5, 4, 2),
        packs=(1, 2),
        layer=layer,
        onto=onto,
    )


def feed_both(x, low_x, where, vec, bias, dy, weights, layer):
    rows, width = x.shape
    hidden = bias.shape[1]
    count = len(weights)
    outs = [
        struct(rows, width),
        struct(rows, width),
        struct(8, 2 * hidden // 8, width // 2, dtype=BF),
        struct(8, 2 * hidden // 8, width // 2, dtype=BF),
        struct(8, width),
        struct(1, hidden),
    ]
    scratch = [
        pltpu.VMEM((hidden, width), BF),
        pltpu.VMEM((width, hidden), BF),
        pltpu.VMEM((rows, width), BF),
        pltpu.VMEM((width, rows), BF),
        pltpu.VMEM((rows, hidden), BF),
        pltpu.VMEM((rows, width), BF),
        pltpu.VMEM((rows, hidden), BF),
        pltpu.VMEM((rows, hidden), BF),
        pltpu.VMEM((rows, width), BF),
        pltpu.VMEM((rows, width), BF),
        pltpu.VMEM((rows, 1), F32),
        copy_sems(count),
        copy_sems(count, hidden // width),
    ]
    return call(
        partial(feed_both_kernel, count, layer),
        outs,
        [SMEM] + [VMEM] * 5 + [ANYWHERE] * count,
        scratch,
        28,
        (where, x, low_x, vec, bias, dy, *weights),
        late=(1,),
        early=(0,),
        packs=(2, 3),
        layer=layer,
    )


def lane_slices(a, lanes):
    return jnp.concatenate([a[:, i : i + lanes] for i in range(0, a.shape[1], lanes)], axis=0)


def lane_join(a, count):
    rows = a.shape[-2] // count
    return jnp.concatenate([a[..., i * rows : (i + 1) * rows, :] for i in range(count)], axis=-1)


def pad_to(a, rows, lanes):
    return jnp.pad(a, ((0, rows - a.shape[0]), (0, lanes - a.shape[1])))


def dynamic(a, index, axis):
    return lax.dynamic_index_in_dim(a, index, axis, keepdims=False)


def after(value, tokens):
    return lax.optimization_barrier((value, tokens))[0] if tokens else value


class Grid:
    def __init__(self):
        pipe, dp = lax.axis_index("pipe"), lax.axis_index("dp")
        self.x, self.core = pipe // 2, pipe % 2
        self.z, self.y = dp // 2, dp % 2
        self.arrived, self.computed, self.slack = [()] * 2, (), 1

    def swap_x(self, a):
        return lax.ppermute(a, "pipe", [(i, i ^ 2) for i in range(4)])

    def swap_core(self, a):
        return lax.ppermute(a, "pipe", [(i, i ^ 1) for i in range(4)])

    def swap_y(self, a):
        return lax.ppermute(a, "dp", [(i, i ^ 1) for i in range(8)])

    def ring_z(self, a, step=1):
        return lax.ppermute(a, "dp", [(i, (i + 2 * step) % 8) for i in range(8)])

    def turn(self, *moves, pre=(), compute=None, args=(), chain=False):
        tokens = (*self.arrived[-self.slack], *self.computed)
        arrived = []

        def begin(asked):
            asked = [ask for group in asked for ask in group()]
            values = after([value for _, value, _ in asked], tokens)
            results = []
            for i, ((move, _, keep), value) in enumerate(zip(asked, values)):
                results.append(move(after(value, (results[i - 2],)) if chain and i >= 5 else value))
                keep(results[-1])
            arrived.extend(results)
            return tuple(values)

        begin(pre)
        values = begin(moves)
        self.arrived.append(tuple(arrived))
        self.computed = ()
        if compute is None:
            return None
        result = compute(*after(tuple(args), tokens + values))
        self.computed = tuple(jax.tree.leaves(result))
        return result


class Gather:
    def __init__(self, grid, piece):
        self.grid, self.here, self.swapped = grid, {(0, 0, 0): piece}, {}

    def get(self, layer, y, z, over):
        sources = {"z": (layer, y, z - 1), "y": (layer, 1 - y, z), "x": (1 - layer, y, z)}
        move = {"z": self.grid.ring_z, "y": self.grid.swap_y, "x": self.grid.swap_x}[over]
        return lambda: [(move, self.here[sources[over]], partial(self.here.__setitem__, (layer, y, z)))]

    def c(self, count=16):
        ready = [key for key in self.here if key not in self.swapped][:count]
        return [(self.grid.swap_core, self.here[key], partial(self.swapped.__setitem__, key)) for key in ready]

    def c3(self):
        return self.c(3)

    def pieces(self):
        keys = [[(layer, y, z) for y in range(2) for z in range(4)] for layer in range(2)]
        return [held[key] for half in keys for held in (self.here, self.swapped) for key in half]


class PairSum:
    def __init__(self, grid, own, other):
        self.grid, self.other = grid, other
        self.own = own.reshape((2, 4, 2) + own.shape[2:])
        self.came, self.got = None, {}

    def c(self):
        def keep(a):
            self.came = a.reshape(self.own.shape)

        return [(self.grid.swap_core, self.other, keep)]

    def block(self, own, y, z):
        layer = 0 if own else 1
        parts = [self.own[layer, z, y], self.came[layer, z, y], *self.got.get((own, y, z), [])]
        return sum(part.astype(F32) for part in parts)

    def move(self, over, own, y, z):
        to = {"z": (own, y, z - 1), "y": (own, 1 - y, z), "x": (True, y, z)}[over]
        move = {"z": self.grid.ring_z, "y": self.grid.swap_y, "x": self.grid.swap_x}[over]

        def ask():
            return [(move, self.block(own, y, z).astype(BF), self.got.setdefault(to, []).append)]

        return ask

    def steps(self):
        own, other = partial(self.move, own=True), partial(self.move, own=False)
        return [
            (other("z", y=0, z=2), other("y", y=1, z=3), other("x", y=1, z=2)),
            (other("z", y=1, z=1), own("y", y=1, z=3), other("x", y=0, z=3)),
            (own("z", y=0, z=3), own("y", y=1, z=2), other("x", y=1, z=0)),
            (own("z", y=0, z=2), own("y", y=1, z=1), other("x", y=0, z=1)),
            (own("z", y=0, z=1), own("y", y=1, z=0), other("x", y=0, z=0)),
        ]

    def total(self):
        return self.block(True, 0, 0)


class BlockSum:
    def __init__(self, grid, a, dtype):
        self.grid, self.a, self.dtype = grid, a, dtype
        self.ring = []

    def step(self, swap, place, axis):
        own = dynamic(self.a, place, axis)

        def keep(came):
            self.a = own.astype(F32) + came.astype(F32)

        return [(swap, dynamic(self.a, 1 - place, axis).astype(self.dtype), keep)]

    def c(self):
        return self.step(self.grid.swap_core, self.grid.core, 1)

    def x(self):
        return self.step(self.grid.swap_x, self.grid.x, 0)

    def x0(self):
        self.halves = [dynamic(self.a, place, 0) for place in (self.grid.x, 1 - self.grid.x)]
        return self.x_half(0)

    def x1(self):
        return self.x_half(1)

    def x_half(self, k):
        own, other = (h[2 * k : 2 * k + 2] for h in self.halves)

        def keep(came):
            total = own.astype(F32) + came.astype(F32)
            self.a = total if k == 0 else jnp.concatenate([self.a, total])

        return [(self.grid.swap_x, other.astype(self.dtype), keep)]

    def y(self):
        return self.step(self.grid.swap_y, self.grid.y, 1)

    def round(self):
        value = self.block(3 - len(self.ring))
        return [(self.grid.ring_z, value.astype(self.dtype), self.ring.append)]

    def block(self, step):
        value = dynamic(self.a, (self.grid.z + step) % 4, 0).astype(F32)
        return value + self.ring[-1].astype(F32) if self.ring else value

    def z(self):
        steps = [dynamic(self.a, (self.grid.z + k) % 4, 0) for k in range(4)]
        self.ring = [steps[0]]
        return [(partial(self.grid.ring_z, step=k), steps[k].astype(self.dtype), self.ring.append) for k in (1, 2, 3)]

    def total(self):
        return self.block(0) if len(self.ring) == 3 else sum(a.astype(F32) for a in self.ring)


def masks(caption_len, phrase_len, box_count, patch_mask, text_rows, patches):
    slots = jnp.arange(phrase_len.shape[1], dtype=jnp.int32)
    phrase_total = jnp.sum(jnp.where(slots[None, :] < box_count[:, None], phrase_len, 0), axis=1)
    lengths = jnp.minimum(caption_len + phrase_total, text_rows)
    first_patch = (jnp.arange(patch_mask.shape[1], dtype=jnp.int32) == 0).astype(jnp.int32)
    keep = jnp.maximum(patch_mask, first_patch[None, :]).astype(F32)
    return lengths, jnp.pad(keep, ((0, 0), (0, patches - keep.shape[1])))


def on_device(
    text_embed,
    image_feats,
    caption_len,
    phrase_len,
    box_count,
    patch_mask,
    attn_qkv,
    attn_out,
    ffn_up,
    ffn_down,
    layer_vectors,
    cross_query,
    cross_kv,
    cross_out,
    cross_vectors,
    cotangent,
):
    n_pipe, n_dp = lax.axis_size("pipe"), lax.axis_size("dp")
    everyone = ("pipe", "dp")
    shards, half = n_pipe * n_dp, n_pipe // 2
    samples, text_rows, width = text_embed.shape
    hidden = ffn_up.shape[1] * n_dp
    lanes = attn_qkv.shape[0]
    patches = -(-image_feats.shape[1] // 32) * 32
    direct = (n_pipe, n_dp) == (4, 8) and lanes % 128 == 0
    lengths, patch_keep = masks(caption_len, phrase_len, box_count, patch_mask, text_rows, patches)
    x = text_embed.reshape(-1, width)

    def padded(image_feats):
        wide = jnp.pad(image_feats, ((0, 0), (0, patches - image_feats.shape[1]), (0, 0)))
        return wide.reshape(samples * patches, -1)


    c_rows = cross_query.shape[0]
    kv_slices = cross_kv.shape[1] // width
    cross_pack = jnp.concatenate([cross_query, cross_out, lane_slices(cross_kv, width)], axis=0)
    v_rows, v_lanes = layer_vectors.shape
    x_rows = cross_vectors.shape[1]
    small = jnp.concatenate([pad_to(layer_vectors, v_rows, 128), pad_to(cross_vectors.T, x_rows, 128)], axis=0)
    small = pad_to(small, 16, 128)
    pack_attn = jnp.concatenate([attn_qkv.T, attn_out.T], axis=0)
    pack_feed = jnp.concatenate([ffn_up.T, lane_slices(ffn_down.T, lanes)], axis=0)
    n_pack = pack_attn.shape[0] + pack_feed.shape[0]

    def cross_weights(blocks):
        blocks = blocks.reshape(shards, -1, width)
        i_rows = cross_kv.shape[0]
        ends = np.cumsum([0, c_rows, c_rows, i_rows, i_rows])
        return [blocks[:, a:b].reshape(-1, width) for a, b in zip(ends[:-1], ends[1:])]

    def vectors_of(blocks):
        blocks = blocks.reshape(n_pipe, n_dp, 16, 128).astype(F32)
        vecs = []
        for layer in range(2):
            v = blocks[layer * half : (layer + 1) * half, :, :v_rows, :v_lanes]
            vecs.append(jnp.moveaxis(v, 1, 2).reshape(12, width))
        cvec = blocks.reshape(shards, 16, 128)[:, v_rows : v_rows + x_rows, :c_rows]
        return vecs, [v[8:12].reshape(1, hidden) for v in vecs], jnp.moveaxis(cvec, 1, 0).reshape(x_rows, width)

    def keys_values(image, wk, wv, cvec):
        keys = jnp.dot(image, wk, preferred_element_type=F32).astype(BF)
        return keys, (jnp.dot(image, wv, preferred_element_type=F32) + cvec[1]).astype(BF)

    def pack_cross(image, dk, dv, g_cq, g_co):
        grads = [g_cq, g_co, dot(image, dk, TN).astype(BF), dot(image, dv, TN).astype(BF)]
        return jnp.concatenate([g.reshape(shards, -1, width) for g in grads], axis=1)

    def vector_block(v_self, v_feed, v_up):
        v = jnp.concatenate([v_self[:5], v_feed[:3], v_up.reshape(4, width)], axis=0)
        return jnp.moveaxis(v.reshape(half, v_rows, n_dp, v_lanes), 2, 1)

    def pack_vectors(text, joining, v_cross):
        section = jnp.concatenate([vector_block(*text), vector_block(*joining)], axis=0)
        cross = jnp.moveaxis(v_cross[:x_rows].reshape(x_rows, n_pipe, n_dp, c_rows), 0, 2)
        wide = [jnp.pad(v, ((0, 0), (0, 0), (0, 0), (0, 128 - v.shape[3]))) for v in (section, cross)]
        wide = jnp.concatenate(wide, axis=2)
        return jnp.pad(wide, ((0, 0), (0, 0), (0, 16 - wide.shape[2]), (0, 0)))

    seed = cotangent.reshape(-1, width)
    if direct:
        grid = Grid()
        turn = grid.turn
        where = jnp.stack([grid.core, grid.z, grid.y, grid.x]).astype(jnp.int32)
        gather = Gather(grid, jnp.concatenate([pack_attn, pack_feed, pad_to(small, 16, lanes)]))
        get = gather.get
        turn(get(0, 0, 1, "z"), get(0, 1, 0, "y"), get(1, 0, 0, "x"), gather.c3, chain=True)
        image = turn(
            get(0, 0, 2, "z"), get(0, 1, 1, "y"), get(1, 0, 1, "x"), gather.c3, chain=True, compute=padded, args=(image_feats,)
        )
        turn(get(0, 0, 3, "z"), get(0, 1, 2, "y"), get(1, 1, 0, "x"), gather.c3, chain=True)
        turn(get(1, 1, 1, "z"), get(0, 1, 3, "y"), get(1, 0, 3, "x"), gather.c3, chain=True)
        turn(get(1, 0, 2, "z"), get(1, 1, 3, "y"), get(1, 1, 2, "x"), gather.c3, chain=True)
        turn(gather.c)
        weights = gather.pieces()
        cross_whole = lax.all_gather(after(cross_pack, grid.arrived[-3]), everyone, axis=0, tiled=True)
        *vectors, cvec = gathered_vectors(weights, where, n_pack, v_rows, v_lanes, x_rows, c_rows)
        vecs, biases = vectors[:2], vectors[2:]
        state, low, s_self, s_feed, s_self2 = text_forward(x, lengths, where, vecs, biases[0], weights)
        wq, wo, wk, wv = cross_weights(cross_whole)
        keys, values = keys_values(image, wk, wv, cvec)
        state, low, s_cross = cross_forward(state, low, patch_keep, keys, values, cvec, wq, wo)
        joined, grad, *g_feed2, v_feed2, v_up2 = feed_both(state, low, where, vecs[1], biases[1], seed, weights, 1)
        grid.computed = (grad,)

        def fourth(grad):
            grad, dk, dv, g_cq, g_co, v_cross = cross_backward(grad, s_cross, cvec, wq, wo)
            return grad, v_cross, pack_cross(image, dk, dv, g_cq, g_co)

        grad, v_cross, cross_grads = fourth(grad)
        sum_cross = BlockSum(grid, cross_grads.reshape(2, 2, 4, 2, -1, width), BF)
        turn(sum_cross.c)
        grad, *g_self, v_self2 = turn(
            sum_cross.x0,
            compute=lambda grad: self_backward(grad, s_self2, where, vecs[1], weights, 1, BF), args=(grad,),
        )
        grad, *g_feed, v_feed, v_up = turn(
            sum_cross.x1,
            compute=lambda grad: feed_backward(grad, s_feed, where, vecs[0], weights, 0, g_feed2), args=(grad,),
        )
        feed = PairSum(grid, *g_feed)
        embed_grad, *g_self, v_self = turn(
            feed.c, sum_cross.y,
            compute=lambda grad: self_backward(grad, s_self, where, vecs[0], weights, 0, F32, g_self), args=(grad,),
        )
        attn = PairSum(grid, *g_self)
        sum_vec = BlockSum(
            grid,
            pack_vectors((v_self, v_feed, v_up), (v_self2, v_feed2, v_up2), v_cross).reshape(2, 2, 4, 2, 16, 128),
            F32,
        )
        f0, f1, f2, f3, f4 = feed.steps()
        a0, a1, a2, a3, a4 = attn.steps()
        turn(*f0, attn.c, sum_cross.round)
        turn(*f1, *a0, sum_vec.c, sum_cross.round)
        turn(*f2, *a1, sum_vec.x, sum_cross.round)
        turn(*f3, *a2, sum_vec.y)
        turn(*f4, *a3)
        turn(*a4, sum_vec.z)
        attn_grads, feed_grads = attn.total(), feed.total()
        n_qkv, n_up = attn_qkv.shape[1], ffn_up.shape[1]
        mine = [attn_grads[:n_qkv], attn_grads[n_qkv:], feed_grads[:n_up], feed_grads[n_up:]]
        cross_grads, small = sum_cross.total(), sum_vec.total()
    else:
        where = jnp.zeros((4,), jnp.int32)
        image = padded(image_feats)
        vectors = lax.all_gather(small, everyone, axis=0, tiled=False)
        whole = lax.all_gather(jnp.concatenate([pack_attn, pack_feed], axis=0), everyone, axis=0, tiled=False)
        whole = whole.reshape(n_pipe, n_dp, -1, lanes)

        def section(piece, layer):
            piece = jnp.moveaxis(piece[layer * half : (layer + 1) * half], 0, 2)
            return piece.reshape(n_dp * piece.shape[1], half * piece.shape[-1])

        counts = [attn_qkv.shape[1], attn_out.shape[1], ffn_up.shape[1], attn_out.shape[1] * (hidden // width)]
        ends = np.cumsum([0] + counts)
        cut = [whole[:, :, a:b] for a, b in zip(ends[:-1], ends[1:])]
        cut[3] = lane_join(cut[3], hidden // width)
        (qkv1, out1, up1, down1), (qkv2, out2, up2, down2) = ([section(c, k) for c in cut] for k in range(2))
        vecs, biases, cvec = vectors_of(vectors)
        wq, wo, wk, wv = cross_weights(lax.all_gather(cross_pack, everyone, axis=0, tiled=False))
        state, low, s_self, s_feed, s_self2 = text_forward(
            x, lengths, where, vecs, biases[0], [qkv1, out1, up1, down1, qkv2, out2]
        )
        keys, values = keys_values(image, wk, wv, cvec)
        state, low, s_cross = cross_forward(state, low, patch_keep, keys, values, cvec, wq, wo)
        joined, grad, *g_feed2, v_feed2, v_up2 = feed_both(state, low, where, vecs[1], biases[1], seed, [up2, down2], 1)
        grad, dk, dv, g_cq, g_co, v_cross = cross_backward(grad, s_cross, cvec, wq, wo)
        grad, *g_self, v_self2 = self_backward(grad, s_self2, where, vecs[1], [qkv2, out2], 1, BF)
        grad, *g_feed, v_feed, v_up = feed_backward(grad, s_feed, where, vecs[0], [up1, down1], 0, g_feed2)
        embed_grad, *g_self, v_self = self_backward(grad, s_self, where, vecs[0], [qkv1, out1], 0, F32, g_self)
        g_self1, g_self2 = ([g[k] for g in g_self] for k in range(2))
        g_feed1, g_feed2 = ([g[k] for g in g_feed] for k in range(2))

        def unpack(pair, rows, slices):
            parts = []
            at = 0
            for r, k in zip(rows, slices):
                sides = [p[:, at : at + r * k] for p in pair]
                sides = [lane_join(p, k).reshape(8 * r, -1) for p in sides]
                parts.append(jnp.concatenate(sides, axis=1))
                at += r * k
            return parts

        def split(first, second):
            both = jnp.stack([first, second])
            rows, k = both.shape[1] // n_dp, both.shape[2] // (half * lanes)
            both = both.reshape(2, n_dp, rows, half, k, lanes)
            return both.transpose(0, 3, 1, 4, 2, 5).reshape(n_pipe, n_dp, k * rows, lanes)

        attn = ((3 * width // 8, width // 8), (1, 1))
        feed = ((hidden // 8, width // 8), (1, hidden // width))
        parts = []
        for first, second, shape in ((g_self1, g_self2, attn), (g_feed1, g_feed2, feed)):
            parts += [split(a, b) for a, b in zip(unpack(first, *shape), unpack(second, *shape))]
        packed = jnp.concatenate(parts, axis=2).reshape(-1, lanes)
        packed = lax.psum_scatter(packed, everyone, scatter_dimension=0, tiled=True).astype(F32)
        mine = [packed[a:b] for a, b in zip(ends[:-1], ends[1:])]
        cross_grads = pack_cross(image, dk, dv, g_cq, g_co).reshape(-1, width)
        cross_grads = lax.psum_scatter(cross_grads, everyone, scatter_dimension=0, tiled=True).astype(F32)
        small = pack_vectors((v_self, v_feed, v_up), (v_self2, v_feed2, v_up2), v_cross)
        small = lax.psum_scatter(small.reshape(-1, 128), everyone, scatter_dimension=0, tiled=True)
    mine[3] = lane_join(mine[3], hidden // width)
    return (
        joined.reshape(text_embed.shape),
        embed_grad.reshape(text_embed.shape),
        mine[0].T,
        mine[1].T,
        mine[2].T,
        mine[3].T,
        small[:v_rows, :v_lanes],
        cross_grads[:c_rows],
        lane_join(cross_grads[2 * c_rows :], kv_slices),
        cross_grads[c_rows : 2 * c_rows],
        small[v_rows : v_rows + x_rows, :c_rows].T,
    )


def solution(mesh):
    in_specs = (
        P(("pipe", "dp"), None, None),
        P(("pipe", "dp"), None, None),
        P(("pipe", "dp")),
        P(("pipe", "dp"), None),
        P(("pipe", "dp")),
        P(("pipe", "dp"), None),
        P("pipe", "dp"),
        P("pipe", "dp"),
        P("pipe", "dp"),
        P("pipe", "dp"),
        P("pipe", "dp"),
        P(("pipe", "dp"), None),
        P(("pipe", "dp"), None),
        P(("pipe", "dp"), None),
        P(("pipe", "dp"), None),
        P(("pipe", "dp"), None, None),
    )
    out_specs = (
        P(("pipe", "dp"), None, None),
        P(("pipe", "dp"), None, None),
        P("pipe", "dp"),
        P("pipe", "dp"),
        P("pipe", "dp"),
        P("pipe", "dp"),
        P("pipe", "dp"),
        P(("pipe", "dp"), None),
        P(("pipe", "dp"), None),
        P(("pipe", "dp"), None),
        P(("pipe", "dp"), None),
    )
    return jax.shard_map(
        on_device, mesh=mesh, in_specs=in_specs, out_specs=out_specs, check_vma=False
    )
```

```python
from functools import partial

import jax
import jax.numpy as jnp
import numpy as np
from jax import lax
from jax.experimental import pallas as pl
from jax.experimental.pallas import tpu as pltpu
from jax.sharding import PartitionSpec as P

HEADS = 12
NORM_EPS = 1e-12
MASKED = -1e30
BF = jnp.bfloat16
F32 = jnp.float32
NT = (((1,), (1,)), ((), ()))
NN = (((1,), (0,)), ((), ()))
TN = (((0,), (0,)), ((), ()))
VMEM_BYTES = 58 * 2**20
TILE = 768
CHUNK = 128
SMALL = 16


def dot(a, b, dims=NN):
    return lax.dot_general(a, b, dims, preferred_element_type=F32)


def span(start, size, unit=128):
    return pl.ds(pl.multiple_of(start, unit), size)


def tiles(count, body):
    def step(i, carry):
        body(i)
        return carry

    lax.fori_loop(0, count, step, 0)


class Copies:
    def __init__(self, sems):
        self.sems, self.used = sems, 0
        self.coming, self.going, self.sent = [], [], []

    def copy(self, source, target):
        self.used += 1
        copy = pltpu.make_async_copy(source, target, self.sems.at[self.used - 1])
        copy.start()
        return copy

    def begin(self, *refs):
        for k, (held, source, _) in enumerate(self.coming):
            if any(held is ref for ref in refs):
                self.coming[k] = (held, source, self.copy(source, held))

    def need(self, *refs):
        for k, (held, source, copy) in enumerate(self.coming):
            if any(held is ref for ref in refs):
                copy.wait()
                self.coming[k] = (None, source, None)

    def send(self, *refs, part=()):
        for held, target in self.going:
            if any(held is ref for ref in refs):
                self.sent.append(self.copy(held.at[part], target.at[part]) if part else self.copy(held, target))

    def finish(self):
        settle(self.sent)


def fetch(copies, sems, here=None):
    started = []
    for k in range(len(copies[0][0])):
        started.append([pltpu.make_async_copy(s[k], t, sems.at[i]) for i, (s, t) in enumerate(copies)])

    def start(group):
        for copy in group:
            copy.start()

    if len(started) == 1:
        start(started[0])
    else:
        pl.when(here)(lambda: start(started[0]))
        pl.when(jnp.logical_not(here))(lambda: start(started[1]))
    return started[0]


def settle(started):
    for copy in started:
        copy.wait()


def placed(refs, where_ref, layout, target, lanes):
    if len(refs) == 1:
        return [(refs, target)]
    core, z, y = where_ref[0], where_ref[1], where_ref[2]
    copies = []
    for i, pair in enumerate(zip(refs[:16], refs[16:])):
        c_rel, y_rel, z_rel = i // 8, (i // 4) % 2, i % 4
        block = lax.rem(z - z_rel + 4, 4) * 2 + lax.rem(y + y_rel, 2)
        side = lax.rem(core + c_rel, 2)
        for first, rows, shift in layout:
            place = target.at[
                span(block * rows, rows, 16),
                span(side * lanes + shift * pair[0].shape[1], pair[0].shape[1]),
            ]
            copies.append(([ref.at[pl.ds(first, rows)] for ref in pair], place))
    return copies


def relative(where_ref, block):
    z = lax.rem(block // 2 - where_ref[1] + 4, 4)
    return z * 2 + lax.rem(block % 2 + where_ref[2], 2)


def norm_rows(x_ref, bias, gain, offset, y_ref, low_ref, n_ref, r_ref):
    for i in range(0, y_ref.shape[0], CHUNK):
        rows = pl.ds(i, CHUNK)
        u = x_ref[rows, :].astype(F32) + (y_ref[rows, :] + bias)
        center = u - jnp.mean(u, axis=-1, keepdims=True)
        scale = lax.rsqrt(jnp.mean(center * center, axis=-1, keepdims=True) + NORM_EPS)
        normed = center * scale
        y = normed * gain + offset
        y_ref[rows, :] = y
        low_ref[rows, :] = y.astype(BF)
        n_ref[rows, :] = normed.astype(BF)
        r_ref[rows, :] = scale


def norm_rows_back(dy_ref, n_ref, r_ref, gain, du_ref, db_ref):
    def chunk(i, sums):
        rows = span(i * CHUNK, CHUNK, CHUNK)
        dy = dy_ref[rows, :].astype(F32)
        n = n_ref[rows, :].astype(F32)
        s = dy * gain
        du = r_ref[rows, :] * (
            s - jnp.mean(s, axis=-1, keepdims=True) - n * jnp.mean(s * n, axis=-1, keepdims=True)
        )
        db = du.astype(BF)
        du_ref[rows, :] = du
        db_ref[rows, :] = db
        terms = (dy * n, dy, db.astype(F32))
        return tuple(a + jnp.sum(t, axis=0, keepdims=True) for a, t in zip(sums, terms))

    zero = jnp.zeros((1, dy_ref.shape[1]), F32)
    return lax.fori_loop(0, dy_ref.shape[0] // CHUNK, chunk, (zero, zero, zero))


def split_heads(a):
    first = lax.broadcasted_iota(jnp.int32, a.shape, 1) < a.shape[1] // 2
    zero = jnp.zeros_like(a)
    return jnp.concatenate([jnp.where(first, a, zero), jnp.where(first, zero, a)], axis=0)


def join_heads(a):
    rows = a.shape[0] // 2
    first = lax.broadcasted_iota(jnp.int32, (rows, a.shape[1]), 1) < a.shape[1] // 2
    return jnp.where(first, a[:rows], a[rows:])


def softmax(scores, mask, axis):
    scores = scores + mask
    e = jnp.exp(scores - jnp.max(scores, axis=axis, keepdims=True))
    return (e * (1.0 / jnp.sum(e, axis=axis, keepdims=True))).astype(BF)


def score_back(weights, d_weights):
    a = weights.astype(F32)
    t = a * d_weights
    return (t - a * jnp.sum(t, axis=0, keepdims=True)).astype(BF)


def project_and_norm(x_ref, o_ref, w_ref, dims, bias, gain, offset, outs):
    y_ref, low_ref, n_ref, r_ref = outs
    width = y_ref.shape[1]

    def tile(j):
        cols = span(j * TILE, TILE)
        w = w_ref[cols, :] if dims is NT else w_ref[:, cols]
        y_ref[:, cols] = dot(o_ref[...], w, dims)

    tiles(width // TILE, tile)
    norm_rows(x_ref, bias, gain, offset, y_ref, low_ref, n_ref, r_ref)


def self_weights(count, layer, where_ref, refs, qkv, out, sems, sems2):
    width, whole = out.shape[1], count == 2
    n, m = qkv.shape[0] // 8, out.shape[0] // 8
    here = where_ref[3] == layer
    return (
        lambda: fetch(placed(refs[:1] if whole else refs, where_ref, [(0, n, 0)], qkv, width // 2), sems, here),
        lambda: fetch(placed(refs[1:] if whole else refs, where_ref, [(n, m, 0)], out, width // 2), sems2, here),
    )


def self_project(x_ref, vec_ref, p_ref, qkv, bias_ref):
    width = x_ref.shape[1]
    bias_ref[:, :width] = vec_ref[0:1, :]
    bias_ref[:, width : 2 * width] = jnp.zeros((1, width), F32)
    bias_ref[:, 2 * width :] = vec_ref[1:2, :]

    def tile(j):
        cols = span(j * TILE, TILE)
        p_ref[:, cols] = (dot(x_ref[...], qkv[cols, :], NT) + bias_ref[:, cols]).astype(BF)

    tiles(3 * width // TILE, tile)


def self_attend(lengths, p_ref, a_ref, o_ref):
    width = o_ref.shape[1]
    pairs = width // 128
    key = lax.broadcasted_iota(jnp.int32, (128, 256), 0)
    query = lax.broadcasted_iota(jnp.int32, (128, 256), 1)
    same = ((query // 64) % 2) == (key // 64)

    def attend(s):
        rows = span(s * 128, 128)
        length = jnp.where(key < 64, lengths[2 * s], lengths[2 * s + 1])
        mask = jnp.where(same & (lax.rem(key, 64) < length), 0.0, MASKED)
        for h in range(pairs):
            q = p_ref[rows, pl.ds(h * 128, 128)]
            k = p_ref[rows, pl.ds(width + h * 128, 128)]
            v = p_ref[rows, pl.ds(2 * width + h * 128, 128)]
            a = softmax(dot(k, split_heads(q * 0.125), NT), mask, 0)
            a_ref[s * pairs + h] = a
            o_ref[rows, pl.ds(h * 128, 128)] = join_heads(dot(a, v, TN)).astype(BF)

    tiles(o_ref.shape[0] // 128, attend)


def self_backward_kernel(count, layer, io, ins, outs, scratch):
    where_ref, dy_ref, x_ref, vec_ref, p_ref, a_ref, o_ref, n_ref, r_ref, *refs = ins
    dx_ref, own_ref, other_ref, gv_ref = outs
    qkv, out, du_ref, db_ref, dmix_ref, dp_ref, rel_ref, g_ref, sems, sems2 = scratch
    width = x_ref.shape[1]
    half = width // 2
    n, m = qkv.shape[0] // 8, out.shape[0] // 8
    whole = count == 2
    here = where_ref[3] == layer
    second = fetch(placed(refs[1:] if whole else refs, where_ref, [(n, m, 0)], out, half), sems2, here)
    io.begin(o_ref, p_ref, a_ref)
    core = where_ref[0]
    g_gain, g_offset, g_bias = norm_rows_back(dy_ref, n_ref, r_ref, vec_ref[3:4, :], du_ref, db_ref)
    settle(second)

    def mix(j):
        cols = span(j * TILE, TILE)
        dmix_ref[:, cols] = dot(db_ref[...], out[:, cols]).astype(BF)

    tiles(width // TILE, mix)
    io.need(o_ref, p_ref, a_ref)
    rel_ref[:, :half] = o_ref[:, span(core * half, half)]
    rel_ref[:, half:] = o_ref[:, span((1 - core) * half, half)]

    g_ref[:width, :] = dot(db_ref[...], rel_ref[...], TN).astype(BF)
    for b in range(8):
        to, at = relative(where_ref, b), pl.ds(b * m, m)
        own_ref[to, n : n + m, :] = g_ref[at, :half]
        other_ref[to, n : n + m, :] = g_ref[at, half:]
    io.begin(x_ref)
    first = fetch(placed(refs[:1] if whole else refs, where_ref, [(0, n, 0)], qkv, half), sems, here)
    pairs = width // 128

    def attend(s):
        rows = span(s * 128, 128)
        for h in range(pairs):
            q2 = split_heads(p_ref[rows, pl.ds(h * 128, 128)])
            k = p_ref[rows, pl.ds(width + h * 128, 128)]
            v = p_ref[rows, pl.ds(2 * width + h * 128, 128)]
            do2 = split_heads(dmix_ref[rows, pl.ds(h * 128, 128)])
            a = a_ref[s * pairs + h]
            ds = score_back(a, dot(v, do2, NT))
            dp_ref[rows, pl.ds(h * 128, 128)] = (join_heads(dot(ds, k, TN)) * 0.125).astype(BF)
            dp_ref[rows, pl.ds(width + h * 128, 128)] = (dot(ds, q2) * 0.125).astype(BF)
            dp_ref[rows, pl.ds(2 * width + h * 128, 128)] = dot(a, do2).astype(BF)

    tiles(x_ref.shape[0] // 128, attend)
    io.need(x_ref)
    rel_ref[:, :half] = x_ref[:, span(core * half, half)]
    rel_ref[:, half:] = x_ref[:, span((1 - core) * half, half)]

    def qkv_grad(j):
        rows = span(j * TILE, TILE)
        g_ref[rows, :] = dot(dp_ref[:, rows], rel_ref[...], TN).astype(BF)

    tiles(3 * width // TILE, qkv_grad)
    for b in range(8):
        to, at = relative(where_ref, b), pl.ds(b * n, n)
        own_ref[to, :n, :] = g_ref[at, :half]
        other_ref[to, :n, :] = g_ref[at, half:]
    io.send(other_ref, own_ref, part=(slice(None), pl.ds(0, n + m)))
    settle(first)

    def back(j):
        cols = span(j * TILE, TILE)
        dx_ref[:, cols] = (du_ref[:, cols] + dot(dp_ref[...], qkv[:, cols])).astype(dx_ref.dtype)

    tiles(width // TILE, back)
    gv_ref[0:1, :] = jnp.sum(dp_ref[:, :width].astype(F32), axis=0, keepdims=True)
    gv_ref[1:2, :] = jnp.sum(dp_ref[:, 2 * width :].astype(F32), axis=0, keepdims=True)
    gv_ref[2:3, :] = g_bias
    gv_ref[3:4, :] = g_gain
    gv_ref[4:5, :] = g_offset


def cross_attend(keep_ref, q_ref, k_ref, v_ref, a_ref, o_ref):
    width = o_ref.shape[1]
    patches = k_ref.shape[0] // keep_ref.shape[0]
    pairs = width // 128

    def attend(s):
        rows, keys = span(s * 64, 64, 64), span(s * patches, patches, 16)
        mask = jnp.where(keep_ref[pl.ds(s, 1), :] > 0, 0.0, MASKED)
        for h in range(pairs):
            q = q_ref[rows, pl.ds(h * 128, 128)]
            k = k_ref[keys, pl.ds(h * 128, 128)]
            v = v_ref[keys, pl.ds(h * 128, 128)]
            a = softmax(dot(split_heads(q * 0.125), k, NT), mask, 1)
            a_ref[s * pairs + h] = a.T
            o_ref[rows, pl.ds(h * 128, 128)] = join_heads(dot(a, v)).astype(BF)

    tiles(keep_ref.shape[0], attend)


def cross_backward_kernel(io, ins, outs, scratch):
    dy_ref, low_x_ref, k_ref, v_ref, vec_ref, wq_ref, wo_ref, q_ref, a_ref, o_ref, n_ref, r_ref = ins
    dx_ref, dk_ref, dv_ref, gq_ref, go_ref, gv_ref = outs
    db_ref, dmix_ref, dq_ref = scratch
    width = low_x_ref.shape[1]
    patches = a_ref.shape[1]
    io.begin(wo_ref, o_ref)
    g_gain, g_offset, g_bias = norm_rows_back(dy_ref, n_ref, r_ref, vec_ref[3:4, :], dx_ref, db_ref)

    io.begin(q_ref, k_ref, v_ref, a_ref)
    io.need(wo_ref, o_ref)

    def mix(j):
        cols = span(j * TILE, TILE)
        dmix_ref[:, cols] = dot(db_ref[...], wo_ref[cols, :], NT).astype(BF)
        go_ref[cols, :] = dot(o_ref[:, cols], db_ref[...], TN).astype(BF)

    tiles(width // TILE, mix)
    io.send(go_ref)
    io.need(q_ref, k_ref, v_ref, a_ref)
    io.begin(wq_ref, low_x_ref)
    pairs = width // 128

    def attend(s):
        rows, keys = span(s * 64, 64, 64), span(s * patches, patches, 16)
        for h in range(pairs):
            q2 = split_heads(q_ref[rows, pl.ds(h * 128, 128)])
            k = k_ref[keys, pl.ds(h * 128, 128)]
            v = v_ref[keys, pl.ds(h * 128, 128)]
            do2 = split_heads(dmix_ref[rows, pl.ds(h * 128, 128)])
            a = a_ref[s * pairs + h]
            ds = score_back(a, dot(v, do2, NT))
            dq_ref[rows, pl.ds(h * 128, 128)] = (join_heads(dot(ds, k, TN)) * 0.125).astype(BF)
            dk_ref[keys, pl.ds(h * 128, 128)] = (dot(ds, q2) * 0.125).astype(BF)
            dv_ref[keys, pl.ds(h * 128, 128)] = dot(a, do2).astype(BF)

    tiles(a_ref.shape[0] // pairs, attend)
    io.send(dk_ref, dv_ref)
    io.need(wq_ref, low_x_ref)

    def back(j):
        cols = span(j * TILE, TILE)
        dx_ref[:, cols] += dot(dq_ref[...], wq_ref[cols, :], NT)
        gq_ref[cols, :] = dot(low_x_ref[:, cols], dq_ref[...], TN).astype(BF)

    tiles(width // TILE, back)
    gv_ref[0:1, :] = jnp.sum(dq_ref[...].astype(F32), axis=0, keepdims=True)
    gv_ref[1:2, :] = jnp.sum(dv_ref[...].astype(F32), axis=0, keepdims=True)
    gv_ref[2:3, :] = g_bias
    gv_ref[3:4, :] = g_gain
    gv_ref[4:5, :] = g_offset


def gelu_parts(h):
    size = jnp.abs(h) * 0.7071067811865476
    t = 1.0 / (1.0 + 0.3275911 * size)
    e = jnp.exp(-size * size)
    poly = t * (0.254829592 + t * (-0.284496736 + t * (1.421413741 + t * (-1.453152027 + t * 1.061405429))))
    tail = 0.5 * poly * e
    cdf = jnp.where(h < 0, tail, 1.0 - tail)
    return h * cdf, cdf + h * (e * 0.3989422804014327)


def feed_weights(count, layer, where_ref, refs, up, down, sems, sems2):
    width, hidden = up.shape[1], up.shape[0]
    n, m, whole = hidden // 8, width // 8, count == 2
    base = 4 * m
    slices = [(base + n + m * i, m, i) for i in range(hidden // width)]
    here = where_ref[3] == layer
    return (
        lambda: fetch(placed(refs[:1] if whole else refs, where_ref, [(base, n, 0)], up, width // 2), sems, here),
        lambda: fetch(placed(refs[1:] if whole else refs, where_ref, slices, down, hidden // 2), sems2, here),
    )


def feed_activate(low_x_ref, up, bias_ref, act_ref, slope_ref):
    def tile(j):
        cols = span(j * TILE, TILE)
        h = dot(low_x_ref[...], up[cols, :], NT) + bias_ref[:, cols]
        act, slope = gelu_parts(h)
        act_ref[:, cols] = act.astype(BF)
        slope_ref[:, cols] = slope.astype(BF)

    tiles(up.shape[0] // TILE, tile)


def text_forward_kernel(count, io, ins, outs, scratch):
    lengths, where_ref, x_ref, vec_ref, vec2_ref, up_bias_ref, *refs = ins
    p1, a1, o1, low1, n1, act, slope, low2, n2, p2, a2, o2, r1, r2, y3, low3, n3, r3 = outs
    qkv, out, up, down, y1, y2, bias_ref, *sems = scratch
    whole = count == 6
    count = 2 if whole else count
    get_qkv, get_out = self_weights(count, 0, where_ref, refs[:2] if whole else refs, qkv, out, *sems[:2])
    get_up, get_down = feed_weights(count, 0, where_ref, refs[2:4] if whole else refs, up, down, *sems[2:])
    get_qkv2, get_out2 = self_weights(count, 1, where_ref, refs[4:] if whole else refs, qkv, out, *sems[:2])
    settle(get_qkv())
    coming = get_out()
    self_project(x_ref, vec_ref, p1, qkv, bias_ref)
    io.send(p1)
    coming_up = get_up()
    self_attend(lengths, p1, a1, o1)
    io.send(a1, o1)
    settle(coming)
    norm = vec_ref[2:3, :], vec_ref[3:4, :], vec_ref[4:5, :]
    project_and_norm(x_ref, o1, out, NT, *norm, (y1, low1, n1, r1))
    io.send(low1, n1)
    coming_down = get_down()
    settle(coming_up)
    coming = get_qkv2()
    feed_activate(low1, up, up_bias_ref, act, slope)
    io.send(act, slope)
    settle(coming_down)
    coming_out = get_out2()
    norm = vec_ref[5:6, :], vec_ref[6:7, :], vec_ref[7:8, :]
    project_and_norm(y1, act, down, NT, *norm, (y2, low2, n2, r2))
    io.send(low2, n2)
    settle(coming)
    self_project(low2, vec2_ref, p2, qkv, bias_ref)
    io.send(p2)
    self_attend(lengths, p2, a2, o2)
    io.send(a2, o2)
    settle(coming_out)
    norm = vec2_ref[2:3, :], vec2_ref[3:4, :], vec2_ref[4:5, :]
    project_and_norm(low2, o2, out, NT, *norm, (y3, low3, n3, r3))


def feed_backward_body(
    io, where_ref, dy_ref, low_x_ref, vec_ref, act_ref, slope_ref, n_ref, r_ref, outs, work, up, down, get_up, get_down
):
    dx_ref, own_ref, other_ref, gv_ref = outs
    db_ref, dbt_ref, dh_ref, rel_ref, gb_ref = work
    width, hidden = up.shape[1], up.shape[0]
    n, m, half = hidden // 8, width // 8, width // 2
    core = where_ref[0]
    second = get_down()
    io.begin(slope_ref)
    g_gain, g_offset, g_bias = norm_rows_back(dy_ref, n_ref, r_ref, vec_ref[6:7, :], dx_ref, db_ref)
    dbt_ref[...] = db_ref[...].T
    settle(second)
    io.need(slope_ref)
    io.begin(act_ref, low_x_ref)

    def down_tile(j):
        cols = span(j * TILE, TILE)
        dh = (dot(db_ref[...], down[:, cols]) * slope_ref[:, cols].astype(F32)).astype(BF)
        dh_ref[:, cols] = dh
        gb_ref[:, cols] = jnp.sum(dh.astype(F32), axis=0, keepdims=True)

    tiles(hidden // TILE, down_tile)
    io.need(act_ref)

    def down_grad(j):
        for ref, side in ((own_ref, core), (other_ref, 1 - core)):
            g = dot(dbt_ref[...], act_ref[:, span(side * (hidden // 2) + j * width, width)]).astype(BF)
            for b in range(8):
                to = relative(where_ref, b)
                for k in range(2):
                    ref[to, span(n + (2 * j + k) * m, m, 16), :] = g[b * m : (b + 1) * m, k * half : (k + 1) * half]

    tiles(hidden // 2 // width, down_grad)
    io.send(other_ref, own_ref, part=(slice(None), pl.ds(n, n)))
    first = get_up()
    io.need(low_x_ref)
    rel_ref[:, :half] = low_x_ref[:, span(core * half, half)]
    rel_ref[:, half:] = low_x_ref[:, span((1 - core) * half, half)]

    def up_grad(j):
        g = dot(dh_ref[:, span(j * 2 * n, 2 * n)], rel_ref[...], TN).astype(BF)
        for k in range(2):
            to = relative(where_ref, 2 * j + k)
            own_ref[to, :n, :] = g[k * n : (k + 1) * n, :half]
            other_ref[to, :n, :] = g[k * n : (k + 1) * n, half:]

    tiles(4, up_grad)
    io.send(other_ref, own_ref, part=(slice(None), pl.ds(0, n)))
    settle(first)

    def back(j):
        cols = span(j * TILE, TILE)
        dx_ref[:, cols] += dot(dh_ref[...], up[:, cols])

    tiles(width // TILE, back)
    gv_ref[0:1, :] = g_bias
    gv_ref[1:2, :] = g_gain
    gv_ref[2:3, :] = g_offset
    for j in range(hidden // width):
        gv_ref[3 + j : 4 + j, :] = gb_ref[:, j * width : (j + 1) * width]


def feed_backward_kernel(count, layer, io, ins, outs, scratch):
    where_ref, dy_ref, low_x_ref, vec_ref, act_ref, slope_ref, n_ref, r_ref, *refs = ins
    up, down, *work, sems, sems2 = scratch
    get = feed_weights(count, layer, where_ref, refs, up, down, sems, sems2)
    feed_backward_body(
        io, where_ref, dy_ref, low_x_ref, vec_ref, act_ref, slope_ref, n_ref, r_ref, outs, work, up, down, *get
    )


def joining_kernel(count, io, ins, outs, scratch):
    where_ref, x_ref, low_x_ref, keep_ref, k_ref, v_ref, cross_ref, wq_ref, wo_ref, vec_ref, bias_ref, dy_ref, *refs = ins
    q_ref, a_ref, o_ref, cross_n, cross_r, y_ref, *grads = outs
    up, down, *work, act_ref, slope_ref, state, low_state, low_ref, n_ref, r_ref, sems, sems2 = scratch
    get_up, get_down = feed_weights(count, 1, where_ref, refs, up, down, sems, sems2)
    width = x_ref.shape[1]
    io.begin(k_ref, v_ref)

    def tile(j):
        cols = span(j * TILE, TILE)
        q_ref[:, cols] = (dot(low_x_ref[...], wq_ref[:, cols]) + cross_ref[0:1, cols]).astype(BF)

    tiles(width // TILE, tile)
    io.need(k_ref, v_ref)
    io.begin(x_ref, wo_ref)
    first = get_up()
    cross_attend(keep_ref, q_ref, k_ref, v_ref, a_ref, o_ref)
    io.send(q_ref, a_ref, o_ref)
    io.need(x_ref, wo_ref)
    norm = cross_ref[2:3, :], cross_ref[3:4, :], cross_ref[4:5, :]
    project_and_norm(x_ref, o_ref, wo_ref, NN, *norm, (state, low_state, cross_n, cross_r))
    io.send(cross_n)
    second = get_down()
    settle(first)
    feed_activate(low_state, up, bias_ref, act_ref, slope_ref)
    settle(second)
    norm = vec_ref[5:6, :], vec_ref[6:7, :], vec_ref[7:8, :]
    project_and_norm(state, act_ref, down, NT, *norm, (y_ref, low_ref, n_ref, r_ref))
    io.send(y_ref)
    feed_backward_body(
        io, where_ref, dy_ref, low_state, vec_ref, act_ref, slope_ref, n_ref, r_ref, grads, work, up, down, list, list
    )


def vector_kernel(first, v_rows, v_lanes, x_rows, c_rows, *refs):
    where_ref, *pieces = refs[:33]
    vec_refs, bias_refs, cross_ref = refs[33:35], refs[35:37], refs[37]
    held, sems = refs[38:]
    core, z, y, x = where_ref[0], where_ref[1], where_ref[2], where_ref[3]
    copies = []
    for i, ref in enumerate(pieces):
        x_rel, c_rel, y_rel, z_rel = i // 16, (i // 8) % 2, (i // 4) % 2, i % 4
        pipe = lax.rem(x + x_rel, 2) * 2 + lax.rem(core + c_rel, 2)
        device = pipe * 8 + lax.rem(z - z_rel + 4, 4) * 2 + lax.rem(y + y_rel, 2)
        copies.append(([ref.at[pl.ds(first, 16), pl.ds(0, 128)]], held.at[device]))
    settle(fetch(copies, sems))
    for device in range(32):
        block = held[device].astype(F32)
        pipe, dp = device // 8, device % 8
        rows = pl.ds(pipe % 2 * v_rows, v_rows)
        vec_refs[pipe // 2][rows, pl.ds(dp * v_lanes, v_lanes)] = block[:v_rows, :v_lanes]
        cross_ref[0:x_rows, pl.ds(device * c_rows, c_rows)] = block[v_rows : v_rows + x_rows, :c_rows]
    width = cross_ref.shape[1]
    for vec_ref, bias_ref in zip(vec_refs, bias_refs):
        for j in range(4):
            bias_ref[:, j * width : (j + 1) * width] = vec_ref[8 + j : 9 + j, :]


def struct(*shape, dtype=F32):
    return jax.ShapeDtypeStruct(shape, dtype)


VMEM = pl.BlockSpec(memory_space=pltpu.VMEM)
SMEM = pl.BlockSpec(memory_space=pltpu.SMEM)
ANYWHERE = pl.BlockSpec(memory_space=pl.ANY)


def call(kernel, outs, specs, scratch, us, args, late=(), early=(), packs=(), layer=0, onto=None):
    n_in, n_out, n_scratch = len(args), len(outs), len(scratch)
    early = (*early, *packs)
    held = [pltpu.VMEM(args[i].shape, args[i].dtype) for i in late]
    held += [pltpu.VMEM(outs[i].shape, outs[i].dtype) for i in early]
    outs = [struct(2, *o.shape, dtype=o.dtype) if i in packs else o for i, o in enumerate(outs)]
    taken = tuple(onto) if onto else ()
    n_all = n_in + len(taken)

    def body(*refs):
        ins, out, rest = list(refs[:n_in]), list(refs[n_all : n_all + n_out]), refs[n_all + n_out :]
        buffers = rest[n_scratch:-1]
        io = Copies(rest[-1])
        for k, i in enumerate(late):
            io.coming.append((buffers[k], ins[i], None))
            ins[i] = buffers[k]
        for k, i in enumerate(early, len(late)):
            target = out[i].at[lax.rem(ins[0][3] + layer, 2)] if i in packs else out[i]
            io.going.append((buffers[k], target))
            out[i] = buffers[k]
        kernel(io, ins, out, rest[:n_scratch])
        io.finish()

    specs = [ANYWHERE if i in late else spec for i, spec in enumerate(specs)] + [ANYWHERE] * len(taken)
    return pl.pallas_call(
        body,
        out_shape=outs,
        in_specs=specs,
        out_specs=[ANYWHERE if i in early else VMEM for i in range(n_out)],
        scratch_shapes=[*scratch, *held, pltpu.SemaphoreType.DMA((24,))],
        input_output_aliases={n_in + k: i for k, i in enumerate(packs)} if taken else {},
        cost_estimate=pl.CostEstimate(flops=int(us * 1.1e9), bytes_accessed=int(us * 3.5e6), transcendentals=0),
        compiler_params=pltpu.CompilerParams(vmem_limit_bytes=VMEM_BYTES),
    )(*args, *taken)


def gathered_vectors(pieces, where, first, v_rows, v_lanes, x_rows, c_rows):
    width = 8 * v_lanes
    return pl.pallas_call(
        partial(vector_kernel, first, v_rows, v_lanes, x_rows, c_rows),
        out_shape=[struct(12, width)] * 2 + [struct(1, 4 * width)] * 2 + [struct(8, width)],
        in_specs=[SMEM] + [ANYWHERE] * len(pieces),
        out_specs=[VMEM] * 5,
        scratch_shapes=[pltpu.VMEM((32, 16, 128), BF), pltpu.SemaphoreType.DMA((32,))],
        cost_estimate=pl.CostEstimate(flops=0, bytes_accessed=10**7, transcendentals=0),
    )(where, *pieces)


def copy_sems(count, parts=1):
    return pltpu.SemaphoreType.DMA((16 * parts if count > 2 else 1,))


def text_forward(x, lengths, where, vecs, bias, weights):
    rows, width = x.shape
    hidden = bias.shape[1]
    blocks = rows // 128 * (width // 128)
    count = len(weights)
    low = struct(rows, width, dtype=BF)
    attention = [struct(rows, 3 * width, dtype=BF), struct(blocks, 128, 256, dtype=BF), low]
    outs = [
        *attention,
        low,
        low,
        struct(rows, hidden, dtype=BF),
        struct(rows, hidden, dtype=BF),
        low,
        low,
        *attention,
        struct(rows, 1),
        struct(rows, 1),
        struct(rows, width),
        low,
        low,
        struct(rows, 1),
    ]
    scratch = [
        pltpu.VMEM((3 * width, width), BF),
        pltpu.VMEM((width, width), BF),
        pltpu.VMEM((hidden, width), BF),
        pltpu.VMEM((width, hidden), BF),
        pltpu.VMEM((rows, width), F32),
        pltpu.VMEM((rows, width), F32),
        pltpu.VMEM((1, 3 * width), F32),
        copy_sems(count),
        copy_sems(count),
        copy_sems(count),
        copy_sems(count, hidden // width),
    ]
    p1, a1, o1, low1, n1, act, slope, low2, n2, p2, a2, o2, r1, r2, y3, low3, n3, r3 = call(
        partial(text_forward_kernel, count),
        outs,
        [SMEM, SMEM] + [VMEM] * 4 + [ANYWHERE] * count,
        scratch,
        38,
        (lengths, where, x, *vecs, bias, *weights),
        early=tuple(range(12)),
    )
    return y3, low3, (x, p1, a1, o1, n1, r1), (low1, act, slope, n2, r2), (low2, p2, a2, o2, n3, r3)


def self_backward(dy, saved, where, vec, weights, layer, dtype=F32, onto=None):
    x, p, a, o, n, r = saved
    rows, width = x.shape
    half = width // 2
    count = len(weights)
    outs = [
        struct(rows, width, dtype=dtype),
        struct(8, width // 2 + SMALL, half, dtype=BF),
        struct(8, width // 2 + SMALL, half, dtype=BF),
        struct(8, width),
    ]
    scratch = [
        pltpu.VMEM((3 * width, width), BF),
        pltpu.VMEM((width, width), BF),
        pltpu.VMEM((rows, width), F32),
        pltpu.VMEM((rows, width), BF),
        pltpu.VMEM((rows, width), BF),
        pltpu.VMEM((rows, 3 * width), BF),
        pltpu.VMEM((rows, width), BF),
        pltpu.VMEM((3 * width, width), BF),
        copy_sems(count),
        copy_sems(count),
    ]
    return call(
        partial(self_backward_kernel, count, layer),
        outs,
        [SMEM] + [VMEM] * 8 + [ANYWHERE] * count,
        scratch,
        22,
        (where, dy, x, vec, p, a, o, n, r, *weights),
        late=(6, 4, 5, 2),
        packs=(1, 2),
        layer=layer,
        onto=onto,
    )


def cross_backward(dy, saved, vec, wq, wo):
    low_x, k, v, q, a, o, n, r = saved
    rows, width = low_x.shape
    outs = [
        struct(rows, width),
        struct(*k.shape, dtype=BF),
        struct(*k.shape, dtype=BF),
        struct(width, width, dtype=BF),
        struct(width, width, dtype=BF),
        struct(8, width),
    ]
    scratch = [pltpu.VMEM((rows, width), BF)] * 3
    return call(
        cross_backward_kernel,
        outs,
        [VMEM] * 12,
        scratch,
        26,
        (dy, low_x, k, v, vec, wq, wo, q, a, o, n, r),
        late=(6, 9, 7, 2, 3, 8, 5, 1),
        early=(1, 2, 4),
    )


def feed_backward(dy, saved, where, vec, weights, layer, onto=None):
    low_x, act, slope, n, r = saved
    rows, width = low_x.shape
    hidden = act.shape[1]
    count = len(weights)
    outs = [
        struct(rows, width),
        struct(8, 2 * hidden // 8, width // 2, dtype=BF),
        struct(8, 2 * hidden // 8, width // 2, dtype=BF),
        struct(8, width),
    ]
    scratch = [
        pltpu.VMEM((hidden, width), BF),
        pltpu.VMEM((width, hidden), BF),
        pltpu.VMEM((rows, width), BF),
        pltpu.VMEM((width, rows), BF),
        pltpu.VMEM((rows, hidden), BF),
        pltpu.VMEM((rows, width), BF),
        pltpu.VMEM((1, hidden), F32),
        copy_sems(count),
        copy_sems(count, hidden // width),
    ]
    return call(
        partial(feed_backward_kernel, count, layer),
        outs,
        [SMEM] + [VMEM] * 7 + [ANYWHERE] * count,
        scratch,
        22,
        (where, dy, low_x, vec, act, slope, n, r, *weights),
        late=(5, 4, 2),
        packs=(1, 2),
        layer=layer,
        onto=onto,
    )


def joining(x, low_x, where, keep, k, v, cross_vec, wq, wo, vec, bias, dy, weights):
    rows, width = x.shape
    samples, patches = keep.shape
    hidden = bias.shape[1]
    count = len(weights)
    low = struct(rows, width, dtype=BF)
    pack = struct(8, 2 * hidden // 8, width // 2, dtype=BF)
    outs = [
        low,
        struct(samples * (width // 128), patches, 128, dtype=BF),
        low,
        low,
        struct(rows, 1),
        struct(rows, width),
        struct(rows, width),
        pack,
        pack,
        struct(8, width),
    ]
    scratch = [
        pltpu.VMEM((hidden, width), BF),
        pltpu.VMEM((width, hidden), BF),
        pltpu.VMEM((rows, width), BF),
        pltpu.VMEM((width, rows), BF),
        pltpu.VMEM((rows, hidden), BF),
        pltpu.VMEM((rows, width), BF),
        pltpu.VMEM((1, hidden), F32),
        pltpu.VMEM((rows, hidden), BF),
        pltpu.VMEM((rows, hidden), BF),
        pltpu.VMEM((rows, width), F32),
        pltpu.VMEM((rows, width), BF),
        pltpu.VMEM((rows, width), BF),
        pltpu.VMEM((rows, width), BF),
        pltpu.VMEM((rows, 1), F32),
        copy_sems(count),
        copy_sems(count, hidden // width),
    ]
    q, a, o, n, r, joined, dx, own, other, gv = call(
        partial(joining_kernel, count),
        outs,
        [SMEM] + [VMEM] * 11 + [ANYWHERE] * count,
        scratch,
        48,
        (where, x, low_x, keep, k, v, cross_vec, wq, wo, vec, bias, dy, *weights),
        late=(4, 5, 8, 1),
        early=(0, 1, 2, 3, 5),
        packs=(7, 8),
        layer=1,
    )
    return (low_x, k, v, q, a, o, n, r), joined, dx, own, other, gv


def lane_slices(a, lanes):
    return jnp.concatenate([a[:, i : i + lanes] for i in range(0, a.shape[1], lanes)], axis=0)


def lane_join(a, count):
    rows = a.shape[-2] // count
    return jnp.concatenate([a[..., i * rows : (i + 1) * rows, :] for i in range(count)], axis=-1)


def pad_to(a, rows, lanes):
    return jnp.pad(a, ((0, rows - a.shape[0]), (0, lanes - a.shape[1])))


def dynamic(a, index, axis):
    return lax.dynamic_index_in_dim(a, index, axis, keepdims=False)


def after(value, tokens):
    return lax.optimization_barrier((value, tokens))[0] if tokens else value


class Grid:
    def __init__(self):
        pipe, dp = lax.axis_index("pipe"), lax.axis_index("dp")
        self.x, self.core = pipe // 2, pipe % 2
        self.z, self.y = dp // 2, dp % 2
        self.arrived, self.computed, self.slack = [()] * 2, (), 1

    def swap_x(self, a):
        return lax.ppermute(a, "pipe", [(i, i ^ 2) for i in range(4)])

    def swap_core(self, a):
        return lax.ppermute(a, "pipe", [(i, i ^ 1) for i in range(4)])

    def swap_y(self, a):
        return lax.ppermute(a, "dp", [(i, i ^ 1) for i in range(8)])

    def ring_z(self, a, step=1):
        return lax.ppermute(a, "dp", [(i, (i + 2 * step) % 8) for i in range(8)])

    def by_distance(self, a):
        for axis, place in ((0, self.x), (1, self.core), (3, self.y)):
            a = jnp.where(place == 0, a, jnp.flip(a, axis))
        return lax.dynamic_slice_in_dim(jnp.concatenate([a, a], axis=2), self.z, 4, 2)

    def turn(self, *moves, pre=(), compute=None, args=(), chain=False):
        tokens = (*self.arrived[-self.slack], *self.computed)
        arrived = []

        def begin(asked):
            asked = [ask for group in asked for ask in group()]
            values = after([value for _, value, _ in asked], tokens)
            results = []
            for i, ((move, _, keep), value) in enumerate(zip(asked, values)):
                results.append(move(after(value, (results[i - 2],)) if chain and i >= 5 else value))
                keep(results[-1])
            arrived.extend(results)
            return tuple(values)

        begin(pre)
        values = begin(moves)
        self.arrived.append(tuple(arrived))
        self.computed = ()
        if compute is None:
            return None
        result = compute(*after(tuple(args), tokens + values))
        self.computed = tuple(jax.tree.leaves(result))
        return result


class Gather:
    def __init__(self, grid, piece):
        self.grid, self.here, self.swapped = grid, {(0, 0, 0): piece}, {}

    def get(self, layer, y, z, over):
        sources = {"z": (layer, y, z - 1), "y": (layer, 1 - y, z), "x": (1 - layer, y, z)}
        move = {"z": self.grid.ring_z, "y": self.grid.swap_y, "x": self.grid.swap_x}[over]
        return lambda: [(move, self.here[sources[over]], partial(self.here.__setitem__, (layer, y, z)))]

    def c(self, count=16):
        ready = [key for key in self.here if key not in self.swapped][:count]
        return [(self.grid.swap_core, self.here[key], partial(self.swapped.__setitem__, key)) for key in ready]

    def c3(self):
        return self.c(3)

    def pieces(self):
        keys = [[(layer, y, z) for y in range(2) for z in range(4)] for layer in range(2)]
        return [held[key] for half in keys for held in (self.here, self.swapped) for key in half]


class PairSum:
    def __init__(self, grid, own, other):
        self.grid, self.other = grid, other
        self.own = own.reshape((2, 4, 2) + own.shape[2:])
        self.came, self.got = None, {}

    def c(self):
        def keep(a):
            self.came = a.reshape(self.own.shape)

        return [(self.grid.swap_core, self.other, keep)]

    def block(self, own, y, z):
        layer = 0 if own else 1
        parts = [self.own[layer, z, y], self.came[layer, z, y], *self.got.get((own, y, z), [])]
        return sum(part.astype(F32) for part in parts)

    def move(self, over, own, y, z):
        to = {"z": (own, y, z - 1), "y": (own, 1 - y, z), "x": (True, y, z)}[over]
        move = {"z": self.grid.ring_z, "y": self.grid.swap_y, "x": self.grid.swap_x}[over]

        def ask():
            return [(move, self.block(own, y, z).astype(BF), self.got.setdefault(to, []).append)]

        return ask

    def steps(self):
        own, other = partial(self.move, own=True), partial(self.move, own=False)
        return [
            (other("z", y=0, z=2), other("y", y=1, z=3), other("x", y=1, z=2)),
            (other("z", y=1, z=1), own("y", y=1, z=3), other("x", y=0, z=3)),
            (own("z", y=0, z=3), own("y", y=1, z=2), other("x", y=1, z=0)),
            (own("z", y=0, z=2), own("y", y=1, z=1), other("x", y=0, z=1)),
            (own("z", y=0, z=1), own("y", y=1, z=0), other("x", y=0, z=0)),
        ]

    def total(self):
        return self.block(True, 0, 0)


class BlockSum:
    def __init__(self, grid, a, dtype):
        self.grid, self.a, self.dtype = grid, a, dtype
        self.ring = []

    def step(self, swap, place, axis):
        own = dynamic(self.a, place, axis)

        def keep(came):
            self.a = own.astype(F32) + came.astype(F32)

        return [(swap, dynamic(self.a, 1 - place, axis).astype(self.dtype), keep)]

    def c(self):
        return self.step(self.grid.swap_core, self.grid.core, 1)

    def x0(self):
        self.halves = [dynamic(self.a, place, 0) for place in (self.grid.x, 1 - self.grid.x)]
        return self.x_half(0)

    def x1(self):
        return self.x_half(1)

    def x_half(self, k):
        own, other = (h[2 * k : 2 * k + 2] for h in self.halves)

        def keep(came):
            total = own.astype(F32) + came.astype(F32)
            self.a = total if k == 0 else jnp.concatenate([self.a, total])

        return [(self.grid.swap_x, other.astype(self.dtype), keep)]

    def y(self):
        return self.step(self.grid.swap_y, self.grid.y, 1)

    def round(self):
        value = self.block(3 - len(self.ring))
        return [(self.grid.ring_z, value.astype(self.dtype), self.ring.append)]

    def block(self, step):
        value = dynamic(self.a, (self.grid.z + step) % 4, 0).astype(F32)
        return value + self.ring[-1].astype(F32) if self.ring else value

    def total(self):
        return self.block(0)


def masks(caption_len, phrase_len, box_count, patch_mask, text_rows, patches):
    slots = jnp.arange(phrase_len.shape[1], dtype=jnp.int32)
    phrase_total = jnp.sum(jnp.where(slots[None, :] < box_count[:, None], phrase_len, 0), axis=1)
    lengths = jnp.minimum(caption_len + phrase_total, text_rows)
    first_patch = (jnp.arange(patch_mask.shape[1], dtype=jnp.int32) == 0).astype(jnp.int32)
    keep = jnp.maximum(patch_mask, first_patch[None, :]).astype(F32)
    return lengths, jnp.pad(keep, ((0, 0), (0, patches - keep.shape[1])))


def on_device(
    text_embed,
    image_feats,
    caption_len,
    phrase_len,
    box_count,
    patch_mask,
    attn_qkv,
    attn_out,
    ffn_up,
    ffn_down,
    layer_vectors,
    cross_query,
    cross_kv,
    cross_out,
    cross_vectors,
    cotangent,
):
    n_pipe, n_dp = lax.axis_size("pipe"), lax.axis_size("dp")
    everyone = ("pipe", "dp")
    shards, half = n_pipe * n_dp, n_pipe // 2
    samples, text_rows, width = text_embed.shape
    hidden = ffn_up.shape[1] * n_dp
    lanes = attn_qkv.shape[0]
    patches = -(-image_feats.shape[1] // 32) * 32
    direct = (n_pipe, n_dp) == (4, 8) and lanes % 128 == 0
    lengths, patch_keep = masks(caption_len, phrase_len, box_count, patch_mask, text_rows, patches)
    x = text_embed.reshape(-1, width)

    def padded(image_feats):
        wide = jnp.pad(image_feats, ((0, 0), (0, patches - image_feats.shape[1]), (0, 0)))
        return wide.reshape(samples * patches, -1)


    c_rows = cross_query.shape[0]
    kv_slices = cross_kv.shape[1] // width
    cross_pack = jnp.concatenate([cross_query, cross_out, lane_slices(cross_kv, width)], axis=0)
    v_rows, v_lanes = layer_vectors.shape
    x_rows = cross_vectors.shape[1]
    small = jnp.concatenate([pad_to(layer_vectors, v_rows, 128), pad_to(cross_vectors.T, x_rows, 128)], axis=0)
    small = pad_to(small, 16, 128)
    pack_attn = jnp.concatenate([attn_qkv.T, attn_out.T], axis=0)
    pack_feed = jnp.concatenate([ffn_up.T, lane_slices(ffn_down.T, lanes)], axis=0)
    n_pack = pack_attn.shape[0] + pack_feed.shape[0]

    def cross_weights(blocks):
        blocks = blocks.reshape(shards, -1, width)
        i_rows = cross_kv.shape[0]
        ends = np.cumsum([0, c_rows, c_rows, i_rows, i_rows])
        return [blocks[:, a:b].reshape(-1, width) for a, b in zip(ends[:-1], ends[1:])]

    def vectors_of(blocks):
        blocks = blocks.reshape(n_pipe, n_dp, 16, 128).astype(F32)
        vecs = []
        for layer in range(2):
            v = blocks[layer * half : (layer + 1) * half, :, :v_rows, :v_lanes]
            vecs.append(jnp.moveaxis(v, 1, 2).reshape(12, width))
        cvec = blocks.reshape(shards, 16, 128)[:, v_rows : v_rows + x_rows, :c_rows]
        return vecs, [v[8:12].reshape(1, hidden) for v in vecs], jnp.moveaxis(cvec, 1, 0).reshape(x_rows, width)

    def keys_values(image, wk, wv, cvec):
        keys = jnp.dot(image, wk, preferred_element_type=F32).astype(BF)
        return keys, (jnp.dot(image, wv, preferred_element_type=F32) + cvec[1]).astype(BF)

    def pack_cross(image, dk, dv, g_cq, g_co):
        grads = [g_cq, g_co, dot(image, dk, TN).astype(BF), dot(image, dv, TN).astype(BF)]
        return jnp.concatenate([g.reshape(shards, -1, width) for g in grads], axis=1)

    def vector_block(v_self, v_feed):
        v = jnp.concatenate([v_self[:5], v_feed[:7]], axis=0)
        return jnp.moveaxis(v.reshape(half, v_rows, n_dp, v_lanes), 2, 1)

    def pack_vectors(text, joining, v_cross):
        section = jnp.concatenate([vector_block(*text), vector_block(*joining)], axis=0)
        cross = jnp.moveaxis(v_cross[:x_rows].reshape(x_rows, n_pipe, n_dp, c_rows), 0, 2)
        wide = [jnp.pad(v, ((0, 0), (0, 0), (0, 0), (0, 128 - v.shape[3]))) for v in (section, cross)]
        wide = jnp.concatenate(wide, axis=2)
        return jnp.pad(wide, ((0, 0), (0, 0), (0, 16 - wide.shape[2]), (0, 0)))

    seed = cotangent.reshape(-1, width)
    if direct:
        grid = Grid()
        turn = grid.turn
        where = jnp.stack([grid.core, grid.z, grid.y, grid.x]).astype(jnp.int32)
        gather = Gather(grid, jnp.concatenate([pack_attn, pack_feed, pad_to(small, 16, lanes)]))
        get = gather.get
        turn(get(0, 0, 1, "z"), get(0, 1, 0, "y"), get(1, 0, 0, "x"), gather.c3, chain=True)
        image = turn(
            get(0, 0, 2, "z"), get(0, 1, 1, "y"), get(1, 0, 1, "x"), gather.c3, chain=True, compute=padded, args=(image_feats,)
        )
        turn(get(0, 0, 3, "z"), get(0, 1, 2, "y"), get(1, 1, 0, "x"), gather.c3, chain=True)
        turn(get(1, 1, 1, "z"), get(0, 1, 3, "y"), get(1, 0, 3, "x"), gather.c3, chain=True)
        turn(get(1, 0, 2, "z"), get(1, 1, 3, "y"), get(1, 1, 2, "x"), gather.c3, chain=True)
        turn(gather.c)
        weights = gather.pieces()
        cross_whole = lax.all_gather(after(cross_pack, grid.arrived[-3]), everyone, axis=0, tiled=True)
        *vectors, cvec = gathered_vectors(weights, where, n_pack, v_rows, v_lanes, x_rows, c_rows)
        vecs, biases = vectors[:2], vectors[2:]
        state, low, s_self, s_feed, s_self2 = text_forward(x, lengths, where, vecs, biases[0], weights)
        wq, wo, wk, wv = cross_weights(cross_whole)
        keys, values = keys_values(image, wk, wv, cvec)
        s_cross, joined, grad, *g_feed2, v_feed2 = joining(
            state, low, where, patch_keep, keys, values, cvec, wq, wo, vecs[1], biases[1], seed, weights
        )
        grid.computed = (grad,)

        def fourth(grad):
            grad, dk, dv, g_cq, g_co, v_cross = cross_backward(grad, s_cross, cvec, wq, wo)
            return grad, v_cross, pack_cross(image, dk, dv, g_cq, g_co)

        grad, v_cross, cross_grads = fourth(grad)
        sum_cross = BlockSum(grid, cross_grads.reshape(2, 2, 4, 2, -1, width), BF)
        turn(sum_cross.c)
        grad, *g_self, v_self2 = turn(
            sum_cross.x0,
            compute=lambda grad: self_backward(grad, s_self2, where, vecs[1], weights, 1, BF), args=(grad,),
        )
        grad, *g_feed, v_feed = turn(
            sum_cross.x1,
            compute=lambda grad: feed_backward(grad, s_feed, where, vecs[0], weights, 0, g_feed2), args=(grad,),
        )
        feed = PairSum(grid, *g_feed)
        embed_grad, *g_self, v_self = turn(
            feed.c, sum_cross.y,
            compute=lambda grad: self_backward(grad, s_self, where, vecs[0], weights, 0, F32, g_self), args=(grad,),
        )
        vectors = pack_vectors((v_self, v_feed), (v_self2, v_feed2), v_cross)
        vectors = grid.by_distance(vectors.reshape(2, 2, 4, 2, SMALL, 128))
        rows = g_self[0].shape[2] - SMALL
        for k in range(2):
            small = jnp.pad(vectors[:, k].reshape(2, 8, SMALL, 128), ((0, 0), (0, 0), (0, 0), (0, lanes - 128)))
            g_self[k] = lax.dynamic_update_slice(g_self[k], small.astype(BF), (0, 0, rows, 0))
        attn = PairSum(grid, *g_self)
        f0, f1, f2, f3, f4 = feed.steps()
        a0, a1, a2, a3, a4 = attn.steps()
        turn(*f0, attn.c, sum_cross.round)
        turn(*f1)
        grid.slack = 2
        turn(*a0)
        turn(*f2)
        turn(*a1)
        turn(*f3)
        turn(*a2, sum_cross.round)
        turn(*f4)
        turn(*a3, sum_cross.round)
        turn(*a4)
        attn_grads, feed_grads = attn.total(), feed.total()
        n_qkv, n_up = attn_qkv.shape[1], ffn_up.shape[1]
        mine = [attn_grads[:n_qkv], attn_grads[n_qkv:rows], feed_grads[:n_up], feed_grads[n_up:]]
        cross_grads, small = sum_cross.total(), attn_grads[rows:, :128]
    else:
        where = jnp.zeros((4,), jnp.int32)
        image = padded(image_feats)
        vectors = lax.all_gather(small, everyone, axis=0, tiled=False)
        whole = lax.all_gather(jnp.concatenate([pack_attn, pack_feed], axis=0), everyone, axis=0, tiled=False)
        whole = whole.reshape(n_pipe, n_dp, -1, lanes)

        def section(piece, layer):
            piece = jnp.moveaxis(piece[layer * half : (layer + 1) * half], 0, 2)
            return piece.reshape(n_dp * piece.shape[1], half * piece.shape[-1])

        counts = [attn_qkv.shape[1], attn_out.shape[1], ffn_up.shape[1], attn_out.shape[1] * (hidden // width)]
        ends = np.cumsum([0] + counts)
        cut = [whole[:, :, a:b] for a, b in zip(ends[:-1], ends[1:])]
        cut[3] = lane_join(cut[3], hidden // width)
        (qkv1, out1, up1, down1), (qkv2, out2, up2, down2) = ([section(c, k) for c in cut] for k in range(2))
        vecs, biases, cvec = vectors_of(vectors)
        wq, wo, wk, wv = cross_weights(lax.all_gather(cross_pack, everyone, axis=0, tiled=False))
        state, low, s_self, s_feed, s_self2 = text_forward(
            x, lengths, where, vecs, biases[0], [qkv1, out1, up1, down1, qkv2, out2]
        )
        keys, values = keys_values(image, wk, wv, cvec)
        s_cross, joined, grad, *g_feed2, v_feed2 = joining(
            state, low, where, patch_keep, keys, values, cvec, wq, wo, vecs[1], biases[1], seed, [up2, down2]
        )
        grad, dk, dv, g_cq, g_co, v_cross = cross_backward(grad, s_cross, cvec, wq, wo)
        grad, *g_self, v_self2 = self_backward(grad, s_self2, where, vecs[1], [qkv2, out2], 1, BF)
        grad, *g_feed, v_feed = feed_backward(grad, s_feed, where, vecs[0], [up1, down1], 0, g_feed2)
        embed_grad, *g_self, v_self = self_backward(grad, s_self, where, vecs[0], [qkv1, out1], 0, F32, g_self)
        g_self1, g_self2 = ([g[k] for g in g_self] for k in range(2))
        g_feed1, g_feed2 = ([g[k] for g in g_feed] for k in range(2))

        def unpack(pair, rows, slices):
            parts = []
            at = 0
            for r, k in zip(rows, slices):
                sides = [p[:, at : at + r * k] for p in pair]
                sides = [lane_join(p, k).reshape(8 * r, -1) for p in sides]
                parts.append(jnp.concatenate(sides, axis=1))
                at += r * k
            return parts

        def split(first, second):
            both = jnp.stack([first, second])
            rows, k = both.shape[1] // n_dp, both.shape[2] // (half * lanes)
            both = both.reshape(2, n_dp, rows, half, k, lanes)
            return both.transpose(0, 3, 1, 4, 2, 5).reshape(n_pipe, n_dp, k * rows, lanes)

        attn = ((3 * width // 8, width // 8), (1, 1))
        feed = ((hidden // 8, width // 8), (1, hidden // width))
        parts = []
        for first, second, shape in ((g_self1, g_self2, attn), (g_feed1, g_feed2, feed)):
            parts += [split(a, b) for a, b in zip(unpack(first, *shape), unpack(second, *shape))]
        packed = jnp.concatenate(parts, axis=2).reshape(-1, lanes)
        packed = lax.psum_scatter(packed, everyone, scatter_dimension=0, tiled=True).astype(F32)
        mine = [packed[a:b] for a, b in zip(ends[:-1], ends[1:])]
        cross_grads = pack_cross(image, dk, dv, g_cq, g_co).reshape(-1, width)
        cross_grads = lax.psum_scatter(cross_grads, everyone, scatter_dimension=0, tiled=True).astype(F32)
        small = pack_vectors((v_self, v_feed), (v_self2, v_feed2), v_cross)
        small = lax.psum_scatter(small.reshape(-1, 128), everyone, scatter_dimension=0, tiled=True)
    mine[3] = lane_join(mine[3], hidden // width)
    return (
        joined.reshape(text_embed.shape),
        embed_grad.reshape(text_embed.shape),
        mine[0].T,
        mine[1].T,
        mine[2].T,
        mine[3].T,
        small[:v_rows, :v_lanes],
        cross_grads[:c_rows],
        lane_join(cross_grads[2 * c_rows :], kv_slices),
        cross_grads[c_rows : 2 * c_rows],
        small[v_rows : v_rows + x_rows, :c_rows].T,
    )


def solution(mesh):
    in_specs = (
        P(("pipe", "dp"), None, None),
        P(("pipe", "dp"), None, None),
        P(("pipe", "dp")),
        P(("pipe", "dp"), None),
        P(("pipe", "dp")),
        P(("pipe", "dp"), None),
        P("pipe", "dp"),
        P("pipe", "dp"),
        P("pipe", "dp"),
        P("pipe", "dp"),
        P("pipe", "dp"),
        P(("pipe", "dp"), None),
        P(("pipe", "dp"), None),
        P(("pipe", "dp"), None),
        P(("pipe", "dp"), None),
        P(("pipe", "dp"), None, None),
    )
    out_specs = (
        P(("pipe", "dp"), None, None),
        P(("pipe", "dp"), None, None),
        P("pipe", "dp"),
        P("pipe", "dp"),
        P("pipe", "dp"),
        P("pipe", "dp"),
        P("pipe", "dp"),
        P(("pipe", "dp"), None),
        P(("pipe", "dp"), None),
        P(("pipe", "dp"), None),
        P(("pipe", "dp"), None),
    )
    return jax.shard_map(
        on_device, mesh=mesh, in_specs=in_specs, out_specs=out_specs, check_vma=False
    )
```

```python
from functools import partial

import jax
import jax.numpy as jnp
import numpy as np
from jax import lax
from jax.experimental import pallas as pl
from jax.experimental.pallas import tpu as pltpu
from jax.sharding import PartitionSpec as P

HEADS = 12
NORM_EPS = 1e-12
MASKED = -1e30
BF = jnp.bfloat16
F32 = jnp.float32
NT = (((1,), (1,)), ((), ()))
NN = (((1,), (0,)), ((), ()))
TN = (((0,), (0,)), ((), ()))
VMEM_BYTES = 58 * 2**20
TILE = 768
CHUNK = 128
SMALL = 16


def dot(a, b, dims=NN):
    return lax.dot_general(a, b, dims, preferred_element_type=F32)


def span(start, size, unit=128):
    return pl.ds(pl.multiple_of(start, unit), size)


def tiles(count, body):
    def step(i, carry):
        body(i)
        return carry

    lax.fori_loop(0, count, step, 0)


class Copies:
    def __init__(self, sems):
        self.sems, self.used = sems, 0
        self.coming, self.going, self.sent = [], [], []

    def copy(self, source, target):
        self.used += 1
        copy = pltpu.make_async_copy(source, target, self.sems.at[self.used - 1])
        copy.start()
        return copy

    def begin(self, *refs):
        for k, (held, source, _) in enumerate(self.coming):
            if any(held is ref for ref in refs):
                self.coming[k] = (held, source, self.copy(source, held))

    def need(self, *refs):
        for k, (held, source, copy) in enumerate(self.coming):
            if any(held is ref for ref in refs):
                copy.wait()
                self.coming[k] = (None, source, None)

    def send(self, *refs, part=()):
        for held, target in self.going:
            if any(held is ref for ref in refs):
                self.sent.append(self.copy(held.at[part], target.at[part]) if part else self.copy(held, target))

    def finish(self):
        settle(self.sent)


def fetch(copies, sems, here=None):
    started = []
    for k in range(len(copies[0][0])):
        started.append([pltpu.make_async_copy(s[k], t, sems.at[i]) for i, (s, t) in enumerate(copies)])

    def start(group):
        for copy in group:
            copy.start()

    if len(started) == 1:
        start(started[0])
    else:
        pl.when(here)(lambda: start(started[0]))
        pl.when(jnp.logical_not(here))(lambda: start(started[1]))
    return started[0]


def settle(started):
    for copy in started:
        copy.wait()


def placed(refs, where_ref, layout, target, lanes):
    if len(refs) == 1:
        return [(refs, target)]
    core, z, y = where_ref[0], where_ref[1], where_ref[2]
    copies = []
    for i, pair in enumerate(zip(refs[:16], refs[16:])):
        c_rel, y_rel, z_rel = i // 8, (i // 4) % 2, i % 4
        block = lax.rem(z - z_rel + 4, 4) * 2 + lax.rem(y + y_rel, 2)
        side = lax.rem(core + c_rel, 2)
        for first, rows, shift in layout:
            place = target.at[
                span(block * rows, rows, 16),
                span(side * lanes + shift * pair[0].shape[1], pair[0].shape[1]),
            ]
            copies.append(([ref.at[pl.ds(first, rows)] for ref in pair], place))
    return copies


def relative(where_ref, block):
    z = lax.rem(block // 2 - where_ref[1] + 4, 4)
    return z * 2 + lax.rem(block % 2 + where_ref[2], 2)


def norm_rows(x_ref, bias, gain, offset, y_ref, low_ref, n_ref, r_ref):
    for i in range(0, y_ref.shape[0], CHUNK):
        rows = pl.ds(i, CHUNK)
        u = x_ref[rows, :].astype(F32) + (y_ref[rows, :] + bias)
        center = u - jnp.mean(u, axis=-1, keepdims=True)
        scale = lax.rsqrt(jnp.mean(center * center, axis=-1, keepdims=True) + NORM_EPS)
        normed = center * scale
        y = normed * gain + offset
        y_ref[rows, :] = y
        low_ref[rows, :] = y.astype(BF)
        n_ref[rows, :] = normed.astype(BF)
        r_ref[rows, :] = scale


def norm_rows_back(dy_ref, n_ref, r_ref, gain, du_ref, db_ref):
    def chunk(i, sums):
        rows = span(i * CHUNK, CHUNK, CHUNK)
        dy = dy_ref[rows, :].astype(F32)
        n = n_ref[rows, :].astype(F32)
        s = dy * gain
        du = r_ref[rows, :] * (
            s - jnp.mean(s, axis=-1, keepdims=True) - n * jnp.mean(s * n, axis=-1, keepdims=True)
        )
        db = du.astype(BF)
        du_ref[rows, :] = du
        db_ref[rows, :] = db
        terms = (dy * n, dy, db.astype(F32))
        return tuple(a + jnp.sum(t, axis=0, keepdims=True) for a, t in zip(sums, terms))

    zero = jnp.zeros((1, dy_ref.shape[1]), F32)
    return lax.fori_loop(0, dy_ref.shape[0] // CHUNK, chunk, (zero, zero, zero))


def split_heads(a):
    first = lax.broadcasted_iota(jnp.int32, a.shape, 1) < a.shape[1] // 2
    zero = jnp.zeros_like(a)
    return jnp.concatenate([jnp.where(first, a, zero), jnp.where(first, zero, a)], axis=0)


def join_heads(a):
    rows = a.shape[0] // 2
    first = lax.broadcasted_iota(jnp.int32, (rows, a.shape[1]), 1) < a.shape[1] // 2
    return jnp.where(first, a[:rows], a[rows:])


def softmax(scores, mask, axis):
    scores = scores + mask
    e = jnp.exp(scores - jnp.max(scores, axis=axis, keepdims=True))
    return (e * (1.0 / jnp.sum(e, axis=axis, keepdims=True))).astype(BF)


def score_back(weights, d_weights):
    a = weights.astype(F32)
    t = a * d_weights
    return (t - a * jnp.sum(t, axis=0, keepdims=True)).astype(BF)


def project_and_norm(x_ref, o_ref, w_ref, dims, bias, gain, offset, outs):
    y_ref, low_ref, n_ref, r_ref = outs
    width = y_ref.shape[1]

    def tile(j):
        cols = span(j * TILE, TILE)
        w = w_ref[cols, :] if dims is NT else w_ref[:, cols]
        y_ref[:, cols] = dot(o_ref[...], w, dims)

    tiles(width // TILE, tile)
    norm_rows(x_ref, bias, gain, offset, y_ref, low_ref, n_ref, r_ref)


def self_weights(count, layer, where_ref, refs, qkv, out, sems, sems2):
    width, whole = out.shape[1], count == 2
    n, m = qkv.shape[0] // 8, out.shape[0] // 8
    here = where_ref[3] == layer
    return (
        lambda: fetch(placed(refs[:1] if whole else refs, where_ref, [(0, n, 0)], qkv, width // 2), sems, here),
        lambda: fetch(placed(refs[1:] if whole else refs, where_ref, [(n, m, 0)], out, width // 2), sems2, here),
    )


def self_project(x_ref, vec_ref, p_ref, qkv, bias_ref):
    width = x_ref.shape[1]
    bias_ref[:, :width] = vec_ref[0:1, :]
    bias_ref[:, width : 2 * width] = jnp.zeros((1, width), F32)
    bias_ref[:, 2 * width :] = vec_ref[1:2, :]

    def tile(j):
        cols = span(j * TILE, TILE)
        p_ref[:, cols] = (dot(x_ref[...], qkv[cols, :], NT) + bias_ref[:, cols]).astype(BF)

    tiles(3 * width // TILE, tile)


def self_attend(lengths, p_ref, a_ref, o_ref):
    width = o_ref.shape[1]
    pairs = width // 128
    key = lax.broadcasted_iota(jnp.int32, (128, 256), 0)
    query = lax.broadcasted_iota(jnp.int32, (128, 256), 1)
    same = ((query // 64) % 2) == (key // 64)

    def attend(s):
        rows = span(s * 128, 128)
        length = jnp.where(key < 64, lengths[2 * s], lengths[2 * s + 1])
        mask = jnp.where(same & (lax.rem(key, 64) < length), 0.0, MASKED)
        for h in range(pairs):
            q = p_ref[rows, pl.ds(h * 128, 128)]
            k = p_ref[rows, pl.ds(width + h * 128, 128)]
            v = p_ref[rows, pl.ds(2 * width + h * 128, 128)]
            a = softmax(dot(k, split_heads(q * 0.125), NT), mask, 0)
            a_ref[s * pairs + h] = a
            o_ref[rows, pl.ds(h * 128, 128)] = join_heads(dot(a, v, TN)).astype(BF)

    tiles(o_ref.shape[0] // 128, attend)


def self_backward_kernel(count, layer, io, ins, outs, scratch):
    where_ref, dy_ref, x_ref, vec_ref, p_ref, a_ref, o_ref, n_ref, r_ref, *refs = ins
    dx_ref, own_ref, other_ref, gv_ref = outs
    qkv, out, du_ref, db_ref, dmix_ref, dp_ref, rel_ref, g_ref, sems, sems2 = scratch
    width = x_ref.shape[1]
    half = width // 2
    n, m = qkv.shape[0] // 8, out.shape[0] // 8
    whole = count == 2
    here = where_ref[3] == layer
    second = fetch(placed(refs[1:] if whole else refs, where_ref, [(n, m, 0)], out, half), sems2, here)
    io.begin(o_ref, p_ref, a_ref)
    core = where_ref[0]
    g_gain, g_offset, g_bias = norm_rows_back(dy_ref, n_ref, r_ref, vec_ref[3:4, :], du_ref, db_ref)
    settle(second)

    def mix(j):
        cols = span(j * TILE, TILE)
        dmix_ref[:, cols] = dot(db_ref[...], out[:, cols]).astype(BF)

    tiles(width // TILE, mix)
    io.need(o_ref, p_ref, a_ref)
    rel_ref[:, :half] = o_ref[:, span(core * half, half)]
    rel_ref[:, half:] = o_ref[:, span((1 - core) * half, half)]

    g_ref[:width, :] = dot(db_ref[...], rel_ref[...], TN).astype(BF)
    for b in range(8):
        to, at = relative(where_ref, b), pl.ds(b * m, m)
        own_ref[to, n : n + m, :] = g_ref[at, :half]
        other_ref[to, n : n + m, :] = g_ref[at, half:]
    io.begin(x_ref)
    first = fetch(placed(refs[:1] if whole else refs, where_ref, [(0, n, 0)], qkv, half), sems, here)
    pairs = width // 128

    def attend(s):
        rows = span(s * 128, 128)
        for h in range(pairs):
            q2 = split_heads(p_ref[rows, pl.ds(h * 128, 128)])
            k = p_ref[rows, pl.ds(width + h * 128, 128)]
            v = p_ref[rows, pl.ds(2 * width + h * 128, 128)]
            do2 = split_heads(dmix_ref[rows, pl.ds(h * 128, 128)])
            a = a_ref[s * pairs + h]
            ds = score_back(a, dot(v, do2, NT))
            dp_ref[rows, pl.ds(h * 128, 128)] = (join_heads(dot(ds, k, TN)) * 0.125).astype(BF)
            dp_ref[rows, pl.ds(width + h * 128, 128)] = (dot(ds, q2) * 0.125).astype(BF)
            dp_ref[rows, pl.ds(2 * width + h * 128, 128)] = dot(a, do2).astype(BF)

    tiles(x_ref.shape[0] // 128, attend)
    io.need(x_ref)
    rel_ref[:, :half] = x_ref[:, span(core * half, half)]
    rel_ref[:, half:] = x_ref[:, span((1 - core) * half, half)]

    def qkv_grad(j):
        rows = span(j * TILE, TILE)
        g_ref[rows, :] = dot(dp_ref[:, rows], rel_ref[...], TN).astype(BF)

    tiles(3 * width // TILE, qkv_grad)
    for b in range(8):
        to, at = relative(where_ref, b), pl.ds(b * n, n)
        own_ref[to, :n, :] = g_ref[at, :half]
        other_ref[to, :n, :] = g_ref[at, half:]
    io.send(other_ref, own_ref, part=(slice(None), pl.ds(0, n + m)))
    settle(first)

    def back(j):
        cols = span(j * TILE, TILE)
        dx_ref[:, cols] = (du_ref[:, cols] + dot(dp_ref[...], qkv[:, cols])).astype(dx_ref.dtype)

    tiles(width // TILE, back)
    gv_ref[0:1, :] = jnp.sum(dp_ref[:, :width].astype(F32), axis=0, keepdims=True)
    gv_ref[1:2, :] = jnp.sum(dp_ref[:, 2 * width :].astype(F32), axis=0, keepdims=True)
    gv_ref[2:3, :] = g_bias
    gv_ref[3:4, :] = g_gain
    gv_ref[4:5, :] = g_offset


def cross_attend(keep_ref, q_ref, k_ref, v_ref, a_ref, o_ref):
    width = o_ref.shape[1]
    patches = k_ref.shape[0] // keep_ref.shape[0]
    pairs = width // 128

    def attend(s):
        rows, keys = span(s * 64, 64, 64), span(s * patches, patches, 16)
        mask = jnp.where(keep_ref[pl.ds(s, 1), :] > 0, 0.0, MASKED)
        for h in range(pairs):
            q = q_ref[rows, pl.ds(h * 128, 128)]
            k = k_ref[keys, pl.ds(h * 128, 128)]
            v = v_ref[keys, pl.ds(h * 128, 128)]
            a = softmax(dot(split_heads(q * 0.125), k, NT), mask, 1)
            a_ref[s * pairs + h] = a.T
            o_ref[rows, pl.ds(h * 128, 128)] = join_heads(dot(a, v)).astype(BF)

    tiles(keep_ref.shape[0], attend)


def cross_backward_kernel(io, ins, outs, scratch):
    dy_ref, low_x_ref, k_ref, v_ref, vec_ref, wq_ref, wo_ref, q_ref, a_ref, o_ref, n_ref, r_ref = ins
    dx_ref, dk_ref, dv_ref, gq_ref, go_ref, gv_ref = outs
    db_ref, dmix_ref, dq_ref = scratch
    width = low_x_ref.shape[1]
    patches = a_ref.shape[1]
    io.begin(wo_ref, o_ref)
    g_gain, g_offset, g_bias = norm_rows_back(dy_ref, n_ref, r_ref, vec_ref[3:4, :], dx_ref, db_ref)

    io.begin(q_ref, k_ref, v_ref, a_ref)
    io.need(wo_ref, o_ref)

    def mix(j):
        cols = span(j * TILE, TILE)
        dmix_ref[:, cols] = dot(db_ref[...], wo_ref[cols, :], NT).astype(BF)
        go_ref[cols, :] = dot(o_ref[:, cols], db_ref[...], TN).astype(BF)

    tiles(width // TILE, mix)
    io.send(go_ref)
    io.need(q_ref, k_ref, v_ref, a_ref)
    io.begin(wq_ref, low_x_ref)
    pairs = width // 128

    def attend(s):
        rows, keys = span(s * 64, 64, 64), span(s * patches, patches, 16)
        for h in range(pairs):
            q2 = split_heads(q_ref[rows, pl.ds(h * 128, 128)])
            k = k_ref[keys, pl.ds(h * 128, 128)]
            v = v_ref[keys, pl.ds(h * 128, 128)]
            do2 = split_heads(dmix_ref[rows, pl.ds(h * 128, 128)])
            a = a_ref[s * pairs + h]
            ds = score_back(a, dot(v, do2, NT))
            dq_ref[rows, pl.ds(h * 128, 128)] = (join_heads(dot(ds, k, TN)) * 0.125).astype(BF)
            dk_ref[keys, pl.ds(h * 128, 128)] = (dot(ds, q2) * 0.125).astype(BF)
            dv_ref[keys, pl.ds(h * 128, 128)] = dot(a, do2).astype(BF)

    tiles(a_ref.shape[0] // pairs, attend)
    io.send(dk_ref, dv_ref)
    io.need(wq_ref, low_x_ref)

    def back(j):
        cols = span(j * TILE, TILE)
        dx_ref[:, cols] += dot(dq_ref[...], wq_ref[cols, :], NT)
        gq_ref[cols, :] = dot(low_x_ref[:, cols], dq_ref[...], TN).astype(BF)

    tiles(width // TILE, back)
    gv_ref[0:1, :] = jnp.sum(dq_ref[...].astype(F32), axis=0, keepdims=True)
    gv_ref[1:2, :] = jnp.sum(dv_ref[...].astype(F32), axis=0, keepdims=True)
    gv_ref[2:3, :] = g_bias
    gv_ref[3:4, :] = g_gain
    gv_ref[4:5, :] = g_offset


def gelu_parts(h):
    size = jnp.abs(h) * 0.7071067811865476
    t = 1.0 / (1.0 + 0.3275911 * size)
    e = jnp.exp(-size * size)
    poly = t * (0.254829592 + t * (-0.284496736 + t * (1.421413741 + t * (-1.453152027 + t * 1.061405429))))
    tail = 0.5 * poly * e
    cdf = jnp.where(h < 0, tail, 1.0 - tail)
    return h * cdf, cdf + h * (e * 0.3989422804014327)


def feed_weights(count, layer, where_ref, refs, up, down, sems, sems2):
    width, hidden = up.shape[1], up.shape[0]
    n, m, whole = hidden // 8, width // 8, count == 2
    base = 4 * m
    slices = [(base + n + m * i, m, i) for i in range(hidden // width)]
    here = where_ref[3] == layer
    return (
        lambda: fetch(placed(refs[:1] if whole else refs, where_ref, [(base, n, 0)], up, width // 2), sems, here),
        lambda: fetch(placed(refs[1:] if whole else refs, where_ref, slices, down, hidden // 2), sems2, here),
    )


def feed_activate(low_x_ref, up, bias_ref, act_ref, slope_ref):
    def tile(j):
        cols = span(j * TILE, TILE)
        h = dot(low_x_ref[...], up[cols, :], NT) + bias_ref[:, cols]
        act, slope = gelu_parts(h)
        act_ref[:, cols] = act.astype(BF)
        slope_ref[:, cols] = slope.astype(BF)

    tiles(up.shape[0] // TILE, tile)


def text_forward_kernel(count, io, ins, outs, scratch):
    lengths, where_ref, x_ref, vec_ref, vec2_ref, up_bias_ref, *refs = ins
    p1, a1, o1, low1, n1, act, slope, low2, n2, p2, a2, o2, r1, r2, y3, low3, n3, r3 = outs
    qkv, out, up, down, y1, y2, bias_ref, *sems = scratch
    whole = count == 6
    count = 2 if whole else count
    get_qkv, get_out = self_weights(count, 0, where_ref, refs[:2] if whole else refs, qkv, out, *sems[:2])
    get_up, get_down = feed_weights(count, 0, where_ref, refs[2:4] if whole else refs, up, down, *sems[2:])
    get_qkv2, get_out2 = self_weights(count, 1, where_ref, refs[4:] if whole else refs, qkv, out, *sems[:2])
    settle(get_qkv())
    coming = get_out()
    self_project(x_ref, vec_ref, p1, qkv, bias_ref)
    io.send(p1)
    coming_up = get_up()
    self_attend(lengths, p1, a1, o1)
    io.send(a1, o1)
    settle(coming)
    norm = vec_ref[2:3, :], vec_ref[3:4, :], vec_ref[4:5, :]
    project_and_norm(x_ref, o1, out, NT, *norm, (y1, low1, n1, r1))
    io.send(low1, n1)
    coming_down = get_down()
    settle(coming_up)
    coming = get_qkv2()
    feed_activate(low1, up, up_bias_ref, act, slope)
    io.send(act, slope)
    settle(coming_down)
    coming_out = get_out2()
    norm = vec_ref[5:6, :], vec_ref[6:7, :], vec_ref[7:8, :]
    project_and_norm(y1, act, down, NT, *norm, (y2, low2, n2, r2))
    io.send(low2, n2)
    settle(coming)
    self_project(low2, vec2_ref, p2, qkv, bias_ref)
    io.send(p2)
    self_attend(lengths, p2, a2, o2)
    io.send(a2, o2)
    settle(coming_out)
    norm = vec2_ref[2:3, :], vec2_ref[3:4, :], vec2_ref[4:5, :]
    project_and_norm(low2, o2, out, NT, *norm, (y3, low3, n3, r3))


def feed_backward_body(
    io, where_ref, dy_ref, low_x_ref, vec_ref, act_ref, slope_ref, n_ref, r_ref, outs, work, up, down, get_up, get_down
):
    dx_ref, own_ref, other_ref, gv_ref = outs
    db_ref, dbt_ref, dh_ref, rel_ref, gb_ref = work
    width, hidden = up.shape[1], up.shape[0]
    n, m, half = hidden // 8, width // 8, width // 2
    core = where_ref[0]
    second = get_down()
    io.begin(slope_ref)
    g_gain, g_offset, g_bias = norm_rows_back(dy_ref, n_ref, r_ref, vec_ref[6:7, :], dx_ref, db_ref)
    dbt_ref[...] = db_ref[...].T
    settle(second)
    io.need(slope_ref)
    io.begin(act_ref, low_x_ref)

    def down_tile(j):
        cols = span(j * TILE, TILE)
        dh = (dot(db_ref[...], down[:, cols]) * slope_ref[:, cols].astype(F32)).astype(BF)
        dh_ref[:, cols] = dh
        gb_ref[:, cols] = jnp.sum(dh.astype(F32), axis=0, keepdims=True)

    tiles(hidden // TILE, down_tile)
    io.need(act_ref)

    def down_grad(j):
        for ref, side in ((own_ref, core), (other_ref, 1 - core)):
            g = dot(dbt_ref[...], act_ref[:, span(side * (hidden // 2) + j * width, width)]).astype(BF)
            for b in range(8):
                to = relative(where_ref, b)
                for k in range(2):
                    ref[to, span(n + (2 * j + k) * m, m, 16), :] = g[b * m : (b + 1) * m, k * half : (k + 1) * half]

    tiles(hidden // 2 // width, down_grad)
    io.send(other_ref, own_ref, part=(slice(None), pl.ds(n, n)))
    first = get_up()
    io.need(low_x_ref)
    rel_ref[:, :half] = low_x_ref[:, span(core * half, half)]
    rel_ref[:, half:] = low_x_ref[:, span((1 - core) * half, half)]

    def up_grad(j):
        g = dot(dh_ref[:, span(j * 2 * n, 2 * n)], rel_ref[...], TN).astype(BF)
        for k in range(2):
            to = relative(where_ref, 2 * j + k)
            own_ref[to, :n, :] = g[k * n : (k + 1) * n, :half]
            other_ref[to, :n, :] = g[k * n : (k + 1) * n, half:]

    tiles(4, up_grad)
    io.send(other_ref, own_ref, part=(slice(None), pl.ds(0, n)))
    settle(first)

    def back(j):
        cols = span(j * TILE, TILE)
        dx_ref[:, cols] += dot(dh_ref[...], up[:, cols])

    tiles(width // TILE, back)
    gv_ref[0:1, :] = g_bias
    gv_ref[1:2, :] = g_gain
    gv_ref[2:3, :] = g_offset
    for j in range(hidden // width):
        gv_ref[3 + j : 4 + j, :] = gb_ref[:, j * width : (j + 1) * width]


def feed_backward_kernel(count, layer, io, ins, outs, scratch):
    where_ref, dy_ref, low_x_ref, vec_ref, act_ref, slope_ref, n_ref, r_ref, *refs = ins
    up, down, *work, sems, sems2 = scratch
    get = feed_weights(count, layer, where_ref, refs, up, down, sems, sems2)
    feed_backward_body(
        io, where_ref, dy_ref, low_x_ref, vec_ref, act_ref, slope_ref, n_ref, r_ref, outs, work, up, down, *get
    )


def joining_kernel(count, io, ins, outs, scratch):
    where_ref, x_ref, low_x_ref, keep_ref, k_ref, v_ref, cross_ref, wq_ref, wo_ref, vec_ref, bias_ref, dy_ref, *refs = ins
    q_ref, a_ref, o_ref, cross_n, cross_r, y_ref, *grads = outs
    up, down, *work, act_ref, slope_ref, state, low_state, low_ref, n_ref, r_ref, sems, sems2 = scratch
    get_up, get_down = feed_weights(count, 1, where_ref, refs, up, down, sems, sems2)
    width = x_ref.shape[1]
    io.begin(k_ref, v_ref)

    def tile(j):
        cols = span(j * TILE, TILE)
        q_ref[:, cols] = (dot(low_x_ref[...], wq_ref[:, cols]) + cross_ref[0:1, cols]).astype(BF)

    tiles(width // TILE, tile)
    io.need(k_ref, v_ref)
    io.begin(x_ref, wo_ref)
    first = get_up()
    cross_attend(keep_ref, q_ref, k_ref, v_ref, a_ref, o_ref)
    io.send(q_ref, a_ref, o_ref)
    io.need(x_ref, wo_ref)
    norm = cross_ref[2:3, :], cross_ref[3:4, :], cross_ref[4:5, :]
    project_and_norm(x_ref, o_ref, wo_ref, NN, *norm, (state, low_state, cross_n, cross_r))
    io.send(cross_n)
    second = get_down()
    settle(first)
    feed_activate(low_state, up, bias_ref, act_ref, slope_ref)
    settle(second)
    norm = vec_ref[5:6, :], vec_ref[6:7, :], vec_ref[7:8, :]
    project_and_norm(state, act_ref, down, NT, *norm, (y_ref, low_ref, n_ref, r_ref))
    io.send(y_ref)
    feed_backward_body(
        io, where_ref, dy_ref, low_state, vec_ref, act_ref, slope_ref, n_ref, r_ref, grads, work, up, down, list, list
    )


def vector_kernel(first, v_rows, v_lanes, x_rows, c_rows, *refs):
    where_ref, *pieces = refs[:33]
    vec_refs, bias_refs, cross_ref = refs[33:35], refs[35:37], refs[37]
    held, sems = refs[38:]
    core, z, y, x = where_ref[0], where_ref[1], where_ref[2], where_ref[3]
    copies = []
    for i, ref in enumerate(pieces):
        x_rel, c_rel, y_rel, z_rel = i // 16, (i // 8) % 2, (i // 4) % 2, i % 4
        pipe = lax.rem(x + x_rel, 2) * 2 + lax.rem(core + c_rel, 2)
        device = pipe * 8 + lax.rem(z - z_rel + 4, 4) * 2 + lax.rem(y + y_rel, 2)
        copies.append(([ref.at[pl.ds(first, 16), pl.ds(0, 128)]], held.at[device]))
    settle(fetch(copies, sems))
    for device in range(32):
        block = held[device].astype(F32)
        pipe, dp = device // 8, device % 8
        rows = pl.ds(pipe % 2 * v_rows, v_rows)
        vec_refs[pipe // 2][rows, pl.ds(dp * v_lanes, v_lanes)] = block[:v_rows, :v_lanes]
        cross_ref[0:x_rows, pl.ds(device * c_rows, c_rows)] = block[v_rows : v_rows + x_rows, :c_rows]
    width = cross_ref.shape[1]
    for vec_ref, bias_ref in zip(vec_refs, bias_refs):
        for j in range(4):
            bias_ref[:, j * width : (j + 1) * width] = vec_ref[8 + j : 9 + j, :]


def struct(*shape, dtype=F32):
    return jax.ShapeDtypeStruct(shape, dtype)


VMEM = pl.BlockSpec(memory_space=pltpu.VMEM)
SMEM = pl.BlockSpec(memory_space=pltpu.SMEM)
ANYWHERE = pl.BlockSpec(memory_space=pl.ANY)


def call(kernel, outs, specs, scratch, us, args, late=(), early=(), packs=(), layer=0, onto=None):
    n_in, n_out, n_scratch = len(args), len(outs), len(scratch)
    early = (*early, *packs)
    held = [pltpu.VMEM(args[i].shape, args[i].dtype) for i in late]
    held += [pltpu.VMEM(outs[i].shape, outs[i].dtype) for i in early]
    outs = [struct(2, *o.shape, dtype=o.dtype) if i in packs else o for i, o in enumerate(outs)]
    taken = tuple(onto) if onto else ()
    n_all = n_in + len(taken)

    def body(*refs):
        ins, out, rest = list(refs[:n_in]), list(refs[n_all : n_all + n_out]), refs[n_all + n_out :]
        buffers = rest[n_scratch:-1]
        io = Copies(rest[-1])
        for k, i in enumerate(late):
            io.coming.append((buffers[k], ins[i], None))
            ins[i] = buffers[k]
        for k, i in enumerate(early, len(late)):
            target = out[i].at[lax.rem(ins[0][3] + layer, 2)] if i in packs else out[i]
            io.going.append((buffers[k], target))
            out[i] = buffers[k]
        kernel(io, ins, out, rest[:n_scratch])
        io.finish()

    specs = [ANYWHERE if i in late else spec for i, spec in enumerate(specs)] + [ANYWHERE] * len(taken)
    return pl.pallas_call(
        body,
        out_shape=outs,
        in_specs=specs,
        out_specs=[ANYWHERE if i in early else VMEM for i in range(n_out)],
        scratch_shapes=[*scratch, *held, pltpu.SemaphoreType.DMA((24,))],
        input_output_aliases={n_in + k: i for k, i in enumerate(packs)} if taken else {},
        cost_estimate=pl.CostEstimate(flops=int(us * 1.1e9), bytes_accessed=int(us * 3.5e6), transcendentals=0),
        compiler_params=pltpu.CompilerParams(vmem_limit_bytes=VMEM_BYTES),
    )(*args, *taken)


def gathered_vectors(pieces, where, first, v_rows, v_lanes, x_rows, c_rows):
    width = 8 * v_lanes
    return pl.pallas_call(
        partial(vector_kernel, first, v_rows, v_lanes, x_rows, c_rows),
        out_shape=[struct(12, width)] * 2 + [struct(1, 4 * width)] * 2 + [struct(8, width)],
        in_specs=[SMEM] + [ANYWHERE] * len(pieces),
        out_specs=[VMEM] * 5,
        scratch_shapes=[pltpu.VMEM((32, 16, 128), BF), pltpu.SemaphoreType.DMA((32,))],
        cost_estimate=pl.CostEstimate(flops=0, bytes_accessed=10**7, transcendentals=0),
    )(where, *pieces)


def copy_sems(count, parts=1):
    return pltpu.SemaphoreType.DMA((16 * parts if count > 2 else 1,))


def text_forward(x, lengths, where, vecs, bias, weights):
    rows, width = x.shape
    hidden = bias.shape[1]
    blocks = rows // 128 * (width // 128)
    count = len(weights)
    low = struct(rows, width, dtype=BF)
    attention = [struct(rows, 3 * width, dtype=BF), struct(blocks, 128, 256, dtype=BF), low]
    outs = [
        *attention,
        low,
        low,
        struct(rows, hidden, dtype=BF),
        struct(rows, hidden, dtype=BF),
        low,
        low,
        *attention,
        struct(rows, 1),
        struct(rows, 1),
        struct(rows, width),
        low,
        low,
        struct(rows, 1),
    ]
    scratch = [
        pltpu.VMEM((3 * width, width), BF),
        pltpu.VMEM((width, width), BF),
        pltpu.VMEM((hidden, width), BF),
        pltpu.VMEM((width, hidden), BF),
        pltpu.VMEM((rows, width), F32),
        pltpu.VMEM((rows, width), F32),
        pltpu.VMEM((1, 3 * width), F32),
        copy_sems(count),
        copy_sems(count),
        copy_sems(count),
        copy_sems(count, hidden // width),
    ]
    p1, a1, o1, low1, n1, act, slope, low2, n2, p2, a2, o2, r1, r2, y3, low3, n3, r3 = call(
        partial(text_forward_kernel, count),
        outs,
        [SMEM, SMEM] + [VMEM] * 4 + [ANYWHERE] * count,
        scratch,
        38,
        (lengths, where, x, *vecs, bias, *weights),
        early=tuple(range(12)),
    )
    return y3, low3, (x, p1, a1, o1, n1, r1), (low1, act, slope, n2, r2), (low2, p2, a2, o2, n3, r3)


def self_backward(dy, saved, where, vec, weights, layer, dtype=F32, onto=None):
    x, p, a, o, n, r = saved
    rows, width = x.shape
    half = width // 2
    count = len(weights)
    outs = [
        struct(rows, width, dtype=dtype),
        struct(8, width // 2 + SMALL, half, dtype=BF),
        struct(8, width // 2 + SMALL, half, dtype=BF),
        struct(8, width),
    ]
    scratch = [
        pltpu.VMEM((3 * width, width), BF),
        pltpu.VMEM((width, width), BF),
        pltpu.VMEM((rows, width), F32),
        pltpu.VMEM((rows, width), BF),
        pltpu.VMEM((rows, width), BF),
        pltpu.VMEM((rows, 3 * width), BF),
        pltpu.VMEM((rows, width), BF),
        pltpu.VMEM((3 * width, width), BF),
        copy_sems(count),
        copy_sems(count),
    ]
    return call(
        partial(self_backward_kernel, count, layer),
        outs,
        [SMEM] + [VMEM] * 8 + [ANYWHERE] * count,
        scratch,
        22,
        (where, dy, x, vec, p, a, o, n, r, *weights),
        late=(6, 4, 5, 2),
        packs=(1, 2),
        layer=layer,
        onto=onto,
    )


def cross_backward(dy, saved, vec, wq, wo):
    low_x, k, v, q, a, o, n, r = saved
    rows, width = low_x.shape
    outs = [
        struct(rows, width),
        struct(*k.shape, dtype=BF),
        struct(*k.shape, dtype=BF),
        struct(width, width, dtype=BF),
        struct(width, width, dtype=BF),
        struct(8, width),
    ]
    scratch = [pltpu.VMEM((rows, width), BF)] * 3
    return call(
        cross_backward_kernel,
        outs,
        [VMEM] * 12,
        scratch,
        26,
        (dy, low_x, k, v, vec, wq, wo, q, a, o, n, r),
        late=(6, 9, 7, 2, 3, 8, 5, 1),
        early=(1, 2, 4),
    )


def feed_backward(dy, saved, where, vec, weights, layer, onto=None):
    low_x, act, slope, n, r = saved
    rows, width = low_x.shape
    hidden = act.shape[1]
    count = len(weights)
    outs = [
        struct(rows, width),
        struct(8, 2 * hidden // 8, width // 2, dtype=BF),
        struct(8, 2 * hidden // 8, width // 2, dtype=BF),
        struct(8, width),
    ]
    scratch = [
        pltpu.VMEM((hidden, width), BF),
        pltpu.VMEM((width, hidden), BF),
        pltpu.VMEM((rows, width), BF),
        pltpu.VMEM((width, rows), BF),
        pltpu.VMEM((rows, hidden), BF),
        pltpu.VMEM((rows, width), BF),
        pltpu.VMEM((1, hidden), F32),
        copy_sems(count),
        copy_sems(count, hidden // width),
    ]
    return call(
        partial(feed_backward_kernel, count, layer),
        outs,
        [SMEM] + [VMEM] * 7 + [ANYWHERE] * count,
        scratch,
        22,
        (where, dy, low_x, vec, act, slope, n, r, *weights),
        late=(5, 4, 2),
        packs=(1, 2),
        layer=layer,
        onto=onto,
    )


def joining(x, low_x, where, keep, k, v, cross_vec, wq, wo, vec, bias, dy, weights):
    rows, width = x.shape
    samples, patches = keep.shape
    hidden = bias.shape[1]
    count = len(weights)
    low = struct(rows, width, dtype=BF)
    pack = struct(8, 2 * hidden // 8, width // 2, dtype=BF)
    outs = [
        low,
        struct(samples * (width // 128), patches, 128, dtype=BF),
        low,
        low,
        struct(rows, 1),
        struct(rows, width),
        struct(rows, width),
        pack,
        pack,
        struct(8, width),
    ]
    scratch = [
        pltpu.VMEM((hidden, width), BF),
        pltpu.VMEM((width, hidden), BF),
        pltpu.VMEM((rows, width), BF),
        pltpu.VMEM((width, rows), BF),
        pltpu.VMEM((rows, hidden), BF),
        pltpu.VMEM((rows, width), BF),
        pltpu.VMEM((1, hidden), F32),
        pltpu.VMEM((rows, hidden), BF),
        pltpu.VMEM((rows, hidden), BF),
        pltpu.VMEM((rows, width), F32),
        pltpu.VMEM((rows, width), BF),
        pltpu.VMEM((rows, width), BF),
        pltpu.VMEM((rows, width), BF),
        pltpu.VMEM((rows, 1), F32),
        copy_sems(count),
        copy_sems(count, hidden // width),
    ]
    q, a, o, n, r, joined, dx, own, other, gv = call(
        partial(joining_kernel, count),
        outs,
        [SMEM] + [VMEM] * 11 + [ANYWHERE] * count,
        scratch,
        48,
        (where, x, low_x, keep, k, v, cross_vec, wq, wo, vec, bias, dy, *weights),
        late=(4, 5, 8, 1),
        early=(0, 1, 2, 3, 5),
        packs=(7, 8),
        layer=1,
    )
    return (low_x, k, v, q, a, o, n, r), joined, dx, own, other, gv


def lane_slices(a, lanes):
    return jnp.concatenate([a[:, i : i + lanes] for i in range(0, a.shape[1], lanes)], axis=0)


def lane_join(a, count):
    rows = a.shape[-2] // count
    return jnp.concatenate([a[..., i * rows : (i + 1) * rows, :] for i in range(count)], axis=-1)


def pad_to(a, rows, lanes):
    return jnp.pad(a, ((0, rows - a.shape[0]), (0, lanes - a.shape[1])))


def dynamic(a, index, axis):
    return lax.dynamic_index_in_dim(a, index, axis, keepdims=False)


def after(value, tokens):
    return lax.optimization_barrier((value, tokens))[0] if tokens else value


class Grid:
    def __init__(self):
        pipe, dp = lax.axis_index("pipe"), lax.axis_index("dp")
        self.x, self.core = pipe // 2, pipe % 2
        self.z, self.y = dp // 2, dp % 2
        self.arrived, self.computed, self.slack = [()] * 2, (), 1

    def swap_x(self, a):
        return lax.ppermute(a, "pipe", [(i, i ^ 2) for i in range(4)])

    def swap_core(self, a):
        return lax.ppermute(a, "pipe", [(i, i ^ 1) for i in range(4)])

    def swap_y(self, a):
        return lax.ppermute(a, "dp", [(i, i ^ 1) for i in range(8)])

    def ring_z(self, a, step=1):
        return lax.ppermute(a, "dp", [(i, (i + 2 * step) % 8) for i in range(8)])

    def by_distance(self, a):
        for axis, place in ((0, self.x), (1, self.core), (3, self.y)):
            a = jnp.where(place == 0, a, jnp.flip(a, axis))
        return lax.dynamic_slice_in_dim(jnp.concatenate([a, a], axis=2), self.z, 4, 2)

    def turn(self, *moves, pre=(), compute=None, args=(), chain=False):
        tokens = (*self.arrived[-self.slack], *self.computed)
        arrived = []

        def begin(asked):
            asked = [ask for group in asked for ask in group()]
            values = after([value for _, value, _ in asked], tokens)
            results = []
            for i, ((move, _, keep), value) in enumerate(zip(asked, values)):
                results.append(move(after(value, (results[i - 2],)) if chain and i >= 5 else value))
                keep(results[-1])
            arrived.extend(results)
            return tuple(values)

        begin(pre)
        values = begin(moves)
        self.arrived.append(tuple(arrived))
        self.computed = ()
        if compute is None:
            return None
        result = compute(*after(tuple(args), tokens + values))
        self.computed = tuple(jax.tree.leaves(result))
        return result


class Gather:
    def __init__(self, grid, piece):
        self.grid, self.here, self.swapped = grid, {(0, 0, 0): piece}, {}

    def get(self, layer, y, z, over):
        sources = {"z": (layer, y, z - 1), "y": (layer, 1 - y, z), "x": (1 - layer, y, z)}
        move = {"z": self.grid.ring_z, "y": self.grid.swap_y, "x": self.grid.swap_x}[over]
        return lambda: [(move, self.here[sources[over]], partial(self.here.__setitem__, (layer, y, z)))]

    def c(self, count=16):
        ready = [key for key in self.here if key not in self.swapped][:count]
        return [(self.grid.swap_core, self.here[key], partial(self.swapped.__setitem__, key)) for key in ready]

    def c3(self):
        return self.c(3)

    def pieces(self):
        keys = [[(layer, y, z) for y in range(2) for z in range(4)] for layer in range(2)]
        return [held[key] for half in keys for held in (self.here, self.swapped) for key in half]


class PairSum:
    def __init__(self, grid, own, other):
        self.grid, self.other = grid, other
        self.own = own.reshape((2, 4, 2) + own.shape[2:])
        self.came, self.got = None, {}

    def c(self):
        def keep(a):
            self.came = a.reshape(self.own.shape)

        return [(self.grid.swap_core, self.other, keep)]

    def block(self, own, y, z):
        layer = 0 if own else 1
        parts = [self.own[layer, z, y], self.came[layer, z, y], *self.got.get((own, y, z), [])]
        return sum(part.astype(F32) for part in parts)

    def move(self, over, own, y, z):
        to = {"z": (own, y, z - 1), "y": (own, 1 - y, z), "x": (True, y, z)}[over]
        move = {"z": self.grid.ring_z, "y": self.grid.swap_y, "x": self.grid.swap_x}[over]

        def ask():
            return [(move, self.block(own, y, z).astype(BF), self.got.setdefault(to, []).append)]

        return ask

    def steps(self):
        own, other = partial(self.move, own=True), partial(self.move, own=False)
        return [
            (other("z", y=0, z=2), other("y", y=1, z=3), other("x", y=1, z=2)),
            (other("z", y=1, z=1), own("y", y=1, z=3), other("x", y=0, z=3)),
            (own("z", y=0, z=3), own("y", y=1, z=2), other("x", y=1, z=0)),
            (own("z", y=0, z=2), own("y", y=1, z=1), other("x", y=0, z=1)),
            (own("z", y=0, z=1), own("y", y=1, z=0), other("x", y=0, z=0)),
        ]

    def total(self):
        return self.block(True, 0, 0)


class BlockSum:
    def __init__(self, grid, own, other, dtype):
        self.grid, self.own, self.other, self.dtype = grid, own, other, dtype
        self.ring = []

    def step(self, swap, place, axis):
        own = dynamic(self.a, place, axis)

        def keep(came):
            self.a = own.astype(F32) + came.astype(F32)

        return [(swap, dynamic(self.a, 1 - place, axis).astype(self.dtype), keep)]

    def c(self):
        def keep(came):
            self.a = self.own.astype(F32) + came.astype(F32)

        return [(self.grid.swap_core, self.other, keep)]

    def x0(self):
        self.halves = [dynamic(self.a, place, 0) for place in (self.grid.x, 1 - self.grid.x)]
        return self.x_half(0)

    def x1(self):
        return self.x_half(1)

    def x_half(self, k):
        own, other = (h[2 * k : 2 * k + 2] for h in self.halves)

        def keep(came):
            total = own.astype(F32) + came.astype(F32)
            self.a = total if k == 0 else jnp.concatenate([self.a, total])

        return [(self.grid.swap_x, other.astype(self.dtype), keep)]

    def y(self):
        return self.step(self.grid.swap_y, self.grid.y, 1)

    def round(self):
        value = self.block(3 - len(self.ring))
        return [(self.grid.ring_z, value.astype(self.dtype), self.ring.append)]

    def block(self, step):
        value = dynamic(self.a, (self.grid.z + step) % 4, 0).astype(F32)
        return value + self.ring[-1].astype(F32) if self.ring else value

    def total(self):
        return self.block(0)


def masks(caption_len, phrase_len, box_count, patch_mask, text_rows, patches):
    slots = jnp.arange(phrase_len.shape[1], dtype=jnp.int32)
    phrase_total = jnp.sum(jnp.where(slots[None, :] < box_count[:, None], phrase_len, 0), axis=1)
    lengths = jnp.minimum(caption_len + phrase_total, text_rows)
    first_patch = (jnp.arange(patch_mask.shape[1], dtype=jnp.int32) == 0).astype(jnp.int32)
    keep = jnp.maximum(patch_mask, first_patch[None, :]).astype(F32)
    return lengths, jnp.pad(keep, ((0, 0), (0, patches - keep.shape[1])))


def on_device(
    text_embed,
    image_feats,
    caption_len,
    phrase_len,
    box_count,
    patch_mask,
    attn_qkv,
    attn_out,
    ffn_up,
    ffn_down,
    layer_vectors,
    cross_query,
    cross_kv,
    cross_out,
    cross_vectors,
    cotangent,
):
    n_pipe, n_dp = lax.axis_size("pipe"), lax.axis_size("dp")
    everyone = ("pipe", "dp")
    shards, half = n_pipe * n_dp, n_pipe // 2
    samples, text_rows, width = text_embed.shape
    hidden = ffn_up.shape[1] * n_dp
    lanes = attn_qkv.shape[0]
    patches = -(-image_feats.shape[1] // 32) * 32
    direct = (n_pipe, n_dp) == (4, 8) and lanes % 128 == 0
    lengths, patch_keep = masks(caption_len, phrase_len, box_count, patch_mask, text_rows, patches)
    x = text_embed.reshape(-1, width)

    def padded(image_feats):
        wide = jnp.pad(image_feats, ((0, 0), (0, patches - image_feats.shape[1]), (0, 0)))
        return wide.reshape(samples * patches, -1)


    c_rows = cross_query.shape[0]
    kv_slices = cross_kv.shape[1] // width
    cross_pack = jnp.concatenate([cross_query, cross_out, lane_slices(cross_kv, width)], axis=0)
    v_rows, v_lanes = layer_vectors.shape
    x_rows = cross_vectors.shape[1]
    small = jnp.concatenate([pad_to(layer_vectors, v_rows, 128), pad_to(cross_vectors.T, x_rows, 128)], axis=0)
    small = pad_to(small, 16, 128)
    pack_attn = jnp.concatenate([attn_qkv.T, attn_out.T], axis=0)
    pack_feed = jnp.concatenate([ffn_up.T, lane_slices(ffn_down.T, lanes)], axis=0)
    n_pack = pack_attn.shape[0] + pack_feed.shape[0]

    def cross_weights(blocks):
        blocks = blocks.reshape(shards, -1, width)
        i_rows = cross_kv.shape[0]
        ends = np.cumsum([0, c_rows, c_rows, i_rows, i_rows])
        return [blocks[:, a:b].reshape(-1, width) for a, b in zip(ends[:-1], ends[1:])]

    def vectors_of(blocks):
        blocks = blocks.reshape(n_pipe, n_dp, 16, 128).astype(F32)
        vecs = []
        for layer in range(2):
            v = blocks[layer * half : (layer + 1) * half, :, :v_rows, :v_lanes]
            vecs.append(jnp.moveaxis(v, 1, 2).reshape(12, width))
        cvec = blocks.reshape(shards, 16, 128)[:, v_rows : v_rows + x_rows, :c_rows]
        return vecs, [v[8:12].reshape(1, hidden) for v in vecs], jnp.moveaxis(cvec, 1, 0).reshape(x_rows, width)

    def keys_values(image, wk, wv, cvec):
        keys = jnp.dot(image, wk, preferred_element_type=F32).astype(BF)
        return keys, (jnp.dot(image, wv, preferred_element_type=F32) + cvec[1]).astype(BF)

    def pack_cross(image, dk, dv, g_cq, g_co):
        grads = [g_cq, g_co, dot(image, dk, TN).astype(BF), dot(image, dv, TN).astype(BF)]
        return [g.reshape(shards, -1, width) for g in grads]

    def vector_block(v_self, v_feed):
        v = jnp.concatenate([v_self[:5], v_feed[:7]], axis=0)
        return jnp.moveaxis(v.reshape(half, v_rows, n_dp, v_lanes), 2, 1)

    def pack_vectors(text, joining, v_cross):
        section = jnp.concatenate([vector_block(*text), vector_block(*joining)], axis=0)
        cross = jnp.moveaxis(v_cross[:x_rows].reshape(x_rows, n_pipe, n_dp, c_rows), 0, 2)
        wide = [jnp.pad(v, ((0, 0), (0, 0), (0, 0), (0, 128 - v.shape[3]))) for v in (section, cross)]
        wide = jnp.concatenate(wide, axis=2)
        return jnp.pad(wide, ((0, 0), (0, 0), (0, 16 - wide.shape[2]), (0, 0)))

    seed = cotangent.reshape(-1, width)
    if direct:
        grid = Grid()
        turn = grid.turn
        where = jnp.stack([grid.core, grid.z, grid.y, grid.x]).astype(jnp.int32)
        gather = Gather(grid, jnp.concatenate([pack_attn, pack_feed, pad_to(small, 16, lanes)]))
        get = gather.get
        turn(get(0, 0, 1, "z"), get(0, 1, 0, "y"), get(1, 0, 0, "x"), gather.c3, chain=True)
        image = turn(
            get(0, 0, 2, "z"), get(0, 1, 1, "y"), get(1, 0, 1, "x"), gather.c3, chain=True, compute=padded, args=(image_feats,)
        )
        turn(get(0, 0, 3, "z"), get(0, 1, 2, "y"), get(1, 1, 0, "x"), gather.c3, chain=True)
        turn(get(1, 1, 1, "z"), get(0, 1, 3, "y"), get(1, 0, 3, "x"), gather.c3, chain=True)
        turn(get(1, 0, 2, "z"), get(1, 1, 3, "y"), get(1, 1, 2, "x"), gather.c3, chain=True)
        turn(gather.c)
        weights = gather.pieces()
        cross_whole = lax.all_gather(after(cross_pack, grid.arrived[-3]), everyone, axis=0, tiled=True)
        *vectors, cvec = gathered_vectors(weights, where, n_pack, v_rows, v_lanes, x_rows, c_rows)
        vecs, biases = vectors[:2], vectors[2:]
        state, low, s_self, s_feed, s_self2 = text_forward(x, lengths, where, vecs, biases[0], weights)
        wq, wo, wk, wv = cross_weights(cross_whole)
        keys, values = keys_values(image, wk, wv, cvec)
        s_cross, joined, grad, *g_feed2, v_feed2 = joining(
            state, low, where, patch_keep, keys, values, cvec, wq, wo, vecs[1], biases[1], seed, weights
        )
        grid.computed = (grad,)

        def fourth(grad):
            grad, dk, dv, g_cq, g_co, v_cross = cross_backward(grad, s_cross, cvec, wq, wo)
            return grad, v_cross, pack_cross(image, dk, dv, g_cq, g_co)

        grad, v_cross, cross_grads = fourth(grad)
        cross_grads = [g.reshape(2, 2, 4, 2, -1, width) for g in cross_grads]
        halves = [jnp.concatenate([dynamic(g, c, 1) for g in cross_grads], axis=3) for c in (grid.core, 1 - grid.core)]
        sum_cross = BlockSum(grid, *halves, BF)
        turn(sum_cross.c)
        grad, *g_self, v_self2 = turn(
            sum_cross.x0,
            compute=lambda grad: self_backward(grad, s_self2, where, vecs[1], weights, 1, BF), args=(grad,),
        )
        grad, *g_feed, v_feed = turn(
            sum_cross.x1,
            compute=lambda grad: feed_backward(grad, s_feed, where, vecs[0], weights, 0, g_feed2), args=(grad,),
        )
        feed = PairSum(grid, *g_feed)
        embed_grad, *g_self, v_self = turn(
            feed.c, sum_cross.y,
            compute=lambda grad: self_backward(grad, s_self, where, vecs[0], weights, 0, F32, g_self), args=(grad,),
        )
        vectors = pack_vectors((v_self, v_feed), (v_self2, v_feed2), v_cross)
        vectors = grid.by_distance(vectors.reshape(2, 2, 4, 2, SMALL, 128))
        rows = g_self[0].shape[2] - SMALL
        for k in range(2):
            small = jnp.pad(vectors[:, k].reshape(2, 8, SMALL, 128), ((0, 0), (0, 0), (0, 0), (0, lanes - 128)))
            g_self[k] = lax.dynamic_update_slice(g_self[k], small.astype(BF), (0, 0, rows, 0))
        attn = PairSum(grid, *g_self)
        f0, f1, f2, f3, f4 = feed.steps()
        a0, a1, a2, a3, a4 = attn.steps()
        turn(*f0, attn.c, sum_cross.round)
        turn(*f1)
        grid.slack = 2
        turn(*a0)
        turn(*f2)
        turn(*a1)
        turn(*f3)
        turn(*a2, sum_cross.round)
        turn(*f4)
        turn(*a3, sum_cross.round)
        turn(*a4)
        attn_grads, feed_grads = attn.total(), feed.total()
        n_qkv, n_up = attn_qkv.shape[1], ffn_up.shape[1]
        mine = [attn_grads[:n_qkv], attn_grads[n_qkv:rows], feed_grads[:n_up], feed_grads[n_up:]]
        cross_grads, small = sum_cross.total(), attn_grads[rows:, :128]
    else:
        where = jnp.zeros((4,), jnp.int32)
        image = padded(image_feats)
        vectors = lax.all_gather(small, everyone, axis=0, tiled=False)
        whole = lax.all_gather(jnp.concatenate([pack_attn, pack_feed], axis=0), everyone, axis=0, tiled=False)
        whole = whole.reshape(n_pipe, n_dp, -1, lanes)

        def section(piece, layer):
            piece = jnp.moveaxis(piece[layer * half : (layer + 1) * half], 0, 2)
            return piece.reshape(n_dp * piece.shape[1], half * piece.shape[-1])

        counts = [attn_qkv.shape[1], attn_out.shape[1], ffn_up.shape[1], attn_out.shape[1] * (hidden // width)]
        ends = np.cumsum([0] + counts)
        cut = [whole[:, :, a:b] for a, b in zip(ends[:-1], ends[1:])]
        cut[3] = lane_join(cut[3], hidden // width)
        (qkv1, out1, up1, down1), (qkv2, out2, up2, down2) = ([section(c, k) for c in cut] for k in range(2))
        vecs, biases, cvec = vectors_of(vectors)
        wq, wo, wk, wv = cross_weights(lax.all_gather(cross_pack, everyone, axis=0, tiled=False))
        state, low, s_self, s_feed, s_self2 = text_forward(
            x, lengths, where, vecs, biases[0], [qkv1, out1, up1, down1, qkv2, out2]
        )
        keys, values = keys_values(image, wk, wv, cvec)
        s_cross, joined, grad, *g_feed2, v_feed2 = joining(
            state, low, where, patch_keep, keys, values, cvec, wq, wo, vecs[1], biases[1], seed, [up2, down2]
        )
        grad, dk, dv, g_cq, g_co, v_cross = cross_backward(grad, s_cross, cvec, wq, wo)
        grad, *g_self, v_self2 = self_backward(grad, s_self2, where, vecs[1], [qkv2, out2], 1, BF)
        grad, *g_feed, v_feed = feed_backward(grad, s_feed, where, vecs[0], [up1, down1], 0, g_feed2)
        embed_grad, *g_self, v_self = self_backward(grad, s_self, where, vecs[0], [qkv1, out1], 0, F32, g_self)
        g_self1, g_self2 = ([g[k] for g in g_self] for k in range(2))
        g_feed1, g_feed2 = ([g[k] for g in g_feed] for k in range(2))

        def unpack(pair, rows, slices):
            parts = []
            at = 0
            for r, k in zip(rows, slices):
                sides = [p[:, at : at + r * k] for p in pair]
                sides = [lane_join(p, k).reshape(8 * r, -1) for p in sides]
                parts.append(jnp.concatenate(sides, axis=1))
                at += r * k
            return parts

        def split(first, second):
            both = jnp.stack([first, second])
            rows, k = both.shape[1] // n_dp, both.shape[2] // (half * lanes)
            both = both.reshape(2, n_dp, rows, half, k, lanes)
            return both.transpose(0, 3, 1, 4, 2, 5).reshape(n_pipe, n_dp, k * rows, lanes)

        attn = ((3 * width // 8, width // 8), (1, 1))
        feed = ((hidden // 8, width // 8), (1, hidden // width))
        parts = []
        for first, second, shape in ((g_self1, g_self2, attn), (g_feed1, g_feed2, feed)):
            parts += [split(a, b) for a, b in zip(unpack(first, *shape), unpack(second, *shape))]
        packed = jnp.concatenate(parts, axis=2).reshape(-1, lanes)
        packed = lax.psum_scatter(packed, everyone, scatter_dimension=0, tiled=True).astype(F32)
        mine = [packed[a:b] for a, b in zip(ends[:-1], ends[1:])]
        cross_grads = jnp.concatenate(pack_cross(image, dk, dv, g_cq, g_co), axis=1).reshape(-1, width)
        cross_grads = lax.psum_scatter(cross_grads, everyone, scatter_dimension=0, tiled=True).astype(F32)
        small = pack_vectors((v_self, v_feed), (v_self2, v_feed2), v_cross)
        small = lax.psum_scatter(small.reshape(-1, 128), everyone, scatter_dimension=0, tiled=True)
    mine[3] = lane_join(mine[3], hidden // width)
    return (
        joined.reshape(text_embed.shape),
        embed_grad.reshape(text_embed.shape),
        mine[0].T,
        mine[1].T,
        mine[2].T,
        mine[3].T,
        small[:v_rows, :v_lanes],
        cross_grads[:c_rows],
        lane_join(cross_grads[2 * c_rows :], kv_slices),
        cross_grads[c_rows : 2 * c_rows],
        small[v_rows : v_rows + x_rows, :c_rows].T,
    )


def solution(mesh):
    in_specs = (
        P(("pipe", "dp"), None, None),
        P(("pipe", "dp"), None, None),
        P(("pipe", "dp")),
        P(("pipe", "dp"), None),
        P(("pipe", "dp")),
        P(("pipe", "dp"), None),
        P("pipe", "dp"),
        P("pipe", "dp"),
        P("pipe", "dp"),
        P("pipe", "dp"),
        P("pipe", "dp"),
        P(("pipe", "dp"), None),
        P(("pipe", "dp"), None),
        P(("pipe", "dp"), None),
        P(("pipe", "dp"), None),
        P(("pipe", "dp"), None, None),
    )
    out_specs = (
        P(("pipe", "dp"), None, None),
        P(("pipe", "dp"), None, None),
        P("pipe", "dp"),
        P("pipe", "dp"),
        P("pipe", "dp"),
        P("pipe", "dp"),
        P("pipe", "dp"),
        P(("pipe", "dp"), None),
        P(("pipe", "dp"), None),
        P(("pipe", "dp"), None),
        P(("pipe", "dp"), None),
    )
    return jax.shard_map(
        on_device, mesh=mesh, in_specs=in_specs, out_specs=out_specs, check_vma=False
    )
```

```python
from functools import partial

import jax
import jax.numpy as jnp
import numpy as np
from jax import lax
from jax.experimental import pallas as pl
from jax.experimental.pallas import tpu as pltpu
from jax.sharding import PartitionSpec as P

HEADS = 12
NORM_EPS = 1e-12
MASKED = -1e30
BF = jnp.bfloat16
F32 = jnp.float32
NT = (((1,), (1,)), ((), ()))
NN = (((1,), (0,)), ((), ()))
TN = (((0,), (0,)), ((), ()))
VMEM_BYTES = 58 * 2**20
TILE = 768
CHUNK = 128
SMALL = 16


def dot(a, b, dims=NN):
    return lax.dot_general(a, b, dims, preferred_element_type=F32)


def span(start, size, unit=128):
    return pl.ds(pl.multiple_of(start, unit), size)


def tiles(count, body):
    def step(i, carry):
        body(i)
        return carry

    lax.fori_loop(0, count, step, 0)


class Copies:
    def __init__(self, sems):
        self.sems, self.used = sems, 0
        self.coming, self.going, self.sent = [], [], []

    def copy(self, source, target):
        self.used += 1
        copy = pltpu.make_async_copy(source, target, self.sems.at[self.used - 1])
        copy.start()
        return copy

    def begin(self, *refs):
        for k, (held, source, _) in enumerate(self.coming):
            if any(held is ref for ref in refs):
                self.coming[k] = (held, source, self.copy(source, held))

    def need(self, *refs):
        for k, (held, source, copy) in enumerate(self.coming):
            if any(held is ref for ref in refs):
                copy.wait()
                self.coming[k] = (None, source, None)

    def send(self, *refs, part=()):
        for held, target in self.going:
            if any(held is ref for ref in refs):
                self.sent.append(self.copy(held.at[part], target.at[part]) if part else self.copy(held, target))

    def finish(self):
        settle(self.sent)


def fetch(copies, sems, here=None):
    started = []
    for k in range(len(copies[0][0])):
        started.append([pltpu.make_async_copy(s[k], t, sems.at[i]) for i, (s, t) in enumerate(copies)])

    def start(group):
        for copy in group:
            copy.start()

    if len(started) == 1:
        start(started[0])
    else:
        pl.when(here)(lambda: start(started[0]))
        pl.when(jnp.logical_not(here))(lambda: start(started[1]))
    return started[0]


def settle(started):
    for copy in started:
        copy.wait()


def placed(refs, where_ref, layout, target, lanes):
    if len(refs) == 1:
        return [(refs, target)]
    core, z, y = where_ref[0], where_ref[1], where_ref[2]
    copies = []
    for i, pair in enumerate(zip(refs[:16], refs[16:])):
        c_rel, y_rel, z_rel = i // 8, (i // 4) % 2, i % 4
        block = lax.rem(z - z_rel + 4, 4) * 2 + lax.rem(y + y_rel, 2)
        side = lax.rem(core + c_rel, 2)
        for first, rows, shift in layout:
            place = target.at[
                span(block * rows, rows, 16),
                span(side * lanes + shift * pair[0].shape[1], pair[0].shape[1]),
            ]
            copies.append(([ref.at[pl.ds(first, rows)] for ref in pair], place))
    return copies


def relative(where_ref, block):
    z = lax.rem(block // 2 - where_ref[1] + 4, 4)
    return z * 2 + lax.rem(block % 2 + where_ref[2], 2)


def norm_rows(x_ref, bias, gain, offset, y_ref, low_ref, n_ref, r_ref):
    for i in range(0, y_ref.shape[0], CHUNK):
        rows = pl.ds(i, CHUNK)
        u = x_ref[rows, :].astype(F32) + (y_ref[rows, :] + bias)
        center = u - jnp.mean(u, axis=-1, keepdims=True)
        scale = lax.rsqrt(jnp.mean(center * center, axis=-1, keepdims=True) + NORM_EPS)
        normed = center * scale
        y = normed * gain + offset
        y_ref[rows, :] = y
        low_ref[rows, :] = y.astype(BF)
        n_ref[rows, :] = normed.astype(BF)
        r_ref[rows, :] = scale


def norm_rows_back(dy_ref, n_ref, r_ref, gain, du_ref, db_ref):
    def chunk(i, sums):
        rows = span(i * CHUNK, CHUNK, CHUNK)
        dy = dy_ref[rows, :].astype(F32)
        n = n_ref[rows, :].astype(F32)
        s = dy * gain
        du = r_ref[rows, :] * (
            s - jnp.mean(s, axis=-1, keepdims=True) - n * jnp.mean(s * n, axis=-1, keepdims=True)
        )
        db = du.astype(BF)
        du_ref[rows, :] = du
        db_ref[rows, :] = db
        terms = (dy * n, dy, db.astype(F32))
        return tuple(a + jnp.sum(t, axis=0, keepdims=True) for a, t in zip(sums, terms))

    zero = jnp.zeros((1, dy_ref.shape[1]), F32)
    return lax.fori_loop(0, dy_ref.shape[0] // CHUNK, chunk, (zero, zero, zero))


def split_heads(a):
    first = lax.broadcasted_iota(jnp.int32, a.shape, 1) < a.shape[1] // 2
    zero = jnp.zeros_like(a)
    return jnp.concatenate([jnp.where(first, a, zero), jnp.where(first, zero, a)], axis=0)


def join_heads(a):
    rows = a.shape[0] // 2
    first = lax.broadcasted_iota(jnp.int32, (rows, a.shape[1]), 1) < a.shape[1] // 2
    return jnp.where(first, a[:rows], a[rows:])


def softmax(scores, mask, axis):
    scores = scores + mask
    e = jnp.exp(scores - jnp.max(scores, axis=axis, keepdims=True))
    return (e * (1.0 / jnp.sum(e, axis=axis, keepdims=True))).astype(BF)


def score_back(weights, d_weights):
    a = weights.astype(F32)
    t = a * d_weights
    return (t - a * jnp.sum(t, axis=0, keepdims=True)).astype(BF)


def project_and_norm(x_ref, o_ref, w_ref, dims, bias, gain, offset, outs):
    y_ref, low_ref, n_ref, r_ref = outs
    width = y_ref.shape[1]

    def tile(j):
        cols = span(j * TILE, TILE)
        w = w_ref[cols, :] if dims is NT else w_ref[:, cols]
        y_ref[:, cols] = dot(o_ref[...], w, dims)

    tiles(width // TILE, tile)
    norm_rows(x_ref, bias, gain, offset, y_ref, low_ref, n_ref, r_ref)


def self_weights(count, layer, where_ref, refs, qkv, out, sems, sems2):
    width, whole = out.shape[1], count == 2
    n, m = qkv.shape[0] // 8, out.shape[0] // 8
    here = where_ref[3] == layer
    return (
        lambda: fetch(placed(refs[:1] if whole else refs, where_ref, [(0, n, 0)], qkv, width // 2), sems, here),
        lambda: fetch(placed(refs[1:] if whole else refs, where_ref, [(n, m, 0)], out, width // 2), sems2, here),
    )


def self_project(x_ref, vec_ref, p_ref, qkv, bias_ref):
    width = x_ref.shape[1]
    bias_ref[:, :width] = vec_ref[0:1, :]
    bias_ref[:, width : 2 * width] = jnp.zeros((1, width), F32)
    bias_ref[:, 2 * width :] = vec_ref[1:2, :]

    def tile(j):
        cols = span(j * TILE, TILE)
        p_ref[:, cols] = (dot(x_ref[...], qkv[cols, :], NT) + bias_ref[:, cols]).astype(BF)

    tiles(3 * width // TILE, tile)


def self_attend(lengths, p_ref, a_ref, o_ref):
    width = o_ref.shape[1]
    pairs = width // 128
    key = lax.broadcasted_iota(jnp.int32, (128, 256), 0)
    query = lax.broadcasted_iota(jnp.int32, (128, 256), 1)
    same = ((query // 64) % 2) == (key // 64)

    def attend(s):
        rows = span(s * 128, 128)
        length = jnp.where(key < 64, lengths[2 * s], lengths[2 * s + 1])
        mask = jnp.where(same & (lax.rem(key, 64) < length), 0.0, MASKED)
        for h in range(pairs):
            q = p_ref[rows, pl.ds(h * 128, 128)]
            k = p_ref[rows, pl.ds(width + h * 128, 128)]
            v = p_ref[rows, pl.ds(2 * width + h * 128, 128)]
            a = softmax(dot(k, split_heads(q * 0.125), NT), mask, 0)
            a_ref[s * pairs + h] = a
            o_ref[rows, pl.ds(h * 128, 128)] = join_heads(dot(a, v, TN)).astype(BF)

    tiles(o_ref.shape[0] // 128, attend)


def self_backward_kernel(count, layer, io, ins, outs, scratch):
    where_ref, dy_ref, x_ref, vec_ref, p_ref, a_ref, o_ref, n_ref, r_ref, *refs = ins
    dx_ref, own_ref, other_ref, gv_ref = outs
    qkv, out, du_ref, db_ref, dmix_ref, dp_ref, rel_ref, g_ref, sems, sems2 = scratch
    width = x_ref.shape[1]
    half = width // 2
    n, m = qkv.shape[0] // 8, out.shape[0] // 8
    whole = count == 2
    here = where_ref[3] == layer
    second = fetch(placed(refs[1:] if whole else refs, where_ref, [(n, m, 0)], out, half), sems2, here)
    io.begin(o_ref, p_ref, a_ref)
    core = where_ref[0]
    g_gain, g_offset, g_bias = norm_rows_back(dy_ref, n_ref, r_ref, vec_ref[3:4, :], du_ref, db_ref)
    settle(second)

    def mix(j):
        cols = span(j * TILE, TILE)
        dmix_ref[:, cols] = dot(db_ref[...], out[:, cols]).astype(BF)

    tiles(width // TILE, mix)
    io.need(o_ref, p_ref, a_ref)
    rel_ref[:, :half] = o_ref[:, span(core * half, half)]
    rel_ref[:, half:] = o_ref[:, span((1 - core) * half, half)]

    g_ref[:width, :] = dot(db_ref[...], rel_ref[...], TN).astype(BF)
    for b in range(8):
        to, at = relative(where_ref, b), pl.ds(b * m, m)
        own_ref[to, n : n + m, :] = g_ref[at, :half]
        other_ref[to, n : n + m, :] = g_ref[at, half:]
    io.begin(x_ref)
    first = fetch(placed(refs[:1] if whole else refs, where_ref, [(0, n, 0)], qkv, half), sems, here)
    pairs = width // 128

    def attend(s):
        rows = span(s * 128, 128)
        for h in range(pairs):
            q2 = split_heads(p_ref[rows, pl.ds(h * 128, 128)])
            k = p_ref[rows, pl.ds(width + h * 128, 128)]
            v = p_ref[rows, pl.ds(2 * width + h * 128, 128)]
            do2 = split_heads(dmix_ref[rows, pl.ds(h * 128, 128)])
            a = a_ref[s * pairs + h]
            ds = score_back(a, dot(v, do2, NT))
            dp_ref[rows, pl.ds(h * 128, 128)] = (join_heads(dot(ds, k, TN)) * 0.125).astype(BF)
            dp_ref[rows, pl.ds(width + h * 128, 128)] = (dot(ds, q2) * 0.125).astype(BF)
            dp_ref[rows, pl.ds(2 * width + h * 128, 128)] = dot(a, do2).astype(BF)

    tiles(x_ref.shape[0] // 128, attend)
    io.need(x_ref)
    rel_ref[:, :half] = x_ref[:, span(core * half, half)]
    rel_ref[:, half:] = x_ref[:, span((1 - core) * half, half)]

    def qkv_grad(j):
        rows = span(j * TILE, TILE)
        g_ref[rows, :] = dot(dp_ref[:, rows], rel_ref[...], TN).astype(BF)

    tiles(3 * width // TILE, qkv_grad)
    for b in range(8):
        to, at = relative(where_ref, b), pl.ds(b * n, n)
        own_ref[to, :n, :] = g_ref[at, :half]
        other_ref[to, :n, :] = g_ref[at, half:]
    io.send(other_ref, own_ref, part=(slice(None), pl.ds(0, n + m)))
    settle(first)

    def back(j):
        cols = span(j * TILE, TILE)
        dx_ref[:, cols] = (du_ref[:, cols] + dot(dp_ref[...], qkv[:, cols])).astype(dx_ref.dtype)

    tiles(width // TILE, back)
    gv_ref[0:1, :] = jnp.sum(dp_ref[:, :width].astype(F32), axis=0, keepdims=True)
    gv_ref[1:2, :] = jnp.sum(dp_ref[:, 2 * width :].astype(F32), axis=0, keepdims=True)
    gv_ref[2:3, :] = g_bias
    gv_ref[3:4, :] = g_gain
    gv_ref[4:5, :] = g_offset


def cross_attend(keep_ref, q_ref, k_ref, v_ref, a_ref, o_ref):
    width = o_ref.shape[1]
    patches = k_ref.shape[0] // keep_ref.shape[0]
    pairs = width // 128

    def attend(s):
        rows, keys = span(s * 64, 64, 64), span(s * patches, patches, 16)
        mask = jnp.where(keep_ref[pl.ds(s, 1), :] > 0, 0.0, MASKED)
        for h in range(pairs):
            q = q_ref[rows, pl.ds(h * 128, 128)]
            k = k_ref[keys, pl.ds(h * 128, 128)]
            v = v_ref[keys, pl.ds(h * 128, 128)]
            a = softmax(dot(split_heads(q * 0.125), k, NT), mask, 1)
            a_ref[s * pairs + h] = a.T
            o_ref[rows, pl.ds(h * 128, 128)] = join_heads(dot(a, v)).astype(BF)

    tiles(keep_ref.shape[0], attend)


def cross_backward_kernel(io, ins, outs, scratch):
    dy_ref, low_x_ref, k_ref, v_ref, vec_ref, wq_ref, wo_ref, q_ref, a_ref, o_ref, n_ref, r_ref = ins
    dx_ref, dk_ref, dv_ref, gq_ref, go_ref, gv_ref = outs
    db_ref, dmix_ref, dq_ref = scratch
    width = low_x_ref.shape[1]
    patches = a_ref.shape[1]
    io.begin(wo_ref, o_ref)
    g_gain, g_offset, g_bias = norm_rows_back(dy_ref, n_ref, r_ref, vec_ref[3:4, :], dx_ref, db_ref)

    io.begin(q_ref, k_ref, v_ref, a_ref)
    io.need(wo_ref, o_ref)

    def mix(j):
        cols = span(j * TILE, TILE)
        dmix_ref[:, cols] = dot(db_ref[...], wo_ref[cols, :], NT).astype(BF)
        go_ref[cols, :] = dot(o_ref[:, cols], db_ref[...], TN).astype(BF)

    tiles(width // TILE, mix)
    io.send(go_ref)
    io.need(q_ref, k_ref, v_ref, a_ref)
    io.begin(wq_ref, low_x_ref)
    pairs = width // 128

    def attend(s):
        rows, keys = span(s * 64, 64, 64), span(s * patches, patches, 16)
        for h in range(pairs):
            q2 = split_heads(q_ref[rows, pl.ds(h * 128, 128)])
            k = k_ref[keys, pl.ds(h * 128, 128)]
            v = v_ref[keys, pl.ds(h * 128, 128)]
            do2 = split_heads(dmix_ref[rows, pl.ds(h * 128, 128)])
            a = a_ref[s * pairs + h]
            ds = score_back(a, dot(v, do2, NT))
            dq_ref[rows, pl.ds(h * 128, 128)] = (join_heads(dot(ds, k, TN)) * 0.125).astype(BF)
            dk_ref[keys, pl.ds(h * 128, 128)] = (dot(ds, q2) * 0.125).astype(BF)
            dv_ref[keys, pl.ds(h * 128, 128)] = dot(a, do2).astype(BF)

    tiles(a_ref.shape[0] // pairs, attend)
    io.send(dk_ref, dv_ref)
    io.need(wq_ref, low_x_ref)

    def back(j):
        cols = span(j * TILE, TILE)
        dx_ref[:, cols] += dot(dq_ref[...], wq_ref[cols, :], NT)
        gq_ref[cols, :] = dot(low_x_ref[:, cols], dq_ref[...], TN).astype(BF)

    tiles(width // TILE, back)
    gv_ref[0:1, :] = jnp.sum(dq_ref[...].astype(F32), axis=0, keepdims=True)
    gv_ref[1:2, :] = jnp.sum(dv_ref[...].astype(F32), axis=0, keepdims=True)
    gv_ref[2:3, :] = g_bias
    gv_ref[3:4, :] = g_gain
    gv_ref[4:5, :] = g_offset


def gelu_parts(h):
    size = jnp.abs(h) * 0.7071067811865476
    t = 1.0 / (1.0 + 0.3275911 * size)
    e = jnp.exp(-size * size)
    poly = t * (0.254829592 + t * (-0.284496736 + t * (1.421413741 + t * (-1.453152027 + t * 1.061405429))))
    tail = 0.5 * poly * e
    cdf = jnp.where(h < 0, tail, 1.0 - tail)
    return h * cdf, cdf + h * (e * 0.3989422804014327)


def feed_weights(count, layer, where_ref, refs, up, down, sems, sems2):
    width, hidden = up.shape[1], up.shape[0]
    n, m, whole = hidden // 8, width // 8, count == 2
    base = 4 * m
    slices = [(base + n + m * i, m, i) for i in range(hidden // width)]
    here = where_ref[3] == layer
    return (
        lambda: fetch(placed(refs[:1] if whole else refs, where_ref, [(base, n, 0)], up, width // 2), sems, here),
        lambda: fetch(placed(refs[1:] if whole else refs, where_ref, slices, down, hidden // 2), sems2, here),
    )


def feed_activate(low_x_ref, up, bias_ref, act_ref, slope_ref):
    def tile(j):
        cols = span(j * TILE, TILE)
        h = dot(low_x_ref[...], up[cols, :], NT) + bias_ref[:, cols]
        act, slope = gelu_parts(h)
        act_ref[:, cols] = act.astype(BF)
        slope_ref[:, cols] = slope.astype(BF)

    tiles(up.shape[0] // TILE, tile)


def text_forward_kernel(count, io, ins, outs, scratch):
    lengths, where_ref, x_ref, vec_ref, vec2_ref, up_bias_ref, *refs = ins
    p1, a1, o1, low1, n1, act, slope, low2, n2, p2, a2, o2, r1, r2, y3, low3, n3, r3 = outs
    qkv, out, up, down, y1, y2, bias_ref, *sems = scratch
    whole = count == 6
    count = 2 if whole else count
    get_qkv, get_out = self_weights(count, 0, where_ref, refs[:2] if whole else refs, qkv, out, *sems[:2])
    get_up, get_down = feed_weights(count, 0, where_ref, refs[2:4] if whole else refs, up, down, *sems[2:])
    get_qkv2, get_out2 = self_weights(count, 1, where_ref, refs[4:] if whole else refs, qkv, out, *sems[:2])
    settle(get_qkv())
    coming = get_out()
    self_project(x_ref, vec_ref, p1, qkv, bias_ref)
    io.send(p1)
    coming_up = get_up()
    self_attend(lengths, p1, a1, o1)
    io.send(a1, o1)
    settle(coming)
    norm = vec_ref[2:3, :], vec_ref[3:4, :], vec_ref[4:5, :]
    project_and_norm(x_ref, o1, out, NT, *norm, (y1, low1, n1, r1))
    io.send(low1, n1)
    coming_down = get_down()
    settle(coming_up)
    coming = get_qkv2()
    feed_activate(low1, up, up_bias_ref, act, slope)
    io.send(act, slope)
    settle(coming_down)
    coming_out = get_out2()
    norm = vec_ref[5:6, :], vec_ref[6:7, :], vec_ref[7:8, :]
    project_and_norm(y1, act, down, NT, *norm, (y2, low2, n2, r2))
    io.send(low2, n2)
    settle(coming)
    self_project(low2, vec2_ref, p2, qkv, bias_ref)
    io.send(p2)
    self_attend(lengths, p2, a2, o2)
    io.send(a2, o2)
    settle(coming_out)
    norm = vec2_ref[2:3, :], vec2_ref[3:4, :], vec2_ref[4:5, :]
    project_and_norm(low2, o2, out, NT, *norm, (y3, low3, n3, r3))


def feed_backward_body(
    io, where_ref, dy_ref, low_x_ref, vec_ref, act_ref, slope_ref, n_ref, r_ref, outs, work, up, down, get_up, get_down
):
    dx_ref, own_ref, other_ref, gv_ref = outs
    db_ref, dbt_ref, dh_ref, rel_ref, gb_ref = work
    width, hidden = up.shape[1], up.shape[0]
    n, m, half = hidden // 8, width // 8, width // 2
    core = where_ref[0]
    second = get_down()
    io.begin(slope_ref)
    g_gain, g_offset, g_bias = norm_rows_back(dy_ref, n_ref, r_ref, vec_ref[6:7, :], dx_ref, db_ref)
    dbt_ref[...] = db_ref[...].T
    settle(second)
    io.need(slope_ref)
    io.begin(act_ref, low_x_ref)

    def down_tile(j):
        cols = span(j * TILE, TILE)
        dh = (dot(db_ref[...], down[:, cols]) * slope_ref[:, cols].astype(F32)).astype(BF)
        dh_ref[:, cols] = dh
        gb_ref[:, cols] = jnp.sum(dh.astype(F32), axis=0, keepdims=True)

    tiles(hidden // TILE, down_tile)
    io.need(act_ref)

    def down_grad(j):
        for ref, side in ((own_ref, core), (other_ref, 1 - core)):
            g = dot(dbt_ref[...], act_ref[:, span(side * (hidden // 2) + j * width, width)]).astype(BF)
            for b in range(8):
                to = relative(where_ref, b)
                for k in range(2):
                    ref[to, span(n + (2 * j + k) * m, m, 16), :] = g[b * m : (b + 1) * m, k * half : (k + 1) * half]

    tiles(hidden // 2 // width, down_grad)
    io.send(other_ref, own_ref, part=(slice(None), pl.ds(n, n)))
    first = get_up()
    io.need(low_x_ref)
    rel_ref[:, :half] = low_x_ref[:, span(core * half, half)]
    rel_ref[:, half:] = low_x_ref[:, span((1 - core) * half, half)]

    def up_grad(j):
        g = dot(dh_ref[:, span(j * 2 * n, 2 * n)], rel_ref[...], TN).astype(BF)
        for k in range(2):
            to = relative(where_ref, 2 * j + k)
            own_ref[to, :n, :] = g[k * n : (k + 1) * n, :half]
            other_ref[to, :n, :] = g[k * n : (k + 1) * n, half:]

    tiles(4, up_grad)
    io.send(other_ref, own_ref, part=(slice(None), pl.ds(0, n)))
    settle(first)

    def back(j):
        cols = span(j * TILE, TILE)
        dx_ref[:, cols] += dot(dh_ref[...], up[:, cols])

    tiles(width // TILE, back)
    gv_ref[0:1, :] = g_bias
    gv_ref[1:2, :] = g_gain
    gv_ref[2:3, :] = g_offset
    for j in range(hidden // width):
        gv_ref[3 + j : 4 + j, :] = gb_ref[:, j * width : (j + 1) * width]


def feed_backward_kernel(count, layer, io, ins, outs, scratch):
    where_ref, dy_ref, low_x_ref, vec_ref, act_ref, slope_ref, n_ref, r_ref, *refs = ins
    up, down, *work, sems, sems2 = scratch
    get = feed_weights(count, layer, where_ref, refs, up, down, sems, sems2)
    feed_backward_body(
        io, where_ref, dy_ref, low_x_ref, vec_ref, act_ref, slope_ref, n_ref, r_ref, outs, work, up, down, *get
    )


def joining_kernel(count, io, ins, outs, scratch):
    where_ref, x_ref, low_x_ref, keep_ref, k_ref, v_ref, cross_ref, wq_ref, wo_ref, vec_ref, bias_ref, dy_ref, *refs = ins
    q_ref, a_ref, o_ref, cross_n, cross_r, y_ref, *grads = outs
    up, down, *work, act_ref, slope_ref, state, low_state, low_ref, n_ref, r_ref, sems, sems2 = scratch
    get_up, get_down = feed_weights(count, 1, where_ref, refs, up, down, sems, sems2)
    width = x_ref.shape[1]
    io.begin(k_ref, v_ref)

    def tile(j):
        cols = span(j * TILE, TILE)
        q_ref[:, cols] = (dot(low_x_ref[...], wq_ref[:, cols]) + cross_ref[0:1, cols]).astype(BF)

    tiles(width // TILE, tile)
    io.need(k_ref, v_ref)
    io.begin(x_ref, wo_ref)
    first = get_up()
    cross_attend(keep_ref, q_ref, k_ref, v_ref, a_ref, o_ref)
    io.send(q_ref, a_ref, o_ref)
    io.need(x_ref, wo_ref)
    norm = cross_ref[2:3, :], cross_ref[3:4, :], cross_ref[4:5, :]
    project_and_norm(x_ref, o_ref, wo_ref, NN, *norm, (state, low_state, cross_n, cross_r))
    io.send(cross_n)
    second = get_down()
    settle(first)
    feed_activate(low_state, up, bias_ref, act_ref, slope_ref)
    settle(second)
    norm = vec_ref[5:6, :], vec_ref[6:7, :], vec_ref[7:8, :]
    project_and_norm(state, act_ref, down, NT, *norm, (y_ref, low_ref, n_ref, r_ref))
    io.send(y_ref)
    feed_backward_body(
        io, where_ref, dy_ref, low_state, vec_ref, act_ref, slope_ref, n_ref, r_ref, grads, work, up, down, list, list
    )


def vector_kernel(first, v_rows, v_lanes, x_rows, c_rows, *refs):
    where_ref, *pieces = refs[:33]
    vec_refs, bias_refs, cross_ref = refs[33:35], refs[35:37], refs[37]
    held, sems = refs[38:]
    core, z, y, x = where_ref[0], where_ref[1], where_ref[2], where_ref[3]
    copies = []
    for i, ref in enumerate(pieces):
        x_rel, c_rel, y_rel, z_rel = i // 16, (i // 8) % 2, (i // 4) % 2, i % 4
        pipe = lax.rem(x + x_rel, 2) * 2 + lax.rem(core + c_rel, 2)
        device = pipe * 8 + lax.rem(z - z_rel + 4, 4) * 2 + lax.rem(y + y_rel, 2)
        copies.append(([ref.at[pl.ds(first, 16), pl.ds(0, 128)]], held.at[device]))
    settle(fetch(copies, sems))
    for device in range(32):
        block = held[device].astype(F32)
        pipe, dp = device // 8, device % 8
        rows = pl.ds(pipe % 2 * v_rows, v_rows)
        vec_refs[pipe // 2][rows, pl.ds(dp * v_lanes, v_lanes)] = block[:v_rows, :v_lanes]
        cross_ref[0:x_rows, pl.ds(device * c_rows, c_rows)] = block[v_rows : v_rows + x_rows, :c_rows]
    width = cross_ref.shape[1]
    for vec_ref, bias_ref in zip(vec_refs, bias_refs):
        for j in range(4):
            bias_ref[:, j * width : (j + 1) * width] = vec_ref[8 + j : 9 + j, :]


def struct(*shape, dtype=F32):
    return jax.ShapeDtypeStruct(shape, dtype)


VMEM = pl.BlockSpec(memory_space=pltpu.VMEM)
SMEM = pl.BlockSpec(memory_space=pltpu.SMEM)
ANYWHERE = pl.BlockSpec(memory_space=pl.ANY)


def call(kernel, outs, specs, scratch, us, args, late=(), early=(), packs=(), layer=0, onto=None):
    n_in, n_out, n_scratch = len(args), len(outs), len(scratch)
    early = (*early, *packs)
    held = [pltpu.VMEM(args[i].shape, args[i].dtype) for i in late]
    held += [pltpu.VMEM(outs[i].shape, outs[i].dtype) for i in early]
    outs = [struct(2, *o.shape, dtype=o.dtype) if i in packs else o for i, o in enumerate(outs)]
    taken = tuple(onto) if onto else ()
    n_all = n_in + len(taken)

    def body(*refs):
        ins, out, rest = list(refs[:n_in]), list(refs[n_all : n_all + n_out]), refs[n_all + n_out :]
        buffers = rest[n_scratch:-1]
        io = Copies(rest[-1])
        for k, i in enumerate(late):
            io.coming.append((buffers[k], ins[i], None))
            ins[i] = buffers[k]
        for k, i in enumerate(early, len(late)):
            target = out[i].at[lax.rem(ins[0][3] + layer, 2)] if i in packs else out[i]
            io.going.append((buffers[k], target))
            out[i] = buffers[k]
        kernel(io, ins, out, rest[:n_scratch])
        io.finish()

    specs = [ANYWHERE if i in late else spec for i, spec in enumerate(specs)] + [ANYWHERE] * len(taken)
    return pl.pallas_call(
        body,
        out_shape=outs,
        in_specs=specs,
        out_specs=[ANYWHERE if i in early else VMEM for i in range(n_out)],
        scratch_shapes=[*scratch, *held, pltpu.SemaphoreType.DMA((24,))],
        input_output_aliases={n_in + k: i for k, i in enumerate(packs)} if taken else {},
        cost_estimate=pl.CostEstimate(flops=int(us * 1.1e9), bytes_accessed=int(us * 3.5e6), transcendentals=0),
        compiler_params=pltpu.CompilerParams(vmem_limit_bytes=VMEM_BYTES),
    )(*args, *taken)


def gathered_vectors(pieces, where, first, v_rows, v_lanes, x_rows, c_rows):
    width = 8 * v_lanes
    return pl.pallas_call(
        partial(vector_kernel, first, v_rows, v_lanes, x_rows, c_rows),
        out_shape=[struct(12, width)] * 2 + [struct(1, 4 * width)] * 2 + [struct(8, width)],
        in_specs=[SMEM] + [ANYWHERE] * len(pieces),
        out_specs=[VMEM] * 5,
        scratch_shapes=[pltpu.VMEM((32, 16, 128), BF), pltpu.SemaphoreType.DMA((32,))],
        cost_estimate=pl.CostEstimate(flops=0, bytes_accessed=10**7, transcendentals=0),
    )(where, *pieces)


def copy_sems(count, parts=1):
    return pltpu.SemaphoreType.DMA((16 * parts if count > 2 else 1,))


def text_forward(x, lengths, where, vecs, bias, weights):
    rows, width = x.shape
    hidden = bias.shape[1]
    blocks = rows // 128 * (width // 128)
    count = len(weights)
    low = struct(rows, width, dtype=BF)
    attention = [struct(rows, 3 * width, dtype=BF), struct(blocks, 128, 256, dtype=BF), low]
    outs = [
        *attention,
        low,
        low,
        struct(rows, hidden, dtype=BF),
        struct(rows, hidden, dtype=BF),
        low,
        low,
        *attention,
        struct(rows, 1),
        struct(rows, 1),
        struct(rows, width),
        low,
        low,
        struct(rows, 1),
    ]
    scratch = [
        pltpu.VMEM((3 * width, width), BF),
        pltpu.VMEM((width, width), BF),
        pltpu.VMEM((hidden, width), BF),
        pltpu.VMEM((width, hidden), BF),
        pltpu.VMEM((rows, width), F32),
        pltpu.VMEM((rows, width), F32),
        pltpu.VMEM((1, 3 * width), F32),
        copy_sems(count),
        copy_sems(count),
        copy_sems(count),
        copy_sems(count, hidden // width),
    ]
    p1, a1, o1, low1, n1, act, slope, low2, n2, p2, a2, o2, r1, r2, y3, low3, n3, r3 = call(
        partial(text_forward_kernel, count),
        outs,
        [SMEM, SMEM] + [VMEM] * 4 + [ANYWHERE] * count,
        scratch,
        38,
        (lengths, where, x, *vecs, bias, *weights),
        early=tuple(range(12)),
    )
    return y3, low3, (x, p1, a1, o1, n1, r1), (low1, act, slope, n2, r2), (low2, p2, a2, o2, n3, r3)


def self_backward(dy, saved, where, vec, weights, layer, dtype=F32, onto=None):
    x, p, a, o, n, r = saved
    rows, width = x.shape
    half = width // 2
    count = len(weights)
    outs = [
        struct(rows, width, dtype=dtype),
        struct(8, width // 2 + SMALL, half, dtype=BF),
        struct(8, width // 2 + SMALL, half, dtype=BF),
        struct(8, width),
    ]
    scratch = [
        pltpu.VMEM((3 * width, width), BF),
        pltpu.VMEM((width, width), BF),
        pltpu.VMEM((rows, width), F32),
        pltpu.VMEM((rows, width), BF),
        pltpu.VMEM((rows, width), BF),
        pltpu.VMEM((rows, 3 * width), BF),
        pltpu.VMEM((rows, width), BF),
        pltpu.VMEM((3 * width, width), BF),
        copy_sems(count),
        copy_sems(count),
    ]
    return call(
        partial(self_backward_kernel, count, layer),
        outs,
        [SMEM] + [VMEM] * 8 + [ANYWHERE] * count,
        scratch,
        22,
        (where, dy, x, vec, p, a, o, n, r, *weights),
        late=(6, 4, 5, 2),
        packs=(1, 2),
        layer=layer,
        onto=onto,
    )


def cross_backward(dy, saved, vec, wq, wo):
    low_x, k, v, q, a, o, n, r = saved
    rows, width = low_x.shape
    outs = [
        struct(rows, width),
        struct(*k.shape, dtype=BF),
        struct(*k.shape, dtype=BF),
        struct(width, width, dtype=BF),
        struct(width, width, dtype=BF),
        struct(8, width),
    ]
    scratch = [pltpu.VMEM((rows, width), BF)] * 3
    return call(
        cross_backward_kernel,
        outs,
        [VMEM] * 12,
        scratch,
        26,
        (dy, low_x, k, v, vec, wq, wo, q, a, o, n, r),
        late=(6, 9, 7, 2, 3, 8, 5, 1),
        early=(1, 2, 4),
    )


def feed_backward(dy, saved, where, vec, weights, layer, onto=None):
    low_x, act, slope, n, r = saved
    rows, width = low_x.shape
    hidden = act.shape[1]
    count = len(weights)
    outs = [
        struct(rows, width),
        struct(8, 2 * hidden // 8, width // 2, dtype=BF),
        struct(8, 2 * hidden // 8, width // 2, dtype=BF),
        struct(8, width),
    ]
    scratch = [
        pltpu.VMEM((hidden, width), BF),
        pltpu.VMEM((width, hidden), BF),
        pltpu.VMEM((rows, width), BF),
        pltpu.VMEM((width, rows), BF),
        pltpu.VMEM((rows, hidden), BF),
        pltpu.VMEM((rows, width), BF),
        pltpu.VMEM((1, hidden), F32),
        copy_sems(count),
        copy_sems(count, hidden // width),
    ]
    return call(
        partial(feed_backward_kernel, count, layer),
        outs,
        [SMEM] + [VMEM] * 7 + [ANYWHERE] * count,
        scratch,
        22,
        (where, dy, low_x, vec, act, slope, n, r, *weights),
        late=(5, 4, 2),
        packs=(1, 2),
        layer=layer,
        onto=onto,
    )


def joining(x, low_x, where, keep, k, v, cross_vec, wq, wo, vec, bias, dy, weights):
    rows, width = x.shape
    samples, patches = keep.shape
    hidden = bias.shape[1]
    count = len(weights)
    low = struct(rows, width, dtype=BF)
    pack = struct(8, 2 * hidden // 8, width // 2, dtype=BF)
    outs = [
        low,
        struct(samples * (width // 128), patches, 128, dtype=BF),
        low,
        low,
        struct(rows, 1),
        struct(rows, width),
        struct(rows, width),
        pack,
        pack,
        struct(8, width),
    ]
    scratch = [
        pltpu.VMEM((hidden, width), BF),
        pltpu.VMEM((width, hidden), BF),
        pltpu.VMEM((rows, width), BF),
        pltpu.VMEM((width, rows), BF),
        pltpu.VMEM((rows, hidden), BF),
        pltpu.VMEM((rows, width), BF),
        pltpu.VMEM((1, hidden), F32),
        pltpu.VMEM((rows, hidden), BF),
        pltpu.VMEM((rows, hidden), BF),
        pltpu.VMEM((rows, width), F32),
        pltpu.VMEM((rows, width), BF),
        pltpu.VMEM((rows, width), BF),
        pltpu.VMEM((rows, width), BF),
        pltpu.VMEM((rows, 1), F32),
        copy_sems(count),
        copy_sems(count, hidden // width),
    ]
    q, a, o, n, r, joined, dx, own, other, gv = call(
        partial(joining_kernel, count),
        outs,
        [SMEM] + [VMEM] * 11 + [ANYWHERE] * count,
        scratch,
        48,
        (where, x, low_x, keep, k, v, cross_vec, wq, wo, vec, bias, dy, *weights),
        late=(4, 5, 8, 1),
        early=(0, 1, 2, 3, 5),
        packs=(7, 8),
        layer=1,
    )
    return (low_x, k, v, q, a, o, n, r), joined, dx, own, other, gv


def lane_slices(a, lanes):
    return jnp.concatenate([a[:, i : i + lanes] for i in range(0, a.shape[1], lanes)], axis=0)


def lane_join(a, count):
    rows = a.shape[-2] // count
    return jnp.concatenate([a[..., i * rows : (i + 1) * rows, :] for i in range(count)], axis=-1)


def pad_to(a, rows, lanes):
    return jnp.pad(a, ((0, rows - a.shape[0]), (0, lanes - a.shape[1])))


def dynamic(a, index, axis):
    return lax.dynamic_index_in_dim(a, index, axis, keepdims=False)


def after(value, tokens):
    return lax.optimization_barrier((value, tokens))[0] if tokens else value


class Grid:
    def __init__(self):
        pipe, dp = lax.axis_index("pipe"), lax.axis_index("dp")
        self.x, self.core = pipe // 2, pipe % 2
        self.z, self.y = dp // 2, dp % 2
        self.arrived, self.computed, self.slack = [()] * 2, (), 1

    def swap_x(self, a):
        return lax.ppermute(a, "pipe", [(i, i ^ 2) for i in range(4)])

    def swap_core(self, a):
        return lax.ppermute(a, "pipe", [(i, i ^ 1) for i in range(4)])

    def swap_y(self, a):
        return lax.ppermute(a, "dp", [(i, i ^ 1) for i in range(8)])

    def ring_z(self, a, step=1):
        return lax.ppermute(a, "dp", [(i, (i + 2 * step) % 8) for i in range(8)])

    def by_distance(self, a):
        for axis, place in ((0, self.x), (1, self.core), (3, self.y)):
            a = jnp.where(place == 0, a, jnp.flip(a, axis))
        return lax.dynamic_slice_in_dim(jnp.concatenate([a, a], axis=2), self.z, 4, 2)

    def turn(self, *moves, pre=(), compute=None, args=(), chain=False):
        tokens = (*self.arrived[-self.slack], *self.computed)
        arrived = []

        def begin(asked):
            asked = [ask for group in asked for ask in group()]
            values = after([value for _, value, _ in asked], tokens)
            results = []
            for i, ((move, _, keep), value) in enumerate(zip(asked, values)):
                results.append(move(after(value, (results[i - 2],)) if chain and i >= 5 else value))
                keep(results[-1])
            arrived.extend(results)
            return tuple(values)

        begin(pre)
        values = begin(moves)
        self.arrived.append(tuple(arrived))
        self.computed = ()
        if compute is None:
            return None
        result = compute(*after(tuple(args), tokens + values))
        self.computed = tuple(jax.tree.leaves(result))
        return result


class Gather:
    def __init__(self, grid, piece):
        self.grid, self.here, self.swapped = grid, {(0, 0, 0): piece}, {}

    def get(self, layer, y, z, over):
        sources = {"z": (layer, y, z - 1), "y": (layer, 1 - y, z), "x": (1 - layer, y, z)}
        move = {"z": self.grid.ring_z, "y": self.grid.swap_y, "x": self.grid.swap_x}[over]
        return lambda: [(move, self.here[sources[over]], partial(self.here.__setitem__, (layer, y, z)))]

    def c(self, count=16):
        ready = [key for key in self.here if key not in self.swapped][:count]
        return [(self.grid.swap_core, self.here[key], partial(self.swapped.__setitem__, key)) for key in ready]

    def c3(self):
        return self.c(3)

    def pieces(self):
        keys = [[(layer, y, z) for y in range(2) for z in range(4)] for layer in range(2)]
        return [held[key] for half in keys for held in (self.here, self.swapped) for key in half]


class PairSum:
    def __init__(self, grid, own, other):
        self.grid, self.other = grid, other
        self.own = own.reshape((2, 4, 2) + own.shape[2:])
        self.came, self.got = None, {}

    def c(self):
        def keep(a):
            self.came = a.reshape(self.own.shape)

        return [(self.grid.swap_core, self.other, keep)]

    def block(self, own, y, z):
        layer = 0 if own else 1
        parts = [self.own[layer, z, y], self.came[layer, z, y], *self.got.get((own, y, z), [])]
        return sum(parts[1:], parts[0])

    def move(self, over, own, y, z):
        to = {"z": (own, y, z - 1), "y": (own, 1 - y, z), "x": (True, y, z)}[over]
        move = {"z": self.grid.ring_z, "y": self.grid.swap_y, "x": self.grid.swap_x}[over]

        def ask():
            return [(move, self.block(own, y, z).astype(BF), self.got.setdefault(to, []).append)]

        return ask

    def steps(self):
        own, other = partial(self.move, own=True), partial(self.move, own=False)
        return [
            (other("z", y=0, z=2), other("y", y=1, z=3), other("x", y=1, z=2)),
            (other("z", y=1, z=1), own("y", y=1, z=3), other("x", y=0, z=3)),
            (own("z", y=0, z=3), own("y", y=1, z=2), other("x", y=1, z=0)),
            (own("z", y=0, z=2), own("y", y=1, z=1), other("x", y=0, z=1)),
            (own("z", y=0, z=1), own("y", y=1, z=0), other("x", y=0, z=0)),
        ]

    def total(self):
        return self.block(True, 0, 0).astype(F32)


class BlockSum:
    def __init__(self, grid, own, other, dtype):
        self.grid, self.own, self.other, self.dtype = grid, own, other, dtype
        self.ring = []

    def step(self, swap, place, axis):
        own = dynamic(self.a, place, axis)

        def keep(came):
            self.a = own.astype(F32) + came.astype(F32)

        return [(swap, dynamic(self.a, 1 - place, axis).astype(self.dtype), keep)]

    def c(self):
        def keep(came):
            self.a = self.own.astype(F32) + came.astype(F32)

        return [(self.grid.swap_core, self.other, keep)]

    def x0(self):
        self.halves = [dynamic(self.a, place, 0) for place in (self.grid.x, 1 - self.grid.x)]
        return self.x_half(0)

    def x1(self):
        return self.x_half(1)

    def x_half(self, k):
        own, other = (h[2 * k : 2 * k + 2] for h in self.halves)

        def keep(came):
            total = own.astype(F32) + came.astype(F32)
            self.a = total if k == 0 else jnp.concatenate([self.a, total])

        return [(self.grid.swap_x, other.astype(self.dtype), keep)]

    def y(self):
        return self.step(self.grid.swap_y, self.grid.y, 1)

    def round(self):
        value = self.block(3 - len(self.ring))
        return [(self.grid.ring_z, value.astype(self.dtype), self.ring.append)]

    def block(self, step):
        value = dynamic(self.a, (self.grid.z + step) % 4, 0).astype(F32)
        return value + self.ring[-1].astype(F32) if self.ring else value

    def total(self):
        return self.block(0)


def masks(caption_len, phrase_len, box_count, patch_mask, text_rows, patches):
    slots = jnp.arange(phrase_len.shape[1], dtype=jnp.int32)
    phrase_total = jnp.sum(jnp.where(slots[None, :] < box_count[:, None], phrase_len, 0), axis=1)
    lengths = jnp.minimum(caption_len + phrase_total, text_rows)
    first_patch = (jnp.arange(patch_mask.shape[1], dtype=jnp.int32) == 0).astype(jnp.int32)
    keep = jnp.maximum(patch_mask, first_patch[None, :]).astype(F32)
    return lengths, jnp.pad(keep, ((0, 0), (0, patches - keep.shape[1])))


def on_device(
    text_embed,
    image_feats,
    caption_len,
    phrase_len,
    box_count,
    patch_mask,
    attn_qkv,
    attn_out,
    ffn_up,
    ffn_down,
    layer_vectors,
    cross_query,
    cross_kv,
    cross_out,
    cross_vectors,
    cotangent,
):
    n_pipe, n_dp = lax.axis_size("pipe"), lax.axis_size("dp")
    everyone = ("pipe", "dp")
    shards, half = n_pipe * n_dp, n_pipe // 2
    samples, text_rows, width = text_embed.shape
    hidden = ffn_up.shape[1] * n_dp
    lanes = attn_qkv.shape[0]
    patches = -(-image_feats.shape[1] // 32) * 32
    direct = (n_pipe, n_dp) == (4, 8) and lanes % 128 == 0
    lengths, patch_keep = masks(caption_len, phrase_len, box_count, patch_mask, text_rows, patches)
    x = text_embed.reshape(-1, width)

    def padded(image_feats):
        wide = jnp.pad(image_feats, ((0, 0), (0, patches - image_feats.shape[1]), (0, 0)))
        return wide.reshape(samples * patches, -1)


    c_rows = cross_query.shape[0]
    kv_slices = cross_kv.shape[1] // width
    cross_pack = jnp.concatenate([cross_query, cross_out, lane_slices(cross_kv, width)], axis=0)
    v_rows, v_lanes = layer_vectors.shape
    x_rows = cross_vectors.shape[1]
    small = jnp.concatenate([pad_to(layer_vectors, v_rows, 128), pad_to(cross_vectors.T, x_rows, 128)], axis=0)
    small = pad_to(small, 16, 128)
    pack_attn = jnp.concatenate([attn_qkv.T, attn_out.T], axis=0)
    pack_feed = jnp.concatenate([ffn_up.T, lane_slices(ffn_down.T, lanes)], axis=0)
    n_pack = pack_attn.shape[0] + pack_feed.shape[0]

    def cross_weights(blocks):
        blocks = blocks.reshape(shards, -1, width)
        i_rows = cross_kv.shape[0]
        ends = np.cumsum([0, c_rows, c_rows, i_rows, i_rows])
        return [blocks[:, a:b].reshape(-1, width) for a, b in zip(ends[:-1], ends[1:])]

    def vectors_of(blocks):
        blocks = blocks.reshape(n_pipe, n_dp, 16, 128).astype(F32)
        vecs = []
        for layer in range(2):
            v = blocks[layer * half : (layer + 1) * half, :, :v_rows, :v_lanes]
            vecs.append(jnp.moveaxis(v, 1, 2).reshape(12, width))
        cvec = blocks.reshape(shards, 16, 128)[:, v_rows : v_rows + x_rows, :c_rows]
        return vecs, [v[8:12].reshape(1, hidden) for v in vecs], jnp.moveaxis(cvec, 1, 0).reshape(x_rows, width)

    def keys_values(image, wk, wv, cvec):
        keys = jnp.dot(image, wk, preferred_element_type=F32).astype(BF)
        return keys, (jnp.dot(image, wv, preferred_element_type=F32) + cvec[1]).astype(BF)

    def pack_cross(image, dk, dv, g_cq, g_co):
        grads = [g_cq, g_co, dot(image, dk, TN).astype(BF), dot(image, dv, TN).astype(BF)]
        return [g.reshape(shards, -1, width) for g in grads]

    def vector_block(v_self, v_feed):
        v = jnp.concatenate([v_self[:5], v_feed[:7]], axis=0)
        return jnp.moveaxis(v.reshape(half, v_rows, n_dp, v_lanes), 2, 1)

    def pack_vectors(text, joining, v_cross):
        section = jnp.concatenate([vector_block(*text), vector_block(*joining)], axis=0)
        cross = jnp.moveaxis(v_cross[:x_rows].reshape(x_rows, n_pipe, n_dp, c_rows), 0, 2)
        wide = [jnp.pad(v, ((0, 0), (0, 0), (0, 0), (0, 128 - v.shape[3]))) for v in (section, cross)]
        wide = jnp.concatenate(wide, axis=2)
        return jnp.pad(wide, ((0, 0), (0, 0), (0, 16 - wide.shape[2]), (0, 0)))

    seed = cotangent.reshape(-1, width)
    if direct:
        grid = Grid()
        turn = grid.turn
        where = jnp.stack([grid.core, grid.z, grid.y, grid.x]).astype(jnp.int32)
        gather = Gather(grid, jnp.concatenate([pack_attn, pack_feed, pad_to(small, 16, lanes)]))
        get = gather.get
        turn(get(0, 0, 1, "z"), get(0, 1, 0, "y"), get(1, 0, 0, "x"), gather.c3, chain=True)
        grid.slack = 2
        image = turn(
            get(0, 0, 2, "z"), get(0, 1, 1, "y"), get(1, 0, 1, "x"), gather.c3, chain=True, compute=padded, args=(image_feats,)
        )
        turn(get(0, 0, 3, "z"), get(0, 1, 2, "y"), get(1, 1, 0, "x"), gather.c3, chain=True)
        turn(get(1, 1, 1, "z"), get(0, 1, 3, "y"), get(1, 0, 3, "x"), gather.c3, chain=True)
        turn(get(1, 0, 2, "z"), get(1, 1, 3, "y"), get(1, 1, 2, "x"), gather.c3, chain=True)
        turn(gather.c)
        grid.slack = 1
        weights = gather.pieces()
        cross_whole = lax.all_gather(after(cross_pack, grid.arrived[-3]), everyone, axis=0, tiled=True)
        *vectors, cvec = gathered_vectors(weights, where, n_pack, v_rows, v_lanes, x_rows, c_rows)
        vecs, biases = vectors[:2], vectors[2:]
        state, low, s_self, s_feed, s_self2 = text_forward(x, lengths, where, vecs, biases[0], weights)
        wq, wo, wk, wv = cross_weights(cross_whole)
        keys, values = keys_values(image, wk, wv, cvec)
        s_cross, joined, grad, *g_feed2, v_feed2 = joining(
            state, low, where, patch_keep, keys, values, cvec, wq, wo, vecs[1], biases[1], seed, weights
        )
        grid.computed = (grad,)

        def fourth(grad):
            grad, dk, dv, g_cq, g_co, v_cross = cross_backward(grad, s_cross, cvec, wq, wo)
            return grad, v_cross, pack_cross(image, dk, dv, g_cq, g_co)

        grad, v_cross, cross_grads = fourth(grad)
        cross_grads = [g.reshape(2, 2, 4, 2, -1, width) for g in cross_grads]
        halves = [jnp.concatenate([dynamic(g, c, 1) for g in cross_grads], axis=3) for c in (grid.core, 1 - grid.core)]
        sum_cross = BlockSum(grid, *halves, BF)
        turn(sum_cross.c)
        grad, *g_self, v_self2 = turn(
            sum_cross.x0,
            compute=lambda grad: self_backward(grad, s_self2, where, vecs[1], weights, 1, BF), args=(grad,),
        )
        grad, *g_feed, v_feed = turn(
            sum_cross.x1,
            compute=lambda grad: feed_backward(grad, s_feed, where, vecs[0], weights, 0, g_feed2), args=(grad,),
        )
        feed = PairSum(grid, *g_feed)
        embed_grad, *g_self, v_self = turn(
            feed.c, sum_cross.y,
            compute=lambda grad: self_backward(grad, s_self, where, vecs[0], weights, 0, F32, g_self), args=(grad,),
        )
        vectors = pack_vectors((v_self, v_feed), (v_self2, v_feed2), v_cross)
        vectors = grid.by_distance(vectors.reshape(2, 2, 4, 2, SMALL, 128))
        rows = g_self[0].shape[2] - SMALL
        for k in range(2):
            small = jnp.pad(vectors[:, k].reshape(2, 8, SMALL, 128), ((0, 0), (0, 0), (0, 0), (0, lanes - 128)))
            g_self[k] = lax.dynamic_update_slice(g_self[k], small.astype(BF), (0, 0, rows, 0))
        attn = PairSum(grid, *g_self)
        f0, f1, f2, f3, f4 = feed.steps()
        a0, a1, a2, a3, a4 = attn.steps()
        turn(*f0, attn.c, sum_cross.round)
        turn(*f1)
        grid.slack = 2
        turn(*a0)
        turn(*f2)
        turn(*a1)
        turn(*f3)
        turn(*a2, sum_cross.round)
        turn(*f4)
        turn(*a3, sum_cross.round)
        turn(*a4)
        attn_grads, feed_grads = attn.total(), feed.total()
        n_qkv, n_up = attn_qkv.shape[1], ffn_up.shape[1]
        mine = [attn_grads[:n_qkv], attn_grads[n_qkv:rows], feed_grads[:n_up], feed_grads[n_up:]]
        cross_grads, small = sum_cross.total(), attn_grads[rows:, :128]
    else:
        where = jnp.zeros((4,), jnp.int32)
        image = padded(image_feats)
        vectors = lax.all_gather(small, everyone, axis=0, tiled=False)
        whole = lax.all_gather(jnp.concatenate([pack_attn, pack_feed], axis=0), everyone, axis=0, tiled=False)
        whole = whole.reshape(n_pipe, n_dp, -1, lanes)

        def section(piece, layer):
            piece = jnp.moveaxis(piece[layer * half : (layer + 1) * half], 0, 2)
            return piece.reshape(n_dp * piece.shape[1], half * piece.shape[-1])

        counts = [attn_qkv.shape[1], attn_out.shape[1], ffn_up.shape[1], attn_out.shape[1] * (hidden // width)]
        ends = np.cumsum([0] + counts)
        cut = [whole[:, :, a:b] for a, b in zip(ends[:-1], ends[1:])]
        cut[3] = lane_join(cut[3], hidden // width)
        (qkv1, out1, up1, down1), (qkv2, out2, up2, down2) = ([section(c, k) for c in cut] for k in range(2))
        vecs, biases, cvec = vectors_of(vectors)
        wq, wo, wk, wv = cross_weights(lax.all_gather(cross_pack, everyone, axis=0, tiled=False))
        state, low, s_self, s_feed, s_self2 = text_forward(
            x, lengths, where, vecs, biases[0], [qkv1, out1, up1, down1, qkv2, out2]
        )
        keys, values = keys_values(image, wk, wv, cvec)
        s_cross, joined, grad, *g_feed2, v_feed2 = joining(
            state, low, where, patch_keep, keys, values, cvec, wq, wo, vecs[1], biases[1], seed, [up2, down2]
        )
        grad, dk, dv, g_cq, g_co, v_cross = cross_backward(grad, s_cross, cvec, wq, wo)
        grad, *g_self, v_self2 = self_backward(grad, s_self2, where, vecs[1], [qkv2, out2], 1, BF)
        grad, *g_feed, v_feed = feed_backward(grad, s_feed, where, vecs[0], [up1, down1], 0, g_feed2)
        embed_grad, *g_self, v_self = self_backward(grad, s_self, where, vecs[0], [qkv1, out1], 0, F32, g_self)
        g_self1, g_self2 = ([g[k] for g in g_self] for k in range(2))
        g_feed1, g_feed2 = ([g[k] for g in g_feed] for k in range(2))

        def unpack(pair, rows, slices):
            parts = []
            at = 0
            for r, k in zip(rows, slices):
                sides = [p[:, at : at + r * k] for p in pair]
                sides = [lane_join(p, k).reshape(8 * r, -1) for p in sides]
                parts.append(jnp.concatenate(sides, axis=1))
                at += r * k
            return parts

        def split(first, second):
            both = jnp.stack([first, second])
            rows, k = both.shape[1] // n_dp, both.shape[2] // (half * lanes)
            both = both.reshape(2, n_dp, rows, half, k, lanes)
            return both.transpose(0, 3, 1, 4, 2, 5).reshape(n_pipe, n_dp, k * rows, lanes)

        attn = ((3 * width // 8, width // 8), (1, 1))
        feed = ((hidden // 8, width // 8), (1, hidden // width))
        parts = []
        for first, second, shape in ((g_self1, g_self2, attn), (g_feed1, g_feed2, feed)):
            parts += [split(a, b) for a, b in zip(unpack(first, *shape), unpack(second, *shape))]
        packed = jnp.concatenate(parts, axis=2).reshape(-1, lanes)
        packed = lax.psum_scatter(packed, everyone, scatter_dimension=0, tiled=True).astype(F32)
        mine = [packed[a:b] for a, b in zip(ends[:-1], ends[1:])]
        cross_grads = jnp.concatenate(pack_cross(image, dk, dv, g_cq, g_co), axis=1).reshape(-1, width)
        cross_grads = lax.psum_scatter(cross_grads, everyone, scatter_dimension=0, tiled=True).astype(F32)
        small = pack_vectors((v_self, v_feed), (v_self2, v_feed2), v_cross)
        small = lax.psum_scatter(small.reshape(-1, 128), everyone, scatter_dimension=0, tiled=True)
    mine[3] = lane_join(mine[3], hidden // width)
    return (
        joined.reshape(text_embed.shape),
        embed_grad.reshape(text_embed.shape),
        mine[0].T,
        mine[1].T,
        mine[2].T,
        mine[3].T,
        small[:v_rows, :v_lanes],
        cross_grads[:c_rows],
        lane_join(cross_grads[2 * c_rows :], kv_slices),
        cross_grads[c_rows : 2 * c_rows],
        small[v_rows : v_rows + x_rows, :c_rows].T,
    )


def solution(mesh):
    in_specs = (
        P(("pipe", "dp"), None, None),
        P(("pipe", "dp"), None, None),
        P(("pipe", "dp")),
        P(("pipe", "dp"), None),
        P(("pipe", "dp")),
        P(("pipe", "dp"), None),
        P("pipe", "dp"),
        P("pipe", "dp"),
        P("pipe", "dp"),
        P("pipe", "dp"),
        P("pipe", "dp"),
        P(("pipe", "dp"), None),
        P(("pipe", "dp"), None),
        P(("pipe", "dp"), None),
        P(("pipe", "dp"), None),
        P(("pipe", "dp"), None, None),
    )
    out_specs = (
        P(("pipe", "dp"), None, None),
        P(("pipe", "dp"), None, None),
        P("pipe", "dp"),
        P("pipe", "dp"),
        P("pipe", "dp"),
        P("pipe", "dp"),
        P("pipe", "dp"),
        P(("pipe", "dp"), None),
        P(("pipe", "dp"), None),
        P(("pipe", "dp"), None),
        P(("pipe", "dp"), None),
    )
    return jax.shard_map(
        on_device, mesh=mesh, in_specs=in_specs, out_specs=out_specs, check_vma=False
    )
```
